32 devices in a mesh: ctx: 8 (over z, y), fsdp: 4 (over x, core).
Axes of the slice: x: 2, y: 2, z: 4, core: 2. Of those that a mesh axis runs over, the one named last changes fastest.
Arguments:
- tokens: bfloat16 [4096, 1536], P(('ctx', 'fsdp')), may hold values from -6 to 6
- lengths: int32 [4], replicated, may hold values from 1 to 3840, 4096 in all
- wq: bfloat16 [1536, 1536], P('fsdp'), may hold values from -0.15625 to 0.15625
- wk: bfloat16 [1536, 512], P('fsdp'), may hold values from -0.15625 to 0.15625
- wv: bfloat16 [1536, 512], P('fsdp'), may hold values from -0.15625 to 0.15625
- wo: bfloat16 [1536, 1536], P('fsdp'), may hold values from -1.25 to 1.25
- w_gate: bfloat16 [1536, 6912], P('fsdp'), may hold values from -0.15625 to 0.15625
- w_up: bfloat16 [1536, 6912], P('fsdp'), may hold values from -0.15625 to 0.15625
- w_down: bfloat16 [6912, 1536], P('fsdp'), may hold values from -0.078125 to 0.078125
- attn_gain: bfloat16 [1536], P('fsdp'), may hold values from 0.099609375 to 1.8984375
- ffn_gain: bfloat16 [1536], P('fsdp'), may hold values from 0.099609375 to 1.8984375
- q_gain: bfloat16 [64], P('fsdp'), may hold values from 0.099609375 to 1.8984375
- key_norm_gain: bfloat16 [64], P('fsdp'), may hold values from 0.099609375 to 1.8984375
- cotangent: bfloat16 [4096, 1536], P(('ctx', 'fsdp')), may hold values from -6 to 6
Outputs:
- layer_out: bfloat16 [4096, 1536], P(('ctx', 'fsdp'))
- tokens_grad: bfloat16 [4096, 1536], P(('ctx', 'fsdp'))
- wq_grad: float32 [1536, 1536], P('fsdp')
- wk_grad: float32 [1536, 512], P('fsdp')
- wv_grad: float32 [1536, 512], P('fsdp')
- wo_grad: float32 [1536, 1536], P('fsdp')
- gate_grad: float32 [1536, 6912], P('fsdp')
- up_grad: float32 [1536, 6912], P('fsdp')
- down_grad: float32 [6912, 1536], P('fsdp')
- attn_gain_grad: float32 [1536], P('fsdp')
- ffn_gain_grad: float32 [1536], P('fsdp')
- q_gain_grad: float32 [64], P('fsdp')
- k_gain_grad: float32 [64], P('fsdp')
The draws below stay inside these ranges and needn't reach their ends.
Inputs may be any that keep to these rules, and one draw needn't show every extreme that they name: The lengths sum to 4096; the largest is exactly min(8192, 3840).
All inputs are finite; a program needn't handle non-finite values.
Results may differ from the reference program's by a relative error of at most 0.024.
Values may be sent and summed in bfloat16 or wider, within the bound.
A program may use at most 704 MiB of HBM per device.

```python
import math
import jax
import jax.numpy as jnp
import numpy as np
from jax import lax

MODEL_WIDTH = 1536
QUERY_HEADS = 24
KEY_VALUE_HEADS = 8
HEAD_SIZE = 64
FF = 6912
SEQ_LEN = 8192
BLOCK = 512
TOKENS = 4096
NDOCS = 4


def level_of(rng, extent, shards, least, top_value):
    def one(position, blocks):
        steps = jax.random.uniform(jax.random.fold_in(jax.random.fold_in(rng, 6), position), (blocks,), jnp.float32, least / len(shards), top_value / len(shards))
        return jnp.repeat(jnp.exp(steps), extent[position] // blocks).reshape((-1,) + (1,) * (len(extent) - position - 1))

    factor_of = one(*shards[0])
    for cut in shards[1:]:
        factor_of = factor_of * one(*cut)
    return factor_of


def split_up(amount, total, bound, skew):
    loads = [(1 << 20) // math.isqrt(rank ** skew) + 1 for rank in range(2, amount + 1)]
    rest, given = total - bound - (amount - 1), [1] * (amount - 1)
    while rest > 0:
        free = [i for i in range(amount - 1) if given[i] < bound]
        mass, remaining = sum([loads[i] for i in free]), rest
        for i in free:
            extra = min(bound - given[i], max(1, remaining * loads[i] // mass), rest)
            given[i] = given[i] + extra
            rest = rest - extra
    return np.array([bound] + given)


def uneven_parts(key, amount, total, most, skew):
    if amount == 2:
        one = jax.random.randint(key, (), max(1, total - most), min(most, total - 1) + 1)
        return jnp.stack([one, total - one])
    sizes = jnp.asarray(split_up(amount, total, most, skew), jnp.int32)
    twos = (amount - 1) // 2
    giver, taker = sizes[1:1 + 2 * twos:2], sizes[2:2 + 2 * twos:2]
    slack = jnp.minimum(giver - 1, most - taker)
    moved = jax.random.randint(jax.random.fold_in(key, 1), (twos,), 0, 1 << 20) % (slack + 1)
    sizes = sizes.at[1:1 + 2 * twos:2].set(giver - moved).at[2:2 + 2 * twos:2].set(taker + moved)
    return sizes[jax.random.permutation(jax.random.fold_in(key, 2), amount)]


def bell_draw(stream_key, shape, scale, limit, cuts=(), kind=jnp.bfloat16):
    entries = scale * jax.random.normal(stream_key, shape, jnp.float32)
    if cuts:
        entries = entries * level_of(stream_key, shape, cuts, -0.22, 0.18)
    return jnp.clip(entries, -limit, limit).astype(kind)


def setup_inputs(seed: int = 0) -> dict:
    keys = jax.random.split(jax.random.key(seed), 15)
    tokens = bell_draw(keys[0], (TOKENS, MODEL_WIDTH), 1.0, 6.0, ((0, 32),))
    lengths = uneven_parts(keys[1], NDOCS, TOKENS, min(SEQ_LEN, TOKENS - BLOCK // 2), 0).astype(jnp.int32)
    wq = bell_draw(keys[2], (MODEL_WIDTH, QUERY_HEADS * HEAD_SIZE), MODEL_WIDTH ** -0.5, 0.15625, ((0, 4),))
    wk = bell_draw(keys[3], (MODEL_WIDTH, KEY_VALUE_HEADS * HEAD_SIZE), MODEL_WIDTH ** -0.5, 0.15625, ((0, 4),))
    wv = bell_draw(keys[4], (MODEL_WIDTH, KEY_VALUE_HEADS * HEAD_SIZE), MODEL_WIDTH ** -0.5, 0.15625, ((0, 4),))
    wo = bell_draw(keys[5], (QUERY_HEADS * HEAD_SIZE, MODEL_WIDTH), (max(1, QUERY_HEADS * HEAD_SIZE * 64 // TOKENS)) ** -0.5, 1.25, ((0, 4),))
    w_gate = bell_draw(keys[6], (MODEL_WIDTH, FF), MODEL_WIDTH ** -0.5, 0.15625, ((0, 4),))
    w_up = bell_draw(keys[7], (MODEL_WIDTH, FF), MODEL_WIDTH ** -0.5, 0.15625, ((0, 4),))
    w_down = bell_draw(keys[8], (FF, MODEL_WIDTH), FF ** -0.5, 0.078125, ((0, 4),))
    attn_gain = jnp.clip(1.0 + 0.18 * jax.random.normal(keys[9], (MODEL_WIDTH,), jnp.float32), 0.099609375, 1.8984375).astype(jnp.bfloat16)
    ffn_gain = jnp.clip(1.0 + 0.18 * jax.random.normal(keys[10], (MODEL_WIDTH,), jnp.float32), 0.099609375, 1.8984375).astype(jnp.bfloat16)
    q_gain = jnp.clip(1.0 + 0.18 * jax.random.normal(keys[11], (HEAD_SIZE,), jnp.float32), 0.099609375, 1.8984375).astype(jnp.bfloat16)
    key_norm_gain = jnp.clip(1.0 + 0.18 * jax.random.normal(keys[12], (HEAD_SIZE,), jnp.float32), 0.099609375, 1.8984375).astype(jnp.bfloat16)
    cotangent = bell_draw(keys[13], (TOKENS, MODEL_WIDTH), 1.0, 6.0, ((0, 32),))
    return dict(tokens=tokens, lengths=lengths, wq=wq, wk=wk, wv=wv, wo=wo, w_gate=w_gate, w_up=w_up, w_down=w_down, attn_gain=attn_gain, ffn_gain=ffn_gain, q_gain=q_gain, key_norm_gain=key_norm_gain, cotangent=cotangent)


EPSILON = 1e-05
ROPE_BASE = 1000000.0
MASKED_SCORE = -1e+30

@jax.custom_vjp
def lower_precision(v):
    return lax.optimization_barrier(v.astype(jnp.bfloat16)).astype(jnp.float32)

@jax.custom_vjp
def low_back(v):
    return v

def low_keep(v):
    return (lower_precision(v), None)

def low_pass(kept, grad):
    return (grad,)

def back_keep(v):
    return (v, None)

def back_low(kept, grad):
    return (lower_precision(grad),)
lower_precision.defvjp(low_keep, low_pass)
low_back.defvjp(back_keep, back_low)

def doc_layout(lengths, token_index):
    doc_ends = jnp.cumsum(lengths).astype(jnp.int32)
    passed = token_index[:, None] >= doc_ends[None, :]
    document_index = lax.optimization_barrier(jnp.sum(passed.astype(jnp.int32), axis=1)).astype(jnp.int32)
    doc_start = lax.optimization_barrier(jnp.max(jnp.where(passed, doc_ends[None, :], 0), axis=1)).astype(jnp.int32)
    return (document_index, (token_index - doc_start).astype(jnp.int32))

def rotation(places, width):
    half_width = width // 2
    inverse_freq = jnp.power(ROPE_BASE, -(jnp.arange(half_width, dtype=jnp.float32) * 2.0 / width))
    angles = places.astype(jnp.float32)[:, None] * inverse_freq[None, :]
    cosine_values = jnp.cos(angles)
    sine_lookup = jnp.sin(angles)
    return (jnp.concatenate([cosine_values, cosine_values], 1), jnp.concatenate([sine_lookup, sine_lookup], 1))

def apply_rotary(values_in, cosine_values, sine_lookup, sign):
    half_width = values_in.shape[-1] // 2
    swapped = jnp.concatenate([-values_in[..., half_width:], values_in[..., :half_width]], -1)
    return values_in * cosine_values + swapped * (sine_lookup * sign)

def root_mean_scaled(values_in, gain_row):
    return values_in * lax.rsqrt(lax.optimization_barrier(jnp.mean(values_in * values_in, -1, keepdims=True)) + EPSILON) * gain_row

def forward_pass(inputs, wq, wk, wv, wo, w_gate, w_up, w_down, attn_gain, ffn_gain, q_gain, key_norm_gain, cosine_values, sine_lookup, document_index):
    highest = lax.Precision.HIGHEST
    token_rows = inputs.shape[0]
    query_group_width = QUERY_HEADS // KEY_VALUE_HEADS
    score_scale = HEAD_SIZE ** (-0.5)
    normed = lower_precision(root_mean_scaled(inputs, attn_gain))
    q_proj = low_back(jnp.dot(normed, wq, precision=highest))
    key_projected = low_back(jnp.dot(normed, wk, precision=highest))
    value_projected = low_back(jnp.dot(normed, wv, precision=highest))
    query_matrix = lower_precision(apply_rotary(root_mean_scaled(q_proj.reshape(token_rows, QUERY_HEADS, HEAD_SIZE), q_gain), cosine_values, sine_lookup, 1.0))
    every_key = lower_precision(apply_rotary(root_mean_scaled(key_projected.reshape(token_rows, KEY_VALUE_HEADS, HEAD_SIZE), key_norm_gain), cosine_values, sine_lookup, 1.0))
    every_value = lower_precision(value_projected).reshape(token_rows, KEY_VALUE_HEADS, HEAD_SIZE)
    block_of_rows = math.gcd(token_rows, 128)
    count_of_blocks = token_rows // block_of_rows
    token_positions = jnp.arange(token_rows, dtype=jnp.int32)

    def attend_heads(pieces):
        query_rows, query_index, query_doc = pieces
        scores = low_back(score_scale * jnp.einsum('tkgd,skd->kgts', query_rows, every_key, precision=highest))
        allowed = (token_positions[None, :] <= query_index[:, None]) & (document_index[None, :] == query_doc[:, None])
        scores = jnp.where(allowed, scores, MASKED_SCORE)
        weights = lower_precision(jax.nn.softmax(scores, axis=-1))
        return jnp.einsum('kgts,skd->tkgd', weights, every_value, precision=highest)
    mixed_heads = lax.map(jax.checkpoint(attend_heads), (query_matrix.reshape(count_of_blocks, block_of_rows, KEY_VALUE_HEADS, query_group_width, HEAD_SIZE), token_positions.reshape(count_of_blocks, block_of_rows), document_index.reshape(count_of_blocks, block_of_rows)))
    mixed_heads = lower_precision(low_back(mixed_heads.reshape(token_rows, QUERY_HEADS * HEAD_SIZE)))
    resid = inputs + low_back(jnp.dot(mixed_heads, wo, precision=highest))
    ffn_rows = math.gcd(token_rows, 4096)

    def feed(resid_rows):
        hidden_in = lower_precision(root_mean_scaled(resid_rows, ffn_gain))
        gate = low_back(jnp.dot(hidden_in, w_gate, precision=highest))
        upper = low_back(jnp.dot(hidden_in, w_up, precision=highest))
        act_rows = lower_precision(jax.nn.silu(gate) * upper)
        return resid_rows + low_back(jnp.dot(act_rows, w_down, precision=highest))
    return lax.map(jax.checkpoint(feed), resid.reshape(token_rows // ffn_rows, ffn_rows, MODEL_WIDTH)).reshape(token_rows, MODEL_WIDTH)

def reference(tokens, lengths, wq, wk, wv, wo, w_gate, w_up, w_down, attn_gain, ffn_gain, q_gain, key_norm_gain, cotangent):
    token_index = jnp.arange(TOKENS, dtype=jnp.int32)
    document_index, places = doc_layout(lengths, token_index)
    cosine_values, sine_lookup = rotation(places, HEAD_SIZE)
    cosine_values = cosine_values[:, None, :]
    sine_lookup = sine_lookup[:, None, :]

    def wrapped(inputs, wq, wk, wv, wo, w_gate, w_up, w_down, attn_gain, ffn_gain, q_gain, key_norm_gain):
        return forward_pass(inputs, wq, wk, wv, wo, w_gate, w_up, w_down, attn_gain, ffn_gain, q_gain, key_norm_gain, cosine_values, sine_lookup, document_index)
    primals = tuple((array_in.astype(jnp.float32) for array_in in (tokens, wq, wk, wv, wo, w_gate, w_up, w_down, attn_gain, ffn_gain, q_gain, key_norm_gain)))
    layer_out, pullback = jax.vjp(wrapped, *primals)
    gradients = pullback(cotangent.astype(jnp.float32))
    return (layer_out.astype(jnp.bfloat16), gradients[0].astype(jnp.bfloat16), gradients[1], gradients[2], gradients[3], gradients[4], gradients[5], gradients[6], gradients[7], gradients[8], gradients[9], gradients[10], gradients[11])
```

```python
import functools

import jax
import jax.numpy as jnp
from jax import lax
from jax.experimental import pallas as pl
from jax.experimental.pallas import tpu as pltpu
from jax.sharding import PartitionSpec as P

QUERY_HEADS = 24
KEY_VALUE_HEADS = 8
HEAD_SIZE = 64
GROUP = QUERY_HEADS // KEY_VALUE_HEADS
QW = GROUP * HEAD_SIZE
LANES = 128

EPSILON = 1e-05
ROPE_BASE = 1000000.0
APART = 16384.0

MESH = pl.DeviceIdType.MESH
F32 = jnp.float32
BF16 = jnp.bfloat16
ANY = pl.BlockSpec(memory_space=pl.ANY)
VMEM = pl.BlockSpec(memory_space=pltpu.VMEM)
VMEM_LIMIT = 56 * 1024 * 1024


class Team:
    def __init__(self, B, F, T):
        self.B, self.F, self.T = B, F, T
        ctx, self.f = lax.axis_index("ctx"), lax.axis_index("fsdp")
        self.t, self.y = lax.div(ctx, B), lax.rem(ctx, B)
        self.p = self.y * F + self.f

    def member(self, p):
        return (self.t * self.B + lax.div(p, self.F), lax.rem(p, self.F))

    def same_row(self, f):
        return (self.t * self.B + self.y, f)

    def other_team(self, t):
        return (t * self.B + self.y, self.f)


def flip(p, bit):
    return p + bit * (1 - 2 * lax.rem(lax.div(p, bit), 2))


def bit_of(p, bit):
    return lax.rem(lax.div(p, bit), 2)


class Sems:
    def __init__(self, send, recv):
        self.send, self.recv, self.used = send, recv, 0

    def copy(self, src, dst, device):
        i = self.used
        self.used += 1
        return pltpu.make_async_remote_copy(
            src_ref=src,
            dst_ref=dst,
            send_sem=self.send.at[i],
            recv_sem=self.recv.at[i],
            device_id=device,
            device_id_type=MESH,
        )


def greet(devices):
    barrier = pltpu.get_barrier_semaphore()
    for device in devices:
        pl.semaphore_signal(barrier, inc=1, device_id=device, device_id_type=MESH)
    pl.semaphore_wait(barrier, len(devices))


def team_peers(team):
    n = team.B * team.F
    return [team.member(lax.rem(team.p + d, n)) for d in range(1, n)]


def line_peers(team):
    return [team.other_team(lax.rem(team.t + d, team.T)) for d in range(1, team.T)]


def row_peers(team):
    return [team.same_row(lax.rem(team.f + d, team.F)) for d in range(1, team.F)]


class Gather:
    def __init__(self, sems, me, count, device, own, block, half):
        self.sems, self.me, self.count, self.device = sems, me, count, device
        self.own, self.block, self.half = own, block, half
        self.pending = []

    def send(self, src, dst, to):
        copy = self.sems.copy(src, dst, self.device(to))
        copy.start()
        self.pending.append(copy)
        return copy

    def begin(self):
        me = self.me
        self.first = [
            self.send(self.own, self.block(me), flip(me, 1 << k))
            for k in range(self.count.bit_length() - 1)
        ]

    def relay(self):
        me = self.me
        one = flip(me, 1)
        two = flip(me, 2)
        self.first[1].wait_recv()
        self.late = [self.send(self.block(two), self.block(two), one)]
        if self.count == 8:
            four = flip(me, 4)
            low = self.send(self.half(two, 0), self.half(two, 0), four)
            self.first[2].wait_recv()
            self.late.append(self.send(self.block(four), self.block(four), one))
            high = self.send(self.half(four, 1), self.half(four, 1), two)
            far = flip(two, 4)
            self.corner = [(low, far, 0), (high, far, 1)]

    def end(self):
        one = flip(self.me, 1)
        if self.count == 8:
            for copy, far, k in self.corner:
                copy.wait_recv()
                self.late.append(self.send(self.half(far, k), self.half(far, k), one))
        self.first[0].wait_recv()
        for copy in self.late:
            copy.wait_recv()
        for copy in self.pending:
            copy.wait_send()

    COPIES = 9


def scatter_shapes(rows, width):
    half = width // 2
    return [
        pltpu.VMEM((2, 2, rows, width), BF16),
        pltpu.VMEM((2, rows, half), BF16),
        pltpu.VMEM((2, rows, half), BF16),
        pltpu.VMEM((2, rows, half), BF16),
        pltpu.VMEM((2, rows, half), BF16),
        pltpu.VMEM((rows, half), BF16),
        pltpu.VMEM((rows, half), BF16),
        pltpu.VMEM((rows, half), BF16),
        pltpu.VMEM((rows, half), BF16),
    ]


SCATTER_COPIES = 5


def reduce_scatter(sems, team, x, scratch, store):
    r0, s1l, s1r, r1l, r1r, s2l, s2r, r2l, r2r = scratch
    p = team.p
    b0, b1, b2 = bit_of(p, 1), bit_of(p, 2), bit_of(p, 4)
    n0, n1, n2 = 1 - b0, 1 - b1, 1 - b2
    width = x.shape[-1]
    left, right = pl.ds(0, width // 2), pl.ds(width // 2, width // 2)
    send = lambda src, dst, bit: sems.copy(src, dst, team.member(flip(p, bit)))
    wide = lambda v: v.astype(F32)

    first = send(x.at[:, :, n0], r0, 1)
    first.start()
    first.wait_recv()
    for k in range(2):
        s1l[k] = (wide(x[k, n1, b0, :, left]) + wide(r0[k, n1, :, left])).astype(BF16)
    l1 = send(s1l, r1l, 2)
    l1.start()
    for k in range(2):
        s1r[k] = (wide(x[n2, k, b0, :, right]) + wide(r0[n2, k, :, right])).astype(BF16)
    r1 = send(s1r, r1r, 4)
    r1.start()
    l1.wait_recv()
    s2l[...] = (
        wide(x[n2, b1, b0, :, left]) + wide(r0[n2, b1, :, left]) + wide(r1l[n2])
    ).astype(BF16)
    l2 = send(s2l, r2l, 4)
    l2.start()
    r1.wait_recv()
    s2r[...] = (
        wide(x[b2, n1, b0, :, right]) + wide(r0[b2, n1, :, right]) + wide(r1r[n1])
    ).astype(BF16)
    r2 = send(s2r, r2r, 2)
    r2.start()
    l2.wait_recv()
    store(
        left,
        wide(x[b2, b1, b0, :, left])
        + wide(r0[b2, b1, :, left])
        + wide(r1l[b2])
        + wide(r2l[...]),
    )
    r2.wait_recv()
    store(
        right,
        wide(x[b2, b1, b0, :, right])
        + wide(r0[b2, b1, :, right])
        + wide(r1r[b1])
        + wide(r2r[...]),
    )
    for copy in (first, l1, r1, l2, r2):
        copy.wait_send()


def kernel_params(collective_id):
    return pltpu.CompilerParams(
        collective_id=collective_id, has_side_effects=True, vmem_limit_bytes=VMEM_LIMIT
    )


def inputs_kernel(dims, tokens, wq, wk, wv, gains, w_gate, w_up, tok_full, wqkv, gains_full, gate_cut, up_cut,
                  q_in, k_in, v_in, qkv_cut, slab_g, slab_u, cut_g, cut_u, send, recv, local):
    team = Team(*dims)
    B, F = team.B, team.F
    sems = Sems(send, recv)
    loads = [
        pltpu.make_async_copy(src, dst, local.at[i])
        for i, (src, dst) in enumerate(
            [(wq, q_in), (wk, k_in), (wv, v_in), (w_gate, slab_g), (w_up, slab_u), (tokens, tok_full.at[team.p]),
             (gains, gains_full.at[team.f])]
        )
    ]
    for load in loads:
        load.start()
    greet(team_peers(team))
    rows = tokens.shape[0]
    gather = Gather(
        sems, team.p, B * F, team.member, tokens,
        lambda i: tok_full.at[i],
        lambda i, k: tok_full.at[i, pl.ds(k * rows // 2, rows // 2)],
    )
    gather.begin()
    small = [sems.copy(gains, gains_full.at[team.f], peer) for peer in row_peers(team)]
    for copy in small:
        copy.start()
    for load in loads[:3]:
        load.wait()
    for f in range(F):
        for y in range(B):
            h = f * B + y

            @pl.when(team.y == y)
            def _():
                qkv_cut[f, :, 0:QW] = q_in[:, h * QW : (h + 1) * QW]
                qkv_cut[f, :, QW : QW + HEAD_SIZE] = k_in[:, h * HEAD_SIZE : (h + 1) * HEAD_SIZE]
                qkv_cut[f, :, QW + HEAD_SIZE : QW + 2 * HEAD_SIZE] = v_in[:, h * HEAD_SIZE : (h + 1) * HEAD_SIZE]

    sent = []
    for d in range(1, F):
        to = lax.rem(team.f + d, F)
        sent.append(sems.copy(qkv_cut.at[to], wqkv.at[team.f], team.same_row(to)))
        sent[-1].start()
    own = pltpu.make_async_copy(qkv_cut.at[team.f], wqkv.at[team.f], local.at[7])
    own.start()
    gather.relay()
    stores = []
    for i, (slab, cut, out) in enumerate([(slab_g, cut_g, gate_cut), (slab_u, cut_u, up_cut)]):
        loads[3 + i].wait()
        width = cut.shape[-1]

        @pl.loop(0, slab.shape[0] // 32)
        def _(r):
            at = pl.ds(pl.multiple_of(r * 32, 32), 32)
            for f in range(F):
                for y in range(B):
                    q = f * B + y

                    @pl.when(team.y == y)
                    def _():
                        cut[f, at, :] = slab[at, q * width : (q + 1) * width]

        stores.append(pltpu.make_async_copy(cut, out, local.at[8 + i]))
        stores[-1].start()
    gather.end()
    for copy in small + sent:
        copy.wait()
    for copy in loads[5:] + [own] + stores:
        copy.wait()


def gather_inputs(dims, tokens, wq, wk, wv, gains, w_gate, w_up):
    B, F, T = dims
    rows, width = tokens.shape
    depth, ff = w_gate.shape
    cols = ff // (B * F)
    copies = Gather.COPIES + 2 * (F - 1)
    heads = QW + 2 * HEAD_SIZE
    return pl.pallas_call(
        functools.partial(inputs_kernel, dims),
        out_shape=(
            jax.ShapeDtypeStruct((B * F, rows, width), BF16),
            jax.ShapeDtypeStruct((F, depth, heads), BF16),
            jax.ShapeDtypeStruct((F,) + gains.shape, BF16),
            jax.ShapeDtypeStruct((F, depth, cols), BF16),
            jax.ShapeDtypeStruct((F, depth, cols), BF16),
        ),
        in_specs=[ANY] * 7,
        out_specs=[ANY] * 5,
        scratch_shapes=[
            pltpu.VMEM(wq.shape, BF16),
            pltpu.VMEM(wk.shape, BF16),
            pltpu.VMEM(wv.shape, BF16),
            pltpu.VMEM((F, depth, heads), BF16),
            pltpu.VMEM(w_gate.shape, BF16),
            pltpu.VMEM(w_up.shape, BF16),
            pltpu.VMEM((F, depth, cols), BF16),
            pltpu.VMEM((F, depth, cols), BF16),
            pltpu.SemaphoreType.DMA((copies,)),
            pltpu.SemaphoreType.DMA((copies,)),
            pltpu.SemaphoreType.DMA((10,)),
        ],
        compiler_params=kernel_params(1),
        name="gather_inputs",
    )(tokens, wq, wk, wv, gains, w_gate, w_up)


def lane_ids(rows):
    return lax.broadcasted_iota(jnp.int32, (rows, LANES), 1)


def widen_keys(kv, spans, first_row, kx, vx):
    rows = kv.shape[0]
    lane = lane_ids(rows)
    row = lax.broadcasted_iota(jnp.int32, (rows, LANES), 0) + first_row
    inside = (row >= spans[0:1, :]) & (row < spans[1:2, :])
    wide = kv.astype(F32)
    kx[...] = jnp.where(lane < HEAD_SIZE, wide, jnp.where(inside, 1.0, 0.0)).astype(BF16)
    vx[...] = jnp.where(lane < HEAD_SIZE, pltpu.roll(wide, HEAD_SIZE, 1), 1.0).astype(BF16)


def dot_last(a, b):
    return lax.dot_general(a, b, (((1,), (1,)), ((), ())), preferred_element_type=F32)


def attend_kernel(dims, qx, kv, spans, dy, wo, gate_cut, up_cut, kv_all, acc, mixed, dy_full, wo_full, w_gate, w_up,
                  kx, vx, packed, send, recv, line_send, line_recv, local):
    team = Team(*dims)
    B, F, T = dims
    t = team.t
    sems = Sems(send, recv)
    rows = kv.shape[0]
    part = rows // 2
    homes = [
        pltpu.make_async_copy(kv, kv_all.at[t], local.at[0]),
        pltpu.make_async_copy(dy, dy_full.at[team.p], local.at[1]),
        pltpu.make_async_copy(wo, wo_full.at[team.f], local.at[2]),
        pltpu.make_async_copy(gate_cut.at[team.f], w_gate.at[team.f], local.at[3]),
        pltpu.make_async_copy(up_cut.at[team.f], w_up.at[team.f], local.at[4]),
    ]
    for copy in homes:
        copy.start()
    greet(team_peers(team) + line_peers(team))

    def line_copy(d, source, to):
        return pltpu.make_async_remote_copy(
            src_ref=kv, dst_ref=kv_all.at[source], send_sem=line_send.at[d], recv_sem=line_recv.at[source],
            device_id=team.other_team(to), device_id_type=MESH,
        )

    for d in range(1, T):

        @pl.when(t + d < T)
        def _():
            line_copy(d, t, t + d).start()

    half_wo, half_dy = wo.shape[0] // 2, dy.shape[0] // 2
    gather_wo = Gather(
        sems, team.f, F, team.same_row, wo, lambda i: wo_full.at[i],
        lambda i, k: wo_full.at[i, pl.ds(k * half_wo, half_wo)],
    )
    gather_wo.begin()
    sent = []
    for cut, full in ((gate_cut, w_gate), (up_cut, w_up)):
        for d in range(1, F):
            to = lax.rem(team.f + d, F)
            sent.append(sems.copy(cut.at[to], full.at[team.f], team.same_row(to)))
            sent[-1].start()
    gather_dy = Gather(
        sems, team.p, B * F, team.member, dy, lambda i: dy_full.at[i],
        lambda i, k: dy_full.at[i, pl.ds(k * half_dy, half_dy)],
    )
    gather_dy.begin()
    homes[0].wait()
    widen_keys(kv_all[t], spans, t * rows, kx, vx)
    causal = lax.broadcasted_iota(jnp.int32, (part, part), 1) <= lax.broadcasted_iota(jnp.int32, (part, part), 0)

    def piece(q, k, masked):
        scores = dot_last(q, kx[k * part : (k + 1) * part, :])
        weights = jnp.exp(scores)
        if masked:
            weights = jnp.where(causal, weights, 0.0)
        return jnp.dot(weights.astype(BF16), vx[k * part : (k + 1) * part, :], preferred_element_type=F32)

    @pl.loop(0, GROUP)
    def _(h):
        acc[h, 0:part, :] = piece(qx[h, 0:part, :], 0, True)
        low = qx[h, part:rows, :]
        acc[h, part:rows, :] = piece(low, 0, False) + piece(low, 1, True)

    gather_wo.relay()

    @pl.loop(1, t + 1)
    def _(j):
        source = t - j
        line_copy(0, source, t).wait_recv()
        widen_keys(kv_all[source], spans, source * rows, kx, vx)

        @pl.loop(0, GROUP)
        def _(h):
            for k in range(2):
                at = pl.ds(k * part, part)
                q = qx[h, at, :]
                acc[h, at, :] = acc[h, at, :] + piece(q, 0, False) + piece(q, 1, False)

    for h in range(GROUP):
        out = acc[h, :, 0:HEAD_SIZE] / acc[h, :, HEAD_SIZE : 2 * HEAD_SIZE]
        out = out.astype(BF16)
        if h < 2:
            packed[0:rows, h * HEAD_SIZE : (h + 1) * HEAD_SIZE] = out
        else:
            packed[rows : rows + part, 0:HEAD_SIZE] = out[0:part]
            packed[rows : rows + part, HEAD_SIZE : 2 * HEAD_SIZE] = out[part:rows]
    home = pltpu.make_async_copy(packed, mixed.at[team.p], local.at[5])
    home.start()
    half_mixed = packed.shape[0] // 2
    gather_mixed = Gather(
        sems, team.p, B * F, team.member, packed, lambda i: mixed.at[i],
        lambda i, k: mixed.at[i, pl.ds(k * half_mixed, half_mixed)],
    )
    gather_mixed.begin()
    gather_mixed.relay()
    gather_dy.relay()
    gather_mixed.end()
    gather_wo.end()
    gather_dy.end()
    for copy in sent:
        copy.wait()
    for copy in homes[1:] + [home]:
        copy.wait()
    for d in range(1, T):

        @pl.when(t + d < T)
        def _():
            line_copy(d, t, t + d).wait_send()


def attend(dims, qx, kv, spans, dy, wo, gate_cut, up_cut):
    B, F, T = dims
    rows = kv.shape[0]
    copies = 3 * Gather.COPIES + 2 * (F - 1)
    packed = (rows + rows // 2, LANES)
    return pl.pallas_call(
        functools.partial(attend_kernel, dims),
        out_shape=(
            jax.ShapeDtypeStruct((T, rows, LANES), BF16),
            jax.ShapeDtypeStruct((GROUP, rows, LANES), F32),
            jax.ShapeDtypeStruct((B * F,) + packed, BF16),
            jax.ShapeDtypeStruct((B * F,) + dy.shape, BF16),
            jax.ShapeDtypeStruct((F,) + wo.shape, BF16),
            jax.ShapeDtypeStruct(gate_cut.shape, BF16),
            jax.ShapeDtypeStruct(up_cut.shape, BF16),
        ),
        in_specs=[VMEM, ANY, VMEM, ANY, ANY, ANY, ANY],
        out_specs=[VMEM, VMEM, ANY, ANY, ANY, ANY, ANY],
        scratch_shapes=[
            pltpu.VMEM((rows, LANES), BF16),
            pltpu.VMEM((rows, LANES), BF16),
            pltpu.VMEM(packed, BF16),
            pltpu.SemaphoreType.DMA((copies,)),
            pltpu.SemaphoreType.DMA((copies,)),
            pltpu.SemaphoreType.DMA((T,)),
            pltpu.SemaphoreType.DMA((T,)),
            pltpu.SemaphoreType.DMA((6,)),
        ],
        compiler_params=kernel_params(2),
        name="attend",
    )(qx, kv, spans, dy, wo, gate_cut, up_cut)


def attend_back_kernel(dims, qx, dox, kv_all, spans, dq, dkv, kx, vx, dk, dv):
    team = Team(*dims)
    t = team.t
    rows = qx.shape[1]
    part = rows // 2
    dq[...] = jnp.zeros_like(dq)
    causal = lax.broadcasted_iota(jnp.int32, (part, part), 0) <= lax.broadcasted_iota(jnp.int32, (part, part), 1)
    lane = lane_ids(part)

    def piece(h, q_rows, k_rows, masked):
        q = qx[h, q_rows, :]
        do = dox[h, q_rows, :]
        keys = kx[k_rows, :]
        weights = jnp.exp(dot_last(keys, q))
        if masked:
            weights = jnp.where(causal, weights, 0.0)
        dscore = (weights * dot_last(vx[k_rows, :], do)).astype(BF16)
        dv[...] += jnp.dot(weights.astype(BF16), do, preferred_element_type=F32)
        dk[...] += jnp.dot(dscore, q, preferred_element_type=F32)
        dq[h, q_rows, :] += lax.dot_general(dscore, keys, (((0,), (0,)), ((), ())), preferred_element_type=F32)

    def block(source, diagonal):
        widen_keys(kv_all[source], spans, source * rows, kx, vx)
        for k in range(2):
            k_rows = slice(k * part, (k + 1) * part)
            dk[...] = jnp.zeros_like(dk)
            dv[...] = jnp.zeros_like(dv)

            @pl.loop(0, GROUP)
            def _(h):
                for q in range(k if diagonal else 0, 2):
                    piece(h, slice(q * part, (q + 1) * part), k_rows, diagonal and q == k)

            dkv[source, k_rows, :] = jnp.where(
                lane < HEAD_SIZE, dk[...], pltpu.roll(dv[...], HEAD_SIZE, 1)
            ).astype(BF16)

    block(t, True)

    @pl.loop(0, t)
    def _(source):
        block(source, False)


def attend_back(dims, qx, dox, kv_all, spans):
    part = qx.shape[1] // 2
    rows = qx.shape[1]
    return pl.pallas_call(
        functools.partial(attend_back_kernel, dims),
        out_shape=(
            jax.ShapeDtypeStruct(qx.shape, F32),
            jax.ShapeDtypeStruct(kv_all.shape, BF16),
        ),
        in_specs=[VMEM] * 4,
        out_specs=[VMEM] * 2,
        scratch_shapes=[
            pltpu.VMEM((rows, LANES), BF16),
            pltpu.VMEM((rows, LANES), BF16),
            pltpu.VMEM((part, LANES), F32),
            pltpu.VMEM((part, LANES), F32),
        ],
        compiler_params=pltpu.CompilerParams(vmem_limit_bytes=VMEM_LIMIT),
        name="attend_back",
    )(qx, dox, kv_all, spans)


def scatter_kernel(dims, x, out, *rest):
    team = Team(*dims)
    scratch, (send, recv) = rest[:-2], rest[-2:]
    greet([team.member(flip(team.p, bit)) for bit in (1, 2, 4)])

    def store(columns, total):
        out[:, columns] = total

    reduce_scatter(Sems(send, recv), team, x, scratch, store)


def team_scatter(dims, x, collective_id):
    rows, width = x.shape[0] // KEY_VALUE_HEADS, x.shape[1]
    return pl.pallas_call(
        functools.partial(scatter_kernel, dims),
        out_shape=jax.ShapeDtypeStruct((rows, width), F32),
        in_specs=[VMEM],
        out_specs=VMEM,
        scratch_shapes=scatter_shapes(rows, width)
        + [pltpu.SemaphoreType.DMA((SCATTER_COPIES,)), pltpu.SemaphoreType.DMA((SCATTER_COPIES,))],
        compiler_params=kernel_params(collective_id),
        name="team_scatter",
    )(x.reshape(2, 2, 2, rows, width))


def gather_kernel(dims, x, full, send, recv, local):
    team = Team(*dims)
    home = pltpu.make_async_copy(x, full.at[team.p], local)
    home.start()
    greet([team.member(flip(team.p, bit)) for bit in (1, 2, 4)])
    half = x.shape[0] // 2
    gather = Gather(
        Sems(send, recv), team.p, team.B * team.F, team.member, x, lambda i: full.at[i],
        lambda i, k: full.at[i, pl.ds(k * half, half)],
    )
    gather.begin()
    gather.relay()
    gather.end()
    home.wait()


def team_gather(dims, x, collective_id):
    full = pl.pallas_call(
        functools.partial(gather_kernel, dims),
        out_shape=jax.ShapeDtypeStruct((KEY_VALUE_HEADS,) + x.shape, x.dtype),
        in_specs=[ANY],
        out_specs=ANY,
        scratch_shapes=[
            pltpu.SemaphoreType.DMA((Gather.COPIES,)),
            pltpu.SemaphoreType.DMA((Gather.COPIES,)),
            pltpu.SemaphoreType.DMA,
        ],
        compiler_params=kernel_params(collective_id),
        name="team_gather",
    )(x)
    return full.reshape((-1,) + x.shape[1:])


def keys_back_kernel(dims, dkv, x, total, out, landed, *rest):
    team = Team(*dims)
    T, t = team.T, team.t
    scratch, (send, recv, line_send, line_recv) = rest[:-4], rest[-4:]
    greet([team.member(flip(team.p, bit)) for bit in (1, 2, 4)] + line_peers(team))

    def line_copy(d, owner, source):
        return pltpu.make_async_remote_copy(
            src_ref=dkv.at[owner], dst_ref=landed.at[source], send_sem=line_send.at[d],
            recv_sem=line_recv.at[source], device_id=team.other_team(owner), device_id_type=MESH,
        )

    for d in range(1, T):

        @pl.when(t - d >= 0)
        def _():
            line_copy(d, t - d, t).start()

    def store(columns, value):
        out[:, columns] = value

    reduce_scatter(Sems(send, recv), team, x, scratch, store)
    total[...] = dkv[t].astype(F32)
    for d in range(1, T):

        @pl.when(t + d < T)
        def _():
            line_copy(0, t, t + d).wait_recv()
            total[...] += landed[t + d].astype(F32)

    for d in range(1, T):

        @pl.when(t - d >= 0)
        def _():
            line_copy(d, t - d, t).wait_send()


def keys_back(dims, dkv, x):
    T = dims[2]
    rows, width = x.shape[0] // KEY_VALUE_HEADS, x.shape[1]
    return pl.pallas_call(
        functools.partial(keys_back_kernel, dims),
        out_shape=(
            jax.ShapeDtypeStruct(dkv.shape[1:], F32),
            jax.ShapeDtypeStruct((rows, width), F32),
        ),
        in_specs=[VMEM] * 2,
        out_specs=[VMEM] * 2,
        scratch_shapes=[pltpu.VMEM(dkv.shape, BF16)]
        + scatter_shapes(rows, width)
        + [
            pltpu.SemaphoreType.DMA((SCATTER_COPIES,)),
            pltpu.SemaphoreType.DMA((SCATTER_COPIES,)),
            pltpu.SemaphoreType.DMA((T,)),
            pltpu.SemaphoreType.DMA((T,)),
        ],
        compiler_params=kernel_params(5),
        name="keys_back",
    )(dkv, x.reshape(2, 2, 2, rows, width))


HOP = 2
LAG = 3


def grads_kernel(dims, step1, step2, g1, g2, out1, out2, land1, land2, fin1, fin2, red_recv, fin_recv, hand_recv,
                 bulk):
    team = Team(*dims)
    B, F, T = dims
    t, y, f = team.t, team.y, team.f
    depth = g1.shape[0]
    half1, half2 = depth // 2, g2.shape[0] // 2
    n1, n2 = half1 // step1, half2 // step2
    total = n1 + n2
    shard = depth // F
    per_shard = shard // step1
    RED, FIN, HAND, OWN, OVER, HOME, INTO = range(7)
    up_peer, down_peer = lax.rem(t + 1, T), lax.rem(t + T - 1, T)
    peers = row_peers(team)
    if B == 2:
        peers = peers + [team.member(lax.rem(team.p + F, B * F))]
    if T == 2:
        greet(peers + [team.other_team(up_peer)])
    else:
        greet(peers + [team.other_team(up_peer), team.other_team(down_peer)])
    kinds = (
        (g1, land1, fin1, step1, half1, 0),
        (g2, land2, fin2, step2, half2, 1),
    )

    def remote(src, dst, send_sem, recv_sem, device):
        return pltpu.make_async_remote_copy(
            src_ref=src, dst_ref=dst, send_sem=send_sem, recv_sem=recv_sem, device_id=device, device_id_type=MESH
        )

    def each(i, way, body):
        @pl.when((i >= 0) & (i < n2))
        def _():
            body(kinds[1], way, i, i)

        @pl.when((i >= n2) & (i < total))
        def _():
            body(kinds[0], way, i - n2, i)

    def chunk_rows(kind, way, c):
        step, half = kind[3], kind[4]
        return pl.ds(pl.multiple_of(way * half + c * step, 16), step)

    def onward(way):
        return t + 1 - 2 * way

    def back(way):
        return t - 1 + 2 * way

    def is_first(way):
        return t == (T - 1 if way else 0)

    def is_last(way):
        return t == (0 if way else T - 1)

    def reduce_copy(kind, way, at, i):
        g, land, fin, step, half, k = kind
        return remote(g.at[at], land.at[at], bulk.at[RED, k, way], red_recv.at[way, i], team.other_team(onward(way)))

    def final_copy(kind, way, at, i):
        g, land, fin, step, half, k = kind
        return remote(fin.at[at], fin.at[at], bulk.at[FIN, k, way], fin_recv.at[way, i], team.other_team(back(way)))

    def reduce(kind, way, c, i):
        g, land, fin, step, half, k = kind
        at = chunk_rows(kind, way, c)

        @pl.when(is_first(way))
        def _():
            reduce_copy(kind, way, at, i).start()

        @pl.when(jnp.logical_not(is_first(way)))
        def _():
            reduce_copy(kind, way, at, i).wait_recv()
            summed = (g[at, :].astype(F32) + land[at, :].astype(F32)).astype(BF16)

            @pl.when(is_last(way))
            def _():
                fin[at, :] = summed

            @pl.when(jnp.logical_not(is_last(way)))
            def _():
                g[at, :] = summed
                reduce_copy(kind, way, at, i).start()

    def hand1(way, c, at):
        row = way * half1 + c * step1
        to = lax.div(row, shard)
        place = lax.rem(row, shard)
        rows = pl.ds(pl.multiple_of(place, 16), step1)
        return to, place, rows

    def finish(kind, way, c, i):
        g, land, fin, step, half, k = kind
        at = chunk_rows(kind, way, c)

        @pl.when(jnp.logical_not(is_last(way)))
        def _():
            final_copy(kind, way, at, i).wait_recv()

        @pl.when(jnp.logical_not(is_first(way)))
        def _():
            final_copy(kind, way, at, i).start()

        if k == 0:
            to, place, rows = hand1(way, c, at)
            dst = out1.at[f * B + y, rows]

            @pl.when(to == f)
            def _():
                pltpu.make_async_copy(fin.at[at], dst, bulk.at[HOME, 0, 0]).start()
                if B == 2:
                    remote(fin.at[at], dst, bulk.at[OVER, 0, 0], bulk.at[INTO, 0, 0],
                           team.member(lax.rem(team.p + F, B * F))).start()

            @pl.when(to != f)
            def _():
                remote(fin.at[at], dst, bulk.at[HAND, 0, 0], hand_recv.at[f, lax.div(place, step1)],
                       team.same_row(to)).start()
        else:
            dst = out2.at[y, at]
            pltpu.make_async_copy(fin.at[at], dst, bulk.at[HOME, 1, 0]).start()
            if B == 2:
                remote(fin.at[at], dst, bulk.at[OVER, 1, 0], bulk.at[INTO, 1, 0],
                       team.member(lax.rem(team.p + F, B * F))).start()

    def pass_over(kind, way, c, i):
        if kind[5] != 0:
            return
        at = chunk_rows(kind, way, c)
        to, place, rows = hand1(way, c, at)

        @pl.when(to == f)
        def _():
            for d in range(1, F):
                source = lax.rem(f + d, F)
                ref = out1.at[source * B + y, rows]
                remote(fin1.at[at], ref, bulk.at[HAND, 0, 0], hand_recv.at[source, lax.div(place, step1)],
                       team.same_row(f)).wait_recv()
                if B == 2:
                    remote(ref, ref, bulk.at[OVER, 0, 1], bulk.at[INTO, 0, 0],
                           team.member(lax.rem(team.p + F, B * F))).start()

    @pl.loop(0, total + 2 * HOP * (T - 1) + LAG)
    def _(s):
        for way in range(2):
            place = T - 1 - t if way else t
            sent = s - HOP * place
            done = s - HOP * (2 * (T - 1) - place)
            each(sent, way, reduce)
            each(done, way, finish)
            each(done - LAG, way, pass_over)

    def drain(ref, sem):
        pltpu.make_async_copy(ref, ref, sem).wait()

    for way in range(2):
        for g, land, fin, step, half, k in kinds:

            @pl.when(jnp.logical_not(is_last(way)))
            def _():
                drain(g.at[pl.ds(0, half)], bulk.at[RED, k, way])

            @pl.when(jnp.logical_not(is_first(way)))
            def _():
                drain(g.at[pl.ds(0, half)], bulk.at[FIN, k, way])

    drain(g1.at[pl.ds(0, depth - shard)], bulk.at[HAND, 0, 0])
    drain(g1.at[pl.ds(0, shard)], bulk.at[HOME, 0, 0])
    drain(g2, bulk.at[HOME, 1, 0])
    if B == 2:
        drain(g1.at[pl.ds(0, shard)], bulk.at[OVER, 0, 0])
        drain(g1.at[pl.ds(0, depth - shard)], bulk.at[OVER, 0, 1])
        drain(g2, bulk.at[OVER, 1, 0])
        drain(g1, bulk.at[INTO, 0, 0])
        drain(g2, bulk.at[INTO, 1, 0])


def sum_grads(dims, g1, g2):
    B, F, T = dims
    depth = g1.shape[0]
    shard = depth // F
    step1, step2 = 32, 48
    chunks = depth // 2 // step1 + g2.shape[0] // 2 // step2
    return pl.pallas_call(
        functools.partial(grads_load_kernel, dims, step1, step2),
        out_shape=(
            jax.ShapeDtypeStruct((B * F, shard, g1.shape[1]), BF16),
            jax.ShapeDtypeStruct((B,) + g2.shape, BF16),
        ),
        in_specs=[ANY] * 2,
        out_specs=[ANY] * 2,
        scratch_shapes=[
            pltpu.VMEM(g1.shape, BF16),
            pltpu.VMEM(g2.shape, BF16),
            pltpu.VMEM(g1.shape, BF16),
            pltpu.VMEM(g2.shape, BF16),
            pltpu.VMEM(g1.shape, BF16),
            pltpu.VMEM(g2.shape, BF16),
            pltpu.SemaphoreType.DMA((2, chunks)),
            pltpu.SemaphoreType.DMA((2, chunks)),
            pltpu.SemaphoreType.DMA((F, shard // step1)),
            pltpu.SemaphoreType.DMA((7, 2, 2)),
            pltpu.SemaphoreType.DMA((2,)),
        ],
        compiler_params=kernel_params(7),
        name="sum_grads",
    )(g1, g2)


def grads_load_kernel(dims, step1, step2, g1, g2, out1, out2, own1, own2, *rest):
    local = rest[-1]
    loads = [pltpu.make_async_copy(g1, own1, local.at[0]), pltpu.make_async_copy(g2, own2, local.at[1])]
    for load in loads:
        load.start()
    for load in loads:
        load.wait()
    grads_kernel(dims, step1, step2, own1, own2, out1, out2, *rest[:-1])


def doc_layout(lengths, token_index):
    doc_ends = jnp.cumsum(lengths)
    passed = token_index[:, None] >= doc_ends[None, :]
    document_index = jnp.sum(passed.astype(jnp.int32), axis=1)
    doc_start = jnp.max(jnp.where(passed, doc_ends[None, :], 0), axis=1)
    return (document_index, token_index - doc_start)


def rotation(places, width):
    half_width = width // 2
    inverse_freq = jnp.power(ROPE_BASE, -(jnp.arange(half_width, dtype=F32) * 2.0 / width))
    angles = places.astype(F32)[:, None] * inverse_freq[None, :]
    cosine_values = jnp.cos(angles)
    sine_lookup = jnp.sin(angles)
    return (
        jnp.concatenate([cosine_values, cosine_values], 1),
        jnp.concatenate([sine_lookup, sine_lookup], 1),
    )


def apply_rotary(values_in, cosine_values, sine_lookup, sign):
    half_width = values_in.shape[-1] // 2
    swapped = jnp.concatenate([-values_in[..., half_width:], values_in[..., :half_width]], -1)
    return values_in * cosine_values + swapped * (sine_lookup * sign)


def scaled_input(values_in):
    factor = lax.rsqrt(jnp.mean(values_in * values_in, -1, keepdims=True) + EPSILON)
    return (values_in * factor, factor)


def norm_back(upstream, unit_rows, factor, gain_row):
    lifted = upstream * gain_row
    return factor * (lifted - unit_rows * jnp.mean(lifted * unit_rows, -1, keepdims=True))


def dot(a, b, dims=((1,), (0,))):
    return lax.dot_general(a, b, (dims, ((), ())), preferred_element_type=F32)


def in_three(values):
    high = lax.reduce_precision(values, 8, 7)
    rest = values - high
    middle = lax.reduce_precision(rest, 8, 7)
    return high.astype(BF16), middle.astype(BF16), (rest - middle).astype(BF16)


def on_device(
    tokens, lengths, wq, wk, wv, wo, w_gate, w_up, w_down, attn_gain, ffn_gain, q_gain, key_norm_gain, cotangent
):
    F = lax.axis_size("fsdp")
    B = KEY_VALUE_HEADS // F
    T = lax.axis_size("ctx") // B
    dims = (B, F, T)
    own_rows, width = tokens.shape
    rows = own_rows * KEY_VALUE_HEADS
    depth = width // F
    ctx, f = lax.axis_index("ctx"), lax.axis_index("fsdp")
    t, y = ctx // B, ctx % B
    p = y * F + f
    hidden = w_down.shape[0] // B

    gains = jnp.zeros((16, max(depth, LANES)), BF16)
    gains = gains.at[0, :depth].set(attn_gain).at[1, :depth].set(ffn_gain)
    gains = gains.at[2, : HEAD_SIZE // F].set(q_gain).at[3, : HEAD_SIZE // F].set(key_norm_gain)
    tok_full, wqkv, gains_full, gate_cut, up_cut = gather_inputs(dims, tokens, wq, wk, wv, gains, w_gate, w_up)
    gains_full = gains_full.astype(F32)
    gain_attn = gains_full[:, 0, :depth].reshape(-1)
    gain_ffn = gains_full[:, 1, :depth].reshape(-1)
    gain_query = gains_full[:, 2, : HEAD_SIZE // F].reshape(-1)
    gain_key = gains_full[:, 3, : HEAD_SIZE // F].reshape(-1)
    wqkv = wqkv.reshape(width, -1)

    token_index = t * rows + jnp.arange(rows, dtype=jnp.int32)
    docs, places = doc_layout(lengths, token_index)
    cosine_values, sine_lookup = rotation(places, HEAD_SIZE)
    cosine_values, sine_lookup = cosine_values[None], sine_lookup[None]
    ends = jnp.cumsum(lengths)
    ndocs = lengths.shape[0]
    big = jnp.int32(2**30)
    spans = jnp.stack([
        jnp.zeros((LANES,), jnp.int32).at[HEAD_SIZE : HEAD_SIZE + ndocs].set(ends - lengths),
        jnp.full((LANES,), big, jnp.int32).at[HEAD_SIZE : HEAD_SIZE + ndocs].set(ends),
    ])
    spans = jnp.concatenate([spans, jnp.zeros((6, LANES), jnp.int32)])

    inputs = tok_full.reshape(rows, width).astype(F32)
    unit_attn, factor_attn = scaled_input(inputs)
    normed = (unit_attn * gain_attn).astype(BF16)
    projected = dot(normed, wqkv)
    heads = jnp.transpose(projected.reshape(rows, GROUP + 2, HEAD_SIZE), (1, 0, 2))
    q_unit, q_factor = scaled_input(heads[:GROUP])
    k_unit, k_factor = scaled_input(heads[GROUP])
    queries = apply_rotary(q_unit * gain_query, cosine_values, sine_lookup, 1.0).astype(BF16)
    own_keys = apply_rotary(k_unit * gain_key, cosine_values[0], sine_lookup[0], 1.0).astype(BF16)
    own_values = heads[GROUP + 1].astype(BF16)
    scale = HEAD_SIZE ** (-0.5)
    apart = jnp.where(docs[:, None] == jnp.arange(ndocs)[None, :], 0.0, -APART).astype(BF16)
    apart = jnp.broadcast_to(apart[None], (GROUP, rows, ndocs))
    queries = (queries * jnp.asarray(scale, BF16)).astype(BF16)
    qx = jnp.concatenate([queries, apart, jnp.zeros((GROUP, rows, LANES - HEAD_SIZE - ndocs), BF16)], -1)
    kv = jnp.concatenate([own_keys, own_values], -1)
    kv_all, acc, mixed, dy_full, wo_full, gate_w, up_w = attend(
        dims, qx, kv, spans, cotangent, wo, gate_cut, up_cut
    )
    sums = acc[..., HEAD_SIZE : HEAD_SIZE + 1]
    out = acc[..., :HEAD_SIZE] / sums
    log_sums = jnp.log(sums)

    both = mixed[:, :rows].reshape(B, F, rows, 2 * HEAD_SIZE)
    third = mixed[:, rows:].reshape(B, F, rows // 2, 2, HEAD_SIZE)
    third = jnp.swapaxes(third, 2, 3).reshape(B, F, rows, HEAD_SIZE)
    mixed_heads = jnp.concatenate([both, third], -1)
    mixed_heads = jnp.transpose(mixed_heads, (2, 1, 0, 3)).reshape(rows, QUERY_HEADS * HEAD_SIZE)
    own_mixed = jnp.transpose(out, (1, 0, 2)).reshape(rows, QW).astype(BF16)
    wo_full = wo_full.reshape(-1, width)
    gate_w = gate_w.reshape(width, hidden)
    up_w = up_w.reshape(width, hidden)
    down_w = lax.dynamic_slice_in_dim(w_down, y * hidden, hidden, 0)
    own_wo = lax.dynamic_slice_in_dim(wo, y * QW, QW, 0)
    dy_full = dy_full.reshape(rows, width)

    resid = inputs + dot(mixed_heads, wo_full)
    unit_ffn, factor_ffn = scaled_input(resid)
    hidden_in = (unit_ffn * gain_ffn).astype(BF16)
    gate = dot(hidden_in, gate_w)
    upper = dot(hidden_in, up_w)
    sigma = jax.nn.sigmoid(gate)
    silu_gate = gate * sigma
    act_rows = (silu_gate * upper).astype(BF16)
    down_out = dot(act_rows, down_w).astype(BF16)

    grad_act = dot(dy_full, down_w, ((1,), (1,)))
    grad_gate = (grad_act * upper * sigma * (1.0 + gate * (1.0 - sigma))).astype(BF16)
    grad_upper = (grad_act * silu_gate).astype(BF16)
    grad_hidden = (dot(grad_gate, gate_w, ((1,), (1,))) + dot(grad_upper, up_w, ((1,), (1,)))).astype(BF16)
    own_grad_hidden = team_scatter(dims, grad_hidden, 3)

    own_at = lambda a: lax.dynamic_slice_in_dim(a, p * own_rows, own_rows, 0)
    own_resid = own_at(resid)
    own_unit, own_factor = scaled_input(own_resid)
    ffn_gain_term = jnp.sum(own_grad_hidden * own_unit, 0)
    grad_resid = cotangent.astype(F32) + norm_back(own_grad_hidden, own_unit, own_factor, gain_ffn)
    grad_attn = team_gather(dims, grad_resid.astype(BF16), 4)

    grad_mixed = dot(grad_attn, own_wo, ((1,), (1,))).astype(BF16)
    grad_mixed = jnp.transpose(grad_mixed.reshape(rows, GROUP, HEAD_SIZE), (1, 0, 2))
    delta = jnp.sum(grad_mixed.astype(F32) * out, -1, keepdims=True)
    zeros = lambda n: jnp.zeros((GROUP, rows, n), BF16)
    qx_back = jnp.concatenate(
        [queries, apart, *in_three(-log_sums), zeros(LANES - HEAD_SIZE - ndocs - 3)], -1
    )
    dox = jnp.concatenate([grad_mixed, *in_three(-delta), zeros(LANES - HEAD_SIZE - 3)], -1)
    dq, dkv = attend_back(dims, qx_back, dox, kv_all, spans)
    dkv, down_sum = keys_back(dims, dkv, down_out)
    layer_out = (own_resid + down_sum).astype(BF16)

    query_turned = apply_rotary(dq[..., :HEAD_SIZE] * scale, cosine_values, sine_lookup, -1.0)
    key_turned = apply_rotary(dkv[:, :HEAD_SIZE], cosine_values[0], sine_lookup[0], -1.0)
    q_gain_term = jnp.sum(query_turned * q_unit, (0, 1))
    k_gain_term = jnp.sum(key_turned * k_unit, 0)
    grad_q = norm_back(query_turned, q_unit, q_factor, gain_query)
    grad_k = norm_back(key_turned, k_unit, k_factor, gain_key)
    grad_heads = jnp.concatenate([grad_q, grad_k[None], dkv[None, :, HEAD_SIZE:]], 0).astype(BF16)
    grad_heads = jnp.transpose(grad_heads, (1, 0, 2)).reshape(rows, QW + 2 * HEAD_SIZE)
    grad_normed = dot(grad_heads, wqkv, ((1,), (1,))).astype(BF16)
    own_grad_normed = team_scatter(dims, grad_normed, 6)
    own_unit, own_factor = scaled_input(tokens.astype(F32))
    attn_gain_term = jnp.sum(own_grad_normed * own_unit, 0)
    tokens_grad = (grad_resid + norm_back(own_grad_normed, own_unit, own_factor, gain_attn)).astype(BF16)

    over_rows = ((0,), (0,))
    g1 = jnp.concatenate(
        [
            dot(hidden_in, grad_gate, over_rows).astype(BF16),
            dot(hidden_in, grad_upper, over_rows).astype(BF16),
            dot(normed, grad_heads, over_rows).astype(BF16),
        ],
        1,
    )
    g2 = jnp.concatenate(
        [dot(act_rows, dy_full, over_rows).astype(BF16), dot(own_mixed, grad_attn, over_rows).astype(BF16)], 0
    )
    out1, out2 = sum_grads(dims, g1, g2)

    gain_terms = jnp.concatenate([attn_gain_term, ffn_gain_term, q_gain_term, k_gain_term])
    gain_sums = lax.psum(gain_terms, ("ctx", "fsdp"))
    take = lambda a, n: lax.dynamic_slice_in_dim(a, f * n, n, 0)
    attn_gain_grad = take(gain_sums[:width], depth)
    ffn_gain_grad = take(gain_sums[width : 2 * width], depth)
    q_gain_grad = take(gain_sums[2 * width : 2 * width + HEAD_SIZE], HEAD_SIZE // F)
    k_gain_grad = take(gain_sums[2 * width + HEAD_SIZE :], HEAD_SIZE // F)

    def columns(first, count):
        return jnp.transpose(out1[:, :, first : first + count], (1, 0, 2)).reshape(depth, -1).astype(F32)

    down_grad = out2[:, :hidden].reshape(-1, width).astype(F32)
    wo_grad = out2[:, hidden:].reshape(-1, width).astype(F32)
    gate_grad = columns(0, hidden)
    up_grad = columns(hidden, hidden)
    wq_grad = columns(2 * hidden, QW)
    wk_grad = columns(2 * hidden + QW, HEAD_SIZE)
    wv_grad = columns(2 * hidden + QW + HEAD_SIZE, HEAD_SIZE)
    return (
        layer_out, tokens_grad, wq_grad, wk_grad, wv_grad, wo_grad, gate_grad, up_grad, down_grad,
        attn_gain_grad, ffn_gain_grad, q_gain_grad, k_gain_grad,
    )


def solution(mesh):
    rows = P(("ctx", "fsdp"), None)
    shard = P("fsdp", None)
    gain = P("fsdp")
    return jax.shard_map(
        on_device,
        mesh=mesh,
        in_specs=(rows, P(), shard, shard, shard, shard, shard, shard, shard, gain, gain, gain, gain, rows),
        out_specs=(rows, rows, shard, shard, shard, shard, shard, shard, shard, gain, gain, gain, gain),
        check_vma=False,
    )
```

```python
import functools

import jax
import jax.numpy as jnp
from jax import lax
from jax.experimental import pallas as pl
from jax.experimental.pallas import tpu as pltpu
from jax.sharding import PartitionSpec as P

QUERY_HEADS = 24
KEY_VALUE_HEADS = 8
HEAD_SIZE = 64
GROUP = QUERY_HEADS // KEY_VALUE_HEADS
QW = GROUP * HEAD_SIZE
LANES = 128
NDOCS = 4

EPSILON = 1e-05
ROPE_BASE = 1000000.0
APART = 16384.0

MESH = pl.DeviceIdType.MESH
F32 = jnp.float32
BF16 = jnp.bfloat16
ANY = pl.BlockSpec(memory_space=pl.ANY)
VMEM = pl.BlockSpec(memory_space=pltpu.VMEM)
VMEM_LIMIT = 56 * 1024 * 1024


class Team:
    def __init__(self, B, F, T):
        self.B, self.F, self.T = B, F, T
        ctx, self.f = lax.axis_index("ctx"), lax.axis_index("fsdp")
        self.t, self.y = lax.div(ctx, B), lax.rem(ctx, B)
        self.p = self.y * F + self.f

    def member(self, p):
        return (self.t * self.B + lax.div(p, self.F), lax.rem(p, self.F))

    def same_row(self, f):
        return (self.t * self.B + self.y, f)

    def other_team(self, t):
        return (t * self.B + self.y, self.f)


def flip(p, bit):
    return p + bit * (1 - 2 * lax.rem(lax.div(p, bit), 2))


def bit_of(p, bit):
    return lax.rem(lax.div(p, bit), 2)


class Sems:
    def __init__(self, send, recv):
        self.send, self.recv, self.used = send, recv, 0

    def copy(self, src, dst, device):
        i = self.used
        self.used += 1
        return pltpu.make_async_remote_copy(
            src_ref=src,
            dst_ref=dst,
            send_sem=self.send.at[i],
            recv_sem=self.recv.at[i],
            device_id=device,
            device_id_type=MESH,
        )


def greet(devices):
    barrier = pltpu.get_barrier_semaphore()
    for device in devices:
        pl.semaphore_signal(barrier, inc=1, device_id=device, device_id_type=MESH)
    pl.semaphore_wait(barrier, len(devices))


def team_peers(team):
    n = team.B * team.F
    return [team.member(lax.rem(team.p + d, n)) for d in range(1, n)]


def line_peers(team):
    return [team.other_team(lax.rem(team.t + d, team.T)) for d in range(1, team.T)]


def row_peers(team):
    return [team.same_row(lax.rem(team.f + d, team.F)) for d in range(1, team.F)]


class Gather:
    def __init__(self, sems, me, count, device, own, block, half):
        bits = count.bit_length() - 1
        one, two = flip(me, 1), flip(me, 2)
        send = lambda src, dst, to: sems.copy(src, dst, device(to))
        again = lambda ref, to: send(ref, ref, to)
        self.first = [send(own, block(me), flip(me, 1 << k)) for k in range(bits)]
        self.over = [again(block(two), one)]
        self.halves, self.corner = [], []
        if count == 8:
            four = flip(me, 4)
            far = flip(two, 4)
            self.over.append(again(block(four), one))
            self.halves = [again(half(two, 0), four), again(half(four, 1), two)]
            self.corner = [again(half(far, 0), one), again(half(far, 1), one)]

    def begin(self):
        for copy in self.first:
            copy.start()

    def relay(self):
        self.first[1].wait_recv()
        self.over[0].start()
        if self.halves:
            self.halves[0].start()
            self.first[2].wait_recv()
            self.over[1].start()
            self.halves[1].start()

    def end(self):
        for arrived, onward in zip(self.halves, self.corner):
            arrived.wait_recv()
            onward.start()
        self.first[0].wait_recv()
        for copy in self.over + self.corner:
            copy.wait_recv()
        for copy in self.first + self.over + self.halves + self.corner:
            copy.wait_send()

    COPIES = 9


def scatter_shapes(rows, width):
    half = width // 2
    return [
        pltpu.VMEM((2, 2, rows, width), BF16),
        pltpu.VMEM((2, rows, half), BF16),
        pltpu.VMEM((2, rows, half), BF16),
        pltpu.VMEM((2, rows, half), BF16),
        pltpu.VMEM((2, rows, half), BF16),
        pltpu.VMEM((rows, half), BF16),
        pltpu.VMEM((rows, half), BF16),
        pltpu.VMEM((rows, half), BF16),
        pltpu.VMEM((rows, half), BF16),
    ]


def wide(v):
    return v.astype(F32)


class Scatter:
    COPIES = 5

    def __init__(self, sems, team, x, scratch):
        self.x, self.scratch = x, scratch
        r0, s1l, s1r, r1l, r1r, s2l, s2r, r2l, r2r = scratch
        p = team.p
        self.b = b0, b1, b2 = bit_of(p, 1), bit_of(p, 2), bit_of(p, 4)
        width = x.shape[-1]
        self.left, self.right = pl.ds(0, width // 2), pl.ds(width // 2, width // 2)
        send = lambda src, dst, bit: sems.copy(src, dst, team.member(flip(p, bit)))
        self.first = send(x.at[:, :, 1 - b0], r0, 1)
        self.l1, self.r1 = send(s1l, r1l, 2), send(s1r, r1r, 4)
        self.l2, self.r2 = send(s2l, r2l, 4), send(s2r, r2r, 2)

    def begin(self):
        self.first.start()

    def relay(self):
        x, (r0, s1l, s1r, *_), (b0, b1, b2) = self.x, self.scratch, self.b
        left, right, n1, n2 = self.left, self.right, 1 - b1, 1 - b2
        self.first.wait_recv()
        for k in range(2):
            s1l[k] = (wide(x[k, n1, b0, :, left]) + wide(r0[k, n1, :, left])).astype(BF16)
        self.l1.start()
        for k in range(2):
            s1r[k] = (wide(x[n2, k, b0, :, right]) + wide(r0[n2, k, :, right])).astype(BF16)
        self.r1.start()

    def relay_again(self):
        x, (r0, s1l, s1r, r1l, r1r, s2l, s2r, r2l, r2r), (b0, b1, b2) = self.x, self.scratch, self.b
        left, right, n1, n2 = self.left, self.right, 1 - b1, 1 - b2
        self.l1.wait_recv()
        s2l[...] = (wide(x[n2, b1, b0, :, left]) + wide(r0[n2, b1, :, left]) + wide(r1l[n2])).astype(BF16)
        self.l2.start()
        self.r1.wait_recv()
        s2r[...] = (wide(x[b2, n1, b0, :, right]) + wide(r0[b2, n1, :, right]) + wide(r1r[n1])).astype(BF16)
        self.r2.start()

    def end(self, store):
        x, (r0, s1l, s1r, r1l, r1r, s2l, s2r, r2l, r2r), (b0, b1, b2) = self.x, self.scratch, self.b
        left, right = self.left, self.right
        self.l2.wait_recv()
        store(
            left,
            wide(x[b2, b1, b0, :, left]) + wide(r0[b2, b1, :, left]) + wide(r1l[b2]) + wide(r2l[...]),
        )
        self.r2.wait_recv()
        store(
            right,
            wide(x[b2, b1, b0, :, right]) + wide(r0[b2, b1, :, right]) + wide(r1r[b1]) + wide(r2r[...]),
        )
        for copy in (self.first, self.l1, self.r1, self.l2, self.r2):
            copy.wait_send()


def kernel_params(collective_id):
    return pltpu.CompilerParams(
        collective_id=collective_id, has_side_effects=True, vmem_limit_bytes=VMEM_LIMIT
    )


def inputs_kernel(dims, tokens, wq, wk, wv, gains, w_gate, w_up, tok_full, wqkv, gains_full, gate_cut, up_cut,
                  q_in, k_in, v_in, qkv_cut, slab_g, slab_u, cut_g, cut_u, send, recv, local):
    team = Team(*dims)
    B, F = team.B, team.F
    sems = Sems(send, recv)
    loads = [
        pltpu.make_async_copy(src, dst, local.at[i])
        for i, (src, dst) in enumerate(
            [(wq, q_in), (wk, k_in), (wv, v_in), (w_gate, slab_g), (w_up, slab_u), (tokens, tok_full.at[team.p]),
             (gains, gains_full.at[team.f])]
        )
    ]
    for load in loads:
        load.start()
    greet(team_peers(team))
    rows = tokens.shape[0]
    gather = Gather(
        sems, team.p, B * F, team.member, tokens,
        lambda i: tok_full.at[i],
        lambda i, k: tok_full.at[i, pl.ds(k * rows // 2, rows // 2)],
    )
    gather.begin()
    small = [sems.copy(gains, gains_full.at[team.f], peer) for peer in row_peers(team)]
    for copy in small:
        copy.start()
    for load in loads[:3]:
        load.wait()
    for f in range(F):
        for y in range(B):
            h = f * B + y

            @pl.when(team.y == y)
            def _():
                qkv_cut[f, :, 0:QW] = q_in[:, h * QW : (h + 1) * QW]
                qkv_cut[f, :, QW : QW + HEAD_SIZE] = k_in[:, h * HEAD_SIZE : (h + 1) * HEAD_SIZE]
                qkv_cut[f, :, QW + HEAD_SIZE : QW + 2 * HEAD_SIZE] = v_in[:, h * HEAD_SIZE : (h + 1) * HEAD_SIZE]

    sent = []
    for d in range(1, F):
        to = lax.rem(team.f + d, F)
        sent.append(sems.copy(qkv_cut.at[to], wqkv.at[team.f], team.same_row(to)))
        sent[-1].start()
    own = pltpu.make_async_copy(qkv_cut.at[team.f], wqkv.at[team.f], local.at[7])
    own.start()
    gather.relay()
    stores = []
    for i, (slab, cut, out) in enumerate([(slab_g, cut_g, gate_cut), (slab_u, cut_u, up_cut)]):
        loads[3 + i].wait()
        width = cut.shape[-1]

        @pl.loop(0, slab.shape[0] // 32)
        def _(r):
            at = pl.ds(pl.multiple_of(r * 32, 32), 32)
            for f in range(F):
                for y in range(B):
                    q = f * B + y

                    @pl.when(team.y == y)
                    def _():
                        cut[f, at, :] = slab[at, q * width : (q + 1) * width]

        stores.append(pltpu.make_async_copy(cut, out, local.at[8 + i]))
        stores[-1].start()
    gather.end()
    for copy in small + sent:
        copy.wait()
    for copy in loads[5:] + [own] + stores:
        copy.wait()


def gather_inputs(dims, tokens, wq, wk, wv, gains, w_gate, w_up):
    B, F, T = dims
    rows, width = tokens.shape
    depth, ff = w_gate.shape
    cols = ff // (B * F)
    copies = Gather.COPIES + 2 * (F - 1)
    heads = QW + 2 * HEAD_SIZE
    return pl.pallas_call(
        functools.partial(inputs_kernel, dims),
        out_shape=(
            jax.ShapeDtypeStruct((B * F, rows, width), BF16),
            jax.ShapeDtypeStruct((F, depth, heads), BF16),
            jax.ShapeDtypeStruct((F,) + gains.shape, BF16),
            jax.ShapeDtypeStruct((F, depth, cols), BF16),
            jax.ShapeDtypeStruct((F, depth, cols), BF16),
        ),
        in_specs=[ANY] * 7,
        out_specs=[ANY] * 5,
        scratch_shapes=[
            pltpu.VMEM(wq.shape, BF16),
            pltpu.VMEM(wk.shape, BF16),
            pltpu.VMEM(wv.shape, BF16),
            pltpu.VMEM((F, depth, heads), BF16),
            pltpu.VMEM(w_gate.shape, BF16),
            pltpu.VMEM(w_up.shape, BF16),
            pltpu.VMEM((F, depth, cols), BF16),
            pltpu.VMEM((F, depth, cols), BF16),
            pltpu.SemaphoreType.DMA((copies,)),
            pltpu.SemaphoreType.DMA((copies,)),
            pltpu.SemaphoreType.DMA((10,)),
        ],
        compiler_params=kernel_params(1),
        name="gather_inputs",
    )(tokens, wq, wk, wv, gains, w_gate, w_up)


def lane_ids(rows):
    return lax.broadcasted_iota(jnp.int32, (rows, LANES), 1)


def widen_keys(kv, spans, first_row, kx, vx):
    rows = kv.shape[0]
    lane = lane_ids(rows)
    row = lax.broadcasted_iota(jnp.int32, (rows, LANES), 0) + first_row
    inside = (row >= spans[0:1, :]) & (row < spans[1:2, :])
    wide = kv.astype(F32)
    kx[...] = jnp.where(lane < HEAD_SIZE, wide, jnp.where(inside, 1.0, 0.0)).astype(BF16)
    vx[...] = jnp.where(lane < HEAD_SIZE, pltpu.roll(wide, HEAD_SIZE, 1), 1.0).astype(BF16)


def dot_last(a, b):
    return lax.dot_general(a, b, (((1,), (1,)), ((), ())), preferred_element_type=F32)


def attend_kernel(dims, qx, kv, spans, dy, wo, gate_cut, up_cut, kv_all, acc, mixed, dy_full, wo_full, w_gate, w_up,
                  kx, vx, packed, send, recv, line_send, line_recv, local):
    team = Team(*dims)
    B, F, T = dims
    t = team.t
    sems = Sems(send, recv)
    rows = kv.shape[0]
    part = rows // 2
    homes = [
        pltpu.make_async_copy(kv, kv_all.at[t], local.at[0]),
        pltpu.make_async_copy(dy, dy_full.at[team.p], local.at[1]),
        pltpu.make_async_copy(wo, wo_full.at[team.f], local.at[2]),
        pltpu.make_async_copy(gate_cut.at[team.f], w_gate.at[team.f], local.at[3]),
        pltpu.make_async_copy(up_cut.at[team.f], w_up.at[team.f], local.at[4]),
    ]
    for copy in homes:
        copy.start()
    greet(team_peers(team) + line_peers(team))

    def line_copy(d, source, to):
        return pltpu.make_async_remote_copy(
            src_ref=kv, dst_ref=kv_all.at[source], send_sem=line_send.at[d], recv_sem=line_recv.at[source],
            device_id=team.other_team(to), device_id_type=MESH,
        )

    for d in range(1, T):

        @pl.when(t + d < T)
        def _():
            line_copy(d, t, t + d).start()

    half_wo, half_dy = wo.shape[0] // 2, dy.shape[0] // 2
    gather_wo = Gather(
        sems, team.f, F, team.same_row, wo, lambda i: wo_full.at[i],
        lambda i, k: wo_full.at[i, pl.ds(k * half_wo, half_wo)],
    )
    gather_wo.begin()
    sent = []
    for cut, full in ((gate_cut, w_gate), (up_cut, w_up)):
        for d in range(1, F):
            to = lax.rem(team.f + d, F)
            sent.append(sems.copy(cut.at[to], full.at[team.f], team.same_row(to)))
            sent[-1].start()
    gather_dy = Gather(
        sems, team.p, B * F, team.member, dy, lambda i: dy_full.at[i],
        lambda i, k: dy_full.at[i, pl.ds(k * half_dy, half_dy)],
    )
    gather_dy.begin()
    homes[0].wait()
    widen_keys(kv_all[t], spans, t * rows, kx, vx)
    causal = lax.broadcasted_iota(jnp.int32, (part, part), 1) <= lax.broadcasted_iota(jnp.int32, (part, part), 0)

    def piece(q, k, masked):
        scores = dot_last(q, kx[k * part : (k + 1) * part, :])
        weights = jnp.exp(scores)
        if masked:
            weights = jnp.where(causal, weights, 0.0)
        return jnp.dot(weights.astype(BF16), vx[k * part : (k + 1) * part, :], preferred_element_type=F32)

    @pl.loop(0, GROUP)
    def _(h):
        acc[h, 0:part, :] = piece(qx[h, 0:part, :], 0, True)
        low = qx[h, part:rows, :]
        acc[h, part:rows, :] = piece(low, 0, False) + piece(low, 1, True)

    gather_wo.relay()

    @pl.loop(1, t + 1)
    def _(j):
        source = t - j
        line_copy(0, source, t).wait_recv()
        widen_keys(kv_all[source], spans, source * rows, kx, vx)

        @pl.loop(0, GROUP)
        def _(h):
            for k in range(2):
                at = pl.ds(k * part, part)
                q = qx[h, at, :]
                acc[h, at, :] = acc[h, at, :] + piece(q, 0, False) + piece(q, 1, False)

    for h in range(GROUP):
        out = acc[h, :, 0:HEAD_SIZE] / acc[h, :, HEAD_SIZE : 2 * HEAD_SIZE]
        out = out.astype(BF16)
        if h < 2:
            packed[0:rows, h * HEAD_SIZE : (h + 1) * HEAD_SIZE] = out
        else:
            packed[rows : rows + part, 0:HEAD_SIZE] = out[0:part]
            packed[rows : rows + part, HEAD_SIZE : 2 * HEAD_SIZE] = out[part:rows]
    home = pltpu.make_async_copy(packed, mixed.at[team.p], local.at[5])
    home.start()
    half_mixed = packed.shape[0] // 2
    gather_mixed = Gather(
        sems, team.p, B * F, team.member, packed, lambda i: mixed.at[i],
        lambda i, k: mixed.at[i, pl.ds(k * half_mixed, half_mixed)],
    )
    gather_mixed.begin()
    gather_mixed.relay()
    gather_dy.relay()
    gather_mixed.end()
    gather_wo.end()
    gather_dy.end()
    for copy in sent:
        copy.wait()
    for copy in homes[1:] + [home]:
        copy.wait()
    for d in range(1, T):

        @pl.when(t + d < T)
        def _():
            line_copy(d, t, t + d).wait_send()


def attend(dims, qx, kv, spans, dy, wo, gate_cut, up_cut):
    B, F, T = dims
    rows = kv.shape[0]
    copies = 3 * Gather.COPIES + 2 * (F - 1)
    packed = (rows + rows // 2, LANES)
    return pl.pallas_call(
        functools.partial(attend_kernel, dims),
        out_shape=(
            jax.ShapeDtypeStruct((T, rows, LANES), BF16),
            jax.ShapeDtypeStruct((GROUP, rows, LANES), F32),
            jax.ShapeDtypeStruct((B * F,) + packed, BF16),
            jax.ShapeDtypeStruct((B * F,) + dy.shape, BF16),
            jax.ShapeDtypeStruct((F,) + wo.shape, BF16),
            jax.ShapeDtypeStruct(gate_cut.shape, BF16),
            jax.ShapeDtypeStruct(up_cut.shape, BF16),
        ),
        in_specs=[VMEM, ANY, VMEM, ANY, ANY, ANY, ANY],
        out_specs=[VMEM, VMEM, ANY, ANY, ANY, ANY, ANY],
        scratch_shapes=[
            pltpu.VMEM((rows, LANES), BF16),
            pltpu.VMEM((rows, LANES), BF16),
            pltpu.VMEM(packed, BF16),
            pltpu.SemaphoreType.DMA((copies,)),
            pltpu.SemaphoreType.DMA((copies,)),
            pltpu.SemaphoreType.DMA((T,)),
            pltpu.SemaphoreType.DMA((T,)),
            pltpu.SemaphoreType.DMA((6,)),
        ],
        compiler_params=kernel_params(2),
        name="attend",
    )(qx, kv, spans, dy, wo, gate_cut, up_cut)


HOP = 2
LAG = 3


class GradSum:
    RED, FIN, HAND, OWN, OVER, HOME, INTO = range(7)

    def __init__(self, team, kinds, red_recv, fin_recv, hand_recvs, bulk):
        self.team, self.kinds = team, kinds
        self.red_recv, self.fin_recv, self.hand_recvs, self.bulk = red_recv, fin_recv, hand_recvs, bulk
        self.opposite = team.member(lax.rem(team.p + team.F, team.B * team.F))

    @staticmethod
    def steps(kinds, T):
        last = max(first + rows // 2 // step for rows, step, first in kinds)
        return last + 2 * HOP * (T - 1) + LAG

    def remote(self, src, dst, send_sem, recv_sem, device):
        return pltpu.make_async_remote_copy(
            src_ref=src, dst_ref=dst, send_sem=send_sem, recv_sem=recv_sem, device_id=device, device_id_type=MESH
        )

    def is_first(self, way):
        return self.team.t == (self.team.T - 1 if way else 0)

    def is_last(self, way):
        return self.team.t == (0 if way else self.team.T - 1)

    def rows(self, k, way, c):
        g, land, out, step, first, how = self.kinds[k]
        return pl.ds(pl.multiple_of(way * (g.shape[0] // 2) + c * step, 16), step)

    def reduce_copy(self, k, way, at, i):
        g, land = self.kinds[k][:2]
        to = self.team.other_team(self.team.t + 1 - 2 * way)
        return self.remote(g.at[at], land.at[at], self.bulk.at[self.RED, k, way], self.red_recv.at[way, i], to)

    def final_copy(self, k, way, at, i):
        land = self.kinds[k][1]
        to = self.team.other_team(self.team.t - 1 + 2 * way)
        return self.remote(land.at[at], land.at[at], self.bulk.at[self.FIN, k, way], self.fin_recv.at[way, i], to)

    def reduce(self, k, way, c, i):
        g, land = self.kinds[k][:2]
        at = self.rows(k, way, c)

        @pl.when(self.is_first(way))
        def _():
            self.reduce_copy(k, way, at, i).start()

        @pl.when(jnp.logical_not(self.is_first(way)))
        def _():
            self.reduce_copy(k, way, at, i).wait_recv()
            summed = (wide(g[at, :]) + wide(land[at, :])).astype(BF16)

            @pl.when(self.is_last(way))
            def _():
                land[at, :] = summed

            @pl.when(jnp.logical_not(self.is_last(way)))
            def _():
                g[at, :] = summed
                self.reduce_copy(k, way, at, i).start()

    def place(self, k, way, c):
        g, land, out, step, first, how = self.kinds[k]
        shard = g.shape[0] // self.team.F
        row = way * (g.shape[0] // 2) + c * step
        return lax.div(row, shard), lax.rem(row, shard)

    def finish(self, k, way, c, i):
        g, land, out, step, first, how = self.kinds[k]
        team, bulk = self.team, self.bulk
        B, F, y, f = team.B, team.F, team.y, team.f
        at = self.rows(k, way, c)

        @pl.when(jnp.logical_not(self.is_last(way)))
        def _():
            self.final_copy(k, way, at, i).wait_recv()

        @pl.when(jnp.logical_not(self.is_first(way)))
        def _():
            self.final_copy(k, way, at, i).start()

        if how == "rows":
            to, row = self.place(k, way, c)
            dst = out.at[f * B + y, pl.ds(pl.multiple_of(row, 16), step)]

            @pl.when(to == f)
            def _():
                pltpu.make_async_copy(land.at[at], dst, bulk.at[self.HOME, k, 0]).start()
                if B == 2:
                    self.remote(land.at[at], dst, bulk.at[self.OVER, k, 0], bulk.at[self.INTO, k, 0],
                                self.opposite).start()

            @pl.when(to != f)
            def _():
                self.remote(land.at[at], dst, bulk.at[self.HAND, k, 0], self.hand_recvs[k].at[f, lax.div(row, step)],
                            team.same_row(to)).start()
        elif how == "stay":
            dst = out.at[y, at]
            pltpu.make_async_copy(land.at[at], dst, bulk.at[self.HOME, k, 0]).start()
            if B == 2:
                self.remote(land.at[at], dst, bulk.at[self.OVER, k, 0], bulk.at[self.INTO, k, 0],
                            self.opposite).start()
        else:
            for j in range(F // 2):
                to = way * (F // 2) + j
                src = land.at[pl.ds(16 * to, 16)]
                for row in range(B):
                    member = row * F + to

                    @pl.when(team.p == member)
                    def _():
                        pltpu.make_async_copy(src, out.at[team.p], bulk.at[self.HOME, k, 0]).start()

                    @pl.when(team.p != member)
                    def _():
                        self.remote(src, out.at[team.p], bulk.at[self.HAND, k, 0], bulk.at[self.INTO, k, 0],
                                    (team.t * B + row, to)).start()

    def pass_over(self, k, way, c, i):
        g, land, out, step, first, how = self.kinds[k]
        if how != "rows":
            return
        team = self.team
        to, row = self.place(k, way, c)

        @pl.when(to == team.f)
        def _():
            for d in range(1, team.F):
                source = lax.rem(team.f + d, team.F)
                ref = out.at[source * team.B + team.y, pl.ds(pl.multiple_of(row, 16), step)]
                self.remote(land.at[self.rows(k, way, c)], ref, self.bulk.at[self.HAND, k, 0],
                            self.hand_recvs[k].at[source, lax.div(row, step)], team.same_row(team.f)).wait_recv()
                if team.B == 2:
                    self.remote(ref, ref, self.bulk.at[self.OVER, k, 1], self.bulk.at[self.INTO, k, 0],
                                self.opposite).start()

    def each(self, i, way, body):
        for k, (g, land, out, step, first, how) in enumerate(self.kinds):
            count = g.shape[0] // 2 // step

            pl.when((i >= first) & (i < first + count))(functools.partial(lambda k, c: body(k, way, c, i), k, i - first))

    def step(self, s):
        T, t = self.team.T, self.team.t
        for way in range(2):
            place = T - 1 - t if way else t
            done = s - HOP * (2 * (T - 1) - place)
            self.each(s - HOP * place, way, self.reduce)
            self.each(done, way, self.finish)
            self.each(done - LAG, way, self.pass_over)

    def drain(self, ref, sem):
        pltpu.make_async_copy(ref, ref, sem).wait()

    def end(self):
        bulk, B, F = self.bulk, self.team.B, self.team.F
        for k, (g, land, out, step, first, how) in enumerate(self.kinds):
            rows = g.shape[0]
            some = lambda n: g.at[pl.ds(0, n)]
            for way in range(2):

                @pl.when(jnp.logical_not(self.is_last(way)))
                def _():
                    self.drain(some(rows // 2), bulk.at[self.RED, k, way])

                @pl.when(jnp.logical_not(self.is_first(way)))
                def _():
                    self.drain(some(rows // 2), bulk.at[self.FIN, k, way])

            if how == "rows":
                shard = rows // F
                self.drain(some(rows - shard), bulk.at[self.HAND, k, 0])
                self.drain(some(shard), bulk.at[self.HOME, k, 0])
                if B == 2:
                    self.drain(some(shard), bulk.at[self.OVER, k, 0])
                    self.drain(some(rows - shard), bulk.at[self.OVER, k, 1])
                    self.drain(g, bulk.at[self.INTO, k, 0])
            elif how == "stay":
                self.drain(g, bulk.at[self.HOME, k, 0])
                if B == 2:
                    self.drain(g, bulk.at[self.OVER, k, 0])
                    self.drain(g, bulk.at[self.INTO, k, 0])
            else:
                others = out.at[pl.ds(0, B * F - 1)]
                self.drain(out.at[0], bulk.at[self.HOME, k, 0])
                self.drain(others, bulk.at[self.HAND, k, 0])
                self.drain(others, bulk.at[self.INTO, k, 0])


def rotate_back(u, cosine, sine):
    half = u.shape[-1] // 2
    swapped = jnp.concatenate([-u[:, half:], u[:, :half]], 1)
    return u * cosine - swapped * sine


def unit_and_factor(x):
    factor = lax.rsqrt(jnp.mean(x * x, -1, keepdims=True) + EPSILON)
    return x * factor, factor


def first_steps(dims):
    T = dims[2]
    attention = 8
    keys = attention + 2 * T + 1
    return dict(scatter1=1, scatter2=3, resid=4, relay=6, heads=7, attention=attention, keys=keys,
                again1=keys + 1, again2=keys + 3, tokens=keys + 4, down1=keys + 5, down2=keys + 6, down3=keys + 7)


def grad_kinds(dims, depth, hidden):
    at = first_steps(dims)
    kinds, place = [], 0
    for rows, width, step, ready, how in (
        (hidden, depth, 48, 0, "stay"),
        (depth, hidden, 64, 0, "rows"),
        (depth, hidden, 64, 0, "rows"),
        (QW, depth, 48, at["heads"] + 1, "stay"),
        (depth, QW + 2 * HEAD_SIZE, 96, at["keys"] + 1, "rows"),
        (16 * dims[1], max(depth // dims[1], LANES), 8 * dims[1], at["tokens"] + 1, "gain"),
    ):
        place = max(place, ready)
        kinds.append((rows, width, step, place, how))
        place += rows // 2 // step
    return kinds


def back_kernel(dims, kinds, steps, grad_hidden, down_out, g_down, g_gate, g_up, resid, tokens, cotangent, gains, acc, qx, kv_all, spans,
                heads, cosine, sine, own_wo, wqkv, normed,
                out_down, out_gate, out_up, out_wo, out_heads, out_gains, layer_out, tokens_grad,
                xs, xd, own_down, own_gate, own_up, own_gwo, own_heads, own_gains,
                land_down, land_gate, land_up, land_wo, land_heads, land_gains,
                grad_resid, attn_own, big, dox, mixed, dq, dkv, kv_in, dkv_sum, turned, small, kx, vx, dk, dv, wq_in, *rest):
    scratch1, rest = rest[:9], rest[9:]
    scratch2, rest = rest[:9], rest[9:]
    send, recv, line_send, line_recv, red_recv, fin_recv, hand_gate, hand_up, hand_heads, bulk, local = rest
    team = Team(*dims)
    B, F, T = dims
    t, p = team.t, team.p
    at = first_steps(dims)
    own_rows, width = resid.shape
    rows = qx.shape[1]
    part = rows // 2
    block = rows // 4
    depth = width // F
    sems = Sems(send, recv)
    loads = [
        pltpu.make_async_copy(src, dst, local.at[i])
        for i, (src, dst) in enumerate(
            [(grad_hidden, xs), (g_down, own_down), (g_gate, own_gate), (g_up, own_up), (down_out, xd), (wqkv, wq_in)]
        )
    ]
    for load in loads:
        load.start()
    own_gains[...] = jnp.zeros_like(own_gains)
    greet(team_peers(team) + line_peers(team))
    loads[0].wait()
    scatter = Scatter(sems, team, xs, scratch1)
    scatter.begin()
    again = Scatter(sems, team, xs, scratch1)
    down = Scatter(sems, team, xd, scratch2)
    half = own_rows // 2
    gather = Gather(
        sems, p, B * F, team.member, attn_own,
        lambda i: big.at[pl.ds(pl.multiple_of(i * own_rows, 16), own_rows)],
        lambda i, k: big.at[pl.ds(pl.multiple_of(i * own_rows + k * half, 16), half)],
    )
    sums = GradSum(
        team,
        [
            (own, land, out) + kind[2:]
            for own, land, out, kind in zip(
                (own_down, own_gate, own_up, own_gwo, own_heads, own_gains),
                (land_down, land_gate, land_up, land_wo, land_heads, land_gains),
                (out_down, out_gate, out_up, out_wo, out_heads, out_gains),
                kinds,
            )
        ],
        red_recv, fin_recv, [None, hand_gate, hand_up, None, hand_heads, None], bulk,
    )
    for load in loads[1:]:
        load.wait()
    gain_attn, gain_ffn = gains[0:1, :], gains[1:2, :]
    gain_q, gain_k = gains[2:3, 0:HEAD_SIZE], gains[3:4, 0:HEAD_SIZE]
    home = pltpu.make_async_copy(attn_own, big.at[pl.ds(pl.multiple_of(p * own_rows, 16), own_rows)], local.at[6])
    fetch = pltpu.make_async_copy(normed, big, local.at[7])

    def resid_phase():
        def store(columns, total):
            grad_resid[:, columns] = total

        scatter.end(store)
        term = jnp.zeros((1, width), F32)
        for r in range(0, own_rows, 32):
            here = slice(r, r + 32)
            unit, factor = unit_and_factor(resid[here, :])
            upstream = grad_resid[here, :]
            term = term + jnp.sum(upstream * unit, 0, keepdims=True)
            total = wide(cotangent[here, :]) + norm_back(upstream, unit, factor, gain_ffn)
            grad_resid[here, :] = total
            attn_own[here, :] = total.astype(BF16)
        small[1:2, :] = term
        home.start()
        gather.begin()

    def heads_phase():
        gather.end()
        home.wait()
        lane = lane_ids(block)

        @pl.loop(0, rows // block)
        def _(r):
            here = pl.ds(pl.multiple_of(r * block, block), block)
            grad = dot_last(big[here, :], own_wo[...]).astype(BF16)
            for h in range(GROUP):
                sums_h = acc[h, here, :]
                total = pltpu.roll(sums_h, HEAD_SIZE, 1)
                out = sums_h / total
                mixed[here, h * HEAD_SIZE : (h + 1) * HEAD_SIZE] = out[:, :HEAD_SIZE].astype(BF16)
                do = wide(grad[:, h * HEAD_SIZE : (h + 1) * HEAD_SIZE])
                do = jnp.concatenate([do, jnp.zeros_like(do)], 1)
                delta = -jnp.sum(jnp.where(lane < HEAD_SIZE, do * out, 0.0), 1, keepdims=True)

                def put(x, first, value):
                    for i in range(3):
                        x = jnp.where(lane == first + i, wide(value.astype(BF16)), x)
                        value = value - wide(value.astype(BF16))
                    return x

                dox[h, here, :] = put(do, HEAD_SIZE, delta).astype(BF16)
                log_sum = -jnp.log(jnp.where(lane < HEAD_SIZE, total, sums_h))
                qx[h, here, :] = put(wide(qx[h, here, :]), HEAD_SIZE + NDOCS, log_sum).astype(BF16)

        own_gwo[...] = lax.dot_general(
            mixed[...], big[...], (((0,), (0,)), ((), ())), preferred_element_type=F32
        ).astype(BF16)
        dq[...] = jnp.zeros_like(dq)

    causal = lax.broadcasted_iota(jnp.int32, (part, part), 0) <= lax.broadcasted_iota(jnp.int32, (part, part), 1)

    def piece(h, q_rows, k_rows, masked):
        q = qx[h, q_rows, :]
        do = dox[h, q_rows, :]
        keys = kx[k_rows, :]
        weights = jnp.exp(dot_last(keys, q))
        if masked:
            weights = jnp.where(causal, weights, 0.0)
        dscore = (weights * dot_last(vx[k_rows, :], do)).astype(BF16)
        dv[...] += jnp.dot(weights.astype(BF16), do, preferred_element_type=F32)
        dk[...] += jnp.dot(dscore, q, preferred_element_type=F32)
        dq[h, q_rows, :] += lax.dot_general(dscore, keys, (((0,), (0,)), ((), ())), preferred_element_type=F32)

    def line_copy(owner, source):
        return pltpu.make_async_remote_copy(
            src_ref=dkv.at[owner], dst_ref=dkv.at[source], send_sem=line_send.at[owner],
            recv_sem=line_recv.at[source], device_id=team.other_team(owner), device_id_type=MESH,
        )

    def fetch_keys(source):
        slot = lax.rem(source, 2)
        return pltpu.make_async_copy(kv_all.at[source], kv_in.at[slot], local.at[8 + slot])

    fetch_keys(t * 0).start()

    def attention_unit(source, k):
        @pl.when(k == 0)
        def _():
            fetch_keys(source).wait()

            @pl.when(source < t)
            def _():
                fetch_keys(source + 1).start()

            widen_keys(kv_in[lax.rem(source, 2)], spans, source * rows, kx, vx)

        k_rows = pl.ds(pl.multiple_of(k * part, part), part)
        dk[...] = jnp.zeros_like(dk)
        dv[...] = jnp.zeros_like(dv)

        @pl.when(source < t)
        def _():
            @pl.loop(0, GROUP)
            def _(h):
                for q in range(2):
                    piece(h, slice(q * part, (q + 1) * part), k_rows, False)

        @pl.when(source == t)
        def _():
            for diagonal in range(2):

                @pl.when(k == diagonal)
                def _():
                    @pl.loop(0, GROUP)
                    def _(h):
                        for q in range(diagonal, 2):
                            piece(h, slice(q * part, (q + 1) * part), slice(diagonal * part, (diagonal + 1) * part),
                                  q == diagonal)

        dkv[source, k_rows, :] = jnp.where(
            lane_ids(part) < HEAD_SIZE, dk[...], pltpu.roll(dv[...], HEAD_SIZE, 1)
        ).astype(BF16)

        @pl.when((k == 1) & (source < t))
        def _():
            line_copy(source, t).start()

    def keys_phase():
        fetch.start()
        dkv_sum[...] = wide(dkv[t])
        for d in range(1, T):

            @pl.when(t + d < T)
            def _():
                line_copy(t, t + d).wait_recv()
                dkv_sum[...] += wide(dkv[t + d])

        small[2:4, :] = jnp.zeros((2, width), F32)

        @pl.loop(0, rows // block)
        def _(r):
            here = pl.ds(pl.multiple_of(r * block, block), block)
            cos, sin = cosine[here, :], sine[here, :]
            q_term = jnp.zeros((1, HEAD_SIZE), F32)
            for h in range(GROUP + 1):
                if h < GROUP:
                    u, gain = dq[h, here, 0:HEAD_SIZE] * HEAD_SIZE ** (-0.5), gain_q
                else:
                    u, gain = dkv_sum[here, 0:HEAD_SIZE], gain_k
                u = rotate_back(u, cos, sin)
                unit, factor = unit_and_factor(heads[h, here, :])
                term = jnp.sum(u * unit, 0, keepdims=True)
                if h < GROUP:
                    q_term = q_term + term
                else:
                    small[3:4, 0:HEAD_SIZE] += term
                turned[here, h * HEAD_SIZE : (h + 1) * HEAD_SIZE] = norm_back(u, unit, factor, gain).astype(BF16)
            small[2:3, 0:HEAD_SIZE] += q_term
            h = GROUP + 1
            turned[here, h * HEAD_SIZE : (h + 1) * HEAD_SIZE] = dkv_sum[here, HEAD_SIZE : 2 * HEAD_SIZE].astype(BF16)

        for m in range(2 * 2 * 2):
            xs[m // 4, m // 2 % 2, m % 2] = dot_last(
                turned[m * own_rows : (m + 1) * own_rows, :], wq_in[...]
            ).astype(BF16)
        again.begin()
        fetch.wait()
        for r in range(0, width, 256):
            own_heads[r : r + 256, :] = lax.dot_general(
                big[:, r : r + 256], turned[...], (((0,), (0,)), ((), ())), preferred_element_type=F32
            ).astype(BF16)

    def tokens_phase():
        def store(columns, total):
            tokens_grad[:, columns] = total

        again.end(store)
        down.begin()
        term = jnp.zeros((1, width), F32)
        for r in range(0, own_rows, 32):
            here = slice(r, r + 32)
            unit, factor = unit_and_factor(wide(tokens[here, :]))
            upstream = tokens_grad[here, :]
            term = term + jnp.sum(upstream * unit, 0, keepdims=True)
            tokens_grad[here, :] = grad_resid[here, :] + norm_back(upstream, unit, factor, gain_attn)
        small[0:1, :] = term
        lanes = own_gains.shape[1]
        row = lax.broadcasted_iota(jnp.int32, (16, lanes), 0)

        def cut(i, first, count):
            value = small[i : i + 1, first : first + count]
            if count < lanes:
                value = jnp.concatenate([value, jnp.zeros((1, lanes - count), F32)], 1)
            return jnp.where(row == i, jnp.broadcast_to(value, (16, lanes)), 0.0)

        for i in range(F):
            few = HEAD_SIZE // F
            own_gains[16 * i : 16 * i + 16, :] = (
                cut(0, i * depth, depth) + cut(1, i * depth, depth) + cut(2, i * few, few) + cut(3, i * few, few)
            ).astype(BF16)

    def down_phase():
        def store(columns, total):
            layer_out[:, columns] = resid[:, columns] + total

        down.end(store)

    @pl.loop(0, steps)
    def _(s):
        sums.step(s)
        for name, body in (
            ("scatter1", scatter.relay), ("scatter2", scatter.relay_again), ("resid", resid_phase),
            ("relay", gather.relay), ("heads", heads_phase), ("keys", keys_phase), ("again1", again.relay),
            ("again2", again.relay_again), ("tokens", tokens_phase), ("down1", down.relay),
            ("down2", down.relay_again), ("down3", down_phase),
        ):
            pl.when(s == at[name])(body)
        unit = s - at["attention"]

        @pl.when((unit >= 0) & (lax.div(unit, 2) <= t))
        def _():
            attention_unit(lax.div(unit, 2), lax.rem(unit, 2))

    for d in range(1, T):

        @pl.when(t - d >= 0)
        def _():
            line_copy(t - d, t).wait_send()

    sums.end()


def backward(dims, grad_hidden, down_out, g_down, g_gate, g_up, resid, tokens, cotangent, gains, acc, qx, kv_all, spans,
             heads, cosine, sine, own_wo, wqkv, normed):
    B, F, T = dims
    own_rows, width = resid.shape
    rows = qx.shape[1]
    part = rows // 2
    hidden = g_down.shape[0]
    n = B * F
    kinds = grad_kinds(dims, width, hidden)
    steps = max(
        GradSum.steps([(rows_, step, first) for rows_, _, step, first, _ in kinds], T), first_steps(dims)["down3"] + 1
    )
    positions = max(first + rows_ // 2 // step for rows_, _, step, first, _ in kinds)
    outs = []
    for rows_, wide_, step, first, how in kinds:
        if how == "rows":
            shape = (n, rows_ // F, wide_)
        elif how == "stay":
            shape = (B, rows_, wide_)
        else:
            shape = (n, 16, wide_)
        outs.append(jax.ShapeDtypeStruct(shape, BF16))
    outs += [jax.ShapeDtypeStruct((own_rows, width), F32), jax.ShapeDtypeStruct((own_rows, width), F32)]
    eight = (2, 2, 2, own_rows, width)
    hands = [pltpu.SemaphoreType.DMA((F, kinds[k][0] // F // kinds[k][2])) for k in (1, 2, 4)]
    copies = 3 * Scatter.COPIES + Gather.COPIES
    return pl.pallas_call(
        functools.partial(back_kernel, dims, kinds, steps),
        out_shape=outs,
        in_specs=[ANY] * 5 + [VMEM] * 6 + [ANY] + [VMEM] * 5 + [ANY] * 2,
        out_specs=[ANY] * 6 + [VMEM] * 2,
        scratch_shapes=[
            pltpu.VMEM(eight, BF16),
            pltpu.VMEM(eight, BF16),
        ]
        + [pltpu.VMEM((kind[0], kind[1]), BF16) for kind in kinds] * 2
        + [
            pltpu.VMEM((own_rows, width), F32),
            pltpu.VMEM((own_rows, width), BF16),
            pltpu.VMEM((rows, width), BF16),
            pltpu.VMEM(qx.shape, BF16),
            pltpu.VMEM((rows, QW), BF16),
            pltpu.VMEM(qx.shape, F32),
            pltpu.VMEM(kv_all.shape, BF16),
            pltpu.VMEM((2,) + kv_all.shape[1:], BF16),
            pltpu.VMEM((rows, LANES), F32),
            pltpu.VMEM((rows, QW + 2 * HEAD_SIZE), BF16),
            pltpu.VMEM((8, width), F32),
            pltpu.VMEM((rows, LANES), BF16),
            pltpu.VMEM((rows, LANES), BF16),
            pltpu.VMEM((part, LANES), F32),
            pltpu.VMEM((part, LANES), F32),
            pltpu.VMEM(wqkv.shape, BF16),
        ]
        + scatter_shapes(own_rows, width) * 2
        + [
            pltpu.SemaphoreType.DMA((copies,)),
            pltpu.SemaphoreType.DMA((copies,)),
            pltpu.SemaphoreType.DMA((T,)),
            pltpu.SemaphoreType.DMA((T,)),
            pltpu.SemaphoreType.DMA((2, positions)),
            pltpu.SemaphoreType.DMA((2, positions)),
            *hands,
            pltpu.SemaphoreType.DMA((7, len(kinds), 2)),
            pltpu.SemaphoreType.DMA((10,)),
        ],
        compiler_params=pltpu.CompilerParams(
            collective_id=3, has_side_effects=True, vmem_limit_bytes=60 * 1024 * 1024
        ),
        name="backward",
    )(grad_hidden.reshape(eight), down_out.reshape(eight), g_down, g_gate, g_up, resid, tokens, cotangent, gains, acc, qx,
      kv_all, spans, heads, cosine, sine, own_wo, wqkv, normed)


def place_kernel(n, gate, up, heads, down, wo, gate_out, up_out, wq_out, wk_out, wv_out, down_out, wo_out):
    hidden = gate.shape[-1]
    for q in range(n):
        gate_out[:, q * hidden : (q + 1) * hidden] = wide(gate[q])
        up_out[:, q * hidden : (q + 1) * hidden] = wide(up[q])
        block = wide(heads[q])
        wq_out[:, q * QW : (q + 1) * QW] = block[:, :QW]
        wk_out[:, q * HEAD_SIZE : (q + 1) * HEAD_SIZE] = block[:, QW : QW + HEAD_SIZE]
        wv_out[:, q * HEAD_SIZE : (q + 1) * HEAD_SIZE] = block[:, QW + HEAD_SIZE :]
    down_out[...] = wide(down[...])
    wo_out[...] = wide(wo[...])


def place(gate, up, heads, down, wo):
    n, depth, hidden = gate.shape
    width = down.shape[-1]
    down, wo = down.reshape(-1, width), wo.reshape(-1, width)
    step = 32
    count = depth // step
    many = lambda w: pl.BlockSpec((n, step, w), lambda i: (0, i, 0))
    cut = lambda a: pl.BlockSpec((a.shape[0] // count, width), lambda i: (i, 0))
    out = lambda w: pl.BlockSpec((step, w), lambda i: (i, 0))
    shape = lambda r, w: jax.ShapeDtypeStruct((r, w), F32)
    wq, wk = QW * n, HEAD_SIZE * n
    return pl.pallas_call(
        functools.partial(place_kernel, n),
        grid=(count,),
        out_shape=(
            shape(depth, n * hidden), shape(depth, n * hidden), shape(depth, wq), shape(depth, wk), shape(depth, wk),
            shape(down.shape[0], width), shape(wo.shape[0], width),
        ),
        in_specs=[many(hidden), many(hidden), many(QW + 2 * HEAD_SIZE), cut(down), cut(wo)],
        out_specs=[out(n * hidden), out(n * hidden), out(wq), out(wk), out(wk), cut(down), cut(wo)],
        compiler_params=pltpu.CompilerParams(vmem_limit_bytes=VMEM_LIMIT),
        name="place",
    )(gate, up, heads, down, wo)


def doc_layout(lengths, token_index):
    doc_ends = jnp.cumsum(lengths)
    passed = token_index[:, None] >= doc_ends[None, :]
    document_index = jnp.sum(passed.astype(jnp.int32), axis=1)
    doc_start = jnp.max(jnp.where(passed, doc_ends[None, :], 0), axis=1)
    return (document_index, token_index - doc_start)


def rotation(places, width):
    half_width = width // 2
    inverse_freq = jnp.power(ROPE_BASE, -(jnp.arange(half_width, dtype=F32) * 2.0 / width))
    angles = places.astype(F32)[:, None] * inverse_freq[None, :]
    cosine_values = jnp.cos(angles)
    sine_lookup = jnp.sin(angles)
    return (
        jnp.concatenate([cosine_values, cosine_values], 1),
        jnp.concatenate([sine_lookup, sine_lookup], 1),
    )


def apply_rotary(values_in, cosine_values, sine_lookup, sign):
    half_width = values_in.shape[-1] // 2
    swapped = jnp.concatenate([-values_in[..., half_width:], values_in[..., :half_width]], -1)
    return values_in * cosine_values + swapped * (sine_lookup * sign)


def scaled_input(values_in):
    factor = lax.rsqrt(jnp.mean(values_in * values_in, -1, keepdims=True) + EPSILON)
    return (values_in * factor, factor)


def norm_back(upstream, unit_rows, factor, gain_row):
    lifted = upstream * gain_row
    return factor * (lifted - unit_rows * jnp.mean(lifted * unit_rows, -1, keepdims=True))


def dot(a, b, dims=((1,), (0,))):
    return lax.dot_general(a, b, (dims, ((), ())), preferred_element_type=F32)


def on_device(
    tokens, lengths, wq, wk, wv, wo, w_gate, w_up, w_down, attn_gain, ffn_gain, q_gain, key_norm_gain, cotangent
):
    F = lax.axis_size("fsdp")
    B = KEY_VALUE_HEADS // F
    T = lax.axis_size("ctx") // B
    dims = (B, F, T)
    own_rows, width = tokens.shape
    rows = own_rows * KEY_VALUE_HEADS
    depth = width // F
    ctx, f = lax.axis_index("ctx"), lax.axis_index("fsdp")
    t, y = ctx // B, ctx % B
    p = y * F + f
    hidden = w_down.shape[0] // B

    gains = jnp.zeros((16, max(depth, LANES)), BF16)
    gains = gains.at[0, :depth].set(attn_gain).at[1, :depth].set(ffn_gain)
    gains = gains.at[2, : HEAD_SIZE // F].set(q_gain).at[3, : HEAD_SIZE // F].set(key_norm_gain)
    tok_full, wqkv, gains_full, gate_cut, up_cut = gather_inputs(dims, tokens, wq, wk, wv, gains, w_gate, w_up)
    gains_full = gains_full.astype(F32)
    gain_attn = gains_full[:, 0, :depth].reshape(-1)
    gain_ffn = gains_full[:, 1, :depth].reshape(-1)
    gain_query = gains_full[:, 2, : HEAD_SIZE // F].reshape(-1)
    gain_key = gains_full[:, 3, : HEAD_SIZE // F].reshape(-1)
    wqkv = wqkv.reshape(width, -1)

    token_index = t * rows + jnp.arange(rows, dtype=jnp.int32)
    docs, places = doc_layout(lengths, token_index)
    cosine_values, sine_lookup = rotation(places, HEAD_SIZE)
    cosine_values, sine_lookup = cosine_values[None], sine_lookup[None]
    ends = jnp.cumsum(lengths)
    ndocs = lengths.shape[0]
    big = jnp.int32(2**30)
    spans = jnp.stack([
        jnp.zeros((LANES,), jnp.int32).at[HEAD_SIZE : HEAD_SIZE + ndocs].set(ends - lengths),
        jnp.full((LANES,), big, jnp.int32).at[HEAD_SIZE : HEAD_SIZE + ndocs].set(ends),
    ])
    spans = jnp.concatenate([spans, jnp.zeros((6, LANES), jnp.int32)])

    inputs = tok_full.reshape(rows, width).astype(F32)
    unit_attn, factor_attn = scaled_input(inputs)
    normed = (unit_attn * gain_attn).astype(BF16)
    projected = dot(normed, wqkv)
    heads = jnp.transpose(projected.reshape(rows, GROUP + 2, HEAD_SIZE), (1, 0, 2))
    q_unit, q_factor = scaled_input(heads[:GROUP])
    k_unit, k_factor = scaled_input(heads[GROUP])
    queries = apply_rotary(q_unit * gain_query, cosine_values, sine_lookup, 1.0).astype(BF16)
    own_keys = apply_rotary(k_unit * gain_key, cosine_values[0], sine_lookup[0], 1.0).astype(BF16)
    own_values = heads[GROUP + 1].astype(BF16)
    scale = HEAD_SIZE ** (-0.5)
    apart = jnp.where(docs[:, None] == jnp.arange(ndocs)[None, :], 0.0, -APART).astype(BF16)
    apart = jnp.broadcast_to(apart[None], (GROUP, rows, ndocs))
    queries = (queries * jnp.asarray(scale, BF16)).astype(BF16)
    qx = jnp.concatenate([queries, apart, jnp.zeros((GROUP, rows, LANES - HEAD_SIZE - ndocs), BF16)], -1)
    kv = jnp.concatenate([own_keys, own_values], -1)
    kv_all, acc, mixed, dy_full, wo_full, gate_w, up_w = attend(
        dims, qx, kv, spans, cotangent, wo, gate_cut, up_cut
    )
    both = mixed[:, :rows].reshape(B, F, rows, 2 * HEAD_SIZE)
    third = mixed[:, rows:].reshape(B, F, rows // 2, 2, HEAD_SIZE)
    third = jnp.swapaxes(third, 2, 3).reshape(B, F, rows, HEAD_SIZE)
    mixed_heads = jnp.concatenate([both, third], -1)
    mixed_heads = jnp.transpose(mixed_heads, (2, 1, 0, 3)).reshape(rows, QUERY_HEADS * HEAD_SIZE)
    wo_full = wo_full.reshape(-1, width)
    gate_w = gate_w.reshape(width, hidden)
    up_w = up_w.reshape(width, hidden)
    down_w = lax.dynamic_slice_in_dim(w_down, y * hidden, hidden, 0)
    own_wo = lax.dynamic_slice_in_dim(wo, y * QW, QW, 0)
    dy_full = dy_full.reshape(rows, width)

    resid = inputs + dot(mixed_heads, wo_full)
    unit_ffn, factor_ffn = scaled_input(resid)
    hidden_in = (unit_ffn * gain_ffn).astype(BF16)
    gate = dot(hidden_in, gate_w)
    upper = dot(hidden_in, up_w)
    sigma = jax.nn.sigmoid(gate)
    silu_gate = gate * sigma
    act_rows = (silu_gate * upper).astype(BF16)
    down_out = dot(act_rows, down_w).astype(BF16)

    grad_act = dot(dy_full, down_w, ((1,), (1,)))
    grad_gate = (grad_act * upper * sigma * (1.0 + gate * (1.0 - sigma))).astype(BF16)
    grad_upper = (grad_act * silu_gate).astype(BF16)
    grad_hidden = (dot(grad_gate, gate_w, ((1,), (1,))) + dot(grad_upper, up_w, ((1,), (1,)))).astype(BF16)
    own_resid = lax.dynamic_slice_in_dim(resid, p * own_rows, own_rows, 0)
    over_rows = ((0,), (0,))
    g_down = dot(act_rows, dy_full, over_rows).astype(BF16)
    g_gate = dot(hidden_in, grad_gate, over_rows).astype(BF16)
    g_up = dot(hidden_in, grad_upper, over_rows).astype(BF16)
    all_gains = jnp.zeros((8, width), F32).at[0].set(gain_attn).at[1].set(gain_ffn)
    all_gains = all_gains.at[2, :HEAD_SIZE].set(gain_query).at[3, :HEAD_SIZE].set(gain_key)
    out_down, out_gate, out_up, out_wo, out_heads, out_gains, layer_out, tokens_grad = backward(
        dims, grad_hidden, down_out, g_down, g_gate, g_up, own_resid, tokens, cotangent, all_gains, acc, qx, kv_all,
        spans, heads, cosine_values[0], sine_lookup[0], own_wo, wqkv, normed,
    )
    gate_grad, up_grad, wq_grad, wk_grad, wv_grad, down_grad, wo_grad = place(
        out_gate, out_up, out_heads, out_down, out_wo
    )
    gain_grads = jnp.sum(out_gains.astype(F32), 0)
    few = HEAD_SIZE // F
    return (
        layer_out.astype(BF16), tokens_grad.astype(BF16), wq_grad, wk_grad, wv_grad, wo_grad, gate_grad, up_grad,
        down_grad, gain_grads[0, :depth], gain_grads[1, :depth], gain_grads[2, :few], gain_grads[3, :few],
    )


def solution(mesh):
    rows = P(("ctx", "fsdp"), None)
    shard = P("fsdp", None)
    gain = P("fsdp")
    return jax.shard_map(
        on_device,
        mesh=mesh,
        in_specs=(rows, P(), shard, shard, shard, shard, shard, shard, shard, gain, gain, gain, gain, rows),
        out_specs=(rows, rows, shard, shard, shard, shard, shard, shard, shard, gain, gain, gain, gain),
        check_vma=False,
    )
```

```python
import functools

import jax
import jax.numpy as jnp
from jax import lax
from jax.experimental import pallas as pl
from jax.experimental.pallas import tpu as pltpu
from jax.sharding import PartitionSpec as P

QUERY_HEADS = 24
KEY_VALUE_HEADS = 8
HEAD_SIZE = 64
GROUP = QUERY_HEADS // KEY_VALUE_HEADS
QW = GROUP * HEAD_SIZE
LANES = 128
NDOCS = 4

EPSILON = 1e-05
ROPE_BASE = 1000000.0
APART = 16384.0

MESH = pl.DeviceIdType.MESH
F32 = jnp.float32
BF16 = jnp.bfloat16
ANY = pl.BlockSpec(memory_space=pl.ANY)
VMEM = pl.BlockSpec(memory_space=pltpu.VMEM)
VMEM_LIMIT = 56 * 1024 * 1024


class Team:
    def __init__(self, B, F, T):
        self.B, self.F, self.T = B, F, T
        ctx, self.f = lax.axis_index("ctx"), lax.axis_index("fsdp")
        self.t, self.y = lax.div(ctx, B), lax.rem(ctx, B)
        self.p = self.y * F + self.f

    def member(self, p):
        return (self.t * self.B + lax.div(p, self.F), lax.rem(p, self.F))

    def same_row(self, f):
        return (self.t * self.B + self.y, f)

    def other_team(self, t):
        return (t * self.B + self.y, self.f)


def flip(p, bit):
    return p + bit * (1 - 2 * lax.rem(lax.div(p, bit), 2))


def bit_of(p, bit):
    return lax.rem(lax.div(p, bit), 2)


class Sems:
    def __init__(self, send, recv):
        self.send, self.recv, self.used = send, recv, 0

    def copy(self, src, dst, device):
        i = self.used
        self.used += 1
        return pltpu.make_async_remote_copy(
            src_ref=src,
            dst_ref=dst,
            send_sem=self.send.at[i],
            recv_sem=self.recv.at[i],
            device_id=device,
            device_id_type=MESH,
        )


def greet(devices):
    barrier = pltpu.get_barrier_semaphore()
    for device in devices:
        pl.semaphore_signal(barrier, inc=1, device_id=device, device_id_type=MESH)
    pl.semaphore_wait(barrier, len(devices))


def team_peers(team):
    n = team.B * team.F
    return [team.member(lax.rem(team.p + d, n)) for d in range(1, n)]


def line_peers(team):
    return [team.other_team(lax.rem(team.t + d, team.T)) for d in range(1, team.T)]


def row_peers(team):
    return [team.same_row(lax.rem(team.f + d, team.F)) for d in range(1, team.F)]


class Gather:
    def __init__(self, sems, me, count, device, own, block, half):
        bits = count.bit_length() - 1
        one, two = flip(me, 1), flip(me, 2)
        send = lambda src, dst, to: sems.copy(src, dst, device(to))
        again = lambda ref, to: send(ref, ref, to)
        self.first = [send(own, block(me), flip(me, 1 << k)) for k in range(bits)]
        self.over = [again(block(two), one)]
        self.halves, self.corner = [], []
        if count == 8:
            four = flip(me, 4)
            far = flip(two, 4)
            self.over.append(again(block(four), one))
            self.halves = [again(half(two, 0), four), again(half(four, 1), two)]
            self.corner = [again(half(far, 0), one), again(half(far, 1), one)]

    def begin(self):
        for copy in self.first:
            copy.start()

    def relay(self):
        self.first[1].wait_recv()
        self.over[0].start()
        if self.halves:
            self.halves[0].start()
            self.first[2].wait_recv()
            self.over[1].start()
            self.halves[1].start()

    def end(self):
        for arrived, onward in zip(self.halves, self.corner):
            arrived.wait_recv()
            onward.start()
        self.first[0].wait_recv()
        for copy in self.over + self.corner:
            copy.wait_recv()
        for copy in self.first + self.over + self.halves + self.corner:
            copy.wait_send()

    COPIES = 9


def scatter_shapes(rows, width):
    half = width // 2
    return [
        pltpu.VMEM((2, 2, rows, width), BF16),
        pltpu.VMEM((2, rows, half), BF16),
        pltpu.VMEM((2, rows, half), BF16),
        pltpu.VMEM((2, rows, half), BF16),
        pltpu.VMEM((2, rows, half), BF16),
        pltpu.VMEM((rows, half), BF16),
        pltpu.VMEM((rows, half), BF16),
        pltpu.VMEM((rows, half), BF16),
        pltpu.VMEM((rows, half), BF16),
    ]


def wide(v):
    return v.astype(F32)


class Scatter:
    COPIES = 5

    def __init__(self, sems, team, x, scratch):
        self.x, self.scratch = x, scratch
        r0, s1l, s1r, r1l, r1r, s2l, s2r, r2l, r2r = scratch
        p = team.p
        self.b = b0, b1, b2 = bit_of(p, 1), bit_of(p, 2), bit_of(p, 4)
        width = x.shape[-1]
        self.left, self.right = pl.ds(0, width // 2), pl.ds(width // 2, width // 2)
        send = lambda src, dst, bit: sems.copy(src, dst, team.member(flip(p, bit)))
        self.first = send(x.at[:, :, 1 - b0], r0, 1)
        self.l1, self.r1 = send(s1l, r1l, 2), send(s1r, r1r, 4)
        self.l2, self.r2 = send(s2l, r2l, 4), send(s2r, r2r, 2)

    def begin(self):
        self.first.start()

    def relay(self):
        x, (r0, s1l, s1r, *_), (b0, b1, b2) = self.x, self.scratch, self.b
        left, right, n1, n2 = self.left, self.right, 1 - b1, 1 - b2
        self.first.wait_recv()
        for k in range(2):
            s1l[k] = (wide(x[k, n1, b0, :, left]) + wide(r0[k, n1, :, left])).astype(BF16)
        self.l1.start()
        for k in range(2):
            s1r[k] = (wide(x[n2, k, b0, :, right]) + wide(r0[n2, k, :, right])).astype(BF16)
        self.r1.start()

    def relay_again(self):
        x, (r0, s1l, s1r, r1l, r1r, s2l, s2r, r2l, r2r), (b0, b1, b2) = self.x, self.scratch, self.b
        left, right, n1, n2 = self.left, self.right, 1 - b1, 1 - b2
        self.l1.wait_recv()
        s2l[...] = (wide(x[n2, b1, b0, :, left]) + wide(r0[n2, b1, :, left]) + wide(r1l[n2])).astype(BF16)
        self.l2.start()
        self.r1.wait_recv()
        s2r[...] = (wide(x[b2, n1, b0, :, right]) + wide(r0[b2, n1, :, right]) + wide(r1r[n1])).astype(BF16)
        self.r2.start()

    def end(self, store):
        x, (r0, s1l, s1r, r1l, r1r, s2l, s2r, r2l, r2r), (b0, b1, b2) = self.x, self.scratch, self.b
        left, right = self.left, self.right
        self.l2.wait_recv()
        store(
            left,
            wide(x[b2, b1, b0, :, left]) + wide(r0[b2, b1, :, left]) + wide(r1l[b2]) + wide(r2l[...]),
        )
        self.r2.wait_recv()
        store(
            right,
            wide(x[b2, b1, b0, :, right]) + wide(r0[b2, b1, :, right]) + wide(r1r[b1]) + wide(r2r[...]),
        )
        for copy in (self.first, self.l1, self.r1, self.l2, self.r2):
            copy.wait_send()


def kernel_params(collective_id):
    return pltpu.CompilerParams(
        collective_id=collective_id, has_side_effects=True, vmem_limit_bytes=VMEM_LIMIT
    )


def unit_and_factor(x):
    factor = lax.rsqrt(jnp.mean(x * x, -1, keepdims=True) + EPSILON)
    return x * factor, factor


def lane_ids(rows):
    return lax.broadcasted_iota(jnp.int32, (rows, LANES), 1)


def inside_document(spans, rows, first_row):
    row = lax.broadcasted_iota(jnp.int32, (rows, LANES), 0) + first_row
    return (row >= spans[0:1, :]) & (row < spans[1:2, :])


def widen_keys(kv, spans, first_row, kx, vx):
    rows = kv.shape[0]
    lane = lane_ids(rows)
    inside = inside_document(spans, rows, first_row)
    both = wide(kv)
    kx[...] = jnp.where(lane < HEAD_SIZE, both, jnp.where(inside, 1.0, 0.0)).astype(BF16)
    vx[...] = jnp.where(lane < HEAD_SIZE, pltpu.roll(both, HEAD_SIZE, 1), 1.0).astype(BF16)


def dot_last(a, b):
    return lax.dot_general(a, b, (((1,), (1,)), ((), ())), preferred_element_type=F32)


def rotate(u, cosine, sine):
    half = u.shape[-1] // 2
    swapped = jnp.concatenate([-u[:, half:], u[:, :half]], 1)
    return u * cosine + swapped * sine


def front_kernel(dims, tokens, wq, wk, wv, wo, w_gate, w_up, dy, gains, cosine, sine, spans,
                 tok_full, wqkv, normed, heads, qx, kv_all, acc, mixed, dy_full, wo_full, gate_full, up_full, all_gains,
                 tok, q_in, k_in, v_in, qkv_cut, qkv, gains_in, slab_g, slab_u, cut_g, cut_u, norm, kv, kx, vx, packed,
                 send, recv, line_send, line_recv, local):
    team = Team(*dims)
    B, F, T = dims
    t, y, f, p = team.t, team.y, team.f, team.p
    sems = Sems(send, recv)
    own_rows, width = tokens.shape
    rows = own_rows * B * F
    depth = width // F
    part, block = rows // 2, rows // 4
    hidden = cut_g.shape[-1]
    parity = lax.rem(t, 2)

    def home(src, dst, i):
        copy = pltpu.make_async_copy(src, dst, local.at[i])
        copy.start()
        return copy

    token_rows = lambda i: pl.ds(pl.multiple_of(i * own_rows, 16), own_rows)
    shard_rows = lambda i: pl.ds(pl.multiple_of(i * depth, 16), depth)
    token_load = home(tokens, tok.at[token_rows(p)], 0)
    small_loads = [home(wq, q_in, 1), home(wk, k_in, 2), home(wv, v_in, 3)]
    gain_load = home(gains, gains_in.at[f], 4)
    slab_loads = [home(w_gate, slab_g, 5), home(w_up, slab_u, 6)]
    homes = [home(dy, dy_full.at[p], 7), home(wo, wo_full.at[f], 8)]
    greet(team_peers(team) + line_peers(team))

    half = own_rows // 2
    gather_tok = Gather(
        sems, p, B * F, team.member, tokens, lambda i: tok.at[token_rows(i)],
        lambda i, k: tok.at[pl.ds(pl.multiple_of(i * own_rows + k * half, 16), half)],
    )
    gather_dy = Gather(
        sems, p, B * F, team.member, dy, lambda i: dy_full.at[i], lambda i, k: dy_full.at[i, pl.ds(k * half, half)]
    )
    few = packed.shape[0] // 2
    gather_mixed = Gather(
        sems, p, B * F, team.member, packed, lambda i: mixed.at[i], lambda i, k: mixed.at[i, pl.ds(k * few, few)]
    )
    partners = []
    for m in range(1, F):
        to = f
        for bit in (1, 2, 4):
            if m & bit:
                to = flip(to, bit)
        partners.append(to)
    gain_sends = [sems.copy(gains, gains_in.at[f], team.same_row(to)) for to in partners]
    qkv_sends = [sems.copy(qkv_cut.at[to], qkv.at[shard_rows(f)], team.same_row(to)) for to in partners]
    half_depth = depth // 2
    some = pl.ds(pl.multiple_of(parity * half_depth, 16), half_depth)
    near = team.other_team(t + 1 - 2 * parity)
    wide_sends, wide_shares = [], []
    for cut, full in ((cut_g, gate_full), (cut_u, up_full)):
        sends = [sems.copy(cut.at[partners[0]], full.at[f], team.same_row(partners[0]))]
        shares = []
        for to in partners[1:]:
            sends.append(sems.copy(cut.at[to, some], full.at[f, some], team.same_row(to)))
            shares.append(sems.copy(full.at[to, some], full.at[to, some], near))
        wide_sends.append(sends)
        wide_shares.append(shares)
    if B == 2 and F == 4:
        one, two = flip(f, 1), flip(f, 2)
        other = team.member(lax.rem(p + F, B * F))
        wo_half = lambda k: pl.ds(pl.multiple_of(k * half_depth, 16), half_depth)
        mine, theirs = wo_half(y), wo_half(1 - y)
        wo_first = [
            sems.copy(wo, wo_full.at[f], team.same_row(one)),
            sems.copy(wo.at[mine], wo_full.at[f, mine], team.same_row(two)),
        ]
        ref = wo_full.at[two, mine]
        wo_relay = [sems.copy(ref, ref, other), sems.copy(ref, ref, team.same_row(one))]
        ref = wo_full.at[two, theirs]
        wo_last = [sems.copy(ref, ref, team.same_row(one))]

    def line_copy(d, source, to):
        return pltpu.make_async_remote_copy(
            src_ref=kv, dst_ref=kv_all.at[source], send_sem=line_send.at[d], recv_sem=line_recv.at[source],
            device_id=team.other_team(to), device_id_type=MESH,
        )

    gather_tok.begin()
    for copy in gain_sends:
        copy.start()
    for load in small_loads:
        load.wait()
    for i in range(F):
        for row in range(B):
            h = i * B + row

            @pl.when(y == row)
            def _():
                qkv_cut[i, :, 0:QW] = q_in[:, h * QW : (h + 1) * QW]
                qkv_cut[i, :, QW : QW + HEAD_SIZE] = k_in[:, h * HEAD_SIZE : (h + 1) * HEAD_SIZE]
                qkv_cut[i, :, QW + HEAD_SIZE : QW + 2 * HEAD_SIZE] = v_in[:, h * HEAD_SIZE : (h + 1) * HEAD_SIZE]

    for copy in qkv_sends:
        copy.start()
    qkv[shard_rows(f), :] = qkv_cut[f]
    gather_tok.relay()
    for i, (slab, cut, full) in enumerate([(slab_g, cut_g, gate_full), (slab_u, cut_u, up_full)]):
        slab_loads[i].wait()

        @pl.loop(0, depth // 32)
        def _(r):
            here = pl.ds(pl.multiple_of(r * 32, 32), 32)
            for j in range(F):
                for row in range(B):
                    q = j * B + row

                    @pl.when(y == row)
                    def _():
                        cut[j, here, :] = slab[here, q * hidden : (q + 1) * hidden]

        for copy in wide_sends[i]:
            copy.start()
        homes.append(home(cut.at[f], full.at[f], 9 + i))
    gather_tok.end()
    token_load.wait()
    gain_load.wait()
    for copy in gain_sends:
        copy.wait_recv()
    homes.append(home(tok, tok_full, 11))

    all_gains[...] = jnp.zeros_like(all_gains)
    for i in range(F):
        for k, count in ((0, depth), (1, depth), (2, HEAD_SIZE // F), (3, HEAD_SIZE // F)):
            all_gains[k : k + 1, i * count : (i + 1) * count] = wide(gains_in[i])[k : k + 1, 0:count]
    gain_q, gain_k = all_gains[2:3, 0:HEAD_SIZE], all_gains[3:4, 0:HEAD_SIZE]

    @pl.loop(0, rows // block)
    def _(r):
        here = pl.ds(pl.multiple_of(r * block, block), block)
        unit, factor = unit_and_factor(wide(tok[here, :]))
        norm[here, :] = (unit * all_gains[0:1, :]).astype(BF16)

    for copy in qkv_sends:
        copy.wait_recv()
    homes += [home(norm, normed, 12), home(qkv, wqkv, 13)]

    @pl.loop(0, rows // block)
    def _(r):
        here = pl.ds(pl.multiple_of(r * block, block), block)
        projected = jnp.dot(norm[here, :], qkv[...], preferred_element_type=F32)
        lane = lane_ids(block)
        apart = jnp.where(inside_document(spans, block, t * rows + r * block), 0.0, -APART)
        cos, sin = cosine[here, :], sine[here, :]
        for h in range(GROUP + 1):
            x = projected[:, h * HEAD_SIZE : (h + 1) * HEAD_SIZE]
            heads[h, here, :] = x
            unit, factor = unit_and_factor(x)
            turned = rotate(unit * (gain_q if h < GROUP else gain_k), cos, sin).astype(BF16)
            if h < GROUP:
                q = wide(turned) * HEAD_SIZE ** (-0.5)
                qx[h, here, :] = jnp.where(lane < HEAD_SIZE, jnp.concatenate([q, q], 1), apart).astype(BF16)
        values = projected[:, (GROUP + 1) * HEAD_SIZE : (GROUP + 2) * HEAD_SIZE]
        kv[here, :] = jnp.concatenate([wide(turned), values], 1).astype(BF16)

    for d in range(1, T):

        @pl.when(t + d < T)
        def _():
            line_copy(d, t, t + d).start()

    if B == 2 and F == 4:
        for copy in wo_first:
            copy.start()
    else:
        gather_wo = Gather(
            sems, f, F, team.same_row, wo, lambda i: wo_full.at[i],
            lambda i, k: wo_full.at[i, pl.ds(k * half_depth, half_depth)],
        )
        gather_wo.begin()
    gather_dy.begin()
    kv_all[t] = kv[...]
    widen_keys(kv[...], spans, t * rows, kx, vx)
    causal = lax.broadcasted_iota(jnp.int32, (part, part), 1) <= lax.broadcasted_iota(jnp.int32, (part, part), 0)

    def piece(q, k, masked):
        scores = dot_last(q, kx[k * part : (k + 1) * part, :])
        weights = jnp.exp(scores)
        if masked:
            weights = jnp.where(causal, weights, 0.0)
        return jnp.dot(weights.astype(BF16), vx[k * part : (k + 1) * part, :], preferred_element_type=F32)

    @pl.loop(0, GROUP)
    def _(h):
        acc[h, 0:part, :] = piece(qx[h, 0:part, :], 0, True)
        low = qx[h, part:rows, :]
        acc[h, part:rows, :] = piece(low, 0, False) + piece(low, 1, True)

    def share(i):
        for arrived, onward in zip(wide_sends[i][1:], wide_shares[i]):
            arrived.wait_recv()
            onward.start()

    share(0)

    @pl.loop(1, t + 1)
    def _(j):
        source = t - j
        line_copy(0, source, t).wait_recv()
        widen_keys(kv_all[source], spans, source * rows, kx, vx)

        @pl.loop(0, GROUP)
        def _(h):
            for k in range(2):
                here = pl.ds(k * part, part)
                q = qx[h, here, :]
                acc[h, here, :] = acc[h, here, :] + piece(q, 0, False) + piece(q, 1, False)

    for h in range(GROUP):
        out = acc[h, :, 0:HEAD_SIZE] / acc[h, :, HEAD_SIZE : 2 * HEAD_SIZE]
        out = out.astype(BF16)
        if h < 2:
            packed[0:rows, h * HEAD_SIZE : (h + 1) * HEAD_SIZE] = out
        else:
            packed[rows : rows + part, 0:HEAD_SIZE] = out[0:part]
            packed[rows : rows + part, HEAD_SIZE : 2 * HEAD_SIZE] = out[part:rows]
    homes.append(home(packed, mixed.at[p], 14))
    gather_mixed.begin()
    share(1)
    if B == 2 and F == 4:
        wo_first[1].wait_recv()
        for copy in wo_relay:
            copy.start()
    else:
        gather_wo.relay()
    gather_dy.relay()
    gather_mixed.relay()
    if B == 2 and F == 4:
        wo_relay[0].wait_recv()
        wo_last[0].start()
    gather_mixed.end()
    gather_dy.end()
    if B == 2 and F == 4:
        for copy in (wo_first[0], wo_relay[1], wo_last[0]):
            copy.wait_recv()
        for copy in wo_first + wo_relay + wo_last:
            copy.wait_send()
    else:
        gather_wo.end()
    for sends, shares in zip(wide_sends, wide_shares):
        sends[0].wait_recv()
        for copy in shares:
            copy.wait_recv()
        for copy in sends + shares:
            copy.wait_send()
    for copy in gain_sends + qkv_sends:
        copy.wait_send()
    for copy in homes:
        copy.wait()
    for d in range(1, T):

        @pl.when(t + d < T)
        def _():
            line_copy(d, t, t + d).wait_send()


def front(dims, tokens, wq, wk, wv, wo, w_gate, w_up, dy, gains, cosine, sine, spans):
    B, F, T = dims
    own_rows, width = tokens.shape
    n = B * F
    rows = own_rows * n
    depth, ff = w_gate.shape
    hidden = ff // n
    few = QW + 2 * HEAD_SIZE
    copies = 4 * Gather.COPIES + 2 * (F - 1) + 2 * (2 * F - 3)
    packed = (rows + rows // 2, LANES)
    shape = lambda *s: jax.ShapeDtypeStruct(s, BF16)
    wide_shape = lambda *s: jax.ShapeDtypeStruct(s, F32)
    vmem = lambda *s: pltpu.VMEM(s, BF16)
    return pl.pallas_call(
        functools.partial(front_kernel, dims),
        out_shape=(
            shape(rows, width), shape(width, few), shape(rows, width), wide_shape(GROUP + 1, rows, HEAD_SIZE),
            shape(GROUP, rows, LANES), shape(T, rows, LANES), wide_shape(GROUP, rows, LANES), shape(n, *packed),
            shape(n, own_rows, width), shape(F, depth, width), shape(F, depth, hidden), shape(F, depth, hidden),
            wide_shape(8, width),
        ),
        in_specs=[ANY] * 9 + [VMEM] * 3,
        out_specs=[ANY] * 3 + [VMEM] * 4 + [ANY] * 5 + [VMEM],
        scratch_shapes=[
            vmem(rows, width), vmem(*wq.shape), vmem(*wk.shape), vmem(*wv.shape), vmem(F, depth, few), vmem(width, few),
            vmem(F, *gains.shape), vmem(depth, ff), vmem(depth, ff), vmem(F, depth, hidden), vmem(F, depth, hidden),
            vmem(rows, width), vmem(rows, LANES), vmem(rows, LANES), vmem(rows, LANES), vmem(*packed),
            pltpu.SemaphoreType.DMA((copies,)),
            pltpu.SemaphoreType.DMA((copies,)),
            pltpu.SemaphoreType.DMA((T,)),
            pltpu.SemaphoreType.DMA((T,)),
            pltpu.SemaphoreType.DMA((15,)),
        ],
        compiler_params=kernel_params(1),
        name="front",
    )(tokens, wq, wk, wv, wo, w_gate, w_up, dy, gains, cosine, sine, spans)


def feed_kernel(dims, tok_in, mixed_in, wo_in, gate_in, up_in, down_in, dy_in, gain, grad_hidden, down_out, g_down,
                g_gate, g_up, own_resid, tok, mixed, wo, w_gate, w_up, w_down, dy, rows_in, hid, act, dgate, dup,
                resid, dhid, down, gd, gg, gu, local):
    B, F, T = dims
    ctx, f = lax.axis_index("ctx"), lax.axis_index("fsdp")
    y = lax.rem(ctx, B)
    p = y * F + f
    rows, width = tok.shape
    own_rows = own_resid.shape[0]
    hidden = w_gate.shape[1]
    block = resid.shape[0]
    n = B * F
    loads = [
        pltpu.make_async_copy(src, dst, local.at[i])
        for i, (src, dst) in enumerate(
            [(mixed_in, mixed), (wo_in, wo), (tok_in, tok), (gate_in, w_gate), (up_in, w_up),
             (down_in.at[pl.ds(pl.multiple_of(y * hidden, 16), hidden)], w_down), (dy_in, dy)]
        )
    ]
    for load in loads:
        load.start()
    for load in loads[:3]:
        load.wait()
    half = rows // 2

    @pl.loop(0, rows // block)
    def _(r):
        here = pl.ds(pl.multiple_of(r * block, block), block)
        third = pl.ds(pl.multiple_of(rows + lax.rem(r * block, half), block), block)
        for i in range(n):
            h = i % F * B + i // F
            first = h * QW
            rows_in[:, first : first + 2 * HEAD_SIZE] = mixed[i, here, :]
            last = mixed[i, third, :]
            last = jnp.where(r * block < half, wide(last[:, :HEAD_SIZE]), wide(last[:, HEAD_SIZE:]))
            rows_in[:, first + 2 * HEAD_SIZE : first + QW] = last.astype(BF16)
        resid[...] = wide(tok[here, :]) + jnp.dot(rows_in[...], wo[...], preferred_element_type=F32)

        @pl.when(r == lax.div(p * own_rows, block))
        def _():
            own_resid[...] = resid[pl.ds(pl.multiple_of(lax.rem(p * own_rows, block), 8), own_rows), :]

        unit, factor = unit_and_factor(resid[...])
        hid[here, :] = (unit * gain[1:2, :]).astype(BF16)

    for load in loads[3:]:
        load.wait()

    @pl.loop(0, rows // block)
    def _(r):
        here = pl.ds(pl.multiple_of(r * block, block), block)
        gate = jnp.dot(hid[here, :], w_gate[...], preferred_element_type=F32)
        upper = jnp.dot(hid[here, :], w_up[...], preferred_element_type=F32)
        sigma = 1.0 / (1.0 + jnp.exp(-gate))
        silu = gate * sigma
        acts = (silu * upper).astype(BF16)
        act[here, :] = acts
        dact = dot_last(dy[here, :], w_down[...])
        dgates = (dact * upper * sigma * (1.0 + gate * (1.0 - sigma))).astype(BF16)
        dups = (dact * silu).astype(BF16)
        dgate[here, :] = dgates
        dup[here, :] = dups
        down[here, :] = jnp.dot(acts, w_down[...], preferred_element_type=F32).astype(BF16)
        dhid[here, :] = (dot_last(dgates, w_gate[...]) + dot_last(dups, w_up[...])).astype(BF16)

    stores = []

    def store(src, dst):
        stores.append(pltpu.make_async_copy(src, dst, local.at[7 + len(stores)]))
        stores[-1].start()

    store(dhid, grad_hidden)
    store(down, down_out)
    over_rows = lambda a, b: lax.dot_general(a, b, (((0,), (0,)), ((), ())), preferred_element_type=F32).astype(BF16)

    for first in range(0, hidden, 256):
        count = min(256, hidden - first)
        gd[first : first + count, :] = over_rows(act[:, first : first + count], dy[...])
    store(gd, g_down)

    @pl.loop(0, width // 256)
    def _(r):
        here = pl.ds(pl.multiple_of(r * 256, 256), 256)
        lhs = hid[:, here]
        gg[here, :] = over_rows(lhs, dgate[...])
        gu[here, :] = over_rows(lhs, dup[...])

    store(gg, g_gate)
    store(gu, g_up)
    for copy in stores:
        copy.wait()


def feed(dims, tok, mixed, wo, w_gate, w_up, w_down, dy, gains):
    rows, width = tok.shape
    hidden = w_gate.shape[1]
    own_rows = rows // KEY_VALUE_HEADS
    block = 256
    shape = lambda s: jax.ShapeDtypeStruct(s, BF16)
    return pl.pallas_call(
        functools.partial(feed_kernel, dims),
        out_shape=(
            shape((rows, width)), shape((rows, width)), shape((hidden, width)), shape((width, hidden)),
            shape((width, hidden)), jax.ShapeDtypeStruct((own_rows, width), F32),
        ),
        in_specs=[ANY] * 7 + [VMEM],
        out_specs=[ANY] * 5 + [VMEM],
        scratch_shapes=[
            pltpu.VMEM((rows, width), BF16),
            pltpu.VMEM(mixed.shape, BF16),
            pltpu.VMEM(wo.shape, BF16),
            pltpu.VMEM(w_gate.shape, BF16),
            pltpu.VMEM(w_up.shape, BF16),
            pltpu.VMEM((hidden, width), BF16),
            pltpu.VMEM((rows, width), BF16),
            pltpu.VMEM((block, width), BF16),
            pltpu.VMEM((rows, width), BF16),
            pltpu.VMEM((rows, hidden), BF16),
            pltpu.VMEM((rows, hidden), BF16),
            pltpu.VMEM((rows, hidden), BF16),
            pltpu.VMEM((block, width), F32),
            pltpu.VMEM((rows, width), BF16),
            pltpu.VMEM((rows, width), BF16),
            pltpu.VMEM((hidden, width), BF16),
            pltpu.VMEM((width, hidden), BF16),
            pltpu.VMEM((width, hidden), BF16),
            pltpu.SemaphoreType.DMA((12,)),
        ],
        compiler_params=pltpu.CompilerParams(vmem_limit_bytes=VMEM_LIMIT),
        name="feed",
    )(tok, mixed, wo, w_gate, w_up, w_down, dy, gains)


HOP = 2
LAG = 3


class GradSum:
    RED, FIN, HAND, OWN, OVER, HOME, INTO = range(7)

    def __init__(self, team, kinds, red_recv, fin_recv, hand_recvs, bulk):
        self.team, self.kinds = team, kinds
        self.red_recv, self.fin_recv, self.hand_recvs, self.bulk = red_recv, fin_recv, hand_recvs, bulk
        self.opposite = team.member(lax.rem(team.p + team.F, team.B * team.F))

    @staticmethod
    def steps(kinds, T):
        last = max(first + rows // 2 // step for rows, step, first in kinds)
        return last + 2 * HOP * (T - 1) + LAG

    def remote(self, src, dst, send_sem, recv_sem, device):
        return pltpu.make_async_remote_copy(
            src_ref=src, dst_ref=dst, send_sem=send_sem, recv_sem=recv_sem, device_id=device, device_id_type=MESH
        )

    def is_first(self, way):
        return self.team.t == (self.team.T - 1 if way else 0)

    def is_last(self, way):
        return self.team.t == (0 if way else self.team.T - 1)

    def rows(self, k, way, c):
        g, land, out, step, first, how = self.kinds[k]
        return pl.ds(pl.multiple_of(way * (g.shape[0] // 2) + c * step, 16), step)

    def reduce_copy(self, k, way, at, i):
        g, land = self.kinds[k][:2]
        to = self.team.other_team(self.team.t + 1 - 2 * way)
        return self.remote(g.at[at], land.at[at], self.bulk.at[self.RED, k, way], self.red_recv.at[way, i], to)

    def final_copy(self, k, way, at, i):
        land = self.kinds[k][1]
        to = self.team.other_team(self.team.t - 1 + 2 * way)
        return self.remote(land.at[at], land.at[at], self.bulk.at[self.FIN, k, way], self.fin_recv.at[way, i], to)

    def reduce(self, k, way, c, i):
        g, land = self.kinds[k][:2]
        at = self.rows(k, way, c)

        @pl.when(self.is_first(way))
        def _():
            self.reduce_copy(k, way, at, i).start()

        @pl.when(jnp.logical_not(self.is_first(way)))
        def _():
            self.reduce_copy(k, way, at, i).wait_recv()
            summed = (wide(g[at, :]) + wide(land[at, :])).astype(BF16)

            @pl.when(self.is_last(way))
            def _():
                land[at, :] = summed

            @pl.when(jnp.logical_not(self.is_last(way)))
            def _():
                g[at, :] = summed
                self.reduce_copy(k, way, at, i).start()

    def place(self, k, way, c):
        g, land, out, step, first, how = self.kinds[k]
        shard = g.shape[0] // self.team.F
        row = way * (g.shape[0] // 2) + c * step
        return lax.div(row, shard), lax.rem(row, shard)

    def finish(self, k, way, c, i):
        g, land, out, step, first, how = self.kinds[k]
        team, bulk = self.team, self.bulk
        B, F, y, f = team.B, team.F, team.y, team.f
        at = self.rows(k, way, c)

        @pl.when(jnp.logical_not(self.is_last(way)))
        def _():
            self.final_copy(k, way, at, i).wait_recv()

        @pl.when(jnp.logical_not(self.is_first(way)))
        def _():
            self.final_copy(k, way, at, i).start()

        if how == "rows":
            to, row = self.place(k, way, c)
            dst = out.at[f * B + y, pl.ds(pl.multiple_of(row, 16), step)]

            @pl.when(to == f)
            def _():
                pltpu.make_async_copy(land.at[at], dst, bulk.at[self.HOME, k, 0]).start()
                if B == 2:
                    self.remote(land.at[at], dst, bulk.at[self.OVER, k, 0], bulk.at[self.INTO, k, 0],
                                self.opposite).start()

            @pl.when(to != f)
            def _():
                self.remote(land.at[at], dst, bulk.at[self.HAND, k, 0], self.hand_recvs[k].at[f, lax.div(row, step)],
                            team.same_row(to)).start()
        elif how == "stay":
            dst = out.at[y, at]
            pltpu.make_async_copy(land.at[at], dst, bulk.at[self.HOME, k, 0]).start()
            if B == 2:
                self.remote(land.at[at], dst, bulk.at[self.OVER, k, 0], bulk.at[self.INTO, k, 0],
                            self.opposite).start()
        else:
            for j in range(F // 2):
                to = way * (F // 2) + j
                src = land.at[pl.ds(16 * to, 16)]
                for row in range(B):
                    member = row * F + to

                    @pl.when(team.p == member)
                    def _():
                        pltpu.make_async_copy(src, out.at[team.p], bulk.at[self.HOME, k, 0]).start()

                    @pl.when(team.p != member)
                    def _():
                        self.remote(src, out.at[team.p], bulk.at[self.HAND, k, 0], bulk.at[self.INTO, k, 0],
                                    (team.t * B + row, to)).start()

    def pass_over(self, k, way, c, i):
        g, land, out, step, first, how = self.kinds[k]
        if how != "rows":
            return
        team = self.team
        to, row = self.place(k, way, c)

        @pl.when(to == team.f)
        def _():
            for d in range(1, team.F):
                source = lax.rem(team.f + d, team.F)
                ref = out.at[source * team.B + team.y, pl.ds(pl.multiple_of(row, 16), step)]
                self.remote(land.at[self.rows(k, way, c)], ref, self.bulk.at[self.HAND, k, 0],
                            self.hand_recvs[k].at[source, lax.div(row, step)], team.same_row(team.f)).wait_recv()
                if team.B == 2:
                    self.remote(ref, ref, self.bulk.at[self.OVER, k, 1], self.bulk.at[self.INTO, k, 0],
                                self.opposite).start()

    def each(self, i, way, body):
        for k, (g, land, out, step, first, how) in enumerate(self.kinds):
            count = g.shape[0] // 2 // step

            pl.when((i >= first) & (i < first + count))(functools.partial(lambda k, c: body(k, way, c, i), k, i - first))

    def step(self, s):
        T, t = self.team.T, self.team.t
        for way in range(2):
            place = T - 1 - t if way else t
            done = s - HOP * (2 * (T - 1) - place)
            self.each(s - HOP * place, way, self.reduce)
            self.each(done, way, self.finish)
            self.each(done - LAG, way, self.pass_over)

    def drain(self, ref, sem):
        pltpu.make_async_copy(ref, ref, sem).wait()

    def end(self):
        bulk, B, F = self.bulk, self.team.B, self.team.F
        for k, (g, land, out, step, first, how) in enumerate(self.kinds):
            rows = g.shape[0]
            some = lambda n: g.at[pl.ds(0, n)]
            for way in range(2):

                @pl.when(jnp.logical_not(self.is_last(way)))
                def _():
                    self.drain(some(rows // 2), bulk.at[self.RED, k, way])

                @pl.when(jnp.logical_not(self.is_first(way)))
                def _():
                    self.drain(some(rows // 2), bulk.at[self.FIN, k, way])

            if how == "rows":
                shard = rows // F
                self.drain(some(rows - shard), bulk.at[self.HAND, k, 0])
                self.drain(some(shard), bulk.at[self.HOME, k, 0])
                if B == 2:
                    self.drain(some(shard), bulk.at[self.OVER, k, 0])
                    self.drain(some(rows - shard), bulk.at[self.OVER, k, 1])
                    self.drain(g, bulk.at[self.INTO, k, 0])
            elif how == "stay":
                self.drain(g, bulk.at[self.HOME, k, 0])
                if B == 2:
                    self.drain(g, bulk.at[self.OVER, k, 0])
                    self.drain(g, bulk.at[self.INTO, k, 0])
            else:
                others = out.at[pl.ds(0, B * F - 1)]
                self.drain(out.at[0], bulk.at[self.HOME, k, 0])
                self.drain(others, bulk.at[self.HAND, k, 0])
                self.drain(others, bulk.at[self.INTO, k, 0])


def first_steps(dims):
    T = dims[2]
    attention = 8
    keys = attention + 2 * T + 1
    return dict(scatter1=1, scatter2=3, resid=4, relay=6, heads=7, attention=attention, keys=keys,
                again1=keys + 1, again2=keys + 3, tokens=keys + 4, down1=keys + 5, down2=keys + 6, down3=keys + 7)


def grad_kinds(dims, depth, hidden):
    at = first_steps(dims)
    kinds, place = [], 0
    for rows, width, step, ready, how in (
        (hidden, depth, 48, 0, "stay"),
        (depth, hidden, 64, 0, "rows"),
        (depth, hidden, 64, 0, "rows"),
        (QW, depth, 48, at["heads"] + 1, "stay"),
        (depth, QW + 2 * HEAD_SIZE, 96, at["keys"] + 1, "rows"),
        (16 * dims[1], max(depth // dims[1], LANES), 8 * dims[1], at["tokens"] + 1, "gain"),
    ):
        place = max(place, ready)
        kinds.append((rows, width, step, place, how))
        place += rows // 2 // step
    return kinds


def back_kernel(dims, kinds, steps, grad_hidden, down_out, g_down, g_gate, g_up, resid, tokens, cotangent, gains, acc, qx, kv_all, spans,
                heads, cosine, sine, own_wo, wqkv, normed,
                out_down, out_gate, out_up, out_wo, out_heads, out_gains, layer_out, tokens_grad,
                xs, xd, own_down, own_gate, own_up, own_gwo, own_heads, own_gains,
                land_down, land_gate, land_up, land_wo, land_heads, land_gains,
                grad_resid, attn_own, big, dox, mixed, dq, dkv, kv_in, dkv_sum, turned, small, kx, vx, dk, dv, wq_in, *rest):
    scratch1, rest = rest[:9], rest[9:]
    scratch2, rest = rest[:9], rest[9:]
    send, recv, line_send, line_recv, red_recv, fin_recv, hand_gate, hand_up, hand_heads, bulk, local = rest
    team = Team(*dims)
    B, F, T = dims
    t, p = team.t, team.p
    at = first_steps(dims)
    own_rows, width = resid.shape
    rows = qx.shape[1]
    part = rows // 2
    block = rows // 4
    depth = width // F
    sems = Sems(send, recv)
    loads = [
        pltpu.make_async_copy(src, dst, local.at[i])
        for i, (src, dst) in enumerate(
            [(grad_hidden, xs), (g_down, own_down), (g_gate, own_gate), (g_up, own_up), (down_out, xd), (wqkv, wq_in)]
        )
    ]
    for load in loads:
        load.start()
    own_gains[...] = jnp.zeros_like(own_gains)
    greet(team_peers(team) + line_peers(team))
    loads[0].wait()
    scatter = Scatter(sems, team, xs, scratch1)
    scatter.begin()
    again = Scatter(sems, team, xs, scratch1)
    down = Scatter(sems, team, xd, scratch2)
    half = own_rows // 2
    gather = Gather(
        sems, p, B * F, team.member, attn_own,
        lambda i: big.at[pl.ds(pl.multiple_of(i * own_rows, 16), own_rows)],
        lambda i, k: big.at[pl.ds(pl.multiple_of(i * own_rows + k * half, 16), half)],
    )
    sums = GradSum(
        team,
        [
            (own, land, out) + kind[2:]
            for own, land, out, kind in zip(
                (own_down, own_gate, own_up, own_gwo, own_heads, own_gains),
                (land_down, land_gate, land_up, land_wo, land_heads, land_gains),
                (out_down, out_gate, out_up, out_wo, out_heads, out_gains),
                kinds,
            )
        ],
        red_recv, fin_recv, [None, hand_gate, hand_up, None, hand_heads, None], bulk,
    )
    for load in loads[1:]:
        load.wait()
    gain_attn, gain_ffn = gains[0:1, :], gains[1:2, :]
    gain_q, gain_k = gains[2:3, 0:HEAD_SIZE], gains[3:4, 0:HEAD_SIZE]
    home = pltpu.make_async_copy(attn_own, big.at[pl.ds(pl.multiple_of(p * own_rows, 16), own_rows)], local.at[6])
    fetch = pltpu.make_async_copy(normed, big, local.at[7])

    def resid_phase():
        def store(columns, total):
            grad_resid[:, columns] = total

        scatter.end(store)
        term = jnp.zeros((1, width), F32)
        for r in range(0, own_rows, 32):
            here = slice(r, r + 32)
            unit, factor = unit_and_factor(resid[here, :])
            upstream = grad_resid[here, :]
            term = term + jnp.sum(upstream * unit, 0, keepdims=True)
            total = wide(cotangent[here, :]) + norm_back(upstream, unit, factor, gain_ffn)
            grad_resid[here, :] = total
            attn_own[here, :] = total.astype(BF16)
        small[1:2, :] = term
        home.start()
        gather.begin()

    def heads_phase():
        gather.end()
        home.wait()
        lane = lane_ids(block)

        @pl.loop(0, rows // block)
        def _(r):
            here = pl.ds(pl.multiple_of(r * block, block), block)
            grad = dot_last(big[here, :], own_wo[...]).astype(BF16)
            for h in range(GROUP):
                sums_h = acc[h, here, :]
                total = pltpu.roll(sums_h, HEAD_SIZE, 1)
                out = sums_h / total
                mixed[here, h * HEAD_SIZE : (h + 1) * HEAD_SIZE] = out[:, :HEAD_SIZE].astype(BF16)
                do = wide(grad[:, h * HEAD_SIZE : (h + 1) * HEAD_SIZE])
                do = jnp.concatenate([do, jnp.zeros_like(do)], 1)
                delta = -jnp.sum(jnp.where(lane < HEAD_SIZE, do * out, 0.0), 1, keepdims=True)

                def put(x, first, value):
                    for i in range(3):
                        x = jnp.where(lane == first + i, wide(value.astype(BF16)), x)
                        value = value - wide(value.astype(BF16))
                    return x

                dox[h, here, :] = put(do, HEAD_SIZE, delta).astype(BF16)
                log_sum = -jnp.log(jnp.where(lane < HEAD_SIZE, total, sums_h))
                qx[h, here, :] = put(wide(qx[h, here, :]), HEAD_SIZE + NDOCS, log_sum).astype(BF16)

        own_gwo[...] = lax.dot_general(
            mixed[...], big[...], (((0,), (0,)), ((), ())), preferred_element_type=F32
        ).astype(BF16)
        dq[...] = jnp.zeros_like(dq)

    causal = lax.broadcasted_iota(jnp.int32, (part, part), 0) <= lax.broadcasted_iota(jnp.int32, (part, part), 1)

    def piece(h, q_rows, k_rows, masked):
        q = qx[h, q_rows, :]
        do = dox[h, q_rows, :]
        keys = kx[k_rows, :]
        weights = jnp.exp(dot_last(keys, q))
        if masked:
            weights = jnp.where(causal, weights, 0.0)
        dscore = (weights * dot_last(vx[k_rows, :], do)).astype(BF16)
        dv[...] += jnp.dot(weights.astype(BF16), do, preferred_element_type=F32)
        dk[...] += jnp.dot(dscore, q, preferred_element_type=F32)
        dq[h, q_rows, :] += lax.dot_general(dscore, keys, (((0,), (0,)), ((), ())), preferred_element_type=F32)

    def line_copy(owner, source):
        return pltpu.make_async_remote_copy(
            src_ref=dkv.at[owner], dst_ref=dkv.at[source], send_sem=line_send.at[owner],
            recv_sem=line_recv.at[source], device_id=team.other_team(owner), device_id_type=MESH,
        )

    def fetch_keys(source):
        slot = lax.rem(source, 2)
        return pltpu.make_async_copy(kv_all.at[source], kv_in.at[slot], local.at[8 + slot])

    fetch_keys(t * 0).start()

    def attention_unit(source, k):
        @pl.when(k == 0)
        def _():
            fetch_keys(source).wait()

            @pl.when(source < t)
            def _():
                fetch_keys(source + 1).start()

            widen_keys(kv_in[lax.rem(source, 2)], spans, source * rows, kx, vx)

        k_rows = pl.ds(pl.multiple_of(k * part, part), part)
        dk[...] = jnp.zeros_like(dk)
        dv[...] = jnp.zeros_like(dv)

        @pl.when(source < t)
        def _():
            @pl.loop(0, GROUP)
            def _(h):
                for q in range(2):
                    piece(h, slice(q * part, (q + 1) * part), k_rows, False)

        @pl.when(source == t)
        def _():
            for diagonal in range(2):

                @pl.when(k == diagonal)
                def _():
                    @pl.loop(0, GROUP)
                    def _(h):
                        for q in range(diagonal, 2):
                            piece(h, slice(q * part, (q + 1) * part), slice(diagonal * part, (diagonal + 1) * part),
                                  q == diagonal)

        dkv[source, k_rows, :] = jnp.where(
            lane_ids(part) < HEAD_SIZE, dk[...], pltpu.roll(dv[...], HEAD_SIZE, 1)
        ).astype(BF16)

        @pl.when((k == 1) & (source < t))
        def _():
            line_copy(source, t).start()

    def keys_phase():
        fetch.start()
        dkv_sum[...] = wide(dkv[t])
        for d in range(1, T):

            @pl.when(t + d < T)
            def _():
                line_copy(t, t + d).wait_recv()
                dkv_sum[...] += wide(dkv[t + d])

        small[2:4, :] = jnp.zeros((2, width), F32)

        @pl.loop(0, rows // block)
        def _(r):
            here = pl.ds(pl.multiple_of(r * block, block), block)
            cos, sin = cosine[here, :], sine[here, :]
            q_term = jnp.zeros((1, HEAD_SIZE), F32)
            for h in range(GROUP + 1):
                if h < GROUP:
                    u, gain = dq[h, here, 0:HEAD_SIZE] * HEAD_SIZE ** (-0.5), gain_q
                else:
                    u, gain = dkv_sum[here, 0:HEAD_SIZE], gain_k
                u = rotate(u, cos, -sin)
                unit, factor = unit_and_factor(heads[h, here, :])
                term = jnp.sum(u * unit, 0, keepdims=True)
                if h < GROUP:
                    q_term = q_term + term
                else:
                    small[3:4, 0:HEAD_SIZE] += term
                turned[here, h * HEAD_SIZE : (h + 1) * HEAD_SIZE] = norm_back(u, unit, factor, gain).astype(BF16)
            small[2:3, 0:HEAD_SIZE] += q_term
            h = GROUP + 1
            turned[here, h * HEAD_SIZE : (h + 1) * HEAD_SIZE] = dkv_sum[here, HEAD_SIZE : 2 * HEAD_SIZE].astype(BF16)

        for m in range(2 * 2 * 2):
            xs[m // 4, m // 2 % 2, m % 2] = dot_last(
                turned[m * own_rows : (m + 1) * own_rows, :], wq_in[...]
            ).astype(BF16)
        again.begin()
        fetch.wait()
        for r in range(0, width, 256):
            own_heads[r : r + 256, :] = lax.dot_general(
                big[:, r : r + 256], turned[...], (((0,), (0,)), ((), ())), preferred_element_type=F32
            ).astype(BF16)

    def tokens_phase():
        def store(columns, total):
            tokens_grad[:, columns] = total

        again.end(store)
        down.begin()
        term = jnp.zeros((1, width), F32)
        for r in range(0, own_rows, 32):
            here = slice(r, r + 32)
            unit, factor = unit_and_factor(wide(tokens[here, :]))
            upstream = tokens_grad[here, :]
            term = term + jnp.sum(upstream * unit, 0, keepdims=True)
            tokens_grad[here, :] = grad_resid[here, :] + norm_back(upstream, unit, factor, gain_attn)
        small[0:1, :] = term
        lanes = own_gains.shape[1]
        row = lax.broadcasted_iota(jnp.int32, (16, lanes), 0)

        def cut(i, first, count):
            value = small[i : i + 1, first : first + count]
            if count < lanes:
                value = jnp.concatenate([value, jnp.zeros((1, lanes - count), F32)], 1)
            return jnp.where(row == i, jnp.broadcast_to(value, (16, lanes)), 0.0)

        for i in range(F):
            few = HEAD_SIZE // F
            own_gains[16 * i : 16 * i + 16, :] = (
                cut(0, i * depth, depth) + cut(1, i * depth, depth) + cut(2, i * few, few) + cut(3, i * few, few)
            ).astype(BF16)

    def down_phase():
        def store(columns, total):
            layer_out[:, columns] = resid[:, columns] + total

        down.end(store)

    @pl.loop(0, steps)
    def _(s):
        sums.step(s)
        for name, body in (
            ("scatter1", scatter.relay), ("scatter2", scatter.relay_again), ("resid", resid_phase),
            ("relay", gather.relay), ("heads", heads_phase), ("keys", keys_phase), ("again1", again.relay),
            ("again2", again.relay_again), ("tokens", tokens_phase), ("down1", down.relay),
            ("down2", down.relay_again), ("down3", down_phase),
        ):
            pl.when(s == at[name])(body)
        unit = s - at["attention"]

        @pl.when((unit >= 0) & (lax.div(unit, 2) <= t))
        def _():
            attention_unit(lax.div(unit, 2), lax.rem(unit, 2))

    for d in range(1, T):

        @pl.when(t - d >= 0)
        def _():
            line_copy(t - d, t).wait_send()

    sums.end()


def backward(dims, grad_hidden, down_out, g_down, g_gate, g_up, resid, tokens, cotangent, gains, acc, qx, kv_all, spans,
             heads, cosine, sine, own_wo, wqkv, normed):
    B, F, T = dims
    own_rows, width = resid.shape
    rows = qx.shape[1]
    part = rows // 2
    hidden = g_down.shape[0]
    n = B * F
    kinds = grad_kinds(dims, width, hidden)
    steps = max(
        GradSum.steps([(rows_, step, first) for rows_, _, step, first, _ in kinds], T), first_steps(dims)["down3"] + 1
    )
    positions = max(first + rows_ // 2 // step for rows_, _, step, first, _ in kinds)
    outs = []
    for rows_, wide_, step, first, how in kinds:
        if how == "rows":
            shape = (n, rows_ // F, wide_)
        elif how == "stay":
            shape = (B, rows_, wide_)
        else:
            shape = (n, 16, wide_)
        outs.append(jax.ShapeDtypeStruct(shape, BF16))
    outs += [jax.ShapeDtypeStruct((own_rows, width), F32), jax.ShapeDtypeStruct((own_rows, width), F32)]
    eight = (2, 2, 2, own_rows, width)
    hands = [pltpu.SemaphoreType.DMA((F, kinds[k][0] // F // kinds[k][2])) for k in (1, 2, 4)]
    copies = 3 * Scatter.COPIES + Gather.COPIES
    return pl.pallas_call(
        functools.partial(back_kernel, dims, kinds, steps),
        out_shape=outs,
        in_specs=[ANY] * 5 + [VMEM] * 6 + [ANY] + [VMEM] * 5 + [ANY] * 2,
        out_specs=[ANY] * 6 + [VMEM] * 2,
        scratch_shapes=[
            pltpu.VMEM(eight, BF16),
            pltpu.VMEM(eight, BF16),
        ]
        + [pltpu.VMEM((kind[0], kind[1]), BF16) for kind in kinds] * 2
        + [
            pltpu.VMEM((own_rows, width), F32),
            pltpu.VMEM((own_rows, width), BF16),
            pltpu.VMEM((rows, width), BF16),
            pltpu.VMEM(qx.shape, BF16),
            pltpu.VMEM((rows, QW), BF16),
            pltpu.VMEM(qx.shape, F32),
            pltpu.VMEM(kv_all.shape, BF16),
            pltpu.VMEM((2,) + kv_all.shape[1:], BF16),
            pltpu.VMEM((rows, LANES), F32),
            pltpu.VMEM((rows, QW + 2 * HEAD_SIZE), BF16),
            pltpu.VMEM((8, width), F32),
            pltpu.VMEM((rows, LANES), BF16),
            pltpu.VMEM((rows, LANES), BF16),
            pltpu.VMEM((part, LANES), F32),
            pltpu.VMEM((part, LANES), F32),
            pltpu.VMEM(wqkv.shape, BF16),
        ]
        + scatter_shapes(own_rows, width) * 2
        + [
            pltpu.SemaphoreType.DMA((copies,)),
            pltpu.SemaphoreType.DMA((copies,)),
            pltpu.SemaphoreType.DMA((T,)),
            pltpu.SemaphoreType.DMA((T,)),
            pltpu.SemaphoreType.DMA((2, positions)),
            pltpu.SemaphoreType.DMA((2, positions)),
            *hands,
            pltpu.SemaphoreType.DMA((7, len(kinds), 2)),
            pltpu.SemaphoreType.DMA((10,)),
        ],
        compiler_params=pltpu.CompilerParams(
            collective_id=3, has_side_effects=True, vmem_limit_bytes=60 * 1024 * 1024
        ),
        name="backward",
    )(grad_hidden.reshape(eight), down_out.reshape(eight), g_down, g_gate, g_up, resid, tokens, cotangent, gains, acc, qx,
      kv_all, spans, heads, cosine, sine, own_wo, wqkv, normed)


def place_kernel(n, gate, up, heads, down, wo, gate_out, up_out, wq_out, wk_out, wv_out, down_out, wo_out):
    hidden = gate.shape[-1]
    for q in range(n):
        gate_out[:, q * hidden : (q + 1) * hidden] = wide(gate[q])
        up_out[:, q * hidden : (q + 1) * hidden] = wide(up[q])
        block = wide(heads[q])
        wq_out[:, q * QW : (q + 1) * QW] = block[:, :QW]
        wk_out[:, q * HEAD_SIZE : (q + 1) * HEAD_SIZE] = block[:, QW : QW + HEAD_SIZE]
        wv_out[:, q * HEAD_SIZE : (q + 1) * HEAD_SIZE] = block[:, QW + HEAD_SIZE :]
    down_out[...] = wide(down[...])
    wo_out[...] = wide(wo[...])


def place(gate, up, heads, down, wo):
    n, depth, hidden = gate.shape
    width = down.shape[-1]
    down, wo = down.reshape(-1, width), wo.reshape(-1, width)
    step = 32
    count = depth // step
    many = lambda w: pl.BlockSpec((n, step, w), lambda i: (0, i, 0))
    cut = lambda a: pl.BlockSpec((a.shape[0] // count, width), lambda i: (i, 0))
    out = lambda w: pl.BlockSpec((step, w), lambda i: (i, 0))
    shape = lambda r, w: jax.ShapeDtypeStruct((r, w), F32)
    wq, wk = QW * n, HEAD_SIZE * n
    return pl.pallas_call(
        functools.partial(place_kernel, n),
        grid=(count,),
        out_shape=(
            shape(depth, n * hidden), shape(depth, n * hidden), shape(depth, wq), shape(depth, wk), shape(depth, wk),
            shape(down.shape[0], width), shape(wo.shape[0], width),
        ),
        in_specs=[many(hidden), many(hidden), many(QW + 2 * HEAD_SIZE), cut(down), cut(wo)],
        out_specs=[out(n * hidden), out(n * hidden), out(wq), out(wk), out(wk), cut(down), cut(wo)],
        compiler_params=pltpu.CompilerParams(vmem_limit_bytes=VMEM_LIMIT),
        name="place",
    )(gate, up, heads, down, wo)


def doc_layout(lengths, token_index):
    doc_ends = jnp.cumsum(lengths)
    passed = token_index[:, None] >= doc_ends[None, :]
    document_index = jnp.sum(passed.astype(jnp.int32), axis=1)
    doc_start = jnp.max(jnp.where(passed, doc_ends[None, :], 0), axis=1)
    return (document_index, token_index - doc_start)


def rotation(places, width):
    half_width = width // 2
    inverse_freq = jnp.power(ROPE_BASE, -(jnp.arange(half_width, dtype=F32) * 2.0 / width))
    angles = places.astype(F32)[:, None] * inverse_freq[None, :]
    cosine_values = jnp.cos(angles)
    sine_lookup = jnp.sin(angles)
    return (
        jnp.concatenate([cosine_values, cosine_values], 1),
        jnp.concatenate([sine_lookup, sine_lookup], 1),
    )


def norm_back(upstream, unit_rows, factor, gain_row):
    lifted = upstream * gain_row
    return factor * (lifted - unit_rows * jnp.mean(lifted * unit_rows, -1, keepdims=True))


def on_device(
    tokens, lengths, wq, wk, wv, wo, w_gate, w_up, w_down, attn_gain, ffn_gain, q_gain, key_norm_gain, cotangent
):
    F = lax.axis_size("fsdp")
    B = KEY_VALUE_HEADS // F
    T = lax.axis_size("ctx") // B
    dims = (B, F, T)
    own_rows, width = tokens.shape
    rows = own_rows * KEY_VALUE_HEADS
    depth = width // F
    ctx, f = lax.axis_index("ctx"), lax.axis_index("fsdp")
    t, y = ctx // B, ctx % B
    p = y * F + f
    hidden = w_down.shape[0] // B

    gains = jnp.zeros((16, max(depth, LANES)), BF16)
    gains = gains.at[0, :depth].set(attn_gain).at[1, :depth].set(ffn_gain)
    gains = gains.at[2, : HEAD_SIZE // F].set(q_gain).at[3, : HEAD_SIZE // F].set(key_norm_gain)
    token_index = t * rows + jnp.arange(rows, dtype=jnp.int32)
    docs, places = doc_layout(lengths, token_index)
    cosine_values, sine_lookup = rotation(places, HEAD_SIZE)
    ends = jnp.cumsum(lengths)
    ndocs = lengths.shape[0]
    big = jnp.int32(2**30)
    spans = jnp.stack([
        jnp.zeros((LANES,), jnp.int32).at[HEAD_SIZE : HEAD_SIZE + ndocs].set(ends - lengths),
        jnp.full((LANES,), big, jnp.int32).at[HEAD_SIZE : HEAD_SIZE + ndocs].set(ends),
    ])
    spans = jnp.concatenate([spans, jnp.zeros((6, LANES), jnp.int32)])

    (tok_full, wqkv, normed, heads, qx, kv_all, acc, mixed, dy_full, wo_full, gate_w, up_w, all_gains) = front(
        dims, tokens, wq, wk, wv, wo, w_gate, w_up, cotangent, gains, cosine_values, sine_lookup, spans
    )
    own_wo = lax.dynamic_slice_in_dim(wo, y * QW, QW, 0)
    grad_hidden, down_out, g_down, g_gate, g_up, own_resid = feed(
        dims, tok_full, mixed, wo_full.reshape(-1, width), gate_w.reshape(width, hidden),
        up_w.reshape(width, hidden), w_down, dy_full.reshape(rows, width), all_gains,
    )
    out_down, out_gate, out_up, out_wo, out_heads, out_gains, layer_out, tokens_grad = backward(
        dims, grad_hidden, down_out, g_down, g_gate, g_up, own_resid, tokens, cotangent, all_gains, acc, qx, kv_all,
        spans, heads, cosine_values, sine_lookup, own_wo, wqkv, normed,
    )
    gate_grad, up_grad, wq_grad, wk_grad, wv_grad, down_grad, wo_grad = place(
        out_gate, out_up, out_heads, out_down, out_wo
    )
    gain_grads = jnp.sum(out_gains.astype(F32), 0)
    few = HEAD_SIZE // F
    return (
        layer_out.astype(BF16), tokens_grad.astype(BF16), wq_grad, wk_grad, wv_grad, wo_grad, gate_grad, up_grad,
        down_grad, gain_grads[0, :depth], gain_grads[1, :depth], gain_grads[2, :few], gain_grads[3, :few],
    )


def solution(mesh):
    rows = P(("ctx", "fsdp"), None)
    shard = P("fsdp", None)
    gain = P("fsdp")
    return jax.shard_map(
        on_device,
        mesh=mesh,
        in_specs=(rows, P(), shard, shard, shard, shard, shard, shard, shard, gain, gain, gain, gain, rows),
        out_specs=(rows, rows, shard, shard, shard, shard, shard, shard, shard, gain, gain, gain, gain),
        check_vma=False,
    )
```

```python
import functools

import jax
import jax.numpy as jnp
import numpy as np
from jax import lax
from jax.experimental import pallas as pl
from jax.experimental.pallas import tpu as pltpu
from jax.sharding import PartitionSpec as P

QUERY_HEADS = 24
KEY_VALUE_HEADS = 8
HEAD_SIZE = 64
GROUP = QUERY_HEADS // KEY_VALUE_HEADS
QW = GROUP * HEAD_SIZE
LANES = 128
NDOCS = 4

EPSILON = 1e-05
ROPE_BASE = 1000000.0
APART = 16384.0

MESH = pl.DeviceIdType.MESH
F32 = jnp.float32
BF16 = jnp.bfloat16
ANY = pl.BlockSpec(memory_space=pl.ANY)
VMEM = pl.BlockSpec(memory_space=pltpu.VMEM)
VMEM_LIMIT = 56 * 1024 * 1024


class Team:
    def __init__(self, B, F, T):
        self.B, self.F, self.T = B, F, T
        ctx, self.f = lax.axis_index("ctx"), lax.axis_index("fsdp")
        self.t, self.y = lax.div(ctx, B), lax.rem(ctx, B)
        self.p = self.y * F + self.f

    def member(self, p):
        return (self.t * self.B + lax.div(p, self.F), lax.rem(p, self.F))

    def same_row(self, f):
        return (self.t * self.B + self.y, f)

    def other_team(self, t):
        return (t * self.B + self.y, self.f)


def flip(p, bit):
    return p + bit * (1 - 2 * lax.rem(lax.div(p, bit), 2))


def bit_of(p, bit):
    return lax.rem(lax.div(p, bit), 2)


class Sems:
    def __init__(self, send, recv):
        self.send, self.recv, self.used = send, recv, 0

    def copy(self, src, dst, device):
        i = self.used
        self.used += 1
        return pltpu.make_async_remote_copy(
            src_ref=src,
            dst_ref=dst,
            send_sem=self.send.at[i],
            recv_sem=self.recv.at[i],
            device_id=device,
            device_id_type=MESH,
        )


def greet(devices):
    barrier = pltpu.get_barrier_semaphore()
    for device in devices:
        pl.semaphore_signal(barrier, inc=1, device_id=device, device_id_type=MESH)
    pl.semaphore_wait(barrier, len(devices))


def team_peers(team):
    n = team.B * team.F
    return [team.member(lax.rem(team.p + d, n)) for d in range(1, n)]


def line_peers(team):
    return [team.other_team(lax.rem(team.t + d, team.T)) for d in range(1, team.T)]


def row_peers(team):
    return [team.same_row(lax.rem(team.f + d, team.F)) for d in range(1, team.F)]


class Gather:
    def __init__(self, sems, me, count, device, own, block, half, order="both"):
        bits = count.bit_length() - 1
        one, two = flip(me, 1), flip(me, 2)
        send = lambda src, dst, to: sems.copy(src, dst, device(to))
        again = lambda ref, to: send(ref, ref, to)
        self.first = [send(own, block(me), flip(me, 1 << k)) for k in range(bits)]
        self.over = [again(block(two), one)]
        self.halves, self.corner = [], []
        if count == 8:
            four = flip(me, 4)
            far = flip(two, 4)
            self.over.append(again(block(four), one))
            if order == "both":
                self.halves = [again(half(two, 0), four), again(half(four, 1), two)]
                self.corner = [again(half(far, 0), one), again(half(far, 1), one)]
            else:
                self.halves = [again(block(two), four)]
                self.corner = [again(block(far), one)]

    def begin(self):
        for copy in self.first:
            copy.start()

    def relay(self):
        self.first[1].wait_recv()
        self.over[0].start()
        if self.halves:
            self.halves[0].start()
            self.first[2].wait_recv()
            for copy in self.halves[1:]:
                copy.start()
            self.over[1].start()

    def end(self):
        for arrived, onward in zip(self.halves, self.corner):
            arrived.wait_recv()
            onward.start()
        self.first[0].wait_recv()
        for copy in self.over + self.corner:
            copy.wait_recv()
        for copy in self.first + self.over + self.halves + self.corner:
            copy.wait_send()

    COPIES = 9


def scatter_parts(width, order):
    if order == "both":
        return [(0, width // 2, 2, 4), (width // 2, width // 2, 4, 2)]
    return [(0, width, 2, 4)]


def scatter_shapes(rows, width, order):
    shapes = [pltpu.VMEM((2, 2, rows, width), BF16)]
    for _, columns, _, _ in scatter_parts(width, order):
        shapes += [pltpu.VMEM((2, rows, columns), BF16)] * 2 + [pltpu.VMEM((rows, columns), BF16)] * 2
    return shapes


def wide(v):
    return v.astype(F32)


class Scatter:
    COPIES = 5

    def __init__(self, sems, team, x, scratch, order):
        self.x, self.r0 = x, scratch[0]
        p = team.p
        self.b = bit_of(p, 1), bit_of(p, 2), bit_of(p, 4)
        send = lambda src, dst, bit: sems.copy(src, dst, team.member(flip(p, bit)))
        self.first = send(x.at[:, :, 1 - self.b[0]], self.r0, 1)
        self.parts = []
        for i, (at, columns, one, two) in enumerate(scatter_parts(x.shape[-1], order)):
            s1, r1, s2, r2 = scratch[1 + 4 * i : 5 + 4 * i]
            self.parts.append((pl.ds(at, columns), one, s1, r1, s2, r2, send(s1, r1, one), send(s2, r2, two)))

    def term(self, b2, b1, columns):
        return wide(self.x[b2, b1, self.b[0], :, columns]) + wide(self.r0[b2, b1, :, columns])

    def begin(self):
        self.first.start()

    def relay(self):
        b0, b1, b2 = self.b
        self.first.wait_recv()
        for columns, one, s1, r1, s2, r2, send1, send2 in self.parts:
            for k in range(2):
                s1[k] = (self.term(k, 1 - b1, columns) if one == 2 else self.term(1 - b2, k, columns)).astype(BF16)
            send1.start()

    def relay_again(self):
        b0, b1, b2 = self.b
        for columns, one, s1, r1, s2, r2, send1, send2 in self.parts:
            send1.wait_recv()
            if one == 2:
                total = self.term(1 - b2, b1, columns) + wide(r1[1 - b2])
            else:
                total = self.term(b2, 1 - b1, columns) + wide(r1[1 - b1])
            s2[...] = total.astype(BF16)
            send2.start()

    def end(self, store):
        b0, b1, b2 = self.b
        for columns, one, s1, r1, s2, r2, send1, send2 in self.parts:
            send2.wait_recv()
            store(columns, self.term(b2, b1, columns) + wide(r1[b2 if one == 2 else b1]) + wide(r2[...]))
        for copy in [self.first] + [copy for part in self.parts for copy in part[6:]]:
            copy.wait_send()


def kernel_params(collective_id):
    return pltpu.CompilerParams(
        collective_id=collective_id, has_side_effects=True, vmem_limit_bytes=VMEM_LIMIT
    )


def unit_and_factor(x):
    factor = lax.rsqrt(jnp.mean(x * x, -1, keepdims=True) + EPSILON)
    return x * factor, factor


def lane_ids(rows):
    return lax.broadcasted_iota(jnp.int32, (rows, LANES), 1)


def inside_document(spans, rows, first_row):
    row = lax.broadcasted_iota(jnp.int32, (rows, LANES), 0) + first_row
    return (row >= spans[0:1, :]) & (row < spans[1:2, :])


def widen_keys(kv, spans, first_row, kx, vx):
    rows = kv.shape[0]
    lane = lane_ids(rows)
    inside = inside_document(spans, rows, first_row)
    both = wide(kv)
    kx[...] = jnp.where(lane < HEAD_SIZE, both, jnp.where(inside, 1.0, 0.0)).astype(BF16)
    vx[...] = jnp.where(lane < HEAD_SIZE, pltpu.roll(both, HEAD_SIZE, 1), 1.0).astype(BF16)


def dot_last(a, b):
    return lax.dot_general(a, b, (((1,), (1,)), ((), ())), preferred_element_type=F32)


def fill_tables(t, lengths, freq, cosine, sine, spans):
    rows = cosine.shape[0]
    ends, total = [], 0
    for d in range(NDOCS):
        total = total + lengths[d]
        ends.append(total)
    lane = lax.broadcasted_iota(jnp.int32, spans.shape, 1)
    row = lax.broadcasted_iota(jnp.int32, spans.shape, 0)
    first, past = jnp.zeros(spans.shape, jnp.int32), jnp.full(spans.shape, 2**30, jnp.int32)
    for d in range(NDOCS):
        first = jnp.where(lane == HEAD_SIZE + d, ends[d] - lengths[d], first)
        past = jnp.where(lane == HEAD_SIZE + d, ends[d], past)
    spans[...] = jnp.where(row == 0, first, past)
    half = HEAD_SIZE // 2
    parts = LANES // half
    few = rows // parts
    shape = (few, LANES)
    token = lax.broadcasted_iota(jnp.int32, shape, 0) + lax.div(lax.broadcasted_iota(jnp.int32, shape, 1), half) * few
    token = token + t * rows
    start = jnp.zeros(shape, jnp.int32)
    for d in range(NDOCS):
        start = jnp.where(token >= ends[d], ends[d], start)
    angles = (token - start).astype(F32) * freq[...]
    cos, sin = jnp.cos(angles), jnp.sin(angles)
    for i in range(parts):
        here, lanes = slice(i * few, (i + 1) * few), slice(i * half, (i + 1) * half)
        cosine[here, :] = jnp.concatenate([cos[:, lanes]] * parts, 1)
        sine[here, :] = jnp.concatenate([-sin[:, lanes], sin[:, lanes]] * (parts // 2), 1)


def front_kernel(dims, tokens, wq, wk, wv, wo, w_gate, w_up, gains, freq, lengths,
                 cosine, sine, spans, tok_full, wqkv, normed, heads, qx, kv_all, acc, mixed, wo_full, wide_full, all_gains,
                 tok, q_in, k_in, v_in, qkv_cut, qkv, gains_in, slab_g, slab_u, cut, norm, kv, kx, vx, packed,
                 send, recv, line_send, line_recv, local):
    team = Team(*dims)
    B, F, T = dims
    t, y, f, p = team.t, team.y, team.f, team.p
    sems = Sems(send, recv)
    own_rows, width = tokens.shape
    rows = own_rows * B * F
    depth = width // F
    part, block = rows // 2, rows // 4
    hidden = cut.shape[-1] // 2
    parity = lax.rem(t, 2)

    def home(src, dst, i):
        copy = pltpu.make_async_copy(src, dst, local.at[i])
        copy.start()
        return copy

    token_rows = lambda i: pl.ds(pl.multiple_of(i * own_rows, 16), own_rows)
    shard_rows = lambda i: pl.ds(pl.multiple_of(i * depth, 16), depth)
    token_load = home(tokens, tok.at[token_rows(p)], 0)
    small_loads = [home(wq, q_in, 1), home(wk, k_in, 2), home(wv, v_in, 3)]
    gain_load = home(gains, gains_in.at[f], 4)
    slab_loads = [home(w_gate, slab_g, 5), home(w_up, slab_u, 6)]
    homes = [home(wo, wo_full.at[f], 7)]
    greet(team_peers(team) + line_peers(team))

    half = own_rows // 2
    gather_tok = Gather(
        sems, p, B * F, team.member, tokens, lambda i: tok.at[token_rows(i)],
        lambda i, k: tok.at[pl.ds(pl.multiple_of(i * own_rows + k * half, 16), half)],
        "tall",
    )
    few = packed.shape[1] // 2

    def gather_half(which):
        return Gather(
            sems, p, B * F, team.member, packed.at[which], lambda i: mixed.at[which, i],
            lambda i, k: mixed.at[which, i, pl.ds(k * few, few)],
            "both" if which else "tall",
        )

    gather_mixed = [gather_half(0), gather_half(1)]
    partners = []
    for m in range(1, F):
        to = f
        for bit in (1, 2, 4):
            if m & bit:
                to = flip(to, bit)
        partners.append(to)
    gain_sends = [sems.copy(gains, gains_in.at[f], team.same_row(to)) for to in partners]
    half_depth = depth // 2
    some = pl.ds(pl.multiple_of(parity * half_depth, 16), half_depth)
    near = team.other_team(t + 1 - 2 * parity)
    some_of = lambda i: pl.ds(pl.multiple_of(i * depth + parity * half_depth, 16), half_depth)
    qkv_sends = [sems.copy(qkv_cut.at[partners[0]], qkv.at[shard_rows(f)], team.same_row(partners[0]))]
    qkv_shares = []
    for to in partners[1:]:
        qkv_sends.append(sems.copy(qkv_cut.at[to, some], qkv.at[some_of(f)], team.same_row(to)))
        qkv_shares.append(sems.copy(qkv.at[some_of(to)], qkv.at[some_of(to)], near))
    wide_near = sems.copy(cut.at[partners[0]], wide_full.at[f], team.same_row(partners[0]))
    wide_sends, wide_shares = [[], []], [[], []]
    quarter = half_depth // 2
    for i in range(2):
        some = pl.ds(pl.multiple_of(parity * half_depth + i * quarter, 16), quarter)
        for to in partners[1:]:
            wide_sends[i].append(sems.copy(cut.at[to, some], wide_full.at[f, some], team.same_row(to)))
            wide_shares[i].append(sems.copy(wide_full.at[to, some], wide_full.at[to, some], near))
    if B == 2 and F == 4:
        one, two = flip(f, 1), flip(f, 2)
        other = team.member(lax.rem(p + F, B * F))
        wo_half = lambda k: pl.ds(pl.multiple_of(k * half_depth, 16), half_depth)
        mine, theirs = wo_half(y), wo_half(1 - y)
        wo_first = [
            sems.copy(wo, wo_full.at[f], team.same_row(one)),
            sems.copy(wo.at[mine], wo_full.at[f, mine], team.same_row(two)),
        ]
        ref = wo_full.at[two, mine]
        wo_relay = [sems.copy(ref, ref, other), sems.copy(ref, ref, team.same_row(one))]
        ref = wo_full.at[two, theirs]
        wo_last = [sems.copy(ref, ref, team.same_row(one))]

    def line_copy(d, source, to, r):
        here = pl.ds(pl.multiple_of(r * block, block), block)
        return pltpu.make_async_remote_copy(
            src_ref=kv.at[here], dst_ref=kv_all.at[source, here], send_sem=line_send.at[d, r],
            recv_sem=line_recv.at[source, r], device_id=team.other_team(to), device_id_type=MESH,
        )

    gather_tok.begin()
    for copy in gain_sends:
        copy.start()
    fill_tables(t, lengths, freq, cosine, sine, spans)
    for load in small_loads:
        load.wait()
    for i in range(F):
        for row in range(B):
            h = i * B + row

            @pl.when(y == row)
            def _():
                qkv_cut[i, :, 0:QW] = q_in[:, h * QW : (h + 1) * QW]
                qkv_cut[i, :, QW : QW + HEAD_SIZE] = k_in[:, h * HEAD_SIZE : (h + 1) * HEAD_SIZE]
                qkv_cut[i, :, QW + HEAD_SIZE : QW + 2 * HEAD_SIZE] = v_in[:, h * HEAD_SIZE : (h + 1) * HEAD_SIZE]

    for copy in qkv_sends:
        copy.start()
    qkv[shard_rows(f), :] = qkv_cut[f]
    for load in slab_loads:
        load.wait()

    @pl.loop(0, depth // 32)
    def _(r):
        here = pl.ds(pl.multiple_of(r * 32, 32), 32)
        for j in range(F):
            for row in range(B):
                q = j * B + row

                @pl.when(y == row)
                def _():
                    cut[j, here, 0:hidden] = slab_g[here, q * hidden : (q + 1) * hidden]
                    cut[j, here, hidden : 2 * hidden] = slab_u[here, q * hidden : (q + 1) * hidden]

    gather_tok.relay()
    for arrived, onward in zip(qkv_sends[1:], qkv_shares):
        arrived.wait_recv()
        onward.start()
    for copy in wide_sends[0] + [wide_near]:
        copy.start()
    if B == 2 and F == 4:
        for copy in wo_first:
            copy.start()
    else:
        gather_wo = Gather(
            sems, f, F, team.same_row, wo, lambda i: wo_full.at[i],
            lambda i, k: wo_full.at[i, pl.ds(k * half_depth, half_depth)],
        )
        gather_wo.begin()
    for copy in wide_sends[1]:
        copy.start()
    homes.append(home(cut.at[f], wide_full.at[f], 9))
    gather_tok.end()
    token_load.wait()
    gain_load.wait()
    for copy in gain_sends:
        copy.wait_recv()
    homes.append(home(tok, tok_full, 11))

    all_gains[...] = jnp.zeros_like(all_gains)
    for i in range(F):
        for k, count in ((0, depth), (1, depth), (2, HEAD_SIZE // F), (3, HEAD_SIZE // F)):
            all_gains[k : k + 1, i * count : (i + 1) * count] = wide(gains_in[i])[k : k + 1, 0:count]
    gain_q, gain_k = all_gains[2:3, 0:HEAD_SIZE], all_gains[3:4, 0:HEAD_SIZE]

    @pl.loop(0, rows // block)
    def _(r):
        here = pl.ds(pl.multiple_of(r * block, block), block)
        unit, factor = unit_and_factor(wide(tok[here, :]))
        norm[here, :] = (unit * all_gains[0:1, :]).astype(BF16)

    for copy in qkv_sends[:1] + qkv_shares:
        copy.wait_recv()
    homes += [home(norm, normed, 12), home(qkv, wqkv, 13)]

    lane = lane_ids(block)
    same_head = lax.div(lax.broadcasted_iota(jnp.int32, (LANES, LANES), 0), HEAD_SIZE) == lax.div(
        lax.broadcasted_iota(jnp.int32, (LANES, LANES), 1), HEAD_SIZE
    )
    same_head = jnp.where(same_head, 1.0, 0.0).astype(BF16)
    gain_pairs = [jnp.concatenate([gain_q, gain_q], 1), jnp.concatenate([gain_q, gain_k], 1)]

    @pl.loop(0, rows // block)
    def _(r):
        here = pl.ds(pl.multiple_of(r * block, block), block)
        projected = jnp.dot(norm[here, :], qkv[...], preferred_element_type=F32)
        apart = jnp.where(inside_document(spans, block, t * rows + r * block), 0.0, -APART)
        cos, sin = cosine[here, :], sine[here, :]
        turned = []
        for i in range(2):
            x = projected[:, i * LANES : (i + 1) * LANES]
            heads[i, here, :] = x
            square = x * x
            high = square.astype(BF16)
            rest = (square - wide(high)).astype(BF16)
            total = jnp.dot(high, same_head, preferred_element_type=F32) + jnp.dot(
                rest, same_head, preferred_element_type=F32
            )
            u = x * lax.rsqrt(total * (1.0 / HEAD_SIZE) + EPSILON) * gain_pairs[i]
            first = lax.rem(lane, HEAD_SIZE) < HEAD_SIZE // 2
            swapped = jnp.where(first, pltpu.roll(u, LANES - HEAD_SIZE // 2, 1), pltpu.roll(u, HEAD_SIZE // 2, 1))
            turned.append(wide((u * cos + swapped * sin).astype(BF16)))
        for h in range(GROUP):
            q = turned[h // 2] * HEAD_SIZE ** (-0.5)
            q = pltpu.roll(q, HEAD_SIZE, 1) if h % 2 else q
            qx[h, here, :] = jnp.where(lane < HEAD_SIZE, q, apart).astype(BF16)
        values = projected[:, (GROUP + 1) * HEAD_SIZE : (GROUP + 2) * HEAD_SIZE]
        keys = pltpu.roll(turned[1], HEAD_SIZE, 1)
        kv[here, :] = jnp.where(lane < HEAD_SIZE, keys, jnp.concatenate([values, values], 1)).astype(BF16)
        for d in range(1, T):

            @pl.when(t + d < T)
            def _():
                line_copy(d, t, t + d, r).start()

    kv_all[t] = kv[...]
    widen_keys(kv[...], spans, t * rows, kx.at[t], vx.at[t])
    causal = lax.broadcasted_iota(jnp.int32, (part, part), 1) <= lax.broadcasted_iota(jnp.int32, (part, part), 0)

    def piece(q, source, k, masked):
        scores = dot_last(q, kx[source, k * part : (k + 1) * part, :])
        weights = jnp.exp(scores)
        if masked:
            weights = jnp.where(causal, weights, 0.0)
        return jnp.dot(weights.astype(BF16), vx[source, k * part : (k + 1) * part, :], preferred_element_type=F32)

    def pass_weights(i):
        for arrived, onward in zip(wide_sends[i], wide_shares[i]):
            arrived.wait_recv()
            onward.start()

    def pass_wo():
        if B == 2 and F == 4:
            wo_first[1].wait_recv()
            for copy in wo_relay:
                copy.start()
        else:
            gather_wo.relay()

    for which in range(2):
        mine = slice(which * part, (which + 1) * part)

        @pl.loop(0, GROUP)
        def _(h):
            q = qx[h, mine, :]
            total = piece(q, t, which, True)
            acc[h, mine, :] = total + piece(q, t, 0, False) if which else total

        pass_weights(which)
        if which:
            gather_mixed[0].relay()

        @pl.loop(1, t + 1)
        def _(j):
            source = t - j
            if which == 0:
                for r in range(4):
                    line_copy(0, source, t, r).wait_recv()
                widen_keys(kv_all[source], spans, source * rows, kx.at[source], vx.at[source])

            @pl.loop(0, GROUP)
            def _(h):
                q = qx[h, mine, :]
                acc[h, mine, :] = acc[h, mine, :] + piece(q, source, 0, False) + piece(q, source, 1, False)

        for h in range(GROUP):
            out = acc[h, mine, 0:HEAD_SIZE] / acc[h, mine, HEAD_SIZE : 2 * HEAD_SIZE]
            out = out.astype(BF16)
            if h < 2:
                packed[which, 0:part, h * HEAD_SIZE : (h + 1) * HEAD_SIZE] = out
            else:
                packed[which, part : part + part // 2, 0:HEAD_SIZE] = out[0 : part // 2]
                packed[which, part : part + part // 2, HEAD_SIZE : 2 * HEAD_SIZE] = out[part // 2 : part]
        homes.append(home(packed.at[which], mixed.at[which, p], 14 + which))
        gather_mixed[which].begin()
        if which == 0:
            pass_wo()

    gather_mixed[0].end()
    gather_mixed[1].relay()
    if B == 2 and F == 4:
        wo_relay[0].wait_recv()
        wo_last[0].start()
    gather_mixed[1].end()
    if B == 2 and F == 4:
        for copy in (wo_first[0], wo_relay[1], wo_last[0]):
            copy.wait_recv()
        for copy in wo_first + wo_relay + wo_last:
            copy.wait_send()
    else:
        gather_wo.end()
    for copy in [wide_near] + wide_shares[0] + wide_shares[1]:
        copy.wait_recv()
    for copy in [wide_near] + wide_sends[0] + wide_sends[1] + wide_shares[0] + wide_shares[1]:
        copy.wait_send()
    for copy in gain_sends + qkv_sends + qkv_shares:
        copy.wait_send()
    for copy in homes:
        copy.wait()
    for d in range(1, T):

        @pl.when(t + d < T)
        def _():
            for r in range(4):
                line_copy(d, t, t + d, r).wait_send()


def front(dims, tokens, wq, wk, wv, wo, w_gate, w_up, gains, freq, lengths):
    B, F, T = dims
    own_rows, width = tokens.shape
    n = B * F
    rows = own_rows * n
    depth, ff = w_gate.shape
    hidden = ff // n
    few = QW + 2 * HEAD_SIZE
    copies = 4 * Gather.COPIES + (F - 1) + 3 * (2 * F - 3)
    packed = (rows // 2 + rows // 4, LANES)
    shape = lambda *s: jax.ShapeDtypeStruct(s, BF16)
    wide_shape = lambda *s: jax.ShapeDtypeStruct(s, F32)
    vmem = lambda *s: pltpu.VMEM(s, BF16)
    return pl.pallas_call(
        functools.partial(front_kernel, dims),
        out_shape=(
            wide_shape(rows, LANES), wide_shape(rows, LANES), jax.ShapeDtypeStruct((8, LANES), jnp.int32),
            shape(rows, width), shape(width, few), shape(rows, width), wide_shape((GROUP + 1) // 2, rows, LANES),
            shape(GROUP, rows, LANES), shape(T, rows, LANES), wide_shape(GROUP, rows, LANES), shape(2, n, *packed),
            shape(F, depth, width), shape(F, depth, 2 * hidden),
            wide_shape(8, width),
        ),
        in_specs=[ANY] * 8 + [VMEM, pl.BlockSpec(memory_space=pltpu.SMEM)],
        out_specs=[VMEM] * 3 + [ANY] * 3 + [VMEM] * 4 + [ANY] * 3 + [VMEM],
        scratch_shapes=[
            vmem(rows, width), vmem(*wq.shape), vmem(*wk.shape), vmem(*wv.shape), vmem(F, depth, few), vmem(width, few),
            vmem(F, *gains.shape), vmem(depth, ff), vmem(depth, ff), vmem(F, depth, 2 * hidden),
            vmem(rows, width), vmem(rows, LANES), vmem(T, rows, LANES), vmem(T, rows, LANES), vmem(2, *packed),
            pltpu.SemaphoreType.DMA((copies,)),
            pltpu.SemaphoreType.DMA((copies,)),
            pltpu.SemaphoreType.DMA((T, 4)),
            pltpu.SemaphoreType.DMA((T, 4)),
            pltpu.SemaphoreType.DMA((16,)),
        ],
        compiler_params=kernel_params(1),
        name="front",
    )(tokens, wq, wk, wv, wo, w_gate, w_up, gains, freq, lengths)


def feed_kernel(dims, tok_in, mixed_in, wo_in, wide_in, down_in, dy_in, gain, grad_hidden, g_down,
                g_wide, g_last, own_resid, layer_out, tok, mixed, wo, w_wide, w_down, dy, rows_in, hid, both, act, dwide,
                resid, down, gd, gw, gl, *rest):
    scratch, (send, recv, local) = rest[:9], rest[9:]
    team = Team(*dims)
    B, F, y, p = team.B, team.F, team.y, team.p
    rows, width = tok.shape
    own_rows = own_resid.shape[0]
    hidden = w_down.shape[0]
    early = gw.shape[1]
    block = resid.shape[0]
    n = B * F
    dy_rows = lambda i: pl.ds(pl.multiple_of(i * own_rows, 16), own_rows)
    loads = [
        pltpu.make_async_copy(src, dst, local.at[i])
        for i, (src, dst) in enumerate(
            [(mixed_in, mixed), (wo_in, wo), (tok_in, tok), (wide_in, w_wide),
             (down_in.at[pl.ds(pl.multiple_of(y * hidden, 16), hidden)], w_down), (dy_in, dy.at[dy_rows(p)])]
        )
    ]
    for load in loads:
        load.start()
    greet([team.member(flip(p, bit)) for bit in (1, 2, 4)])
    sems = Sems(send, recv)
    scatter = Scatter(sems, team, down, scratch, "both")
    half = own_rows // 2
    gather = Gather(
        sems, p, n, team.member, dy_in, lambda i: dy.at[dy_rows(i)],
        lambda i, k: dy.at[pl.ds(pl.multiple_of(i * own_rows + k * half, 16), half)],
    )
    gather.begin()
    for load in loads[:3]:
        load.wait()

    @pl.loop(0, rows // block)
    def _(r):
        here = pl.ds(pl.multiple_of(r * block, block), block)
        which, later = lax.div(r, 2), lax.rem(r, 2)
        place = pl.ds(pl.multiple_of(later * block, block), block)
        for i in range(n):
            h = i % F * B + i // F
            first = h * QW
            rows_in[:, first : first + 2 * HEAD_SIZE] = mixed[which, i, place, :]
            last = mixed[which, i, 2 * block : 3 * block, :]
            last = jnp.where(later == 0, wide(last[:, :HEAD_SIZE]), wide(last[:, HEAD_SIZE:]))
            rows_in[:, first + 2 * HEAD_SIZE : first + QW] = last.astype(BF16)
        pl.when(r == 2)(gather.relay)
        resid[...] = wide(tok[here, :]) + jnp.dot(rows_in[...], wo[...], preferred_element_type=F32)

        @pl.when(r == lax.div(p * own_rows, block))
        def _():
            own_resid[...] = resid[pl.ds(pl.multiple_of(lax.rem(p * own_rows, block), 8), own_rows), :]

        unit, factor = unit_and_factor(resid[...])
        hid[here, :] = (unit * gain[1:2, :]).astype(BF16)

    for load in loads[3:]:
        load.wait()

    @pl.loop(0, rows // block)
    def _(r):
        here = pl.ds(pl.multiple_of(r * block, block), block)
        product = jnp.dot(hid[here, :], w_wide[...], preferred_element_type=F32)
        gate, upper = product[:, :hidden], product[:, hidden:]
        both[0, here, :] = gate
        both[1, here, :] = upper
        sigma = 1.0 / (1.0 + jnp.exp(-gate))
        acts = (gate * sigma * upper).astype(BF16)
        act[here, :] = acts
        out = jnp.dot(acts, w_down[...], preferred_element_type=F32).astype(BF16)
        for i in range(block // own_rows):
            m = r * (block // own_rows) + i
            down[lax.div(m, 4), lax.rem(lax.div(m, 2), 2), lax.rem(m, 2)] = out[i * own_rows : (i + 1) * own_rows]

    scatter.begin()
    gather.end()

    @pl.loop(0, rows // block)
    def _(r):
        here = pl.ds(pl.multiple_of(r * block, block), block)
        pl.when(r == 1)(scatter.relay)
        gate, upper = both[0, here, :], both[1, here, :]
        sigma = 1.0 / (1.0 + jnp.exp(-gate))
        dact = dot_last(dy[here, :], w_down[...])
        dwide[here, 0:hidden] = (dact * upper * sigma * (1.0 + gate * (1.0 - sigma))).astype(BF16)
        dwide[here, hidden : 2 * hidden] = (dact * (gate * sigma)).astype(BF16)
        tok[here, :] = dot_last(dwide[here, :], w_wide[...]).astype(BF16)

    stores = []

    def store(src, dst):
        stores.append(pltpu.make_async_copy(src, dst, local.at[6 + len(stores)]))
        stores[-1].start()

    store(tok, grad_hidden)
    scatter.relay_again()
    over_rows = lambda a, b: lax.dot_general(a, b, (((0,), (0,)), ((), ())), preferred_element_type=F32).astype(BF16)

    for first in range(0, hidden, 256):
        count = min(256, hidden - first)
        gd[first : first + count, :] = over_rows(act[:, first : first + count], dy[...])
    store(gd, g_down)

    @pl.loop(0, width // 256)
    def _(r):
        here = pl.ds(pl.multiple_of(r * 256, 256), 256)
        product = over_rows(hid[:, here], dwide[...])
        gw[here, :] = product[:, :early]
        gl[here, 0 : 2 * hidden - early] = product[:, early:]
        pltpu.make_async_copy(gw.at[here], g_wide.at[here], local.at[10]).start()
        pltpu.make_async_copy(gl.at[here], g_last.at[here], local.at[11]).start()

    def put(columns, total):
        layer_out[:, columns] = own_resid[:, columns] + total

    scatter.end(put)
    for copy in stores:
        copy.wait()
    pltpu.make_async_copy(gw, g_wide, local.at[10]).wait()
    pltpu.make_async_copy(gl, g_last, local.at[11]).wait()


def feed(dims, tok, mixed, wo, w_wide, w_down, dy, gains):
    rows, width = tok.shape
    hidden = w_wide.shape[1] // 2
    own_rows = rows // KEY_VALUE_HEADS
    early = early_lanes(hidden)
    last = 2 * hidden - early + QW + 2 * HEAD_SIZE
    block = rows // 4
    shape = lambda s: jax.ShapeDtypeStruct(s, BF16)
    return pl.pallas_call(
        functools.partial(feed_kernel, dims),
        out_shape=(
            shape((rows, width)), shape((hidden, width)), shape((width, early)), shape((width, last)),
            jax.ShapeDtypeStruct((own_rows, width), F32), jax.ShapeDtypeStruct((own_rows, width), F32),
        ),
        in_specs=[ANY] * 6 + [VMEM],
        out_specs=[ANY] * 4 + [VMEM] * 2,
        scratch_shapes=[
            pltpu.VMEM((rows, width), BF16),
            pltpu.VMEM(mixed.shape, BF16),
            pltpu.VMEM(wo.shape, BF16),
            pltpu.VMEM(w_wide.shape, BF16),
            pltpu.VMEM((hidden, width), BF16),
            pltpu.VMEM((rows, width), BF16),
            pltpu.VMEM((block, width), BF16),
            pltpu.VMEM((rows, width), BF16),
            pltpu.VMEM((2, rows, hidden), F32),
            pltpu.VMEM((rows, hidden), BF16),
            pltpu.VMEM((rows, 2 * hidden), BF16),
            pltpu.VMEM((block, width), F32),
            pltpu.VMEM((2, 2, 2, own_rows, width), BF16),
            pltpu.VMEM((hidden, width), BF16),
            pltpu.VMEM((width, early), BF16),
            pltpu.VMEM((width, last), BF16),
        ]
        + scatter_shapes(own_rows, width, "both")
        + [
            pltpu.SemaphoreType.DMA((Scatter.COPIES + Gather.COPIES,)),
            pltpu.SemaphoreType.DMA((Scatter.COPIES + Gather.COPIES,)),
            pltpu.SemaphoreType.DMA((12,)),
        ],
        compiler_params=pltpu.CompilerParams(
            collective_id=2, has_side_effects=True, vmem_limit_bytes=60 * 1024 * 1024
        ),
        name="feed",
    )(tok, mixed, wo, w_wide, w_down, dy, gains)


HOP = 2
LAG = 3
ORDER = "both"


class GradSum:
    RED, LEFT, RIGHT, HAND, OVER, HOME, INTO = range(7)

    def __init__(self, team, kinds, red_recv, fin_recv, hand_recvs, bulk):
        self.team, self.kinds = team, kinds
        self.red_recv, self.fin_recv, self.hand_recvs, self.bulk = red_recv, fin_recv, hand_recvs, bulk
        self.opposite = team.member(lax.rem(team.p + team.F, team.B * team.F))
        self.low, self.high = team.T // 2 - 1, team.T // 2

    @staticmethod
    def steps(kinds, T):
        return max(first + rows // step for rows, step, first in kinds) + HOP * T + LAG

    def remote(self, src, dst, send_sem, recv_sem, device):
        return pltpu.make_async_remote_copy(
            src_ref=src, dst_ref=dst, send_sem=send_sem, recv_sem=recv_sem, device_id=device, device_id_type=MESH
        )

    def where(self, k, c):
        g, step, how = self.kinds[k][0], self.kinds[k][4], self.kinds[k][6]
        if how != "rows":
            return pl.ds(pl.multiple_of(c * step, 16), step), None, None
        F = self.team.F
        turn = lax.rem(c, F)
        to = lax.rem(turn, 2) * (F // 2) + lax.div(turn, 2)
        row = lax.div(c, F) * step
        return pl.ds(pl.multiple_of(to * (g.shape[0] // F) + row, 16), step), to, row

    def spare(self, k, c):
        step = self.kinds[k][4]
        return pl.ds(pl.multiple_of(lax.div(c, 2) * step, 16), step)

    def reduce(self, k, c, i, root):
        g, land, land2 = self.kinds[k][:3]
        team = self.team
        t, T = team.t, team.T
        at, _, _ = self.where(k, c)
        red = self.bulk.at[self.RED, k, 0]

        def inward(side, dst):
            to = team.other_team(t + 1 - 2 * side)
            self.remote(g.at[at], dst, red, self.red_recv.at[side, i], to).start()

        def add():
            g[at, :] = (wide(g[at, :]) + wide(land[at, :])).astype(BF16)

        @pl.when(t < root)
        def _():
            @pl.when(t > 0)
            def _():
                self.remote(g.at[at], land.at[at], red, self.red_recv.at[0, i], team.other_team(t)).wait_recv()
                add()

            inward(0, land.at[at])

        @pl.when(t > root)
        def _():
            @pl.when(t < T - 1)
            def _():
                self.remote(g.at[at], land.at[at], red, self.red_recv.at[1, i], team.other_team(t)).wait_recv()
                add()

            @pl.when(t - 1 == root)
            def _():
                inward(1, land2.at[self.spare(k, c)])

            @pl.when(t - 1 != root)
            def _():
                inward(1, land.at[at])

    def finish(self, k, c, i, root):
        g, land, land2, out, step, first, how = self.kinds[k]
        team, bulk = self.team, self.bulk
        B, F, T, t, y, f = team.B, team.F, team.T, team.t, team.y, team.f
        at, to, row = self.where(k, c)
        red = bulk.at[self.RED, k, 0]

        def outward(side):
            to_team = team.other_team(t - 1 + 2 * side)
            sem = bulk.at[self.RIGHT if side else self.LEFT, k, 0]
            return self.remote(land.at[at], land.at[at], sem, self.fin_recv.at[i], to_team)

        @pl.when(t == root)
        def _():
            total = wide(g[at, :])
            if self.low > 0:
                self.remote(g.at[at], land.at[at], red, self.red_recv.at[0, i], team.other_team(t)).wait_recv()
                total = total + wide(land[at, :])
                self.remote(g.at[at], land2.at[self.spare(k, c)], red, self.red_recv.at[1, i],
                            team.other_team(t)).wait_recv()
                total = total + wide(land2[self.spare(k, c), :])
            land[at, :] = total.astype(BF16)

        @pl.when(t != root)
        def _():
            outward(0).wait_recv()

        @pl.when((t <= root) & (t > 0))
        def _():
            outward(0).start()

        @pl.when((t >= root) & (t < T - 1))
        def _():
            outward(1).start()

        if how == "rows":
            dst = out.at[f * B + y, pl.ds(pl.multiple_of(row, 16), step)]

            @pl.when(to == f)
            def _():
                pltpu.make_async_copy(land.at[at], dst, bulk.at[self.HOME, k, 0]).start()
                if B == 2:
                    self.remote(land.at[at], dst, bulk.at[self.OVER, k, 0], bulk.at[self.INTO, k, 0],
                                self.opposite).start()

            @pl.when(to != f)
            def _():
                self.remote(land.at[at], dst, bulk.at[self.HAND, k, 0], self.hand_recvs[k].at[f, lax.div(row, step)],
                            team.same_row(to)).start()
        elif how == "stay":
            dst = out.at[y, at]
            pltpu.make_async_copy(land.at[at], dst, bulk.at[self.HOME, k, 0]).start()
            if B == 2:
                self.remote(land.at[at], dst, bulk.at[self.OVER, k, 0], bulk.at[self.INTO, k, 0],
                            self.opposite).start()
        else:
            for index in range(F):
                src = land.at[pl.ds(16 * index, 16)]
                for line in range(B):

                    @pl.when(team.p == line * F + index)
                    def _():
                        pltpu.make_async_copy(src, out.at[team.p], bulk.at[self.HOME, k, 0]).start()

                    @pl.when(team.p != line * F + index)
                    def _():
                        self.remote(src, out.at[team.p], bulk.at[self.HAND, k, 0], bulk.at[self.INTO, k, 0],
                                    (t * B + line, index)).start()

    def pass_over(self, k, c, i, root):
        g, land, land2, out, step, first, how = self.kinds[k]
        if how != "rows":
            return
        team = self.team
        at, to, row = self.where(k, c)

        @pl.when(to == team.f)
        def _():
            for d in range(1, team.F):
                source = lax.rem(team.f + d, team.F)
                ref = out.at[source * team.B + team.y, pl.ds(pl.multiple_of(row, 16), step)]
                self.remote(land.at[at], ref, self.bulk.at[self.HAND, k, 0],
                            self.hand_recvs[k].at[source, lax.div(row, step)], team.same_row(team.f)).wait_recv()
                if team.B == 2:
                    self.remote(ref, ref, self.bulk.at[self.OVER, k, 1], self.bulk.at[self.INTO, k, 0],
                                self.opposite).start()

    def each(self, i, body):
        root = self.low + lax.rem(lax.max(i, 0), 2)
        for k, (g, land, land2, out, step, first, how) in enumerate(self.kinds):
            count = g.shape[0] // step
            pl.when((i >= first) & (i < first + count))(functools.partial(body, k, i - first, i, root))

    def step(self, s):
        T, t = self.team.T, self.team.t
        self.each(s - HOP * lax.min(t, T - 1 - t), self.reduce)
        for parity in range(2):
            root = self.low + parity
            distance = jnp.where(t < root, root - t, t - root)
            i = s - HOP * (T // 2 + distance)
            for wait, body in ((0, self.finish), (LAG, self.pass_over)):
                j = i - wait
                pl.when((j >= 0) & (lax.rem(lax.max(j, 0), 2) == parity))(functools.partial(self.each, j, body))

    def drain(self, ref, sem):
        pltpu.make_async_copy(ref, ref, sem).wait()

    def end(self):
        bulk, B, F, T, t = self.bulk, self.team.B, self.team.F, self.team.T, self.team.t
        low, high = self.low, self.high
        for k, (g, land, land2, out, step, first, how) in enumerate(self.kinds):
            rows = g.shape[0]
            some = lambda n: g.at[pl.ds(0, n)]
            count = rows // step
            even = (count + 1 - first % 2) // 2 * step
            odd = rows - even

            def drain_some(condition, n, which):
                if n:

                    @pl.when(condition)
                    def _():
                        self.drain(some(n), bulk.at[which, k, 0])

            drain_some((t != low) & (t != high), rows, self.RED)
            drain_some(t == low, odd, self.RED)
            drain_some(t == high, even, self.RED)
            drain_some((t > 0) & (t <= low), rows, self.LEFT)
            drain_some(t == high, odd, self.LEFT)
            drain_some((t < T - 1) & (t >= high), rows, self.RIGHT)
            drain_some(t == low, even, self.RIGHT)
            if how == "rows":
                shard = rows // F
                self.drain(some(rows - shard), bulk.at[self.HAND, k, 0])
                self.drain(some(shard), bulk.at[self.HOME, k, 0])
                if B == 2:
                    self.drain(some(shard), bulk.at[self.OVER, k, 0])
                    self.drain(some(rows - shard), bulk.at[self.OVER, k, 1])
                    self.drain(g, bulk.at[self.INTO, k, 0])
            elif how == "stay":
                self.drain(g, bulk.at[self.HOME, k, 0])
                if B == 2:
                    self.drain(g, bulk.at[self.OVER, k, 0])
                    self.drain(g, bulk.at[self.INTO, k, 0])
            else:
                others = out.at[pl.ds(0, B * F - 1)]
                self.drain(out.at[0], bulk.at[self.HOME, k, 0])
                self.drain(others, bulk.at[self.HAND, k, 0])
                self.drain(others, bulk.at[self.INTO, k, 0])


def first_steps(dims):
    at = dict(scatter1=3, scatter2=12, resid=18, relay=24, heads=31, own_wo=35)
    at["attention"] = at["own_wo"] + 1
    at["keys"] = at["attention"] + 2 * GROUP * dims[2] + 2
    at["turn"] = at["keys"] + 1
    at["normed"] = at["turn"] + 4
    at["products"] = at["normed"] + 2
    at["again1"] = at["products"] + 3
    at["again2"] = at["again1"] + 6
    at["tokens"] = at["again2"] + 7
    return at


def early_lanes(hidden):
    return 2 * hidden // LANES * LANES


def grad_kinds(dims, depth, hidden):
    at = first_steps(dims)
    early = early_lanes(hidden)
    kinds, place = [], 0
    for rows, width, step, ready, how in (
        (hidden, depth, 32, 0, "stay"),
        (depth, early, 32, 0, "rows"),
        (QW, depth, 48, at["own_wo"] + 1, "stay"),
        (depth, 2 * hidden - early + QW + 2 * HEAD_SIZE, 96, at["products"] + 3, "rows"),
        (16 * dims[1], max(depth // dims[1], LANES), 16 * dims[1], at["tokens"] + 1, "gain"),
    ):
        place = max(place, ready)
        kinds.append((rows, width, step, place, how))
        place += rows // step
    return kinds


def back_kernel(dims, kinds, steps, grad_hidden, g_down, g_wide, g_last, resid, tokens, cotangent, gains, acc, qx, kv_all, spans,
                heads, cosine, sine, wo, wqkv, normed,
                out_down, out_wide, out_wo, out_last, out_gains, tokens_grad,
                xs, own_down, own_wide, own_gwo, own_last, own_gains,
                land_down, land_wide, land_wo, land_last, land_gains,
                also_down, also_wide, also_wo, also_last, also_gains,
                grad_resid, attn_own, big, dox, mixed, dq, dkv, kv_in, dkv_sum, turned, small, kx, vx, dk, dv, wq_in, own_wo, *rest):
    count = len(scatter_parts(resid.shape[-1], ORDER)) * 4 + 1
    scratch1, rest = rest[:count], rest[count:]
    send, recv, line_send, line_recv, red_recv, fin_recv, hand_wide, hand_last, bulk, local = rest
    team = Team(*dims)
    B, F, T = dims
    t, p = team.t, team.p
    at = first_steps(dims)
    own_rows, width = resid.shape
    rows = qx.shape[1]
    part = rows // 2
    block = rows // 4
    depth = width // F
    sems = Sems(send, recv)
    loads = [
        pltpu.make_async_copy(src, dst, local.at[i])
        for i, (src, dst) in enumerate(
            [(grad_hidden, xs), (g_down, own_down), (g_wide, own_wide), (g_last, own_last), (wqkv, wq_in),
             (wo.at[pl.ds(pl.multiple_of(team.y * QW, 16), QW)], own_wo)]
        )
    ]
    for load in loads:
        load.start()
    own_gains[...] = jnp.zeros_like(own_gains)
    greet(team_peers(team) + line_peers(team))
    loads[0].wait()
    scatter = Scatter(sems, team, xs, scratch1, ORDER)
    scatter.begin()
    again = Scatter(sems, team, xs, scratch1, ORDER)
    half = own_rows // 2
    gather = Gather(
        sems, p, B * F, team.member, attn_own,
        lambda i: big.at[pl.ds(pl.multiple_of(i * own_rows, 16), own_rows)],
        lambda i, k: big.at[pl.ds(pl.multiple_of(i * own_rows + k * half, 16), half)],
    )
    sums = GradSum(
        team,
        [
            (own, land, also, out) + kind[2:]
            for own, land, also, out, kind in zip(
                (own_down, own_wide, own_gwo, own_last, own_gains),
                (land_down, land_wide, land_wo, land_last, land_gains),
                (also_down, also_wide, also_wo, also_last, also_gains),
                (out_down, out_wide, out_wo, out_last, out_gains),
                kinds,
            )
        ],
        red_recv, fin_recv, [None, hand_wide, None, hand_last, None], bulk,
    )
    loads[1].wait()
    gain_attn, gain_ffn = gains[0:1, :], gains[1:2, :]
    gain_q, gain_k = gains[2:3, 0:HEAD_SIZE], gains[3:4, 0:HEAD_SIZE]
    home = pltpu.make_async_copy(attn_own, big.at[pl.ds(pl.multiple_of(p * own_rows, 16), own_rows)], local.at[6])
    fetch = pltpu.make_async_copy(normed, big, local.at[7])

    def resid_phase():
        def store(columns, total):
            grad_resid[:, columns] = total

        scatter.end(store)
        term = jnp.zeros((1, width), F32)
        for r in range(0, own_rows, 32):
            here = slice(r, r + 32)
            unit, factor = unit_and_factor(resid[here, :])
            upstream = grad_resid[here, :]
            term = term + jnp.sum(upstream * unit, 0, keepdims=True)
            total = wide(cotangent[here, :]) + norm_back(upstream, unit, factor, gain_ffn)
            grad_resid[here, :] = total
            attn_own[here, :] = total.astype(BF16)
        small[1:2, :] = term
        home.start()
        gather.begin()

    def heads_phase():
        gather.end()
        home.wait()

    def heads_unit(r):
        lane = lane_ids(block)
        here = pl.ds(pl.multiple_of(r * block, block), block)
        grad = dot_last(big[here, :], own_wo[...]).astype(BF16)
        for h in range(GROUP):
            sums_h = acc[h, here, :]
            total = pltpu.roll(sums_h, HEAD_SIZE, 1)
            out = sums_h / total
            mixed[here, h * HEAD_SIZE : (h + 1) * HEAD_SIZE] = out[:, :HEAD_SIZE].astype(BF16)
            do = wide(grad[:, h * HEAD_SIZE : (h + 1) * HEAD_SIZE])
            do = jnp.concatenate([do, jnp.zeros_like(do)], 1)
            delta = -jnp.sum(jnp.where(lane < HEAD_SIZE, do * out, 0.0), 1, keepdims=True)

            def put(x, first, value):
                for i in range(3):
                    x = jnp.where(lane == first + i, wide(value.astype(BF16)), x)
                    value = value - wide(value.astype(BF16))
                return x

            dox[h, here, :] = put(do, HEAD_SIZE, delta).astype(BF16)
            log_sum = -jnp.log(jnp.where(lane < HEAD_SIZE, total, sums_h))
            qx[h, here, :] = put(wide(qx[h, here, :]), HEAD_SIZE + NDOCS, log_sum).astype(BF16)

    def own_wo_phase():
        own_gwo[...] = lax.dot_general(
            mixed[...], big[...], (((0,), (0,)), ((), ())), preferred_element_type=F32
        ).astype(BF16)
        dq[...] = jnp.zeros_like(dq)

    causal = lax.broadcasted_iota(jnp.int32, (part, part), 0) <= lax.broadcasted_iota(jnp.int32, (part, part), 1)

    def piece(h, q_rows, k_rows, masked):
        q = qx[h, q_rows, :]
        do = dox[h, q_rows, :]
        keys = kx[k_rows, :]
        weights = jnp.exp(dot_last(keys, q))
        if masked:
            weights = jnp.where(causal, weights, 0.0)
        dscore = (weights * dot_last(vx[k_rows, :], do)).astype(BF16)
        dv[...] += jnp.dot(weights.astype(BF16), do, preferred_element_type=F32)
        dk[...] += jnp.dot(dscore, q, preferred_element_type=F32)
        dq[h, q_rows, :] += lax.dot_general(dscore, keys, (((0,), (0,)), ((), ())), preferred_element_type=F32)

    def line_copy(owner, source):
        return pltpu.make_async_remote_copy(
            src_ref=dkv.at[owner], dst_ref=dkv.at[source], send_sem=line_send.at[owner],
            recv_sem=line_recv.at[source], device_id=team.other_team(owner), device_id_type=MESH,
        )

    def fetch_keys(source):
        slot = lax.rem(source, 2)
        return pltpu.make_async_copy(kv_all.at[source], kv_in.at[slot], local.at[8 + slot])

    fetch_keys(t * 0).start()

    def attention_unit(source, k, h):
        @pl.when((k == 0) & (h == 0))
        def _():
            fetch_keys(source).wait()

            @pl.when(source < t)
            def _():
                fetch_keys(source + 1).start()

            widen_keys(kv_in[lax.rem(source, 2)], spans, source * rows, kx, vx)

        @pl.when(h == 0)
        def _():
            dk[...] = jnp.zeros_like(dk)
            dv[...] = jnp.zeros_like(dv)

        k_rows = pl.ds(pl.multiple_of(k * part, part), part)

        @pl.when(source < t)
        def _():
            for q in range(2):
                piece(h, slice(q * part, (q + 1) * part), k_rows, False)

        @pl.when(source == t)
        def _():
            for diagonal in range(2):

                @pl.when(k == diagonal)
                def _():
                    for q in range(diagonal, 2):
                        piece(h, slice(q * part, (q + 1) * part), slice(diagonal * part, (diagonal + 1) * part),
                              q == diagonal)

        @pl.when(h == GROUP - 1)
        def _():
            dkv[source, k_rows, :] = jnp.where(
                lane_ids(part) < HEAD_SIZE, dk[...], pltpu.roll(dv[...], HEAD_SIZE, 1)
            ).astype(BF16)

            @pl.when((k == 1) & (source < t))
            def _():
                line_copy(source, t).start()

    def keys_phase():
        fetch.start()
        dkv_sum[...] = wide(dkv[t])
        for d in range(1, T):

            @pl.when(t + d < T)
            def _():
                line_copy(t, t + d).wait_recv()
                dkv_sum[...] += wide(dkv[t + d])

        small[2:4, :] = jnp.zeros((2, width), F32)

    def turn_unit(r):
        here = pl.ds(pl.multiple_of(r * block, block), block)
        cos, sin = cosine[here, 0:HEAD_SIZE], sine[here, 0:HEAD_SIZE]
        q_term = jnp.zeros((1, HEAD_SIZE), F32)
        for h in range(GROUP + 1):
            if h < GROUP:
                u, gain = dq[h, here, 0:HEAD_SIZE] * HEAD_SIZE ** (-0.5), gain_q
            else:
                u, gain = dkv_sum[here, 0:HEAD_SIZE], gain_k
            u = u * cos - jnp.concatenate([u[:, HEAD_SIZE // 2 :], u[:, : HEAD_SIZE // 2]], 1) * sin
            unit, factor = unit_and_factor(heads[h // 2, here, h % 2 * HEAD_SIZE : (h % 2 + 1) * HEAD_SIZE])
            term = jnp.sum(u * unit, 0, keepdims=True)
            if h < GROUP:
                q_term = q_term + term
            else:
                small[3:4, 0:HEAD_SIZE] += term
            turned[here, h * HEAD_SIZE : (h + 1) * HEAD_SIZE] = norm_back(u, unit, factor, gain).astype(BF16)
        small[2:3, 0:HEAD_SIZE] += q_term
        h = GROUP + 1
        turned[here, h * HEAD_SIZE : (h + 1) * HEAD_SIZE] = dkv_sum[here, HEAD_SIZE : 2 * HEAD_SIZE].astype(BF16)

    def normed_unit(i):
        for m in range(4):
            here = pl.ds(pl.multiple_of((4 * i + m) * own_rows, own_rows), own_rows)
            xs[i, m // 2, m % 2] = dot_last(turned[here, :], wq_in[...]).astype(BF16)

    def products_phase():
        again.begin()
        fetch.wait()

    def products_unit(i):
        for j in range(2):
            r = pl.multiple_of((2 * i + j) * (width // 6), LANES)
            here = pl.ds(r, width // 6)
            own_last[here, own_last.shape[1] - turned.shape[1] :] = lax.dot_general(
                big[:, here], turned[...], (((0,), (0,)), ((), ())), preferred_element_type=F32
            ).astype(BF16)

    def tokens_phase():
        def store(columns, total):
            tokens_grad[:, columns] = total

        again.end(store)
        term = jnp.zeros((1, width), F32)
        for r in range(0, own_rows, 32):
            here = slice(r, r + 32)
            unit, factor = unit_and_factor(wide(tokens[here, :]))
            upstream = tokens_grad[here, :]
            term = term + jnp.sum(upstream * unit, 0, keepdims=True)
            tokens_grad[here, :] = grad_resid[here, :] + norm_back(upstream, unit, factor, gain_attn)
        small[0:1, :] = term
        lanes = own_gains.shape[1]
        row = lax.broadcasted_iota(jnp.int32, (16, lanes), 0)

        def cut(i, first, count):
            value = small[i : i + 1, first : first + count]
            if count < lanes:
                value = jnp.concatenate([value, jnp.zeros((1, lanes - count), F32)], 1)
            return jnp.where(row == i, jnp.broadcast_to(value, (16, lanes)), 0.0)

        for i in range(F):
            few = HEAD_SIZE // F
            own_gains[16 * i : 16 * i + 16, :] = (
                cut(0, i * depth, depth) + cut(1, i * depth, depth) + cut(2, i * few, few) + cut(3, i * few, few)
            ).astype(BF16)

    def late_loads():
        for load in loads[2:]:
            load.wait()

    @pl.loop(0, steps)
    def _(s):
        pl.when(s == at["scatter1"])(late_loads)
        sums.step(s)
        for name, body in (
            ("scatter1", scatter.relay), ("scatter2", scatter.relay_again), ("resid", resid_phase),
            ("relay", gather.relay), ("heads", heads_phase), ("own_wo", own_wo_phase), ("keys", keys_phase),
            ("products", products_phase), ("again1", again.relay), ("again2", again.relay_again),
            ("tokens", tokens_phase),
        ):
            pl.when(s == at[name])(body)
        for name, count, body in (
            ("heads", 4, heads_unit), ("turn", 4, turn_unit), ("normed", 2, normed_unit),
            ("products", 3, products_unit),
        ):
            i = s - at[name]
            pl.when((i >= 0) & (i < count))(functools.partial(body, i))
        unit = s - at["attention"]
        source = lax.div(unit, 2 * GROUP)

        @pl.when((unit >= 0) & (source <= t))
        def _():
            attention_unit(source, lax.rem(lax.div(unit, GROUP), 2), lax.rem(unit, GROUP))

    for d in range(1, T):

        @pl.when(t - d >= 0)
        def _():
            line_copy(t - d, t).wait_send()

    sums.end()


def backward(dims, grad_hidden, g_down, g_wide, g_last, resid, tokens, cotangent, gains, acc, qx, kv_all, spans,
             heads, cosine, sine, wo, wqkv, normed):
    B, F, T = dims
    own_rows, width = resid.shape
    rows = qx.shape[1]
    part = rows // 2
    hidden = g_down.shape[0]
    n = B * F
    kinds = grad_kinds(dims, width, hidden)
    steps = max(
        GradSum.steps([(rows_, step, first) for rows_, _, step, first, _ in kinds], T), first_steps(dims)["tokens"] + 1
    )
    positions = max(first + rows_ // step for rows_, _, step, first, _ in kinds)
    outs = []
    for rows_, wide_, step, first, how in kinds:
        if how == "rows":
            shape = (n, rows_ // F, wide_)
        elif how == "stay":
            shape = (B, rows_, wide_)
        else:
            shape = (n, 16, wide_)
        outs.append(jax.ShapeDtypeStruct(shape, BF16))
    outs.append(jax.ShapeDtypeStruct((own_rows, width), F32))
    eight = (2, 2, 2, own_rows, width)
    hands = [pltpu.SemaphoreType.DMA((F, kinds[k][0] // F // kinds[k][2])) for k in (1, 3)]
    copies = 2 * Scatter.COPIES + Gather.COPIES
    return pl.pallas_call(
        functools.partial(back_kernel, dims, kinds, steps),
        out_shape=outs,
        in_specs=[ANY] * 4 + [VMEM] * 6 + [ANY] + [VMEM] * 4 + [ANY] * 3,
        out_specs=[ANY] * 5 + [VMEM],
        scratch_shapes=[pltpu.VMEM(eight, BF16)]
        + [pltpu.VMEM((kind[0], kind[1]), BF16) for kind in kinds] * 2
        + [pltpu.VMEM(((kind[0] // kind[2] + 1) // 2 * kind[2], kind[1]), BF16) for kind in kinds]
        + [
            pltpu.VMEM((own_rows, width), F32),
            pltpu.VMEM((own_rows, width), BF16),
            pltpu.VMEM((rows, width), BF16),
            pltpu.VMEM(qx.shape, BF16),
            pltpu.VMEM((rows, QW), BF16),
            pltpu.VMEM(qx.shape, F32),
            pltpu.VMEM(kv_all.shape, BF16),
            pltpu.VMEM((2,) + kv_all.shape[1:], BF16),
            pltpu.VMEM((rows, LANES), F32),
            pltpu.VMEM((rows, QW + 2 * HEAD_SIZE), BF16),
            pltpu.VMEM((8, width), F32),
            pltpu.VMEM((rows, LANES), BF16),
            pltpu.VMEM((rows, LANES), BF16),
            pltpu.VMEM((part, LANES), F32),
            pltpu.VMEM((part, LANES), F32),
            pltpu.VMEM(wqkv.shape, BF16),
            pltpu.VMEM((QW, width), BF16),
        ]
        + scatter_shapes(own_rows, width, ORDER)
        + [
            pltpu.SemaphoreType.DMA((copies,)),
            pltpu.SemaphoreType.DMA((copies,)),
            pltpu.SemaphoreType.DMA((T,)),
            pltpu.SemaphoreType.DMA((T,)),
            pltpu.SemaphoreType.DMA((2, positions)),
            pltpu.SemaphoreType.DMA((positions,)),
            *hands,
            pltpu.SemaphoreType.DMA((7, len(kinds), 2)),
            pltpu.SemaphoreType.DMA((11,)),
        ],
        compiler_params=pltpu.CompilerParams(
            collective_id=3, has_side_effects=True, vmem_limit_bytes=60 * 1024 * 1024
        ),
        name="backward",
    )(grad_hidden.reshape(eight), g_down, g_wide, g_last, resid, tokens, cotangent, gains, acc, qx,
      kv_all, spans, heads, cosine, sine, wo, wqkv, normed)


def place_kernel(n, hidden, both, last, down, wo, layer, tokens, gains, gate_out, up_out, wq_out, wk_out, wv_out, down_out,
                 wo_out, layer_out, tokens_out, *gain_outs):
    early = both.shape[-1]
    tail = 2 * hidden - early
    for q in range(n):
        block, rest = wide(both[q]), wide(last[q])
        gate_out[:, q * hidden : (q + 1) * hidden] = block[:, :hidden]
        up_out[:, q * hidden : (q + 1) * hidden] = jnp.concatenate([block[:, hidden:], rest[:, :tail]], 1)
        wq_out[:, q * QW : (q + 1) * QW] = rest[:, tail : tail + QW]
        wk_out[:, q * HEAD_SIZE : (q + 1) * HEAD_SIZE] = rest[:, tail + QW : tail + QW + HEAD_SIZE]
        wv_out[:, q * HEAD_SIZE : (q + 1) * HEAD_SIZE] = rest[:, tail + QW + HEAD_SIZE :]
    down_out[...] = wide(down[...])
    wo_out[...] = wide(wo[...])

    @pl.when(pl.program_id(0) == 0)
    def _():
        layer_out[...] = layer[...].astype(BF16)
        tokens_out[...] = tokens[...].astype(BF16)
        total = wide(gains[0])
        for i in range(1, n):
            total = total + wide(gains[i])
        for i, gain_out in enumerate(gain_outs):
            gain_out[...] = total[i, : gain_out.shape[0]]


def place(hidden, both, last, down, wo, layer, tokens, gains):
    n, depth, early = both.shape
    width = down.shape[-1]
    down, wo = down.reshape(-1, width), wo.reshape(-1, width)
    step = 64
    count = depth // step
    many = lambda a: pl.BlockSpec((n, step, a.shape[-1]), lambda i: (0, i, 0))
    cut = lambda a: pl.BlockSpec((a.shape[0] // count, width), lambda i: (i, 0))
    out = lambda w: pl.BlockSpec((step, w), lambda i: (i, 0))
    whole = lambda dims: pl.BlockSpec(dims, lambda i: (0,) * len(dims))
    shape = lambda r, w: jax.ShapeDtypeStruct((r, w), F32)
    wq, wk = QW * n, HEAD_SIZE * n
    sizes = [depth, depth, HEAD_SIZE * depth // width, HEAD_SIZE * depth // width]
    return pl.pallas_call(
        functools.partial(place_kernel, n, hidden),
        grid=(count,),
        out_shape=(
            shape(depth, n * hidden), shape(depth, n * hidden), shape(depth, wq), shape(depth, wk), shape(depth, wk),
            shape(down.shape[0], width), shape(wo.shape[0], width), jax.ShapeDtypeStruct(layer.shape, BF16),
            jax.ShapeDtypeStruct(tokens.shape, BF16), *[jax.ShapeDtypeStruct((size,), F32) for size in sizes],
        ),
        in_specs=[many(both), many(last), cut(down), cut(wo), whole(layer.shape), whole(tokens.shape),
                  whole(gains.shape)],
        out_specs=[out(n * hidden), out(n * hidden), out(wq), out(wk), out(wk), cut(down), cut(wo),
                   whole(layer.shape), whole(tokens.shape), *[whole((size,)) for size in sizes]],
        compiler_params=pltpu.CompilerParams(vmem_limit_bytes=VMEM_LIMIT),
        name="place",
    )(both, last, down, wo, layer, tokens, gains)


def norm_back(upstream, unit_rows, factor, gain_row):
    lifted = upstream * gain_row
    return factor * (lifted - unit_rows * jnp.mean(lifted * unit_rows, -1, keepdims=True))


def on_device(
    tokens, lengths, wq, wk, wv, wo, w_gate, w_up, w_down, attn_gain, ffn_gain, q_gain, key_norm_gain, cotangent
):
    F = lax.axis_size("fsdp")
    B = KEY_VALUE_HEADS // F
    T = lax.axis_size("ctx") // B
    dims = (B, F, T)
    own_rows, width = tokens.shape
    rows = own_rows * KEY_VALUE_HEADS
    depth = width // F
    t = lax.axis_index("ctx") // B
    hidden = w_down.shape[0] // B

    lanes = max(depth, LANES)
    line = lambda a: jnp.pad(a, (0, lanes - a.shape[0]))
    gains = jnp.concatenate([line(attn_gain), line(ffn_gain), line(q_gain), line(key_norm_gain)])
    gains = jnp.pad(gains.reshape(4, lanes), ((0, 12), (0, 0)))
    half = HEAD_SIZE // 2
    freq = np.power(np.float32(ROPE_BASE), -(np.arange(LANES, dtype=np.float32) % half * np.float32(2.0) / HEAD_SIZE))
    freq = jnp.asarray(np.broadcast_to(freq, (8, LANES))[:1], F32)
    (cosine, sine, spans, tok_full, wqkv, normed, heads, qx, kv_all, acc, mixed, wo_full, wide_w, all_gains) = front(
        dims, tokens, wq, wk, wv, wo, w_gate, w_up, gains, freq, lengths
    )
    grad_hidden, g_down, g_wide, g_last, own_resid, layer_out = feed(
        dims, tok_full, mixed, wo_full.reshape(-1, width), wide_w.reshape(width, 2 * hidden), w_down,
        cotangent, all_gains,
    )
    out_down, out_wide, out_wo, out_last, out_gains, tokens_grad = backward(
        dims, grad_hidden, g_down, g_wide, g_last, own_resid, tokens, cotangent, all_gains, acc, qx, kv_all,
        spans, heads, cosine, sine, wo, wqkv, normed,
    )
    (gate_grad, up_grad, wq_grad, wk_grad, wv_grad, down_grad, wo_grad, layer_out, tokens_grad, *gain_grads) = place(
        hidden, out_wide, out_last, out_down, out_wo, layer_out, tokens_grad, out_gains
    )
    return (
        layer_out, tokens_grad, wq_grad, wk_grad, wv_grad, wo_grad, gate_grad, up_grad,
        down_grad, *gain_grads,
    )


def solution(mesh):
    rows = P(("ctx", "fsdp"), None)
    shard = P("fsdp", None)
    gain = P("fsdp")
    return jax.shard_map(
        on_device,
        mesh=mesh,
        in_specs=(rows, P(), shard, shard, shard, shard, shard, shard, shard, gain, gain, gain, gain, rows),
        out_specs=(rows, rows, shard, shard, shard, shard, shard, shard, shard, gain, gain, gain, gain),
        check_vma=False,
    )
```

```python
import functools

import jax
import jax.numpy as jnp
import numpy as np
from jax import lax
from jax.experimental import pallas as pl
from jax.experimental.pallas import tpu as pltpu
from jax.sharding import PartitionSpec as P

QUERY_HEADS = 24
KEY_VALUE_HEADS = 8
HEAD_SIZE = 64
GROUP = QUERY_HEADS // KEY_VALUE_HEADS
QW = GROUP * HEAD_SIZE
LANES = 128
NDOCS = 4

EPSILON = 1e-05
ROPE_BASE = 1000000.0
APART = 16384.0

MESH = pl.DeviceIdType.MESH
F32 = jnp.float32
BF16 = jnp.bfloat16
ANY = pl.BlockSpec(memory_space=pl.ANY)
VMEM = pl.BlockSpec(memory_space=pltpu.VMEM)
VMEM_LIMIT = 56 * 1024 * 1024


class Team:
    def __init__(self, B, F, T):
        self.B, self.F, self.T = B, F, T
        ctx, self.f = lax.axis_index("ctx"), lax.axis_index("fsdp")
        self.t, self.y = lax.div(ctx, B), lax.rem(ctx, B)
        self.p = self.y * F + self.f

    def member(self, p):
        return (self.t * self.B + lax.div(p, self.F), lax.rem(p, self.F))

    def same_row(self, f):
        return (self.t * self.B + self.y, f)

    def other_team(self, t):
        return (t * self.B + self.y, self.f)


def flip(p, bit):
    return p + bit * (1 - 2 * lax.rem(lax.div(p, bit), 2))


def bit_of(p, bit):
    return lax.rem(lax.div(p, bit), 2)


class Sems:
    def __init__(self, send, recv):
        self.send, self.recv, self.used = send, recv, 0

    def copy(self, src, dst, device):
        i = self.used
        self.used += 1
        return pltpu.make_async_remote_copy(
            src_ref=src,
            dst_ref=dst,
            send_sem=self.send.at[i],
            recv_sem=self.recv.at[i],
            device_id=device,
            device_id_type=MESH,
        )


def greet(devices):
    barrier = pltpu.get_barrier_semaphore()
    for device in devices:
        pl.semaphore_signal(barrier, inc=1, device_id=device, device_id_type=MESH)
    pl.semaphore_wait(barrier, len(devices))


def team_peers(team):
    n = team.B * team.F
    return [team.member(lax.rem(team.p + d, n)) for d in range(1, n)]


def line_peers(team):
    return [team.other_team(lax.rem(team.t + d, team.T)) for d in range(1, team.T)]


def row_peers(team):
    return [team.same_row(lax.rem(team.f + d, team.F)) for d in range(1, team.F)]


class Gather:
    def __init__(self, sems, me, count, device, own, block, half, order="both"):
        bits = count.bit_length() - 1
        one, two = flip(me, 1), flip(me, 2)
        send = lambda src, dst, to: sems.copy(src, dst, device(to))
        again = lambda ref, to: send(ref, ref, to)
        self.first = [send(own, block(me), flip(me, 1 << k)) for k in range(bits)]
        self.over = [again(block(two), one)]
        self.halves, self.corner = [], []
        if count == 8:
            four = flip(me, 4)
            far = flip(two, 4)
            self.over.append(again(block(four), one))
            if order == "both":
                self.halves = [again(half(two, 0), four), again(half(four, 1), two)]
                self.corner = [again(half(far, 0), one), again(half(far, 1), one)]
            else:
                self.halves = [again(block(two), four)]
                self.corner = [again(block(far), one)]

    def begin(self):
        for copy in self.first:
            copy.start()

    def relay(self):
        self.first[1].wait_recv()
        self.over[0].start()
        if self.halves:
            self.halves[0].start()
            self.first[2].wait_recv()
            for copy in self.halves[1:]:
                copy.start()
            self.over[1].start()

    def end(self):
        for arrived, onward in zip(self.halves, self.corner):
            arrived.wait_recv()
            onward.start()
        self.first[0].wait_recv()
        for copy in self.over + self.corner:
            copy.wait_recv()
        for copy in self.first + self.over + self.halves + self.corner:
            copy.wait_send()

    COPIES = 9


def scatter_parts(width, order):
    if order == "both":
        return [(0, width // 2, 2, 4), (width // 2, width // 2, 4, 2)]
    return [(0, width, 2, 4)]


def scatter_shapes(rows, width, order):
    shapes = [pltpu.VMEM((2, 2, rows, width), BF16)]
    for _, columns, _, _ in scatter_parts(width, order):
        shapes += [pltpu.VMEM((2, rows, columns), BF16)] * 2 + [pltpu.VMEM((rows, columns), BF16)] * 2
    return shapes


def wide(v):
    return v.astype(F32)


class Scatter:
    COPIES = 5

    def __init__(self, sems, team, x, scratch, order):
        self.x, self.r0 = x, scratch[0]
        p = team.p
        self.b = bit_of(p, 1), bit_of(p, 2), bit_of(p, 4)
        send = lambda src, dst, bit: sems.copy(src, dst, team.member(flip(p, bit)))
        self.first = send(x.at[:, :, 1 - self.b[0]], self.r0, 1)
        self.parts = []
        for i, (at, columns, one, two) in enumerate(scatter_parts(x.shape[-1], order)):
            s1, r1, s2, r2 = scratch[1 + 4 * i : 5 + 4 * i]
            self.parts.append((pl.ds(at, columns), one, s1, r1, s2, r2, send(s1, r1, one), send(s2, r2, two)))

    def term(self, b2, b1, columns):
        return wide(self.x[b2, b1, self.b[0], :, columns]) + wide(self.r0[b2, b1, :, columns])

    def begin(self):
        self.first.start()

    def relay(self):
        b0, b1, b2 = self.b
        self.first.wait_recv()
        for columns, one, s1, r1, s2, r2, send1, send2 in self.parts:
            for k in range(2):
                s1[k] = (self.term(k, 1 - b1, columns) if one == 2 else self.term(1 - b2, k, columns)).astype(BF16)
            send1.start()

    def relay_again(self):
        b0, b1, b2 = self.b
        for columns, one, s1, r1, s2, r2, send1, send2 in self.parts:
            send1.wait_recv()
            if one == 2:
                total = self.term(1 - b2, b1, columns) + wide(r1[1 - b2])
            else:
                total = self.term(b2, 1 - b1, columns) + wide(r1[1 - b1])
            s2[...] = total.astype(BF16)
            send2.start()

    def end(self, store):
        b0, b1, b2 = self.b
        for columns, one, s1, r1, s2, r2, send1, send2 in self.parts:
            send2.wait_recv()
            store(columns, self.term(b2, b1, columns) + wide(r1[b2 if one == 2 else b1]) + wide(r2[...]))
        for copy in [self.first] + [copy for part in self.parts for copy in part[6:]]:
            copy.wait_send()


def kernel_params(collective_id):
    return pltpu.CompilerParams(
        collective_id=collective_id, has_side_effects=True, vmem_limit_bytes=VMEM_LIMIT
    )


def unit_and_factor(x):
    factor = lax.rsqrt(jnp.mean(x * x, -1, keepdims=True) + EPSILON)
    return x * factor, factor


def lane_ids(rows):
    return lax.broadcasted_iota(jnp.int32, (rows, LANES), 1)


def inside_document(spans, rows, first_row):
    row = lax.broadcasted_iota(jnp.int32, (rows, LANES), 0) + first_row
    return (row >= spans[0:1, :]) & (row < spans[1:2, :])


def widen_keys(kv, spans, first_row, kx, vx):
    rows = kv.shape[0]
    lane = lane_ids(rows)
    inside = inside_document(spans, rows, first_row)
    both = wide(kv)
    kx[...] = jnp.where(lane < HEAD_SIZE, both, jnp.where(inside, 1.0, 0.0)).astype(BF16)
    vx[...] = jnp.where(lane < HEAD_SIZE, pltpu.roll(both, HEAD_SIZE, 1), 1.0).astype(BF16)


def dot_last(a, b):
    return lax.dot_general(a, b, (((1,), (1,)), ((), ())), preferred_element_type=F32)


def fill_tables(t, lengths, freq, cosine, sine, spans):
    rows = cosine.shape[0]
    ends, total = [], 0
    for d in range(NDOCS):
        total = total + lengths[d]
        ends.append(total)
    lane = lax.broadcasted_iota(jnp.int32, spans.shape, 1)
    row = lax.broadcasted_iota(jnp.int32, spans.shape, 0)
    first, past = jnp.zeros(spans.shape, jnp.int32), jnp.full(spans.shape, 2**30, jnp.int32)
    for d in range(NDOCS):
        first = jnp.where(lane == HEAD_SIZE + d, ends[d] - lengths[d], first)
        past = jnp.where(lane == HEAD_SIZE + d, ends[d], past)
    spans[...] = jnp.where(row == 0, first, past)
    half = HEAD_SIZE // 2
    parts = LANES // half
    few = rows // parts
    shape = (few, LANES)
    token = lax.broadcasted_iota(jnp.int32, shape, 0) + lax.div(lax.broadcasted_iota(jnp.int32, shape, 1), half) * few
    token = token + t * rows
    start = jnp.zeros(shape, jnp.int32)
    for d in range(NDOCS):
        start = jnp.where(token >= ends[d], ends[d], start)
    angles = (token - start).astype(F32) * freq[...]
    cos, sin = jnp.cos(angles), jnp.sin(angles)
    for i in range(parts):
        here, lanes = slice(i * few, (i + 1) * few), slice(i * half, (i + 1) * half)
        cosine[here, :] = jnp.concatenate([cos[:, lanes]] * parts, 1)
        sine[here, :] = jnp.concatenate([-sin[:, lanes], sin[:, lanes]] * (parts // 2), 1)


def front_kernel(dims, tokens, wq, wk, wv, wo, w_gate, w_up, gains, freq, lengths,
                 cosine, sine, spans, tok_full, wqkv, normed, heads, qx, kv_all, acc, mixed, wo_full, wide_full, all_gains,
                 tok, q_in, k_in, v_in, qkv_cut, qkv, gains_in, slab_g, slab_u, cut, norm, kv, kx, vx, packed,
                 send, recv, line_send, line_recv, local):
    team = Team(*dims)
    B, F, T = dims
    t, y, f, p = team.t, team.y, team.f, team.p
    sems = Sems(send, recv)
    own_rows, width = tokens.shape
    rows = own_rows * B * F
    depth = width // F
    part, block = rows // 2, rows // 4
    hidden = cut.shape[-1] // 2
    parity = lax.rem(t, 2)

    def home(src, dst, i):
        copy = pltpu.make_async_copy(src, dst, local.at[i])
        copy.start()
        return copy

    token_rows = lambda i: pl.ds(pl.multiple_of(i * own_rows, 16), own_rows)
    shard_rows = lambda i: pl.ds(pl.multiple_of(i * depth, 16), depth)
    token_load = home(tokens, tok.at[token_rows(p)], 0)
    small_loads = [home(wq, q_in, 1), home(wk, k_in, 2), home(wv, v_in, 3)]
    gain_load = home(gains, gains_in.at[f], 4)
    slab_loads = [home(w_gate, slab_g, 5), home(w_up, slab_u, 6)]
    homes = [home(wo, wo_full.at[f], 7)]
    greet(team_peers(team) + line_peers(team))

    half = own_rows // 2
    gather_tok = Gather(
        sems, p, B * F, team.member, tokens, lambda i: tok.at[token_rows(i)],
        lambda i, k: tok.at[pl.ds(pl.multiple_of(i * own_rows + k * half, 16), half)],
        "tall",
    )
    few = packed.shape[1] // 2

    def gather_half(which):
        return Gather(
            sems, p, B * F, team.member, packed.at[which], lambda i: mixed.at[which, i],
            lambda i, k: mixed.at[which, i, pl.ds(k * few, few)],
            "both" if which else "tall",
        )

    gather_mixed = [gather_half(0), gather_half(1)]
    partners = []
    for m in range(1, F):
        to = f
        for bit in (1, 2, 4):
            if m & bit:
                to = flip(to, bit)
        partners.append(to)
    gain_sends = [sems.copy(gains, gains_in.at[f], team.same_row(to)) for to in partners]
    half_depth = depth // 2
    some = pl.ds(pl.multiple_of(parity * half_depth, 16), half_depth)
    near = team.other_team(t + 1 - 2 * parity)
    some_of = lambda i: pl.ds(pl.multiple_of(i * depth + parity * half_depth, 16), half_depth)
    qkv_sends = [sems.copy(qkv_cut.at[partners[0]], qkv.at[shard_rows(f)], team.same_row(partners[0]))]
    qkv_shares = []
    for to in partners[1:]:
        qkv_sends.append(sems.copy(qkv_cut.at[to, some], qkv.at[some_of(f)], team.same_row(to)))
        qkv_shares.append(sems.copy(qkv.at[some_of(to)], qkv.at[some_of(to)], near))
    wide_near = sems.copy(cut.at[partners[0]], wide_full.at[f], team.same_row(partners[0]))
    wide_sends, wide_shares = [[], []], [[], []]
    quarter = half_depth // 2
    for i in range(2):
        some = pl.ds(pl.multiple_of(parity * half_depth + i * quarter, 16), quarter)
        for to in partners[1:]:
            wide_sends[i].append(sems.copy(cut.at[to, some], wide_full.at[f, some], team.same_row(to)))
            wide_shares[i].append(sems.copy(wide_full.at[to, some], wide_full.at[to, some], near))
    if B == 2 and F == 4:
        one, two = flip(f, 1), flip(f, 2)
        other = team.member(lax.rem(p + F, B * F))
        wo_half = lambda k: pl.ds(pl.multiple_of(k * half_depth, 16), half_depth)
        mine, theirs = wo_half(y), wo_half(1 - y)
        wo_first = [
            sems.copy(wo, wo_full.at[f], team.same_row(one)),
            sems.copy(wo.at[mine], wo_full.at[f, mine], team.same_row(two)),
        ]
        ref = wo_full.at[two, mine]
        wo_relay = [sems.copy(ref, ref, other), sems.copy(ref, ref, team.same_row(one))]
        ref = wo_full.at[two, theirs]
        wo_last = [sems.copy(ref, ref, team.same_row(one))]

    def line_copy(d, source, to, r):
        here = pl.ds(pl.multiple_of(r * block, block), block)
        return pltpu.make_async_remote_copy(
            src_ref=kv.at[here], dst_ref=kv_all.at[source, here], send_sem=line_send.at[d, r],
            recv_sem=line_recv.at[source, r], device_id=team.other_team(to), device_id_type=MESH,
        )

    gather_tok.begin()
    for copy in gain_sends:
        copy.start()
    fill_tables(t, lengths, freq, cosine, sine, spans)
    for load in small_loads:
        load.wait()
    for i in range(F):
        for row in range(B):
            h = i * B + row

            @pl.when(y == row)
            def _():
                qkv_cut[i, :, 0:QW] = q_in[:, h * QW : (h + 1) * QW]
                qkv_cut[i, :, QW : QW + HEAD_SIZE] = k_in[:, h * HEAD_SIZE : (h + 1) * HEAD_SIZE]
                qkv_cut[i, :, QW + HEAD_SIZE : QW + 2 * HEAD_SIZE] = v_in[:, h * HEAD_SIZE : (h + 1) * HEAD_SIZE]

    for copy in qkv_sends:
        copy.start()
    qkv[shard_rows(f), :] = qkv_cut[f]
    for load in slab_loads:
        load.wait()

    @pl.loop(0, depth // 32)
    def _(r):
        here = pl.ds(pl.multiple_of(r * 32, 32), 32)
        for j in range(F):
            for row in range(B):
                q = j * B + row

                @pl.when(y == row)
                def _():
                    cut[j, here, 0:hidden] = slab_g[here, q * hidden : (q + 1) * hidden]
                    cut[j, here, hidden : 2 * hidden] = slab_u[here, q * hidden : (q + 1) * hidden]

    gather_tok.relay()
    for arrived, onward in zip(qkv_sends[1:], qkv_shares):
        arrived.wait_recv()
        onward.start()
    for copy in wide_sends[0] + [wide_near]:
        copy.start()
    if B == 2 and F == 4:
        for copy in wo_first:
            copy.start()
    else:
        gather_wo = Gather(
            sems, f, F, team.same_row, wo, lambda i: wo_full.at[i],
            lambda i, k: wo_full.at[i, pl.ds(k * half_depth, half_depth)],
        )
        gather_wo.begin()
    for copy in wide_sends[1]:
        copy.start()
    homes.append(home(cut.at[f], wide_full.at[f], 9))
    gather_tok.end()
    token_load.wait()
    gain_load.wait()
    for copy in gain_sends:
        copy.wait_recv()
    homes.append(home(tok, tok_full, 11))

    all_gains[...] = jnp.zeros_like(all_gains)
    for i in range(F):
        for k, count in ((0, depth), (1, depth), (2, HEAD_SIZE // F), (3, HEAD_SIZE // F)):
            all_gains[k : k + 1, i * count : (i + 1) * count] = wide(gains_in[i])[k : k + 1, 0:count]
    gain_q, gain_k = all_gains[2:3, 0:HEAD_SIZE], all_gains[3:4, 0:HEAD_SIZE]

    @pl.loop(0, rows // block)
    def _(r):
        here = pl.ds(pl.multiple_of(r * block, block), block)
        unit, factor = unit_and_factor(wide(tok[here, :]))
        norm[here, :] = (unit * all_gains[0:1, :]).astype(BF16)

    for copy in qkv_sends[:1] + qkv_shares:
        copy.wait_recv()
    homes += [home(norm, normed, 12), home(qkv, wqkv, 13)]

    lane = lane_ids(block)
    same_head = lax.div(lax.broadcasted_iota(jnp.int32, (LANES, LANES), 0), HEAD_SIZE) == lax.div(
        lax.broadcasted_iota(jnp.int32, (LANES, LANES), 1), HEAD_SIZE
    )
    same_head = jnp.where(same_head, 1.0, 0.0).astype(BF16)
    gain_pairs = [jnp.concatenate([gain_q, gain_q], 1), jnp.concatenate([gain_q, gain_k], 1)]

    @pl.loop(0, rows // block)
    def _(r):
        here = pl.ds(pl.multiple_of(r * block, block), block)
        projected = jnp.dot(norm[here, :], qkv[...], preferred_element_type=F32)
        apart = jnp.where(inside_document(spans, block, t * rows + r * block), 0.0, -APART)
        cos, sin = cosine[here, :], sine[here, :]
        turned = []
        for i in range(2):
            x = projected[:, i * LANES : (i + 1) * LANES]
            heads[i, here, :] = x
            square = x * x
            high = square.astype(BF16)
            rest = (square - wide(high)).astype(BF16)
            total = jnp.dot(high, same_head, preferred_element_type=F32) + jnp.dot(
                rest, same_head, preferred_element_type=F32
            )
            u = x * lax.rsqrt(total * (1.0 / HEAD_SIZE) + EPSILON) * gain_pairs[i]
            first = lax.rem(lane, HEAD_SIZE) < HEAD_SIZE // 2
            swapped = jnp.where(first, pltpu.roll(u, LANES - HEAD_SIZE // 2, 1), pltpu.roll(u, HEAD_SIZE // 2, 1))
            turned.append(wide((u * cos + swapped * sin).astype(BF16)))
        for h in range(GROUP):
            q = turned[h // 2] * HEAD_SIZE ** (-0.5)
            q = pltpu.roll(q, HEAD_SIZE, 1) if h % 2 else q
            qx[h, here, :] = jnp.where(lane < HEAD_SIZE, q, apart).astype(BF16)
        values = projected[:, (GROUP + 1) * HEAD_SIZE : (GROUP + 2) * HEAD_SIZE]
        keys = pltpu.roll(turned[1], HEAD_SIZE, 1)
        kv[here, :] = jnp.where(lane < HEAD_SIZE, keys, jnp.concatenate([values, values], 1)).astype(BF16)
        for d in range(1, T):

            @pl.when(t + d < T)
            def _():
                line_copy(d, t, t + d, r).start()

    kv_all[t] = kv[...]
    widen_keys(kv[...], spans, t * rows, kx.at[t], vx.at[t])
    causal = lax.broadcasted_iota(jnp.int32, (part, part), 1) <= lax.broadcasted_iota(jnp.int32, (part, part), 0)

    def piece(q, source, k, masked):
        scores = dot_last(q, kx[source, k * part : (k + 1) * part, :])
        weights = jnp.exp(scores)
        if masked:
            weights = jnp.where(causal, weights, 0.0)
        return jnp.dot(weights.astype(BF16), vx[source, k * part : (k + 1) * part, :], preferred_element_type=F32)

    def pass_weights(i):
        for arrived, onward in zip(wide_sends[i], wide_shares[i]):
            arrived.wait_recv()
            onward.start()

    def pass_wo():
        if B == 2 and F == 4:
            wo_first[1].wait_recv()
            for copy in wo_relay:
                copy.start()
        else:
            gather_wo.relay()

    for which in range(2):
        mine = slice(which * part, (which + 1) * part)

        @pl.loop(0, GROUP)
        def _(h):
            q = qx[h, mine, :]
            total = piece(q, t, which, True)
            acc[h, mine, :] = total + piece(q, t, 0, False) if which else total

        pass_weights(which)
        if which:
            gather_mixed[0].relay()

        @pl.loop(1, t + 1)
        def _(j):
            source = t - j
            if which == 0:
                for r in range(4):
                    line_copy(0, source, t, r).wait_recv()
                widen_keys(kv_all[source], spans, source * rows, kx.at[source], vx.at[source])

            @pl.loop(0, GROUP)
            def _(h):
                q = qx[h, mine, :]
                acc[h, mine, :] = acc[h, mine, :] + piece(q, source, 0, False) + piece(q, source, 1, False)

        for h in range(GROUP):
            out = acc[h, mine, 0:HEAD_SIZE] / acc[h, mine, HEAD_SIZE : 2 * HEAD_SIZE]
            out = out.astype(BF16)
            if h < 2:
                packed[which, 0:part, h * HEAD_SIZE : (h + 1) * HEAD_SIZE] = out
            else:
                packed[which, part : part + part // 2, 0:HEAD_SIZE] = out[0 : part // 2]
                packed[which, part : part + part // 2, HEAD_SIZE : 2 * HEAD_SIZE] = out[part // 2 : part]
        homes.append(home(packed.at[which], mixed.at[which, p], 14 + which))
        gather_mixed[which].begin()
        if which == 0:
            pass_wo()

    gather_mixed[0].end()
    gather_mixed[1].relay()
    if B == 2 and F == 4:
        wo_relay[0].wait_recv()
        wo_last[0].start()
    gather_mixed[1].end()
    if B == 2 and F == 4:
        for copy in (wo_first[0], wo_relay[1], wo_last[0]):
            copy.wait_recv()
        for copy in wo_first + wo_relay + wo_last:
            copy.wait_send()
    else:
        gather_wo.end()
    for copy in [wide_near] + wide_shares[0] + wide_shares[1]:
        copy.wait_recv()
    for copy in [wide_near] + wide_sends[0] + wide_sends[1] + wide_shares[0] + wide_shares[1]:
        copy.wait_send()
    for copy in gain_sends + qkv_sends + qkv_shares:
        copy.wait_send()
    for copy in homes:
        copy.wait()
    for d in range(1, T):

        @pl.when(t + d < T)
        def _():
            for r in range(4):
                line_copy(d, t, t + d, r).wait_send()


def front(dims, tokens, wq, wk, wv, wo, w_gate, w_up, gains, freq, lengths):
    B, F, T = dims
    own_rows, width = tokens.shape
    n = B * F
    rows = own_rows * n
    depth, ff = w_gate.shape
    hidden = ff // n
    few = QW + 2 * HEAD_SIZE
    copies = 4 * Gather.COPIES + (F - 1) + 3 * (2 * F - 3)
    packed = (rows // 2 + rows // 4, LANES)
    shape = lambda *s: jax.ShapeDtypeStruct(s, BF16)
    wide_shape = lambda *s: jax.ShapeDtypeStruct(s, F32)
    vmem = lambda *s: pltpu.VMEM(s, BF16)
    return pl.pallas_call(
        functools.partial(front_kernel, dims),
        out_shape=(
            wide_shape(rows, LANES), wide_shape(rows, LANES), jax.ShapeDtypeStruct((8, LANES), jnp.int32),
            shape(rows, width), shape(width, few), shape(rows, width), wide_shape((GROUP + 1) // 2, rows, LANES),
            shape(GROUP, rows, LANES), shape(T, rows, LANES), wide_shape(GROUP, rows, LANES), shape(2, n, *packed),
            shape(F, depth, width), shape(F, depth, 2 * hidden),
            wide_shape(8, width),
        ),
        in_specs=[ANY] * 8 + [VMEM, pl.BlockSpec(memory_space=pltpu.SMEM)],
        out_specs=[VMEM] * 3 + [ANY] * 3 + [VMEM] * 4 + [ANY] * 3 + [VMEM],
        scratch_shapes=[
            vmem(rows, width), vmem(*wq.shape), vmem(*wk.shape), vmem(*wv.shape), vmem(F, depth, few), vmem(width, few),
            vmem(F, *gains.shape), vmem(depth, ff), vmem(depth, ff), vmem(F, depth, 2 * hidden),
            vmem(rows, width), vmem(rows, LANES), vmem(T, rows, LANES), vmem(T, rows, LANES), vmem(2, *packed),
            pltpu.SemaphoreType.DMA((copies,)),
            pltpu.SemaphoreType.DMA((copies,)),
            pltpu.SemaphoreType.DMA((T, 4)),
            pltpu.SemaphoreType.DMA((T, 4)),
            pltpu.SemaphoreType.DMA((16,)),
        ],
        compiler_params=kernel_params(1),
        name="front",
    )(tokens, wq, wk, wv, wo, w_gate, w_up, gains, freq, lengths)


def feed_kernel(dims, tok_in, mixed_in, wo_in, wide_in, down_in, dy_in, gain, grad_hidden, g_down,
                g_wide, g_last, own_resid, layer_out, tok, mixed, wo, w_wide, w_down, dy, rows_in, hid, both, act, dwide,
                resid, down, gd, gw, gl, *rest):
    scratch, (send, recv, local) = rest[:9], rest[9:]
    team = Team(*dims)
    B, F, y, p = team.B, team.F, team.y, team.p
    rows, width = tok.shape
    own_rows = own_resid.shape[0]
    hidden = w_down.shape[0]
    early = gw.shape[1]
    block = resid.shape[0]
    n = B * F
    dy_rows = lambda i: pl.ds(pl.multiple_of(i * own_rows, 16), own_rows)
    loads = [
        pltpu.make_async_copy(src, dst, local.at[i])
        for i, (src, dst) in enumerate(
            [(mixed_in, mixed), (wo_in, wo), (tok_in, tok), (wide_in, w_wide),
             (down_in.at[pl.ds(pl.multiple_of(y * hidden, 16), hidden)], w_down), (dy_in, dy.at[dy_rows(p)])]
        )
    ]
    for load in loads:
        load.start()
    greet([team.member(flip(p, bit)) for bit in (1, 2, 4)])
    sems = Sems(send, recv)
    scatter = Scatter(sems, team, down, scratch, "both")
    half = own_rows // 2
    gather = Gather(
        sems, p, n, team.member, dy_in, lambda i: dy.at[dy_rows(i)],
        lambda i, k: dy.at[pl.ds(pl.multiple_of(i * own_rows + k * half, 16), half)],
    )
    gather.begin()
    for load in loads[:3]:
        load.wait()

    @pl.loop(0, rows // block)
    def _(r):
        here = pl.ds(pl.multiple_of(r * block, block), block)
        which, later = lax.div(r, 2), lax.rem(r, 2)
        place = pl.ds(pl.multiple_of(later * block, block), block)
        for i in range(n):
            h = i % F * B + i // F
            first = h * QW
            rows_in[:, first : first + 2 * HEAD_SIZE] = mixed[which, i, place, :]
            last = mixed[which, i, 2 * block : 3 * block, :]
            last = jnp.where(later == 0, wide(last[:, :HEAD_SIZE]), wide(last[:, HEAD_SIZE:]))
            rows_in[:, first + 2 * HEAD_SIZE : first + QW] = last.astype(BF16)
        resid[...] = wide(tok[here, :]) + jnp.dot(rows_in[...], wo[...], preferred_element_type=F32)

        @pl.when(r == lax.div(p * own_rows, block))
        def _():
            own_resid[...] = resid[pl.ds(pl.multiple_of(lax.rem(p * own_rows, block), 8), own_rows), :]

        unit, factor = unit_and_factor(resid[...])
        hid[here, :] = (unit * gain[1:2, :]).astype(BF16)

    for load in loads[3:]:
        load.wait()
    gather.relay()

    @pl.loop(0, rows // block)
    def _(r):
        here = pl.ds(pl.multiple_of(r * block, block), block)
        product = jnp.dot(hid[here, :], w_wide[...], preferred_element_type=F32)
        gate, upper = product[:, :hidden], product[:, hidden:]
        both[0, here, :] = gate
        both[1, here, :] = upper
        sigma = 1.0 / (1.0 + jnp.exp(-gate))
        acts = (gate * sigma * upper).astype(BF16)
        act[here, :] = acts
        out = jnp.dot(acts, w_down[...], preferred_element_type=F32).astype(BF16)
        for i in range(block // own_rows):
            m = r * (block // own_rows) + i
            down[lax.div(m, 4), lax.rem(lax.div(m, 2), 2), lax.rem(m, 2)] = out[i * own_rows : (i + 1) * own_rows]

    scatter.begin()
    gather.end()

    @pl.loop(0, rows // block)
    def _(r):
        here = pl.ds(pl.multiple_of(r * block, block), block)
        pl.when(r == 1)(scatter.relay)
        gate, upper = both[0, here, :], both[1, here, :]
        sigma = 1.0 / (1.0 + jnp.exp(-gate))
        dact = dot_last(dy[here, :], w_down[...])
        dwide[here, 0:hidden] = (dact * upper * sigma * (1.0 + gate * (1.0 - sigma))).astype(BF16)
        dwide[here, hidden : 2 * hidden] = (dact * (gate * sigma)).astype(BF16)
        tok[here, :] = dot_last(dwide[here, :], w_wide[...]).astype(BF16)

    stores = []

    def store(src, dst):
        stores.append(pltpu.make_async_copy(src, dst, local.at[6 + len(stores)]))
        stores[-1].start()

    store(tok, grad_hidden)
    over_rows = lambda a, b: lax.dot_general(a, b, (((0,), (0,)), ((), ())), preferred_element_type=F32).astype(BF16)

    for first in range(0, hidden, 256):
        count = min(256, hidden - first)
        gd[first : first + count, :] = over_rows(act[:, first : first + count], dy[...])
    store(gd, g_down)
    scatter.relay_again()

    @pl.loop(0, width // 256)
    def _(r):
        here = pl.ds(pl.multiple_of(r * 256, 256), 256)
        product = over_rows(hid[:, here], dwide[...])
        gw[here, :] = product[:, :early]
        gl[here, 0 : 2 * hidden - early] = product[:, early:]
        pltpu.make_async_copy(gw.at[here], g_wide.at[here], local.at[10]).start()
        pltpu.make_async_copy(gl.at[here], g_last.at[here], local.at[11]).start()

    def put(columns, total):
        layer_out[:, columns] = own_resid[:, columns] + total

    scatter.end(put)
    for copy in stores:
        copy.wait()
    pltpu.make_async_copy(gw, g_wide, local.at[10]).wait()
    pltpu.make_async_copy(gl, g_last, local.at[11]).wait()


def feed(dims, tok, mixed, wo, w_wide, w_down, dy, gains):
    rows, width = tok.shape
    hidden = w_wide.shape[1] // 2
    own_rows = rows // KEY_VALUE_HEADS
    early = early_lanes(hidden)
    last = 2 * hidden - early + QW + 2 * HEAD_SIZE
    block = rows // 4
    shape = lambda s: jax.ShapeDtypeStruct(s, BF16)
    return pl.pallas_call(
        functools.partial(feed_kernel, dims),
        out_shape=(
            shape((rows, width)), shape((hidden, width)), shape((width, early)), shape((width, last)),
            jax.ShapeDtypeStruct((own_rows, width), F32), jax.ShapeDtypeStruct((own_rows, width), F32),
        ),
        in_specs=[ANY] * 6 + [VMEM],
        out_specs=[ANY] * 4 + [VMEM] * 2,
        scratch_shapes=[
            pltpu.VMEM((rows, width), BF16),
            pltpu.VMEM(mixed.shape, BF16),
            pltpu.VMEM(wo.shape, BF16),
            pltpu.VMEM(w_wide.shape, BF16),
            pltpu.VMEM((hidden, width), BF16),
            pltpu.VMEM((rows, width), BF16),
            pltpu.VMEM((block, width), BF16),
            pltpu.VMEM((rows, width), BF16),
            pltpu.VMEM((2, rows, hidden), F32),
            pltpu.VMEM((rows, hidden), BF16),
            pltpu.VMEM((rows, 2 * hidden), BF16),
            pltpu.VMEM((block, width), F32),
            pltpu.VMEM((2, 2, 2, own_rows, width), BF16),
            pltpu.VMEM((hidden, width), BF16),
            pltpu.VMEM((width, early), BF16),
            pltpu.VMEM((width, last), BF16),
        ]
        + scatter_shapes(own_rows, width, "both")
        + [
            pltpu.SemaphoreType.DMA((Scatter.COPIES + Gather.COPIES,)),
            pltpu.SemaphoreType.DMA((Scatter.COPIES + Gather.COPIES,)),
            pltpu.SemaphoreType.DMA((12,)),
        ],
        compiler_params=pltpu.CompilerParams(
            collective_id=2, has_side_effects=True, vmem_limit_bytes=60 * 1024 * 1024
        ),
        name="feed",
    )(tok, mixed, wo, w_wide, w_down, dy, gains)


HOP = 2
LAG = 3
UNITS = 8
ORDER = "both"


class GradSum:
    RED, LEFT, RIGHT, HAND, OVER, HOME, INTO = range(7)

    def __init__(self, team, kinds, red_recv, fin_recv, hand_recvs, bulk):
        self.team, self.kinds = team, kinds
        self.red_recv, self.fin_recv, self.hand_recvs, self.bulk = red_recv, fin_recv, hand_recvs, bulk
        self.opposite = team.member(lax.rem(team.p + team.F, team.B * team.F))
        self.low, self.high = team.T // 2 - 1, team.T // 2

    @staticmethod
    def steps(kinds, T):
        return max(first + rows // step for rows, step, first in kinds) + HOP * T + LAG

    def remote(self, src, dst, send_sem, recv_sem, device):
        return pltpu.make_async_remote_copy(
            src_ref=src, dst_ref=dst, send_sem=send_sem, recv_sem=recv_sem, device_id=device, device_id_type=MESH
        )

    def where(self, k, c):
        g, step, how = self.kinds[k][0], self.kinds[k][4], self.kinds[k][6]
        if how != "rows":
            return pl.ds(pl.multiple_of(c * step, 16), step), None, None
        F = self.team.F
        turn = lax.rem(c, F)
        to = lax.rem(turn, 2) * (F // 2) + lax.div(turn, 2)
        row = lax.div(c, F) * step
        return pl.ds(pl.multiple_of(to * (g.shape[0] // F) + row, 16), step), to, row

    def spare(self, k, c):
        step = self.kinds[k][4]
        return pl.ds(pl.multiple_of(lax.div(c, 2) * step, 16), step)

    def reduce(self, k, c, i, root):
        g, land, land2 = self.kinds[k][:3]
        team = self.team
        t, T = team.t, team.T
        at, _, _ = self.where(k, c)
        red = self.bulk.at[self.RED, k, 0]

        def inward(side, dst):
            to = team.other_team(t + 1 - 2 * side)
            self.remote(g.at[at], dst, red, self.red_recv.at[side, i], to).start()

        def add():
            g[at, :] = (wide(g[at, :]) + wide(land[at, :])).astype(BF16)

        @pl.when(t < root)
        def _():
            @pl.when(t > 0)
            def _():
                self.remote(g.at[at], land.at[at], red, self.red_recv.at[0, i], team.other_team(t)).wait_recv()
                add()

            inward(0, land.at[at])

        @pl.when(t > root)
        def _():
            @pl.when(t < T - 1)
            def _():
                self.remote(g.at[at], land.at[at], red, self.red_recv.at[1, i], team.other_team(t)).wait_recv()
                add()

            @pl.when(t - 1 == root)
            def _():
                inward(1, land2.at[self.spare(k, c)])

            @pl.when(t - 1 != root)
            def _():
                inward(1, land.at[at])

    def finish(self, k, c, i, root):
        g, land, land2, out, step, first, how = self.kinds[k]
        team, bulk = self.team, self.bulk
        B, F, T, t, y, f = team.B, team.F, team.T, team.t, team.y, team.f
        at, to, row = self.where(k, c)
        red = bulk.at[self.RED, k, 0]

        def outward(side):
            to_team = team.other_team(t - 1 + 2 * side)
            sem = bulk.at[self.RIGHT if side else self.LEFT, k, 0]
            return self.remote(land.at[at], land.at[at], sem, self.fin_recv.at[i], to_team)

        @pl.when(t == root)
        def _():
            total = wide(g[at, :])
            if self.low > 0:
                self.remote(g.at[at], land.at[at], red, self.red_recv.at[0, i], team.other_team(t)).wait_recv()
                total = total + wide(land[at, :])
                self.remote(g.at[at], land2.at[self.spare(k, c)], red, self.red_recv.at[1, i],
                            team.other_team(t)).wait_recv()
                total = total + wide(land2[self.spare(k, c), :])
            land[at, :] = total.astype(BF16)

        @pl.when(t != root)
        def _():
            outward(0).wait_recv()

        @pl.when((t <= root) & (t > 0))
        def _():
            outward(0).start()

        @pl.when((t >= root) & (t < T - 1))
        def _():
            outward(1).start()

        if how == "rows":
            dst = out.at[f * B + y, pl.ds(pl.multiple_of(row, 16), step)]

            @pl.when(to == f)
            def _():
                pltpu.make_async_copy(land.at[at], dst, bulk.at[self.HOME, k, 0]).start()
                if B == 2:
                    self.remote(land.at[at], dst, bulk.at[self.OVER, k, 0], bulk.at[self.INTO, k, 0],
                                self.opposite).start()

            @pl.when(to != f)
            def _():
                self.remote(land.at[at], dst, bulk.at[self.HAND, k, 0], self.hand_recvs[k].at[f, lax.div(row, step)],
                            team.same_row(to)).start()
        elif how == "stay":
            dst = out.at[y, at]
            pltpu.make_async_copy(land.at[at], dst, bulk.at[self.HOME, k, 0]).start()
            if B == 2:
                self.remote(land.at[at], dst, bulk.at[self.OVER, k, 0], bulk.at[self.INTO, k, 0],
                            self.opposite).start()
        else:
            for index in range(F):
                src = land.at[pl.ds(16 * index, 16)]
                for line in range(B):

                    @pl.when(team.p == line * F + index)
                    def _():
                        pltpu.make_async_copy(src, out.at[team.p], bulk.at[self.HOME, k, 0]).start()

                    @pl.when(team.p != line * F + index)
                    def _():
                        self.remote(src, out.at[team.p], bulk.at[self.HAND, k, 0], bulk.at[self.INTO, k, 0],
                                    (t * B + line, index)).start()

    def pass_over(self, k, c, i, root):
        g, land, land2, out, step, first, how = self.kinds[k]
        if how != "rows":
            return
        team = self.team
        at, to, row = self.where(k, c)

        @pl.when(to == team.f)
        def _():
            for d in range(1, team.F):
                source = lax.rem(team.f + d, team.F)
                ref = out.at[source * team.B + team.y, pl.ds(pl.multiple_of(row, 16), step)]
                self.remote(land.at[at], ref, self.bulk.at[self.HAND, k, 0],
                            self.hand_recvs[k].at[source, lax.div(row, step)], team.same_row(team.f)).wait_recv()
                if team.B == 2:
                    self.remote(ref, ref, self.bulk.at[self.OVER, k, 1], self.bulk.at[self.INTO, k, 0],
                                self.opposite).start()

    def each(self, i, body):
        root = self.low + lax.rem(lax.max(i, 0), 2)
        for k, (g, land, land2, out, step, first, how) in enumerate(self.kinds):
            count = g.shape[0] // step
            pl.when((i >= first) & (i < first + count))(functools.partial(body, k, i - first, i, root))

    def step(self, s):
        T, t = self.team.T, self.team.t
        self.each(s - HOP * lax.min(t, T - 1 - t), self.reduce)
        for parity in range(2):
            root = self.low + parity
            distance = jnp.where(t < root, root - t, t - root)
            i = s - HOP * (T // 2 + distance)
            for wait, body in ((0, self.finish), (LAG, self.pass_over)):
                j = i - wait
                pl.when((j >= 0) & (lax.rem(lax.max(j, 0), 2) == parity))(functools.partial(self.each, j, body))

    def drain(self, ref, sem):
        pltpu.make_async_copy(ref, ref, sem).wait()

    def end(self):
        bulk, B, F, T, t = self.bulk, self.team.B, self.team.F, self.team.T, self.team.t
        low, high = self.low, self.high
        for k, (g, land, land2, out, step, first, how) in enumerate(self.kinds):
            rows = g.shape[0]
            some = lambda n: g.at[pl.ds(0, n)]
            count = rows // step
            even = (count + 1 - first % 2) // 2 * step
            odd = rows - even

            def drain_some(condition, n, which):
                if n:

                    @pl.when(condition)
                    def _():
                        self.drain(some(n), bulk.at[which, k, 0])

            drain_some((t != low) & (t != high), rows, self.RED)
            drain_some(t == low, odd, self.RED)
            drain_some(t == high, even, self.RED)
            drain_some((t > 0) & (t <= low), rows, self.LEFT)
            drain_some(t == high, odd, self.LEFT)
            drain_some((t < T - 1) & (t >= high), rows, self.RIGHT)
            drain_some(t == low, even, self.RIGHT)
            if how == "rows":
                shard = rows // F
                self.drain(some(rows - shard), bulk.at[self.HAND, k, 0])
                self.drain(some(shard), bulk.at[self.HOME, k, 0])
                if B == 2:
                    self.drain(some(shard), bulk.at[self.OVER, k, 0])
                    self.drain(some(rows - shard), bulk.at[self.OVER, k, 1])
                    self.drain(g, bulk.at[self.INTO, k, 0])
            elif how == "stay":
                self.drain(g, bulk.at[self.HOME, k, 0])
                if B == 2:
                    self.drain(g, bulk.at[self.OVER, k, 0])
                    self.drain(g, bulk.at[self.INTO, k, 0])
            else:
                others = out.at[pl.ds(0, B * F - 1)]
                self.drain(out.at[0], bulk.at[self.HOME, k, 0])
                self.drain(others, bulk.at[self.HAND, k, 0])
                self.drain(others, bulk.at[self.INTO, k, 0])


def first_steps(dims):
    at = dict(scatter1=3, scatter2=12, resid=18, relay=24, heads=30, own_wo=30 + UNITS)
    at["attention"] = at["own_wo"] + 1
    at["keys"] = at["attention"] + 2 * GROUP * dims[2] + 1
    at["turn"] = at["keys"] + 1
    at["normed"] = at["turn"] + UNITS
    at["products"] = at["normed"] + 2
    at["again1"] = at["products"] + 3
    at["again2"] = at["again1"] + 6
    at["tokens"] = at["again2"] + 6
    return at


def early_lanes(hidden):
    return 2 * hidden // LANES * LANES


def grad_kinds(dims, depth, hidden):
    at = first_steps(dims)
    early = early_lanes(hidden)
    kinds, place = [], 0
    for rows, width, step, ready, how in (
        (hidden, depth, 32, 0, "stay"),
        (depth, early, 32, 0, "rows"),
        (QW, depth, 48, at["own_wo"] + 1, "stay"),
        (depth, 2 * hidden - early + QW + 2 * HEAD_SIZE, 192, at["products"] + 3, "rows"),
        (16 * dims[1], max(depth // dims[1], LANES), 16 * dims[1], at["tokens"] + 1, "gain"),
    ):
        place = max(place, ready)
        kinds.append((rows, width, step, place, how))
        place += rows // step
    return kinds


def back_kernel(dims, kinds, steps, grad_hidden, g_down, g_wide, g_last, resid, tokens, cotangent, gains, acc_in, qx_in,
                kv_all, spans, heads_in, cosine_in, sine_in, wo, wqkv, normed,
                out_down, out_wide, out_wo, out_last, out_gains, tokens_grad,
                xs, own_down, own_wide, own_gwo, own_last, own_gains,
                land_down, land_wide, land_wo, land_last, land_gains,
                also_down, also_wide, also_wo, also_last, also_gains,
                grad_resid, attn_own, big, dox, mixed, dq, dkv, kv_in, dkv_sum, turned, small, kx, vx, dk, dv, wq_in, own_wo,
                acc, qx, heads, cosine, sine, *rest):
    count = len(scatter_parts(resid.shape[-1], ORDER)) * 4 + 1
    scratch1, rest = rest[:count], rest[count:]
    send, recv, line_send, line_recv, red_recv, fin_recv, hand_wide, hand_last, bulk, local = rest
    team = Team(*dims)
    B, F, T = dims
    t, p = team.t, team.p
    at = first_steps(dims)
    own_rows, width = resid.shape
    rows = qx.shape[1]
    part = rows // 2
    small_block = rows // UNITS
    depth = width // F
    sems = Sems(send, recv)
    loads = [
        pltpu.make_async_copy(src, dst, local.at[i])
        for i, (src, dst) in enumerate(
            [(grad_hidden, xs), (g_down, own_down), (g_wide, own_wide), (g_last, own_last), (wqkv, wq_in),
             (wo.at[pl.ds(pl.multiple_of(team.y * QW, 16), QW)], own_wo), (acc_in, acc), (qx_in, qx),
             (heads_in, heads), (cosine_in, cosine), (sine_in, sine)]
        )
    ]
    for load in loads:
        load.start()
    own_gains[...] = jnp.zeros_like(own_gains)
    greet(team_peers(team) + line_peers(team))
    loads[0].wait()
    scatter = Scatter(sems, team, xs, scratch1, ORDER)
    scatter.begin()
    again = Scatter(sems, team, xs, scratch1, ORDER)
    half = own_rows // 2
    gather = Gather(
        sems, p, B * F, team.member, attn_own,
        lambda i: big.at[pl.ds(pl.multiple_of(i * own_rows, 16), own_rows)],
        lambda i, k: big.at[pl.ds(pl.multiple_of(i * own_rows + k * half, 16), half)],
    )
    sums = GradSum(
        team,
        [
            (own, land, also, out) + kind[2:]
            for own, land, also, out, kind in zip(
                (own_down, own_wide, own_gwo, own_last, own_gains),
                (land_down, land_wide, land_wo, land_last, land_gains),
                (also_down, also_wide, also_wo, also_last, also_gains),
                (out_down, out_wide, out_wo, out_last, out_gains),
                kinds,
            )
        ],
        red_recv, fin_recv, [None, hand_wide, None, hand_last, None], bulk,
    )
    loads[1].wait()
    gain_attn, gain_ffn = gains[0:1, :], gains[1:2, :]
    gain_q, gain_k = gains[2:3, 0:HEAD_SIZE], gains[3:4, 0:HEAD_SIZE]
    home = pltpu.make_async_copy(attn_own, big.at[pl.ds(pl.multiple_of(p * own_rows, 16), own_rows)], local.at[11])
    fetch = pltpu.make_async_copy(normed, big, local.at[12])

    def resid_phase():
        def store(columns, total):
            grad_resid[:, columns] = total

        scatter.end(store)
        term = jnp.zeros((1, width), F32)
        for r in range(0, own_rows, 32):
            here = slice(r, r + 32)
            unit, factor = unit_and_factor(resid[here, :])
            upstream = grad_resid[here, :]
            term = term + jnp.sum(upstream * unit, 0, keepdims=True)
            total = wide(cotangent[here, :]) + norm_back(upstream, unit, factor, gain_ffn)
            grad_resid[here, :] = total
            attn_own[here, :] = total.astype(BF16)
        small[1:2, :] = term
        home.start()
        gather.begin()

    def heads_phase():
        gather.end()
        home.wait()

    def heads_unit(r):
        lane = lane_ids(small_block)
        here = pl.ds(pl.multiple_of(r * small_block, small_block), small_block)
        grad = dot_last(big[here, :], own_wo[...]).astype(BF16)
        for h in range(GROUP):
            sums_h = acc[h, here, :]
            total = pltpu.roll(sums_h, HEAD_SIZE, 1)
            out = sums_h / total
            mixed[here, h * HEAD_SIZE : (h + 1) * HEAD_SIZE] = out[:, :HEAD_SIZE].astype(BF16)
            do = wide(grad[:, h * HEAD_SIZE : (h + 1) * HEAD_SIZE])
            do = jnp.concatenate([do, jnp.zeros_like(do)], 1)
            delta = -jnp.sum(jnp.where(lane < HEAD_SIZE, do * out, 0.0), 1, keepdims=True)

            def put(x, first, value):
                for i in range(3):
                    x = jnp.where(lane == first + i, wide(value.astype(BF16)), x)
                    value = value - wide(value.astype(BF16))
                return x

            dox[h, here, :] = put(do, HEAD_SIZE, delta).astype(BF16)
            log_sum = -jnp.log(jnp.where(lane < HEAD_SIZE, total, sums_h))
            qx[h, here, :] = put(wide(qx[h, here, :]), HEAD_SIZE + NDOCS, log_sum).astype(BF16)

    def own_wo_phase():
        own_gwo[...] = lax.dot_general(
            mixed[...], big[...], (((0,), (0,)), ((), ())), preferred_element_type=F32
        ).astype(BF16)
        dq[...] = jnp.zeros_like(dq)

    causal = lax.broadcasted_iota(jnp.int32, (part, part), 0) <= lax.broadcasted_iota(jnp.int32, (part, part), 1)

    def piece(h, q_rows, k_rows, masked):
        q = qx[h, q_rows, :]
        do = dox[h, q_rows, :]
        keys = kx[k_rows, :]
        weights = jnp.exp(dot_last(keys, q))
        if masked:
            weights = jnp.where(causal, weights, 0.0)
        dscore = (weights * dot_last(vx[k_rows, :], do)).astype(BF16)
        dv[...] += jnp.dot(weights.astype(BF16), do, preferred_element_type=F32)
        dk[...] += jnp.dot(dscore, q, preferred_element_type=F32)
        dq[h, q_rows, :] += lax.dot_general(dscore, keys, (((0,), (0,)), ((), ())), preferred_element_type=F32)

    def line_copy(owner, source):
        return pltpu.make_async_remote_copy(
            src_ref=dkv.at[owner], dst_ref=dkv.at[source], send_sem=line_send.at[owner],
            recv_sem=line_recv.at[source], device_id=team.other_team(owner), device_id_type=MESH,
        )

    def fetch_keys(source):
        slot = lax.rem(source, 2)
        return pltpu.make_async_copy(kv_all.at[source], kv_in.at[slot], local.at[13 + slot])

    fetch_keys(t * 0).start()

    def attention_unit(source, k, h):
        @pl.when((k == 0) & (h == 0))
        def _():
            fetch_keys(source).wait()

            @pl.when(source < t)
            def _():
                fetch_keys(source + 1).start()

            widen_keys(kv_in[lax.rem(source, 2)], spans, source * rows, kx, vx)

        @pl.when(h == 0)
        def _():
            dk[...] = jnp.zeros_like(dk)
            dv[...] = jnp.zeros_like(dv)

        k_rows = pl.ds(pl.multiple_of(k * part, part), part)

        @pl.when(source < t)
        def _():
            for q in range(2):
                piece(h, slice(q * part, (q + 1) * part), k_rows, False)

        @pl.when(source == t)
        def _():
            for diagonal in range(2):

                @pl.when(k == diagonal)
                def _():
                    for q in range(diagonal, 2):
                        piece(h, slice(q * part, (q + 1) * part), slice(diagonal * part, (diagonal + 1) * part),
                              q == diagonal)

        @pl.when(h == GROUP - 1)
        def _():
            dkv[source, k_rows, :] = jnp.where(
                lane_ids(part) < HEAD_SIZE, dk[...], pltpu.roll(dv[...], HEAD_SIZE, 1)
            ).astype(BF16)

            @pl.when((k == 1) & (source < t))
            def _():
                line_copy(source, t).start()

    def keys_phase():
        fetch.start()
        dkv_sum[...] = wide(dkv[t])
        for d in range(1, T):

            @pl.when(t + d < T)
            def _():
                line_copy(t, t + d).wait_recv()
                dkv_sum[...] += wide(dkv[t + d])

        small[2:4, :] = jnp.zeros((2, width), F32)

    def turn_unit(r):
        here = pl.ds(pl.multiple_of(r * small_block, small_block), small_block)
        cos, sin = cosine[here, 0:HEAD_SIZE], sine[here, 0:HEAD_SIZE]
        q_term = jnp.zeros((1, HEAD_SIZE), F32)
        for h in range(GROUP + 1):
            if h < GROUP:
                u, gain = dq[h, here, 0:HEAD_SIZE] * HEAD_SIZE ** (-0.5), gain_q
            else:
                u, gain = dkv_sum[here, 0:HEAD_SIZE], gain_k
            u = u * cos - jnp.concatenate([u[:, HEAD_SIZE // 2 :], u[:, : HEAD_SIZE // 2]], 1) * sin
            unit, factor = unit_and_factor(heads[h // 2, here, h % 2 * HEAD_SIZE : (h % 2 + 1) * HEAD_SIZE])
            term = jnp.sum(u * unit, 0, keepdims=True)
            if h < GROUP:
                q_term = q_term + term
            else:
                small[3:4, 0:HEAD_SIZE] += term
            turned[here, h * HEAD_SIZE : (h + 1) * HEAD_SIZE] = norm_back(u, unit, factor, gain).astype(BF16)
        small[2:3, 0:HEAD_SIZE] += q_term
        h = GROUP + 1
        turned[here, h * HEAD_SIZE : (h + 1) * HEAD_SIZE] = dkv_sum[here, HEAD_SIZE : 2 * HEAD_SIZE].astype(BF16)

    def normed_unit(i):
        for m in range(4):
            here = pl.ds(pl.multiple_of((4 * i + m) * own_rows, own_rows), own_rows)
            xs[i, m // 2, m % 2] = dot_last(turned[here, :], wq_in[...]).astype(BF16)

    def products_phase():
        again.begin()
        fetch.wait()

    def products_unit(i):
        for j in range(2):
            r = pl.multiple_of((2 * i + j) * (width // 6), LANES)
            here = pl.ds(r, width // 6)
            own_last[here, own_last.shape[1] - turned.shape[1] :] = lax.dot_general(
                big[:, here], turned[...], (((0,), (0,)), ((), ())), preferred_element_type=F32
            ).astype(BF16)

    def tokens_phase():
        def store(columns, total):
            tokens_grad[:, columns] = total

        again.end(store)
        term = jnp.zeros((1, width), F32)
        for r in range(0, own_rows, 32):
            here = slice(r, r + 32)
            unit, factor = unit_and_factor(wide(tokens[here, :]))
            upstream = tokens_grad[here, :]
            term = term + jnp.sum(upstream * unit, 0, keepdims=True)
            tokens_grad[here, :] = grad_resid[here, :] + norm_back(upstream, unit, factor, gain_attn)
        small[0:1, :] = term
        lanes = own_gains.shape[1]
        row = lax.broadcasted_iota(jnp.int32, (16, lanes), 0)

        def cut(i, first, count):
            value = small[i : i + 1, first : first + count]
            if count < lanes:
                value = jnp.concatenate([value, jnp.zeros((1, lanes - count), F32)], 1)
            return jnp.where(row == i, jnp.broadcast_to(value, (16, lanes)), 0.0)

        for i in range(F):
            few = HEAD_SIZE // F
            own_gains[16 * i : 16 * i + 16, :] = (
                cut(0, i * depth, depth) + cut(1, i * depth, depth) + cut(2, i * few, few) + cut(3, i * few, few)
            ).astype(BF16)

    def late_loads():
        for load in loads[2:]:
            load.wait()

    @pl.loop(0, steps)
    def _(s):
        pl.when(s == at["scatter1"])(late_loads)
        sums.step(s)
        for name, body in (
            ("scatter1", scatter.relay), ("scatter2", scatter.relay_again), ("resid", resid_phase),
            ("relay", gather.relay), ("heads", heads_phase), ("own_wo", own_wo_phase), ("keys", keys_phase),
            ("products", products_phase), ("again1", again.relay), ("again2", again.relay_again),
            ("tokens", tokens_phase),
        ):
            pl.when(s == at[name])(body)
        for name, count, body in (
            ("heads", UNITS, heads_unit), ("turn", UNITS, turn_unit), ("normed", 2, normed_unit),
            ("products", 3, products_unit),
        ):
            i = s - at[name]
            pl.when((i >= 0) & (i < count))(functools.partial(body, i))
        unit = s - at["attention"]
        source = lax.div(unit, 2 * GROUP)

        @pl.when((unit >= 0) & (source <= t))
        def _():
            attention_unit(source, lax.rem(lax.div(unit, GROUP), 2), lax.rem(unit, GROUP))

    for d in range(1, T):

        @pl.when(t - d >= 0)
        def _():
            line_copy(t - d, t).wait_send()

    sums.end()


def backward(dims, grad_hidden, g_down, g_wide, g_last, resid, tokens, cotangent, gains, acc, qx, kv_all, spans,
             heads, cosine, sine, wo, wqkv, normed):
    B, F, T = dims
    own_rows, width = resid.shape
    rows = qx.shape[1]
    part = rows // 2
    hidden = g_down.shape[0]
    n = B * F
    kinds = grad_kinds(dims, width, hidden)
    steps = max(
        GradSum.steps([(rows_, step, first) for rows_, _, step, first, _ in kinds], T), first_steps(dims)["tokens"] + 1
    )
    positions = max(first + rows_ // step for rows_, _, step, first, _ in kinds)
    outs = []
    for rows_, wide_, step, first, how in kinds:
        if how == "rows":
            shape = (n, rows_ // F, wide_)
        elif how == "stay":
            shape = (B, rows_, wide_)
        else:
            shape = (n, 16, wide_)
        outs.append(jax.ShapeDtypeStruct(shape, BF16))
    outs.append(jax.ShapeDtypeStruct((own_rows, width), F32))
    eight = (2, 2, 2, own_rows, width)
    hands = [pltpu.SemaphoreType.DMA((F, kinds[k][0] // F // kinds[k][2])) for k in (1, 3)]
    copies = 2 * Scatter.COPIES + Gather.COPIES
    return pl.pallas_call(
        functools.partial(back_kernel, dims, kinds, steps),
        out_shape=outs,
        in_specs=[ANY] * 4 + [VMEM] * 4 + [ANY] * 3 + [VMEM] + [ANY] * 6,
        out_specs=[ANY] * 5 + [VMEM],
        scratch_shapes=[pltpu.VMEM(eight, BF16)]
        + [pltpu.VMEM((kind[0], kind[1]), BF16) for kind in kinds] * 2
        + [pltpu.VMEM(((kind[0] // kind[2] + 1) // 2 * kind[2], kind[1]), BF16) for kind in kinds]
        + [
            pltpu.VMEM((own_rows, width), F32),
            pltpu.VMEM((own_rows, width), BF16),
            pltpu.VMEM((rows, width), BF16),
            pltpu.VMEM(qx.shape, BF16),
            pltpu.VMEM((rows, QW), BF16),
            pltpu.VMEM(qx.shape, F32),
            pltpu.VMEM(kv_all.shape, BF16),
            pltpu.VMEM((2,) + kv_all.shape[1:], BF16),
            pltpu.VMEM((rows, LANES), F32),
            pltpu.VMEM((rows, QW + 2 * HEAD_SIZE), BF16),
            pltpu.VMEM((8, width), F32),
            pltpu.VMEM((rows, LANES), BF16),
            pltpu.VMEM((rows, LANES), BF16),
            pltpu.VMEM((part, LANES), F32),
            pltpu.VMEM((part, LANES), F32),
            pltpu.VMEM(wqkv.shape, BF16),
            pltpu.VMEM((QW, width), BF16),
            pltpu.VMEM(acc.shape, F32),
            pltpu.VMEM(qx.shape, BF16),
            pltpu.VMEM(heads.shape, F32),
            pltpu.VMEM(cosine.shape, F32),
            pltpu.VMEM(sine.shape, F32),
        ]
        + scatter_shapes(own_rows, width, ORDER)
        + [
            pltpu.SemaphoreType.DMA((copies,)),
            pltpu.SemaphoreType.DMA((copies,)),
            pltpu.SemaphoreType.DMA((T,)),
            pltpu.SemaphoreType.DMA((T,)),
            pltpu.SemaphoreType.DMA((2, positions)),
            pltpu.SemaphoreType.DMA((positions,)),
            *hands,
            pltpu.SemaphoreType.DMA((7, len(kinds), 2)),
            pltpu.SemaphoreType.DMA((15,)),
        ],
        compiler_params=pltpu.CompilerParams(
            collective_id=3, has_side_effects=True, vmem_limit_bytes=60 * 1024 * 1024
        ),
        name="backward",
    )(grad_hidden.reshape(eight), g_down, g_wide, g_last, resid, tokens, cotangent, gains, acc, qx,
      kv_all, spans, heads, cosine, sine, wo, wqkv, normed)


def place_kernel(n, hidden, both, last, down, wo, layer, tokens, gains, gate_out, up_out, wq_out, wk_out, wv_out, down_out,
                 wo_out, layer_out, tokens_out, *gain_outs):
    early = both.shape[-1]
    tail = 2 * hidden - early
    for q in range(n):
        block, rest = wide(both[q]), wide(last[q])
        gate_out[:, q * hidden : (q + 1) * hidden] = block[:, :hidden]
        up_out[:, q * hidden : (q + 1) * hidden] = jnp.concatenate([block[:, hidden:], rest[:, :tail]], 1)
        wq_out[:, q * QW : (q + 1) * QW] = rest[:, tail : tail + QW]
        wk_out[:, q * HEAD_SIZE : (q + 1) * HEAD_SIZE] = rest[:, tail + QW : tail + QW + HEAD_SIZE]
        wv_out[:, q * HEAD_SIZE : (q + 1) * HEAD_SIZE] = rest[:, tail + QW + HEAD_SIZE :]
    down_out[...] = wide(down[...])
    wo_out[...] = wide(wo[...])

    @pl.when(pl.program_id(0) == 0)
    def _():
        layer_out[...] = layer[...].astype(BF16)
        tokens_out[...] = tokens[...].astype(BF16)
        total = wide(gains[0])
        for i in range(1, n):
            total = total + wide(gains[i])
        for i, gain_out in enumerate(gain_outs):
            gain_out[...] = total[i, : gain_out.shape[0]]


def place(hidden, both, last, down, wo, layer, tokens, gains):
    n, depth, early = both.shape
    width = down.shape[-1]
    down, wo = down.reshape(-1, width), wo.reshape(-1, width)
    step = 64
    count = depth // step
    many = lambda a: pl.BlockSpec((n, step, a.shape[-1]), lambda i: (0, i, 0))
    cut = lambda a: pl.BlockSpec((a.shape[0] // count, width), lambda i: (i, 0))
    out = lambda w: pl.BlockSpec((step, w), lambda i: (i, 0))
    whole = lambda dims: pl.BlockSpec(dims, lambda i: (0,) * len(dims))
    shape = lambda r, w: jax.ShapeDtypeStruct((r, w), F32)
    wq, wk = QW * n, HEAD_SIZE * n
    sizes = [depth, depth, HEAD_SIZE * depth // width, HEAD_SIZE * depth // width]
    return pl.pallas_call(
        functools.partial(place_kernel, n, hidden),
        grid=(count,),
        out_shape=(
            shape(depth, n * hidden), shape(depth, n * hidden), shape(depth, wq), shape(depth, wk), shape(depth, wk),
            shape(down.shape[0], width), shape(wo.shape[0], width), jax.ShapeDtypeStruct(layer.shape, BF16),
            jax.ShapeDtypeStruct(tokens.shape, BF16), *[jax.ShapeDtypeStruct((size,), F32) for size in sizes],
        ),
        in_specs=[many(both), many(last), cut(down), cut(wo), whole(layer.shape), whole(tokens.shape),
                  whole(gains.shape)],
        out_specs=[out(n * hidden), out(n * hidden), out(wq), out(wk), out(wk), cut(down), cut(wo),
                   whole(layer.shape), whole(tokens.shape), *[whole((size,)) for size in sizes]],
        compiler_params=pltpu.CompilerParams(vmem_limit_bytes=VMEM_LIMIT),
        name="place",
    )(both, last, down, wo, layer, tokens, gains)


def norm_back(upstream, unit_rows, factor, gain_row):
    lifted = upstream * gain_row
    return factor * (lifted - unit_rows * jnp.mean(lifted * unit_rows, -1, keepdims=True))


def on_device(
    tokens, lengths, wq, wk, wv, wo, w_gate, w_up, w_down, attn_gain, ffn_gain, q_gain, key_norm_gain, cotangent
):
    F = lax.axis_size("fsdp")
    B = KEY_VALUE_HEADS // F
    T = lax.axis_size("ctx") // B
    dims = (B, F, T)
    own_rows, width = tokens.shape
    rows = own_rows * KEY_VALUE_HEADS
    depth = width // F
    t = lax.axis_index("ctx") // B
    hidden = w_down.shape[0] // B

    lanes = max(depth, LANES)
    line = lambda a: jnp.pad(a, (0, lanes - a.shape[0]))
    gains = jnp.concatenate([line(attn_gain), line(ffn_gain), line(q_gain), line(key_norm_gain)])
    gains = jnp.pad(gains.reshape(4, lanes), ((0, 12), (0, 0)))
    half = HEAD_SIZE // 2
    freq = np.power(np.float32(ROPE_BASE), -(np.arange(LANES, dtype=np.float32) % half * np.float32(2.0) / HEAD_SIZE))
    freq = jnp.asarray(np.broadcast_to(freq, (8, LANES))[:1], F32)
    (cosine, sine, spans, tok_full, wqkv, normed, heads, qx, kv_all, acc, mixed, wo_full, wide_w, all_gains) = front(
        dims, tokens, wq, wk, wv, wo, w_gate, w_up, gains, freq, lengths
    )
    grad_hidden, g_down, g_wide, g_last, own_resid, layer_out = feed(
        dims, tok_full, mixed, wo_full.reshape(-1, width), wide_w.reshape(width, 2 * hidden), w_down,
        cotangent, all_gains,
    )
    out_down, out_wide, out_wo, out_last, out_gains, tokens_grad = backward(
        dims, grad_hidden, g_down, g_wide, g_last, own_resid, tokens, cotangent, all_gains, acc, qx, kv_all,
        spans, heads, cosine, sine, wo, wqkv, normed,
    )
    (gate_grad, up_grad, wq_grad, wk_grad, wv_grad, down_grad, wo_grad, layer_out, tokens_grad, *gain_grads) = place(
        hidden, out_wide, out_last, out_down, out_wo, layer_out, tokens_grad, out_gains
    )
    return (
        layer_out, tokens_grad, wq_grad, wk_grad, wv_grad, wo_grad, gate_grad, up_grad,
        down_grad, *gain_grads,
    )


def solution(mesh):
    rows = P(("ctx", "fsdp"), None)
    shard = P("fsdp", None)
    gain = P("fsdp")
    return jax.shard_map(
        on_device,
        mesh=mesh,
        in_specs=(rows, P(), shard, shard, shard, shard, shard, shard, shard, gain, gain, gain, gain, rows),
        out_specs=(rows, rows, shard, shard, shard, shard, shard, shard, shard, gain, gain, gain, gain),
        check_vma=False,
    )
```

```python
import functools

import jax
import jax.numpy as jnp
import numpy as np
from jax import lax
from jax.experimental import pallas as pl
from jax.experimental.pallas import tpu as pltpu
from jax.sharding import PartitionSpec as P

QUERY_HEADS = 24
KEY_VALUE_HEADS = 8
HEAD_SIZE = 64
GROUP = QUERY_HEADS // KEY_VALUE_HEADS
QW = GROUP * HEAD_SIZE
LANES = 128
NDOCS = 4

EPSILON = 1e-05
ROPE_BASE = 1000000.0
APART = 16384.0

MESH = pl.DeviceIdType.MESH
F32 = jnp.float32
BF16 = jnp.bfloat16
ANY = pl.BlockSpec(memory_space=pl.ANY)
VMEM = pl.BlockSpec(memory_space=pltpu.VMEM)
VMEM_LIMIT = 56 * 1024 * 1024


class Team:
    def __init__(self, B, F, T):
        self.B, self.F, self.T = B, F, T
        ctx, self.f = lax.axis_index("ctx"), lax.axis_index("fsdp")
        self.t, self.y = lax.div(ctx, B), lax.rem(ctx, B)
        self.p = self.y * F + self.f

    def member(self, p):
        return (self.t * self.B + lax.div(p, self.F), lax.rem(p, self.F))

    def same_row(self, f):
        return (self.t * self.B + self.y, f)

    def other_team(self, t):
        return (t * self.B + self.y, self.f)


def flip(p, bit):
    return p + bit * (1 - 2 * lax.rem(lax.div(p, bit), 2))


def bit_of(p, bit):
    return lax.rem(lax.div(p, bit), 2)


class Sems:
    def __init__(self, send, recv):
        self.send, self.recv, self.used = send, recv, 0

    def copy(self, src, dst, device):
        i = self.used
        self.used += 1
        return pltpu.make_async_remote_copy(
            src_ref=src,
            dst_ref=dst,
            send_sem=self.send.at[i],
            recv_sem=self.recv.at[i],
            device_id=device,
            device_id_type=MESH,
        )


def greet(devices):
    barrier = pltpu.get_barrier_semaphore()
    for device in devices:
        pl.semaphore_signal(barrier, inc=1, device_id=device, device_id_type=MESH)
    pl.semaphore_wait(barrier, len(devices))


def team_peers(team):
    n = team.B * team.F
    return [team.member(lax.rem(team.p + d, n)) for d in range(1, n)]


def line_peers(team):
    return [team.other_team(lax.rem(team.t + d, team.T)) for d in range(1, team.T)]


def row_peers(team):
    return [team.same_row(lax.rem(team.f + d, team.F)) for d in range(1, team.F)]


class Gather:
    def __init__(self, sems, me, count, device, own, block, half, order="both"):
        bits = count.bit_length() - 1
        one, two = flip(me, 1), flip(me, 2)
        send = lambda src, dst, to: sems.copy(src, dst, device(to))
        again = lambda ref, to: send(ref, ref, to)
        self.first = [send(own, block(me), flip(me, 1 << k)) for k in range(bits)]
        self.over = [again(block(two), one)]
        self.halves, self.corner = [], []
        if count == 8:
            four = flip(me, 4)
            far = flip(two, 4)
            self.over.append(again(block(four), one))
            if order == "both":
                self.halves = [again(half(two, 0), four), again(half(four, 1), two)]
                self.corner = [again(half(far, 0), one), again(half(far, 1), one)]
            else:
                self.halves = [again(block(two), four)]
                self.corner = [again(block(far), one)]

    def begin(self):
        for copy in self.first:
            copy.start()

    def relay(self):
        self.first[1].wait_recv()
        self.over[0].start()
        if self.halves:
            self.halves[0].start()
            self.first[2].wait_recv()
            for copy in self.halves[1:]:
                copy.start()
            self.over[1].start()

    def end(self):
        for arrived, onward in zip(self.halves, self.corner):
            arrived.wait_recv()
            onward.start()
        self.first[0].wait_recv()
        for copy in self.over + self.corner:
            copy.wait_recv()
        for copy in self.first + self.over + self.halves + self.corner:
            copy.wait_send()

    COPIES = 9


def scatter_parts(width, order):
    if order == "both":
        return [(0, width // 2, 2, 4), (width // 2, width // 2, 4, 2)]
    return [(0, width, 2, 4)]


def scatter_shapes(rows, width, order):
    shapes = [pltpu.VMEM((2, 2, rows, width), BF16)]
    for _, columns, _, _ in scatter_parts(width, order):
        shapes += [pltpu.VMEM((2, rows, columns), BF16)] * 2 + [pltpu.VMEM((rows, columns), BF16)] * 2
    return shapes


def wide(v):
    return v.astype(F32)


class Scatter:
    COPIES = 5

    def __init__(self, sems, team, x, scratch, order):
        self.x, self.r0 = x, scratch[0]
        p = team.p
        self.b = bit_of(p, 1), bit_of(p, 2), bit_of(p, 4)
        send = lambda src, dst, bit: sems.copy(src, dst, team.member(flip(p, bit)))
        self.first = send(x.at[:, :, 1 - self.b[0]], self.r0, 1)
        self.parts = []
        for i, (at, columns, one, two) in enumerate(scatter_parts(x.shape[-1], order)):
            s1, r1, s2, r2 = scratch[1 + 4 * i : 5 + 4 * i]
            self.parts.append((pl.ds(at, columns), one, s1, r1, s2, r2, send(s1, r1, one), send(s2, r2, two)))

    def term(self, b2, b1, columns):
        return wide(self.x[b2, b1, self.b[0], :, columns]) + wide(self.r0[b2, b1, :, columns])

    def begin(self):
        self.first.start()

    def relay(self):
        b0, b1, b2 = self.b
        self.first.wait_recv()
        for columns, one, s1, r1, s2, r2, send1, send2 in self.parts:
            for k in range(2):
                s1[k] = (self.term(k, 1 - b1, columns) if one == 2 else self.term(1 - b2, k, columns)).astype(BF16)
            send1.start()

    def relay_again(self):
        b0, b1, b2 = self.b
        for columns, one, s1, r1, s2, r2, send1, send2 in self.parts:
            send1.wait_recv()
            if one == 2:
                total = self.term(1 - b2, b1, columns) + wide(r1[1 - b2])
            else:
                total = self.term(b2, 1 - b1, columns) + wide(r1[1 - b1])
            s2[...] = total.astype(BF16)
            send2.start()

    def end(self, store):
        b0, b1, b2 = self.b
        for columns, one, s1, r1, s2, r2, send1, send2 in self.parts:
            send2.wait_recv()
            store(columns, self.term(b2, b1, columns) + wide(r1[b2 if one == 2 else b1]) + wide(r2[...]))
        for copy in [self.first] + [copy for part in self.parts for copy in part[6:]]:
            copy.wait_send()


def kernel_params(collective_id):
    return pltpu.CompilerParams(
        collective_id=collective_id, has_side_effects=True, vmem_limit_bytes=VMEM_LIMIT
    )


def unit_and_factor(x):
    factor = lax.rsqrt(jnp.mean(x * x, -1, keepdims=True) + EPSILON)
    return x * factor, factor


def lane_ids(rows):
    return lax.broadcasted_iota(jnp.int32, (rows, LANES), 1)


def inside_document(spans, rows, first_row):
    row = lax.broadcasted_iota(jnp.int32, (rows, LANES), 0) + first_row
    return (row >= spans[0:1, :]) & (row < spans[1:2, :])


def widen_keys(kv, spans, first_row, kx, vx):
    rows = kv.shape[0]
    lane = lane_ids(rows)
    inside = inside_document(spans, rows, first_row)
    both = wide(kv)
    kx[...] = jnp.where(lane < HEAD_SIZE, both, jnp.where(inside, 1.0, 0.0)).astype(BF16)
    vx[...] = jnp.where(lane < HEAD_SIZE, pltpu.roll(both, HEAD_SIZE, 1), 1.0).astype(BF16)


def dot_last(a, b):
    return lax.dot_general(a, b, (((1,), (1,)), ((), ())), preferred_element_type=F32)


def fill_tables(t, lengths, freq, cosine, sine, spans):
    rows = cosine.shape[0]
    ends, total = [], 0
    for d in range(NDOCS):
        total = total + lengths[d]
        ends.append(total)
    lane = lax.broadcasted_iota(jnp.int32, spans.shape, 1)
    row = lax.broadcasted_iota(jnp.int32, spans.shape, 0)
    first, past = jnp.zeros(spans.shape, jnp.int32), jnp.full(spans.shape, 2**30, jnp.int32)
    for d in range(NDOCS):
        first = jnp.where(lane == HEAD_SIZE + d, ends[d] - lengths[d], first)
        past = jnp.where(lane == HEAD_SIZE + d, ends[d], past)
    spans[...] = jnp.where(row == 0, first, past)
    half = HEAD_SIZE // 2
    parts = LANES // half
    few = rows // parts
    shape = (few, LANES)
    token = lax.broadcasted_iota(jnp.int32, shape, 0) + lax.div(lax.broadcasted_iota(jnp.int32, shape, 1), half) * few
    token = token + t * rows
    start = jnp.zeros(shape, jnp.int32)
    for d in range(NDOCS):
        start = jnp.where(token >= ends[d], ends[d], start)
    angles = (token - start).astype(F32) * freq[...]
    cos, sin = jnp.cos(angles), jnp.sin(angles)
    for i in range(parts):
        here, lanes = slice(i * few, (i + 1) * few), slice(i * half, (i + 1) * half)
        cosine[here, :] = jnp.concatenate([cos[:, lanes]] * parts, 1)
        sine[here, :] = jnp.concatenate([-sin[:, lanes], sin[:, lanes]] * (parts // 2), 1)


def front_kernel(dims, tokens, wq, wk, wv, wo, w_gate, w_up, gains, freq, lengths,
                 cosine, sine, spans, tok_full, wqkv, normed, heads, qx, kv_all, acc, mixed, wo_full, wide_full, all_gains,
                 tok, q_in, k_in, v_in, qkv_cut, qkv, gains_in, slab_g, slab_u, cut, norm, kv, kx, vx, packed,
                 send, recv, line_send, line_recv, local):
    team = Team(*dims)
    B, F, T = dims
    t, y, f, p = team.t, team.y, team.f, team.p
    sems = Sems(send, recv)
    own_rows, width = tokens.shape
    rows = own_rows * B * F
    depth = width // F
    part, block = rows // 2, rows // 4
    hidden = cut.shape[-1] // 2
    parity = lax.rem(t, 2)

    def home(src, dst, i):
        copy = pltpu.make_async_copy(src, dst, local.at[i])
        copy.start()
        return copy

    token_rows = lambda i: pl.ds(pl.multiple_of(i * own_rows, 16), own_rows)
    shard_rows = lambda i: pl.ds(pl.multiple_of(i * depth, 16), depth)
    token_load = home(tokens, tok.at[token_rows(p)], 0)
    small_loads = [home(wq, q_in, 1), home(wk, k_in, 2), home(wv, v_in, 3)]
    gain_load = home(gains, gains_in.at[f], 4)
    slab_loads = [home(w_gate, slab_g, 5), home(w_up, slab_u, 6)]
    homes = [home(wo, wo_full.at[f], 7)]
    greet(team_peers(team) + line_peers(team))

    half = own_rows // 2
    gather_tok = Gather(
        sems, p, B * F, team.member, tokens, lambda i: tok.at[token_rows(i)],
        lambda i, k: tok.at[pl.ds(pl.multiple_of(i * own_rows + k * half, 16), half)],
        "tall",
    )
    few = packed.shape[1] // 2

    def gather_half(which):
        return Gather(
            sems, p, B * F, team.member, packed.at[which], lambda i: mixed.at[which, i],
            lambda i, k: mixed.at[which, i, pl.ds(k * few, few)],
            "both" if which else "tall",
        )

    gather_mixed = [gather_half(0), gather_half(1)]
    partners = []
    for m in range(1, F):
        to = f
        for bit in (1, 2, 4):
            if m & bit:
                to = flip(to, bit)
        partners.append(to)
    gain_sends = [sems.copy(gains, gains_in.at[f], team.same_row(to)) for to in partners]
    half_depth = depth // 2
    some = pl.ds(pl.multiple_of(parity * half_depth, 16), half_depth)
    near = team.other_team(t + 1 - 2 * parity)
    some_of = lambda i: pl.ds(pl.multiple_of(i * depth + parity * half_depth, 16), half_depth)
    qkv_sends = [sems.copy(qkv_cut.at[partners[0]], qkv.at[shard_rows(f)], team.same_row(partners[0]))]
    qkv_shares = []
    for to in partners[1:]:
        qkv_sends.append(sems.copy(qkv_cut.at[to, some], qkv.at[some_of(f)], team.same_row(to)))
        qkv_shares.append(sems.copy(qkv.at[some_of(to)], qkv.at[some_of(to)], near))
    wide_near = sems.copy(cut.at[partners[0]], wide_full.at[f], team.same_row(partners[0]))
    wide_sends, wide_shares = [[], []], [[], []]
    quarter = half_depth // 2
    for i in range(2):
        some = pl.ds(pl.multiple_of(parity * half_depth + i * quarter, 16), quarter)
        for to in partners[1:]:
            wide_sends[i].append(sems.copy(cut.at[to, some], wide_full.at[f, some], team.same_row(to)))
            wide_shares[i].append(sems.copy(wide_full.at[to, some], wide_full.at[to, some], near))
    if B == 2 and F == 4:
        one, two = flip(f, 1), flip(f, 2)
        other = team.member(lax.rem(p + F, B * F))
        wo_half = lambda k: pl.ds(pl.multiple_of(k * half_depth, 16), half_depth)
        mine, theirs = wo_half(y), wo_half(1 - y)
        wo_first = [
            sems.copy(wo, wo_full.at[f], team.same_row(one)),
            sems.copy(wo.at[mine], wo_full.at[f, mine], team.same_row(two)),
        ]
        ref = wo_full.at[two, mine]
        wo_relay = [sems.copy(ref, ref, other), sems.copy(ref, ref, team.same_row(one))]
        ref = wo_full.at[two, theirs]
        wo_last = [sems.copy(ref, ref, team.same_row(one))]

    def line_copy(d, source, to, r):
        here = pl.ds(pl.multiple_of(r * block, block), block)
        return pltpu.make_async_remote_copy(
            src_ref=kv.at[here], dst_ref=kv_all.at[source, here], send_sem=line_send.at[d, r],
            recv_sem=line_recv.at[source, r], device_id=team.other_team(to), device_id_type=MESH,
        )

    gather_tok.begin()
    for copy in gain_sends:
        copy.start()
    fill_tables(t, lengths, freq, cosine, sine, spans)
    for load in small_loads:
        load.wait()
    for i in range(F):
        for row in range(B):
            h = i * B + row

            @pl.when(y == row)
            def _():
                qkv_cut[i, :, 0:QW] = q_in[:, h * QW : (h + 1) * QW]
                qkv_cut[i, :, QW : QW + HEAD_SIZE] = k_in[:, h * HEAD_SIZE : (h + 1) * HEAD_SIZE]
                qkv_cut[i, :, QW + HEAD_SIZE : QW + 2 * HEAD_SIZE] = v_in[:, h * HEAD_SIZE : (h + 1) * HEAD_SIZE]

    for copy in qkv_sends:
        copy.start()
    qkv[shard_rows(f), :] = qkv_cut[f]
    for load in slab_loads:
        load.wait()

    @pl.loop(0, depth // 32)
    def _(r):
        here = pl.ds(pl.multiple_of(r * 32, 32), 32)
        for j in range(F):
            for row in range(B):
                q = j * B + row

                @pl.when(y == row)
                def _():
                    cut[j, here, 0:hidden] = slab_g[here, q * hidden : (q + 1) * hidden]
                    cut[j, here, hidden : 2 * hidden] = slab_u[here, q * hidden : (q + 1) * hidden]

    gather_tok.relay()
    for arrived, onward in zip(qkv_sends[1:], qkv_shares):
        arrived.wait_recv()
        onward.start()
    for copy in wide_sends[0] + [wide_near]:
        copy.start()
    if B == 2 and F == 4:
        for copy in wo_first:
            copy.start()
    else:
        gather_wo = Gather(
            sems, f, F, team.same_row, wo, lambda i: wo_full.at[i],
            lambda i, k: wo_full.at[i, pl.ds(k * half_depth, half_depth)],
        )
        gather_wo.begin()
    for copy in wide_sends[1]:
        copy.start()
    homes.append(home(cut.at[f], wide_full.at[f], 9))
    gather_tok.end()
    token_load.wait()
    gain_load.wait()
    for copy in gain_sends:
        copy.wait_recv()
    homes.append(home(tok, tok_full, 11))

    all_gains[...] = jnp.zeros_like(all_gains)
    for i in range(F):
        for k, count in ((0, depth), (1, depth), (2, HEAD_SIZE // F), (3, HEAD_SIZE // F)):
            all_gains[k : k + 1, i * count : (i + 1) * count] = wide(gains_in[i])[k : k + 1, 0:count]
    gain_q, gain_k = all_gains[2:3, 0:HEAD_SIZE], all_gains[3:4, 0:HEAD_SIZE]

    @pl.loop(0, rows // block)
    def _(r):
        here = pl.ds(pl.multiple_of(r * block, block), block)
        unit, factor = unit_and_factor(wide(tok[here, :]))
        norm[here, :] = (unit * all_gains[0:1, :]).astype(BF16)

    for copy in qkv_sends[:1] + qkv_shares:
        copy.wait_recv()
    homes += [home(norm, normed, 12), home(qkv, wqkv, 13)]

    lane = lane_ids(block)
    same_head = lax.div(lax.broadcasted_iota(jnp.int32, (LANES, LANES), 0), HEAD_SIZE) == lax.div(
        lax.broadcasted_iota(jnp.int32, (LANES, LANES), 1), HEAD_SIZE
    )
    same_head = jnp.where(same_head, 1.0, 0.0).astype(BF16)
    gain_pairs = [jnp.concatenate([gain_q, gain_q], 1), jnp.concatenate([gain_q, gain_k], 1)]

    @pl.loop(0, rows // block)
    def _(r):
        here = pl.ds(pl.multiple_of(r * block, block), block)
        projected = jnp.dot(norm[here, :], qkv[...], preferred_element_type=F32)
        apart = jnp.where(inside_document(spans, block, t * rows + r * block), 0.0, -APART)
        cos, sin = cosine[here, :], sine[here, :]
        turned = []
        for i in range(2):
            x = projected[:, i * LANES : (i + 1) * LANES]
            heads[i, here, :] = x
            square = x * x
            high = square.astype(BF16)
            rest = (square - wide(high)).astype(BF16)
            total = jnp.dot(high, same_head, preferred_element_type=F32) + jnp.dot(
                rest, same_head, preferred_element_type=F32
            )
            u = x * lax.rsqrt(total * (1.0 / HEAD_SIZE) + EPSILON) * gain_pairs[i]
            first = lax.rem(lane, HEAD_SIZE) < HEAD_SIZE // 2
            swapped = jnp.where(first, pltpu.roll(u, LANES - HEAD_SIZE // 2, 1), pltpu.roll(u, HEAD_SIZE // 2, 1))
            turned.append(wide((u * cos + swapped * sin).astype(BF16)))
        for h in range(GROUP):
            q = turned[h // 2] * HEAD_SIZE ** (-0.5)
            q = pltpu.roll(q, HEAD_SIZE, 1) if h % 2 else q
            qx[h, here, :] = jnp.where(lane < HEAD_SIZE, q, apart).astype(BF16)
        values = projected[:, (GROUP + 1) * HEAD_SIZE : (GROUP + 2) * HEAD_SIZE]
        keys = pltpu.roll(turned[1], HEAD_SIZE, 1)
        kv[here, :] = jnp.where(lane < HEAD_SIZE, keys, jnp.concatenate([values, values], 1)).astype(BF16)
        for d in range(1, T):

            @pl.when(t + d < T)
            def _():
                line_copy(d, t, t + d, r).start()

    kv_all[t] = kv[...]
    widen_keys(kv[...], spans, t * rows, kx.at[t], vx.at[t])
    causal = lax.broadcasted_iota(jnp.int32, (part, part), 1) <= lax.broadcasted_iota(jnp.int32, (part, part), 0)

    def piece(q, source, k, masked):
        scores = dot_last(q, kx[source, k * part : (k + 1) * part, :])
        weights = jnp.exp(scores)
        if masked:
            weights = jnp.where(causal, weights, 0.0)
        return jnp.dot(weights.astype(BF16), vx[source, k * part : (k + 1) * part, :], preferred_element_type=F32)

    def pass_weights(i):
        for arrived, onward in zip(wide_sends[i], wide_shares[i]):
            arrived.wait_recv()
            onward.start()

    def pass_wo():
        if B == 2 and F == 4:
            wo_first[1].wait_recv()
            for copy in wo_relay:
                copy.start()
        else:
            gather_wo.relay()

    for which in range(2):
        mine = slice(which * part, (which + 1) * part)

        @pl.loop(0, GROUP)
        def _(h):
            q = qx[h, mine, :]
            total = piece(q, t, which, True)
            acc[h, mine, :] = total + piece(q, t, 0, False) if which else total

        pass_weights(which)
        if which:
            gather_mixed[0].relay()

        @pl.loop(1, t + 1)
        def _(j):
            source = t - j
            if which == 0:
                for r in range(4):
                    line_copy(0, source, t, r).wait_recv()
                widen_keys(kv_all[source], spans, source * rows, kx.at[source], vx.at[source])

            @pl.loop(0, GROUP)
            def _(h):
                q = qx[h, mine, :]
                acc[h, mine, :] = acc[h, mine, :] + piece(q, source, 0, False) + piece(q, source, 1, False)

        for h in range(GROUP):
            out = acc[h, mine, 0:HEAD_SIZE] / acc[h, mine, HEAD_SIZE : 2 * HEAD_SIZE]
            out = out.astype(BF16)
            if h < 2:
                packed[which, 0:part, h * HEAD_SIZE : (h + 1) * HEAD_SIZE] = out
            else:
                packed[which, part : part + part // 2, 0:HEAD_SIZE] = out[0 : part // 2]
                packed[which, part : part + part // 2, HEAD_SIZE : 2 * HEAD_SIZE] = out[part // 2 : part]
        homes.append(home(packed.at[which], mixed.at[which, p], 14 + which))
        gather_mixed[which].begin()
        if which == 0:
            pass_wo()

    gather_mixed[0].end()
    gather_mixed[1].relay()
    if B == 2 and F == 4:
        wo_relay[0].wait_recv()
        wo_last[0].start()
    gather_mixed[1].end()
    if B == 2 and F == 4:
        for copy in (wo_first[0], wo_relay[1], wo_last[0]):
            copy.wait_recv()
        for copy in wo_first + wo_relay + wo_last:
            copy.wait_send()
    else:
        gather_wo.end()
    for copy in [wide_near] + wide_shares[0] + wide_shares[1]:
        copy.wait_recv()
    for copy in [wide_near] + wide_sends[0] + wide_sends[1] + wide_shares[0] + wide_shares[1]:
        copy.wait_send()
    for copy in gain_sends + qkv_sends + qkv_shares:
        copy.wait_send()
    for copy in homes:
        copy.wait()
    for d in range(1, T):

        @pl.when(t + d < T)
        def _():
            for r in range(4):
                line_copy(d, t, t + d, r).wait_send()


def front(dims, tokens, wq, wk, wv, wo, w_gate, w_up, gains, freq, lengths):
    B, F, T = dims
    own_rows, width = tokens.shape
    n = B * F
    rows = own_rows * n
    depth, ff = w_gate.shape
    hidden = ff // n
    few = QW + 2 * HEAD_SIZE
    copies = 4 * Gather.COPIES + (F - 1) + 3 * (2 * F - 3)
    packed = (rows // 2 + rows // 4, LANES)
    shape = lambda *s: jax.ShapeDtypeStruct(s, BF16)
    wide_shape = lambda *s: jax.ShapeDtypeStruct(s, F32)
    vmem = lambda *s: pltpu.VMEM(s, BF16)
    return pl.pallas_call(
        functools.partial(front_kernel, dims),
        out_shape=(
            wide_shape(rows, LANES), wide_shape(rows, LANES), jax.ShapeDtypeStruct((8, LANES), jnp.int32),
            shape(rows, width), shape(width, few), shape(rows, width), wide_shape((GROUP + 1) // 2, rows, LANES),
            shape(GROUP, rows, LANES), shape(T, rows, LANES), wide_shape(GROUP, rows, LANES), shape(2, n, *packed),
            shape(F, depth, width), shape(F, depth, 2 * hidden),
            wide_shape(8, width),
        ),
        in_specs=[ANY] * 8 + [VMEM, pl.BlockSpec(memory_space=pltpu.SMEM)],
        out_specs=[VMEM] * 3 + [ANY] * 3 + [VMEM] * 4 + [ANY] * 3 + [VMEM],
        scratch_shapes=[
            vmem(rows, width), vmem(*wq.shape), vmem(*wk.shape), vmem(*wv.shape), vmem(F, depth, few), vmem(width, few),
            vmem(F, *gains.shape), vmem(depth, ff), vmem(depth, ff), vmem(F, depth, 2 * hidden),
            vmem(rows, width), vmem(rows, LANES), vmem(T, rows, LANES), vmem(T, rows, LANES), vmem(2, *packed),
            pltpu.SemaphoreType.DMA((copies,)),
            pltpu.SemaphoreType.DMA((copies,)),
            pltpu.SemaphoreType.DMA((T, 4)),
            pltpu.SemaphoreType.DMA((T, 4)),
            pltpu.SemaphoreType.DMA((16,)),
        ],
        compiler_params=kernel_params(1),
        name="front",
    )(tokens, wq, wk, wv, wo, w_gate, w_up, gains, freq, lengths)


def feed_kernel(dims, tok_in, mixed_in, wo_in, wide_in, down_in, dy_in, gain, grad_hidden, g_down,
                g_wide, g_last, own_resid, layer_out, tok, mixed, wo, w_wide, w_down, dy, rows_in, hid, both, act, dwide,
                resid, down, gd, gw, gl, *rest):
    scratch, (send, recv, local) = rest[:9], rest[9:]
    team = Team(*dims)
    B, F, y, p = team.B, team.F, team.y, team.p
    rows, width = tok.shape
    own_rows = own_resid.shape[0]
    hidden = w_down.shape[0]
    early = gw.shape[1]
    block = resid.shape[0]
    n = B * F
    dy_rows = lambda i: pl.ds(pl.multiple_of(i * own_rows, 16), own_rows)
    loads = [
        pltpu.make_async_copy(src, dst, local.at[i])
        for i, (src, dst) in enumerate(
            [(mixed_in, mixed), (wo_in, wo), (tok_in, tok), (wide_in, w_wide),
             (down_in.at[pl.ds(pl.multiple_of(y * hidden, 16), hidden)], w_down), (dy_in, dy.at[dy_rows(p)])]
        )
    ]
    for load in loads:
        load.start()
    greet([team.member(flip(p, bit)) for bit in (1, 2, 4)])
    sems = Sems(send, recv)
    scatter = Scatter(sems, team, down, scratch, "both")
    half = own_rows // 2
    gather = Gather(
        sems, p, n, team.member, dy_in, lambda i: dy.at[dy_rows(i)],
        lambda i, k: dy.at[pl.ds(pl.multiple_of(i * own_rows + k * half, 16), half)],
    )
    gather.begin()
    for load in loads[:3]:
        load.wait()

    @pl.loop(0, rows // block)
    def _(r):
        here = pl.ds(pl.multiple_of(r * block, block), block)
        which, later = lax.div(r, 2), lax.rem(r, 2)
        place = pl.ds(pl.multiple_of(later * block, block), block)
        for i in range(n):
            h = i % F * B + i // F
            first = h * QW
            rows_in[:, first : first + 2 * HEAD_SIZE] = mixed[which, i, place, :]
            last = mixed[which, i, 2 * block : 3 * block, :]
            last = jnp.where(later == 0, wide(last[:, :HEAD_SIZE]), wide(last[:, HEAD_SIZE:]))
            rows_in[:, first + 2 * HEAD_SIZE : first + QW] = last.astype(BF16)
        resid[...] = wide(tok[here, :]) + jnp.dot(rows_in[...], wo[...], preferred_element_type=F32)

        @pl.when(r == lax.div(p * own_rows, block))
        def _():
            own_resid[...] = resid[pl.ds(pl.multiple_of(lax.rem(p * own_rows, block), 8), own_rows), :]

        unit, factor = unit_and_factor(resid[...])
        hid[here, :] = (unit * gain[1:2, :]).astype(BF16)

    for load in loads[3:]:
        load.wait()
    gather.relay()

    @pl.loop(0, rows // block)
    def _(r):
        here = pl.ds(pl.multiple_of(r * block, block), block)
        product = jnp.dot(hid[here, :], w_wide[...], preferred_element_type=F32)
        gate, upper = product[:, :hidden], product[:, hidden:]
        both[0, here, :] = gate
        both[1, here, :] = upper
        sigma = 1.0 / (1.0 + jnp.exp(-gate))
        acts = (gate * sigma * upper).astype(BF16)
        act[here, :] = acts
        out = jnp.dot(acts, w_down[...], preferred_element_type=F32).astype(BF16)
        for i in range(block // own_rows):
            m = r * (block // own_rows) + i
            down[lax.div(m, 4), lax.rem(lax.div(m, 2), 2), lax.rem(m, 2)] = out[i * own_rows : (i + 1) * own_rows]

    scatter.begin()
    gather.end()

    @pl.loop(0, rows // block)
    def _(r):
        here = pl.ds(pl.multiple_of(r * block, block), block)
        pl.when(r == 1)(scatter.relay)
        gate, upper = both[0, here, :], both[1, here, :]
        sigma = 1.0 / (1.0 + jnp.exp(-gate))
        dact = dot_last(dy[here, :], w_down[...])
        dwide[here, 0:hidden] = (dact * upper * sigma * (1.0 + gate * (1.0 - sigma))).astype(BF16)
        dwide[here, hidden : 2 * hidden] = (dact * (gate * sigma)).astype(BF16)
        tok[here, :] = dot_last(dwide[here, :], w_wide[...]).astype(BF16)

    stores = []

    def store(src, dst):
        stores.append(pltpu.make_async_copy(src, dst, local.at[6 + len(stores)]))
        stores[-1].start()

    store(tok, grad_hidden)
    over_rows = lambda a, b: lax.dot_general(a, b, (((0,), (0,)), ((), ())), preferred_element_type=F32).astype(BF16)

    for first in range(0, hidden, 256):
        count = min(256, hidden - first)
        gd[first : first + count, :] = over_rows(act[:, first : first + count], dy[...])
    store(gd, g_down)
    scatter.relay_again()

    @pl.loop(0, width // 256)
    def _(r):
        here = pl.ds(pl.multiple_of(r * 256, 256), 256)
        product = over_rows(hid[:, here], dwide[...])
        gw[here, :] = product[:, :early]
        gl[here, 0 : 2 * hidden - early] = product[:, early:]
        pltpu.make_async_copy(gw.at[here], g_wide.at[here], local.at[10]).start()
        pltpu.make_async_copy(gl.at[here], g_last.at[here], local.at[11]).start()

    def put(columns, total):
        layer_out[:, columns] = own_resid[:, columns] + total

    scatter.end(put)
    for copy in stores:
        copy.wait()
    pltpu.make_async_copy(gw, g_wide, local.at[10]).wait()
    pltpu.make_async_copy(gl, g_last, local.at[11]).wait()


def feed(dims, tok, mixed, wo, w_wide, w_down, dy, gains):
    rows, width = tok.shape
    hidden = w_wide.shape[1] // 2
    own_rows = rows // KEY_VALUE_HEADS
    early = early_lanes(hidden)
    last = 2 * hidden - early + QW + 2 * HEAD_SIZE
    block = rows // 4
    shape = lambda s: jax.ShapeDtypeStruct(s, BF16)
    return pl.pallas_call(
        functools.partial(feed_kernel, dims),
        out_shape=(
            shape((rows, width)), shape((hidden, width)), shape((width, early)), shape((width, last)),
            jax.ShapeDtypeStruct((own_rows, width), F32), jax.ShapeDtypeStruct((own_rows, width), F32),
        ),
        in_specs=[ANY] * 6 + [VMEM],
        out_specs=[ANY] * 4 + [VMEM] * 2,
        scratch_shapes=[
            pltpu.VMEM((rows, width), BF16),
            pltpu.VMEM(mixed.shape, BF16),
            pltpu.VMEM(wo.shape, BF16),
            pltpu.VMEM(w_wide.shape, BF16),
            pltpu.VMEM((hidden, width), BF16),
            pltpu.VMEM((rows, width), BF16),
            pltpu.VMEM((block, width), BF16),
            pltpu.VMEM((rows, width), BF16),
            pltpu.VMEM((2, rows, hidden), F32),
            pltpu.VMEM((rows, hidden), BF16),
            pltpu.VMEM((rows, 2 * hidden), BF16),
            pltpu.VMEM((block, width), F32),
            pltpu.VMEM((2, 2, 2, own_rows, width), BF16),
            pltpu.VMEM((hidden, width), BF16),
            pltpu.VMEM((width, early), BF16),
            pltpu.VMEM((width, last), BF16),
        ]
        + scatter_shapes(own_rows, width, "both")
        + [
            pltpu.SemaphoreType.DMA((Scatter.COPIES + Gather.COPIES,)),
            pltpu.SemaphoreType.DMA((Scatter.COPIES + Gather.COPIES,)),
            pltpu.SemaphoreType.DMA((12,)),
        ],
        compiler_params=pltpu.CompilerParams(
            collective_id=2, has_side_effects=True, vmem_limit_bytes=60 * 1024 * 1024
        ),
        name="feed",
    )(tok, mixed, wo, w_wide, w_down, dy, gains)


HOP = 2
LAG = 3
UNITS = 4
ORDER = "both"


class GradSum:
    RED, LEFT, RIGHT, HAND, OVER, HOME, INTO = range(7)

    def __init__(self, team, kinds, red_recv, fin_recv, hand_recvs, bulk):
        self.team, self.kinds = team, kinds
        self.red_recv, self.fin_recv, self.hand_recvs, self.bulk = red_recv, fin_recv, hand_recvs, bulk
        self.opposite = team.member(lax.rem(team.p + team.F, team.B * team.F))
        self.low, self.high = team.T // 2 - 1, team.T // 2

    @staticmethod
    def steps(kinds, T):
        return max(first + rows // step for rows, step, first in kinds) + HOP * T + LAG

    def remote(self, src, dst, send_sem, recv_sem, device):
        return pltpu.make_async_remote_copy(
            src_ref=src, dst_ref=dst, send_sem=send_sem, recv_sem=recv_sem, device_id=device, device_id_type=MESH
        )

    def where(self, k, c):
        g, step, how = self.kinds[k][0], self.kinds[k][4], self.kinds[k][6]
        if how != "rows":
            return pl.ds(pl.multiple_of(c * step, 16), step), None, None
        F = self.team.F
        turn = lax.rem(c, F)
        to = lax.rem(turn, 2) * (F // 2) + lax.div(turn, 2)
        row = lax.div(c, F) * step
        return pl.ds(pl.multiple_of(to * (g.shape[0] // F) + row, 16), step), to, row

    def spare(self, k, c):
        step = self.kinds[k][4]
        return pl.ds(pl.multiple_of(lax.div(c, 2) * step, 16), step)

    def reduce(self, k, c, i, root):
        g, land, land2 = self.kinds[k][:3]
        team = self.team
        t, T = team.t, team.T
        at, _, _ = self.where(k, c)
        red = self.bulk.at[self.RED, k, 0]

        def inward(side, dst):
            to = team.other_team(t + 1 - 2 * side)
            self.remote(g.at[at], dst, red, self.red_recv.at[side, i], to).start()

        def add():
            g[at, :] = (wide(g[at, :]) + wide(land[at, :])).astype(BF16)

        @pl.when(t < root)
        def _():
            @pl.when(t > 0)
            def _():
                self.remote(g.at[at], land.at[at], red, self.red_recv.at[0, i], team.other_team(t)).wait_recv()
                add()

            inward(0, land.at[at])

        @pl.when(t > root)
        def _():
            @pl.when(t < T - 1)
            def _():
                self.remote(g.at[at], land.at[at], red, self.red_recv.at[1, i], team.other_team(t)).wait_recv()
                add()

            @pl.when(t - 1 == root)
            def _():
                inward(1, land2.at[self.spare(k, c)])

            @pl.when(t - 1 != root)
            def _():
                inward(1, land.at[at])

    def finish(self, k, c, i, root):
        g, land, land2, out, step, first, how = self.kinds[k]
        team, bulk = self.team, self.bulk
        B, F, T, t, y, f = team.B, team.F, team.T, team.t, team.y, team.f
        at, to, row = self.where(k, c)
        red = bulk.at[self.RED, k, 0]

        def outward(side):
            to_team = team.other_team(t - 1 + 2 * side)
            sem = bulk.at[self.RIGHT if side else self.LEFT, k, 0]
            return self.remote(land.at[at], land.at[at], sem, self.fin_recv.at[i], to_team)

        @pl.when(t == root)
        def _():
            total = wide(g[at, :])
            if self.low > 0:
                self.remote(g.at[at], land.at[at], red, self.red_recv.at[0, i], team.other_team(t)).wait_recv()
                total = total + wide(land[at, :])
                self.remote(g.at[at], land2.at[self.spare(k, c)], red, self.red_recv.at[1, i],
                            team.other_team(t)).wait_recv()
                total = total + wide(land2[self.spare(k, c), :])
            land[at, :] = total.astype(BF16)

        @pl.when(t != root)
        def _():
            outward(0).wait_recv()

        @pl.when((t <= root) & (t > 0))
        def _():
            outward(0).start()

        @pl.when((t >= root) & (t < T - 1))
        def _():
            outward(1).start()

        if how == "rows":
            dst = out.at[f * B + y, pl.ds(pl.multiple_of(row, 16), step)]

            @pl.when(to == f)
            def _():
                pltpu.make_async_copy(land.at[at], dst, bulk.at[self.HOME, k, 0]).start()
                if B == 2:
                    self.remote(land.at[at], dst, bulk.at[self.OVER, k, 0], bulk.at[self.INTO, k, 0],
                                self.opposite).start()

            @pl.when(to != f)
            def _():
                self.remote(land.at[at], dst, bulk.at[self.HAND, k, 0], self.hand_recvs[k].at[f, lax.div(row, step)],
                            team.same_row(to)).start()
        elif how == "stay":
            dst = out.at[y, at]
            pltpu.make_async_copy(land.at[at], dst, bulk.at[self.HOME, k, 0]).start()
            if B == 2:
                self.remote(land.at[at], dst, bulk.at[self.OVER, k, 0], bulk.at[self.INTO, k, 0],
                            self.opposite).start()
        else:
            for index in range(F):
                src = land.at[pl.ds(16 * index, 16)]
                for line in range(B):

                    @pl.when(team.p == line * F + index)
                    def _():
                        pltpu.make_async_copy(src, out.at[team.p], bulk.at[self.HOME, k, 0]).start()

                    @pl.when(team.p != line * F + index)
                    def _():
                        self.remote(src, out.at[team.p], bulk.at[self.HAND, k, 0], bulk.at[self.INTO, k, 0],
                                    (t * B + line, index)).start()

    def pass_over(self, k, c, i, root):
        g, land, land2, out, step, first, how = self.kinds[k]
        if how != "rows":
            return
        team = self.team
        at, to, row = self.where(k, c)

        @pl.when(to == team.f)
        def _():
            for d in range(1, team.F):
                source = lax.rem(team.f + d, team.F)
                ref = out.at[source * team.B + team.y, pl.ds(pl.multiple_of(row, 16), step)]
                self.remote(land.at[at], ref, self.bulk.at[self.HAND, k, 0],
                            self.hand_recvs[k].at[source, lax.div(row, step)], team.same_row(team.f)).wait_recv()
                if team.B == 2:
                    self.remote(ref, ref, self.bulk.at[self.OVER, k, 1], self.bulk.at[self.INTO, k, 0],
                                self.opposite).start()

    def each(self, i, body):
        root = self.low + lax.rem(lax.max(i, 0), 2)
        for k, (g, land, land2, out, step, first, how) in enumerate(self.kinds):
            count = g.shape[0] // step
            pl.when((i >= first) & (i < first + count))(functools.partial(body, k, i - first, i, root))

    def step(self, s):
        T, t = self.team.T, self.team.t
        self.each(s - HOP * lax.min(t, T - 1 - t), self.reduce)
        for parity in range(2):
            root = self.low + parity
            distance = jnp.where(t < root, root - t, t - root)
            i = s - HOP * (T // 2 + distance)
            for wait, body in ((0, self.finish), (LAG, self.pass_over)):
                j = i - wait
                pl.when((j >= 0) & (lax.rem(lax.max(j, 0), 2) == parity))(functools.partial(self.each, j, body))

    def drain(self, ref, sem):
        pltpu.make_async_copy(ref, ref, sem).wait()

    def end(self):
        bulk, B, F, T, t = self.bulk, self.team.B, self.team.F, self.team.T, self.team.t
        low, high = self.low, self.high
        for k, (g, land, land2, out, step, first, how) in enumerate(self.kinds):
            rows = g.shape[0]
            some = lambda n: g.at[pl.ds(0, n)]
            count = rows // step
            even = (count + 1 - first % 2) // 2 * step
            odd = rows - even

            def drain_some(condition, n, which):
                if n:

                    @pl.when(condition)
                    def _():
                        self.drain(some(n), bulk.at[which, k, 0])

            drain_some((t != low) & (t != high), rows, self.RED)
            drain_some(t == low, odd, self.RED)
            drain_some(t == high, even, self.RED)
            drain_some((t > 0) & (t <= low), rows, self.LEFT)
            drain_some(t == high, odd, self.LEFT)
            drain_some((t < T - 1) & (t >= high), rows, self.RIGHT)
            drain_some(t == low, even, self.RIGHT)
            if how == "rows":
                shard = rows // F
                self.drain(some(rows - shard), bulk.at[self.HAND, k, 0])
                self.drain(some(shard), bulk.at[self.HOME, k, 0])
                if B == 2:
                    self.drain(some(shard), bulk.at[self.OVER, k, 0])
                    self.drain(some(rows - shard), bulk.at[self.OVER, k, 1])
                    self.drain(g, bulk.at[self.INTO, k, 0])
            elif how == "stay":
                self.drain(g, bulk.at[self.HOME, k, 0])
                if B == 2:
                    self.drain(g, bulk.at[self.OVER, k, 0])
                    self.drain(g, bulk.at[self.INTO, k, 0])
            else:
                others = out.at[pl.ds(0, B * F - 1)]
                self.drain(out.at[0], bulk.at[self.HOME, k, 0])
                self.drain(others, bulk.at[self.HAND, k, 0])
                self.drain(others, bulk.at[self.INTO, k, 0])


def first_steps(dims):
    at = dict(scatter1=3, scatter2=12, resid=18, relay=24, heads=30, own_wo=30 + UNITS)
    at["attention"] = at["own_wo"] + 1
    at["keys"] = at["attention"] + 2 * GROUP * dims[2] + 1
    at["turn"] = at["keys"] + 1
    at["normed"] = at["turn"] + UNITS
    at["products"] = at["normed"] + 2
    at["again1"] = at["products"] + 3
    at["again2"] = at["again1"] + 6
    at["tokens"] = at["again2"] + 6
    return at


def early_lanes(hidden):
    return 2 * hidden // LANES * LANES


def grad_kinds(dims, depth, hidden):
    at = first_steps(dims)
    early = early_lanes(hidden)
    kinds, place = [], 0
    for rows, width, step, ready, how in (
        (hidden, depth, 32, 0, "stay"),
        (depth, early, 32, 0, "rows"),
        (QW, depth, 48, at["own_wo"] + 1, "stay"),
        (depth, 2 * hidden - early + QW + 2 * HEAD_SIZE, 192, at["products"] + 3, "rows"),
        (16 * dims[1], max(depth // dims[1], LANES), 16 * dims[1], at["tokens"] + 1, "gain"),
    ):
        place = max(place, ready)
        kinds.append((rows, width, step, place, how))
        place += rows // step
    return kinds


def back_kernel(dims, kinds, steps, grad_hidden, g_down, g_wide, g_last, resid, tokens, cotangent, gains, acc_in, qx_in,
                kv_all, spans, heads_in, cosine_in, sine_in, wo, wqkv, normed,
                out_down, out_wide, out_wo, out_last, out_gains, tokens_grad,
                xs, own_down, own_wide, own_gwo, own_last, own_gains,
                land_down, land_wide, land_wo, land_last, land_gains,
                also_down, also_wide, also_wo, also_last, also_gains,
                grad_resid, attn_own, big, dox, mixed, dq, dkv, kv_in, dkv_sum, turned, small, kx, vx, dk, dv, wq_in, own_wo,
                acc, qx, heads, cosine, sine, *rest):
    count = len(scatter_parts(resid.shape[-1], ORDER)) * 4 + 1
    scratch1, rest = rest[:count], rest[count:]
    send, recv, line_send, line_recv, red_recv, fin_recv, hand_wide, hand_last, bulk, local = rest
    team = Team(*dims)
    B, F, T = dims
    t, p = team.t, team.p
    at = first_steps(dims)
    own_rows, width = resid.shape
    rows = qx.shape[1]
    part = rows // 2
    small_block = rows // UNITS
    depth = width // F
    sems = Sems(send, recv)
    loads = [
        pltpu.make_async_copy(src, dst, local.at[i])
        for i, (src, dst) in enumerate(
            [(grad_hidden, xs), (g_down, own_down), (g_wide, own_wide), (g_last, own_last), (wqkv, wq_in),
             (wo.at[pl.ds(pl.multiple_of(team.y * QW, 16), QW)], own_wo), (acc_in, acc), (qx_in, qx),
             (heads_in, heads), (cosine_in, cosine), (sine_in, sine)]
        )
    ]
    for load in loads:
        load.start()
    own_gains[...] = jnp.zeros_like(own_gains)
    greet(team_peers(team) + line_peers(team))
    loads[0].wait()
    scatter = Scatter(sems, team, xs, scratch1, ORDER)
    scatter.begin()
    again = Scatter(sems, team, xs, scratch1, ORDER)
    half = own_rows // 2
    gather = Gather(
        sems, p, B * F, team.member, attn_own,
        lambda i: big.at[pl.ds(pl.multiple_of(i * own_rows, 16), own_rows)],
        lambda i, k: big.at[pl.ds(pl.multiple_of(i * own_rows + k * half, 16), half)],
    )
    sums = GradSum(
        team,
        [
            (own, land, also, out) + kind[2:]
            for own, land, also, out, kind in zip(
                (own_down, own_wide, own_gwo, own_last, own_gains),
                (land_down, land_wide, land_wo, land_last, land_gains),
                (also_down, also_wide, also_wo, also_last, also_gains),
                (out_down, out_wide, out_wo, out_last, out_gains),
                kinds,
            )
        ],
        red_recv, fin_recv, [None, hand_wide, None, hand_last, None], bulk,
    )
    loads[1].wait()
    gain_attn, gain_ffn = gains[0:1, :], gains[1:2, :]
    gain_q, gain_k = gains[2:3, 0:HEAD_SIZE], gains[3:4, 0:HEAD_SIZE]
    home = pltpu.make_async_copy(attn_own, big.at[pl.ds(pl.multiple_of(p * own_rows, 16), own_rows)], local.at[11])
    fetch = pltpu.make_async_copy(normed, big, local.at[12])

    def resid_phase():
        def store(columns, total):
            grad_resid[:, columns] = total

        scatter.end(store)
        term = jnp.zeros((1, width), F32)
        for r in range(0, own_rows, 32):
            here = slice(r, r + 32)
            unit, factor = unit_and_factor(resid[here, :])
            upstream = grad_resid[here, :]
            term = term + jnp.sum(upstream * unit, 0, keepdims=True)
            total = wide(cotangent[here, :]) + norm_back(upstream, unit, factor, gain_ffn)
            grad_resid[here, :] = total
            attn_own[here, :] = total.astype(BF16)
        small[1:2, :] = term
        home.start()
        gather.begin()

    def heads_phase():
        gather.end()
        home.wait()

    def heads_unit(r):
        lane = lane_ids(small_block)
        here = pl.ds(pl.multiple_of(r * small_block, small_block), small_block)
        grad = dot_last(big[here, :], own_wo[...]).astype(BF16)
        for h in range(GROUP):
            sums_h = acc[h, here, :]
            total = pltpu.roll(sums_h, HEAD_SIZE, 1)
            out = sums_h / total
            mixed[here, h * HEAD_SIZE : (h + 1) * HEAD_SIZE] = out[:, :HEAD_SIZE].astype(BF16)
            do = wide(grad[:, h * HEAD_SIZE : (h + 1) * HEAD_SIZE])
            do = jnp.concatenate([do, jnp.zeros_like(do)], 1)
            delta = -jnp.sum(jnp.where(lane < HEAD_SIZE, do * out, 0.0), 1, keepdims=True)

            def put(x, first, value):
                for i in range(3):
                    x = jnp.where(lane == first + i, wide(value.astype(BF16)), x)
                    value = value - wide(value.astype(BF16))
                return x

            dox[h, here, :] = put(do, HEAD_SIZE, delta).astype(BF16)
            log_sum = -jnp.log(jnp.where(lane < HEAD_SIZE, total, sums_h))
            qx[h, here, :] = put(wide(qx[h, here, :]), HEAD_SIZE + NDOCS, log_sum).astype(BF16)

    def own_wo_phase():
        own_gwo[...] = lax.dot_general(
            mixed[...], big[...], (((0,), (0,)), ((), ())), preferred_element_type=F32
        ).astype(BF16)
        dq[...] = jnp.zeros_like(dq)

    causal = lax.broadcasted_iota(jnp.int32, (part, part), 0) <= lax.broadcasted_iota(jnp.int32, (part, part), 1)

    def piece(h, q_rows, k_rows, masked):
        q = qx[h, q_rows, :]
        do = dox[h, q_rows, :]
        keys = kx[k_rows, :]
        weights = jnp.exp(dot_last(keys, q))
        if masked:
            weights = jnp.where(causal, weights, 0.0)
        dscore = (weights * dot_last(vx[k_rows, :], do)).astype(BF16)
        dv[...] += jnp.dot(weights.astype(BF16), do, preferred_element_type=F32)
        dk[...] += jnp.dot(dscore, q, preferred_element_type=F32)
        dq[h, q_rows, :] += lax.dot_general(dscore, keys, (((0,), (0,)), ((), ())), preferred_element_type=F32)

    def line_copy(owner, source):
        return pltpu.make_async_remote_copy(
            src_ref=dkv.at[owner], dst_ref=dkv.at[source], send_sem=line_send.at[owner],
            recv_sem=line_recv.at[source], device_id=team.other_team(owner), device_id_type=MESH,
        )

    def fetch_keys(source):
        slot = lax.rem(source, 2)
        return pltpu.make_async_copy(kv_all.at[source], kv_in.at[slot], local.at[13 + slot])

    fetch_keys(t * 0).start()

    def attention_unit(source, k, h):
        @pl.when((k == 0) & (h == 0))
        def _():
            fetch_keys(source).wait()

            @pl.when(source < t)
            def _():
                fetch_keys(source + 1).start()

            widen_keys(kv_in[lax.rem(source, 2)], spans, source * rows, kx, vx)

        @pl.when(h == 0)
        def _():
            dk[...] = jnp.zeros_like(dk)
            dv[...] = jnp.zeros_like(dv)

        k_rows = pl.ds(pl.multiple_of(k * part, part), part)

        @pl.when(source < t)
        def _():
            for q in range(2):
                piece(h, slice(q * part, (q + 1) * part), k_rows, False)

        @pl.when(source == t)
        def _():
            for diagonal in range(2):

                @pl.when(k == diagonal)
                def _():
                    for q in range(diagonal, 2):
                        piece(h, slice(q * part, (q + 1) * part), slice(diagonal * part, (diagonal + 1) * part),
                              q == diagonal)

        @pl.when(h == GROUP - 1)
        def _():
            dkv[source, k_rows, :] = jnp.where(
                lane_ids(part) < HEAD_SIZE, dk[...], pltpu.roll(dv[...], HEAD_SIZE, 1)
            ).astype(BF16)

            @pl.when((k == 1) & (source < t))
            def _():
                line_copy(source, t).start()

    def keys_phase():
        fetch.start()
        dkv_sum[...] = wide(dkv[t])
        for d in range(1, T):

            @pl.when(t + d < T)
            def _():
                line_copy(t, t + d).wait_recv()
                dkv_sum[...] += wide(dkv[t + d])

        small[2:4, :] = jnp.zeros((2, width), F32)

    def turn_unit(r):
        here = pl.ds(pl.multiple_of(r * small_block, small_block), small_block)
        cos, sin = cosine[here, 0:HEAD_SIZE], sine[here, 0:HEAD_SIZE]
        q_term = jnp.zeros((1, HEAD_SIZE), F32)
        for h in range(GROUP + 1):
            if h < GROUP:
                u, gain = dq[h, here, 0:HEAD_SIZE] * HEAD_SIZE ** (-0.5), gain_q
            else:
                u, gain = dkv_sum[here, 0:HEAD_SIZE], gain_k
            u = u * cos - jnp.concatenate([u[:, HEAD_SIZE // 2 :], u[:, : HEAD_SIZE // 2]], 1) * sin
            unit, factor = unit_and_factor(heads[h // 2, here, h % 2 * HEAD_SIZE : (h % 2 + 1) * HEAD_SIZE])
            term = jnp.sum(u * unit, 0, keepdims=True)
            if h < GROUP:
                q_term = q_term + term
            else:
                small[3:4, 0:HEAD_SIZE] += term
            turned[here, h * HEAD_SIZE : (h + 1) * HEAD_SIZE] = norm_back(u, unit, factor, gain).astype(BF16)
        small[2:3, 0:HEAD_SIZE] += q_term
        h = GROUP + 1
        turned[here, h * HEAD_SIZE : (h + 1) * HEAD_SIZE] = dkv_sum[here, HEAD_SIZE : 2 * HEAD_SIZE].astype(BF16)

    def normed_unit(i):
        for m in range(4):
            here = pl.ds(pl.multiple_of((4 * i + m) * own_rows, own_rows), own_rows)
            xs[i, m // 2, m % 2] = dot_last(turned[here, :], wq_in[...]).astype(BF16)

    def products_phase():
        again.begin()
        fetch.wait()

    def products_unit(i):
        for j in range(2):
            r = pl.multiple_of((2 * i + j) * (width // 6), LANES)
            here = pl.ds(r, width // 6)
            own_last[here, own_last.shape[1] - turned.shape[1] :] = lax.dot_general(
                big[:, here], turned[...], (((0,), (0,)), ((), ())), preferred_element_type=F32
            ).astype(BF16)

    def tokens_phase():
        def store(columns, total):
            tokens_grad[:, columns] = total

        again.end(store)
        term = jnp.zeros((1, width), F32)
        for r in range(0, own_rows, 32):
            here = slice(r, r + 32)
            unit, factor = unit_and_factor(wide(tokens[here, :]))
            upstream = tokens_grad[here, :]
            term = term + jnp.sum(upstream * unit, 0, keepdims=True)
            tokens_grad[here, :] = grad_resid[here, :] + norm_back(upstream, unit, factor, gain_attn)
        small[0:1, :] = term
        lanes = own_gains.shape[1]
        row = lax.broadcasted_iota(jnp.int32, (16, lanes), 0)

        def cut(i, first, count):
            value = small[i : i + 1, first : first + count]
            if count < lanes:
                value = jnp.concatenate([value, jnp.zeros((1, lanes - count), F32)], 1)
            return jnp.where(row == i, jnp.broadcast_to(value, (16, lanes)), 0.0)

        for i in range(F):
            few = HEAD_SIZE // F
            own_gains[16 * i : 16 * i + 16, :] = (
                cut(0, i * depth, depth) + cut(1, i * depth, depth) + cut(2, i * few, few) + cut(3, i * few, few)
            ).astype(BF16)

    def late_loads():
        for load in loads[2:]:
            load.wait()

    @pl.loop(0, steps)
    def _(s):
        pl.when(s == at["scatter1"])(late_loads)
        sums.step(s)
        for name, body in (
            ("scatter1", scatter.relay), ("scatter2", scatter.relay_again), ("resid", resid_phase),
            ("relay", gather.relay), ("heads", heads_phase), ("own_wo", own_wo_phase), ("keys", keys_phase),
            ("products", products_phase), ("again1", again.relay), ("again2", again.relay_again),
            ("tokens", tokens_phase),
        ):
            pl.when(s == at[name])(body)
        for name, count, body in (
            ("heads", UNITS, heads_unit), ("turn", UNITS, turn_unit), ("normed", 2, normed_unit),
            ("products", 3, products_unit),
        ):
            i = s - at[name]
            pl.when((i >= 0) & (i < count))(functools.partial(body, i))
        unit = s - at["attention"]
        source = lax.div(unit, 2 * GROUP)

        @pl.when((unit >= 0) & (source <= t))
        def _():
            attention_unit(source, lax.rem(lax.div(unit, GROUP), 2), lax.rem(unit, GROUP))

    for d in range(1, T):

        @pl.when(t - d >= 0)
        def _():
            line_copy(t - d, t).wait_send()

    sums.end()


def backward(dims, grad_hidden, g_down, g_wide, g_last, resid, tokens, cotangent, gains, acc, qx, kv_all, spans,
             heads, cosine, sine, wo, wqkv, normed):
    B, F, T = dims
    own_rows, width = resid.shape
    rows = qx.shape[1]
    part = rows // 2
    hidden = g_down.shape[0]
    n = B * F
    kinds = grad_kinds(dims, width, hidden)
    steps = max(
        GradSum.steps([(rows_, step, first) for rows_, _, step, first, _ in kinds], T), first_steps(dims)["tokens"] + 1
    )
    positions = max(first + rows_ // step for rows_, _, step, first, _ in kinds)
    outs = []
    for rows_, wide_, step, first, how in kinds:
        if how == "rows":
            shape = (n, rows_ // F, wide_)
        elif how == "stay":
            shape = (B, rows_, wide_)
        else:
            shape = (n, 16, wide_)
        outs.append(jax.ShapeDtypeStruct(shape, BF16))
    outs.append(jax.ShapeDtypeStruct((own_rows, width), F32))
    eight = (2, 2, 2, own_rows, width)
    hands = [pltpu.SemaphoreType.DMA((F, kinds[k][0] // F // kinds[k][2])) for k in (1, 3)]
    copies = 2 * Scatter.COPIES + Gather.COPIES
    return pl.pallas_call(
        functools.partial(back_kernel, dims, kinds, steps),
        out_shape=outs,
        in_specs=[ANY] * 4 + [VMEM] * 4 + [ANY] * 3 + [VMEM] + [ANY] * 6,
        out_specs=[ANY] * 5 + [VMEM],
        scratch_shapes=[pltpu.VMEM(eight, BF16)]
        + [pltpu.VMEM((kind[0], kind[1]), BF16) for kind in kinds] * 2
        + [pltpu.VMEM(((kind[0] // kind[2] + 1) // 2 * kind[2], kind[1]), BF16) for kind in kinds]
        + [
            pltpu.VMEM((own_rows, width), F32),
            pltpu.VMEM((own_rows, width), BF16),
            pltpu.VMEM((rows, width), BF16),
            pltpu.VMEM(qx.shape, BF16),
            pltpu.VMEM((rows, QW), BF16),
            pltpu.VMEM(qx.shape, F32),
            pltpu.VMEM(kv_all.shape, BF16),
            pltpu.VMEM((2,) + kv_all.shape[1:], BF16),
            pltpu.VMEM((rows, LANES), F32),
            pltpu.VMEM((rows, QW + 2 * HEAD_SIZE), BF16),
            pltpu.VMEM((8, width), F32),
            pltpu.VMEM((rows, LANES), BF16),
            pltpu.VMEM((rows, LANES), BF16),
            pltpu.VMEM((part, LANES), F32),
            pltpu.VMEM((part, LANES), F32),
            pltpu.VMEM(wqkv.shape, BF16),
            pltpu.VMEM((QW, width), BF16),
            pltpu.VMEM(acc.shape, F32),
            pltpu.VMEM(qx.shape, BF16),
            pltpu.VMEM(heads.shape, F32),
            pltpu.VMEM(cosine.shape, F32),
            pltpu.VMEM(sine.shape, F32),
        ]
        + scatter_shapes(own_rows, width, ORDER)
        + [
            pltpu.SemaphoreType.DMA((copies,)),
            pltpu.SemaphoreType.DMA((copies,)),
            pltpu.SemaphoreType.DMA((T,)),
            pltpu.SemaphoreType.DMA((T,)),
            pltpu.SemaphoreType.DMA((2, positions)),
            pltpu.SemaphoreType.DMA((positions,)),
            *hands,
            pltpu.SemaphoreType.DMA((7, len(kinds), 2)),
            pltpu.SemaphoreType.DMA((15,)),
        ],
        compiler_params=pltpu.CompilerParams(
            collective_id=3, has_side_effects=True, vmem_limit_bytes=60 * 1024 * 1024
        ),
        name="backward",
    )(grad_hidden.reshape(eight), g_down, g_wide, g_last, resid, tokens, cotangent, gains, acc, qx,
      kv_all, spans, heads, cosine, sine, wo, wqkv, normed)


def place_kernel(n, hidden, both, last, down, wo, layer, tokens, gains, gate_out, up_out, wq_out, wk_out, wv_out, down_out,
                 wo_out, layer_out, tokens_out, *gain_outs):
    early = both.shape[-1]
    tail = 2 * hidden - early
    for q in range(n):
        block, rest = wide(both[q]), wide(last[q])
        gate_out[:, q * hidden : (q + 1) * hidden] = block[:, :hidden]
        up_out[:, q * hidden : (q + 1) * hidden] = jnp.concatenate([block[:, hidden:], rest[:, :tail]], 1)
        wq_out[:, q * QW : (q + 1) * QW] = rest[:, tail : tail + QW]
        wk_out[:, q * HEAD_SIZE : (q + 1) * HEAD_SIZE] = rest[:, tail + QW : tail + QW + HEAD_SIZE]
        wv_out[:, q * HEAD_SIZE : (q + 1) * HEAD_SIZE] = rest[:, tail + QW + HEAD_SIZE :]
    down_out[...] = wide(down[...])
    wo_out[...] = wide(wo[...])

    @pl.when(pl.program_id(0) == 0)
    def _():
        layer_out[...] = layer[...].astype(BF16)
        tokens_out[...] = tokens[...].astype(BF16)
        total = wide(gains[0])
        for i in range(1, n):
            total = total + wide(gains[i])
        for i, gain_out in enumerate(gain_outs):
            gain_out[...] = total[i, : gain_out.shape[0]]


def place(hidden, both, last, down, wo, layer, tokens, gains):
    n, depth, early = both.shape
    width = down.shape[-1]
    down, wo = down.reshape(-1, width), wo.reshape(-1, width)
    step = 64
    count = depth // step
    many = lambda a: pl.BlockSpec((n, step, a.shape[-1]), lambda i: (0, i, 0))
    cut = lambda a: pl.BlockSpec((a.shape[0] // count, width), lambda i: (i, 0))
    out = lambda w: pl.BlockSpec((step, w), lambda i: (i, 0))
    whole = lambda dims: pl.BlockSpec(dims, lambda i: (0,) * len(dims))
    shape = lambda r, w: jax.ShapeDtypeStruct((r, w), F32)
    wq, wk = QW * n, HEAD_SIZE * n
    sizes = [depth, depth, HEAD_SIZE * depth // width, HEAD_SIZE * depth // width]
    return pl.pallas_call(
        functools.partial(place_kernel, n, hidden),
        grid=(count,),
        out_shape=(
            shape(depth, n * hidden), shape(depth, n * hidden), shape(depth, wq), shape(depth, wk), shape(depth, wk),
            shape(down.shape[0], width), shape(wo.shape[0], width), jax.ShapeDtypeStruct(layer.shape, BF16),
            jax.ShapeDtypeStruct(tokens.shape, BF16), *[jax.ShapeDtypeStruct((size,), F32) for size in sizes],
        ),
        in_specs=[many(both), many(last), cut(down), cut(wo), whole(layer.shape), whole(tokens.shape),
                  whole(gains.shape)],
        out_specs=[out(n * hidden), out(n * hidden), out(wq), out(wk), out(wk), cut(down), cut(wo),
                   whole(layer.shape), whole(tokens.shape), *[whole((size,)) for size in sizes]],
        compiler_params=pltpu.CompilerParams(vmem_limit_bytes=VMEM_LIMIT),
        name="place",
    )(both, last, down, wo, layer, tokens, gains)


def norm_back(upstream, unit_rows, factor, gain_row):
    lifted = upstream * gain_row
    return factor * (lifted - unit_rows * jnp.mean(lifted * unit_rows, -1, keepdims=True))


def on_device(
    tokens, lengths, wq, wk, wv, wo, w_gate, w_up, w_down, attn_gain, ffn_gain, q_gain, key_norm_gain, cotangent
):
    F = lax.axis_size("fsdp")
    B = KEY_VALUE_HEADS // F
    T = lax.axis_size("ctx") // B
    dims = (B, F, T)
    own_rows, width = tokens.shape
    rows = own_rows * KEY_VALUE_HEADS
    depth = width // F
    t = lax.axis_index("ctx") // B
    hidden = w_down.shape[0] // B

    lanes = max(depth, LANES)
    line = lambda a: jnp.pad(a, (0, lanes - a.shape[0]))
    gains = jnp.concatenate([line(attn_gain), line(ffn_gain), line(q_gain), line(key_norm_gain)])
    gains = jnp.pad(gains.reshape(4, lanes), ((0, 12), (0, 0)))
    half = HEAD_SIZE // 2
    freq = np.power(np.float32(ROPE_BASE), -(np.arange(LANES, dtype=np.float32) % half * np.float32(2.0) / HEAD_SIZE))
    freq = jnp.asarray(np.broadcast_to(freq, (8, LANES))[:1], F32)
    (cosine, sine, spans, tok_full, wqkv, normed, heads, qx, kv_all, acc, mixed, wo_full, wide_w, all_gains) = front(
        dims, tokens, wq, wk, wv, wo, w_gate, w_up, gains, freq, lengths
    )
    grad_hidden, g_down, g_wide, g_last, own_resid, layer_out = feed(
        dims, tok_full, mixed, wo_full.reshape(-1, width), wide_w.reshape(width, 2 * hidden), w_down,
        cotangent, all_gains,
    )
    out_down, out_wide, out_wo, out_last, out_gains, tokens_grad = backward(
        dims, grad_hidden, g_down, g_wide, g_last, own_resid, tokens, cotangent, all_gains, acc, qx, kv_all,
        spans, heads, cosine, sine, wo, wqkv, normed,
    )
    (gate_grad, up_grad, wq_grad, wk_grad, wv_grad, down_grad, wo_grad, layer_out, tokens_grad, *gain_grads) = place(
        hidden, out_wide, out_last, out_down, out_wo, layer_out, tokens_grad, out_gains
    )
    return (
        layer_out, tokens_grad, wq_grad, wk_grad, wv_grad, wo_grad, gate_grad, up_grad,
        down_grad, *gain_grads,
    )


def solution(mesh):
    rows = P(("ctx", "fsdp"), None)
    shard = P("fsdp", None)
    gain = P("fsdp")
    return jax.shard_map(
        on_device,
        mesh=mesh,
        in_specs=(rows, P(), shard, shard, shard, shard, shard, shard, shard, gain, gain, gain, gain, rows),
        out_specs=(rows, rows, shard, shard, shard, shard, shard, shard, shard, gain, gain, gain, gain),
        check_vma=False,
    )
```

```python
import functools

import jax
import jax.numpy as jnp
import numpy as np
from jax import lax
from jax.experimental import pallas as pl
from jax.experimental.pallas import tpu as pltpu
from jax.sharding import PartitionSpec as P

QUERY_HEADS = 24
KEY_VALUE_HEADS = 8
HEAD_SIZE = 64
GROUP = QUERY_HEADS // KEY_VALUE_HEADS
QW = GROUP * HEAD_SIZE
LANES = 128
NDOCS = 4

EPSILON = 1e-05
ROPE_BASE = 1000000.0
APART = 16384.0

MESH = pl.DeviceIdType.MESH
F32 = jnp.float32
BF16 = jnp.bfloat16
ANY = pl.BlockSpec(memory_space=pl.ANY)
VMEM = pl.BlockSpec(memory_space=pltpu.VMEM)
VMEM_LIMIT = 56 * 1024 * 1024


class Team:
    def __init__(self, B, F, T):
        self.B, self.F, self.T = B, F, T
        ctx, self.f = lax.axis_index("ctx"), lax.axis_index("fsdp")
        self.t, self.y = lax.div(ctx, B), lax.rem(ctx, B)
        self.p = self.y * F + self.f

    def member(self, p):
        return (self.t * self.B + lax.div(p, self.F), lax.rem(p, self.F))

    def same_row(self, f):
        return (self.t * self.B + self.y, f)

    def other_team(self, t):
        return (t * self.B + self.y, self.f)


def flip(p, bit):
    return p + bit * (1 - 2 * lax.rem(lax.div(p, bit), 2))


def bit_of(p, bit):
    return lax.rem(lax.div(p, bit), 2)


class Sems:
    def __init__(self, send, recv):
        self.send, self.recv, self.used = send, recv, 0

    def copy(self, src, dst, device):
        i = self.used
        self.used += 1
        return pltpu.make_async_remote_copy(
            src_ref=src,
            dst_ref=dst,
            send_sem=self.send.at[i],
            recv_sem=self.recv.at[i],
            device_id=device,
            device_id_type=MESH,
        )


def greet(devices):
    barrier = pltpu.get_barrier_semaphore()
    for device in devices:
        pl.semaphore_signal(barrier, inc=1, device_id=device, device_id_type=MESH)
    pl.semaphore_wait(barrier, len(devices))


def team_peers(team):
    n = team.B * team.F
    return [team.member(lax.rem(team.p + d, n)) for d in range(1, n)]


def line_peers(team):
    return [team.other_team(lax.rem(team.t + d, team.T)) for d in range(1, team.T)]


def row_peers(team):
    return [team.same_row(lax.rem(team.f + d, team.F)) for d in range(1, team.F)]


class Gather:
    def __init__(self, sems, me, count, device, own, block, half, order="both"):
        bits = count.bit_length() - 1
        one, two = flip(me, 1), flip(me, 2)
        send = lambda src, dst, to: sems.copy(src, dst, device(to))
        again = lambda ref, to: send(ref, ref, to)
        self.first = [send(own, block(me), flip(me, 1 << k)) for k in range(bits)]
        self.over = [again(block(two), one)]
        self.halves, self.corner = [], []
        if count == 8:
            four = flip(me, 4)
            far = flip(two, 4)
            self.over.append(again(block(four), one))
            if order == "both":
                self.halves = [again(half(two, 0), four), again(half(four, 1), two)]
                self.corner = [again(half(far, 0), one), again(half(far, 1), one)]
            else:
                self.halves = [again(block(two), four)]
                self.corner = [again(block(far), one)]

    def begin(self):
        for copy in self.first:
            copy.start()

    def relay(self):
        self.first[1].wait_recv()
        self.over[0].start()
        if self.halves:
            self.halves[0].start()
            self.first[2].wait_recv()
            for copy in self.halves[1:]:
                copy.start()
            self.over[1].start()

    def end(self):
        for arrived, onward in zip(self.halves, self.corner):
            arrived.wait_recv()
            onward.start()
        self.first[0].wait_recv()
        for copy in self.over + self.corner:
            copy.wait_recv()
        for copy in self.first + self.over + self.halves + self.corner:
            copy.wait_send()

    COPIES = 9


def scatter_parts(width, order):
    if order == "both":
        return [(0, width // 2, 2, 4), (width // 2, width // 2, 4, 2)]
    return [(0, width, 2, 4)]


def scatter_shapes(rows, width, order):
    shapes = [pltpu.VMEM((2, 2, rows, width), BF16)]
    for _, columns, _, _ in scatter_parts(width, order):
        shapes += [pltpu.VMEM((2, rows, columns), BF16)] * 2 + [pltpu.VMEM((rows, columns), BF16)] * 2
    return shapes


def wide(v):
    return v.astype(F32)


class Scatter:
    COPIES = 5

    def __init__(self, sems, team, x, scratch, order):
        self.x, self.r0 = x, scratch[0]
        p = team.p
        self.b = bit_of(p, 1), bit_of(p, 2), bit_of(p, 4)
        send = lambda src, dst, bit: sems.copy(src, dst, team.member(flip(p, bit)))
        self.first = send(x.at[:, :, 1 - self.b[0]], self.r0, 1)
        self.parts = []
        for i, (at, columns, one, two) in enumerate(scatter_parts(x.shape[-1], order)):
            s1, r1, s2, r2 = scratch[1 + 4 * i : 5 + 4 * i]
            self.parts.append((pl.ds(at, columns), one, s1, r1, s2, r2, send(s1, r1, one), send(s2, r2, two)))

    def term(self, b2, b1, columns):
        return wide(self.x[b2, b1, self.b[0], :, columns]) + wide(self.r0[b2, b1, :, columns])

    def begin(self):
        self.first.start()

    def relay(self):
        b0, b1, b2 = self.b
        self.first.wait_recv()
        for columns, one, s1, r1, s2, r2, send1, send2 in self.parts:
            for k in range(2):
                s1[k] = (self.term(k, 1 - b1, columns) if one == 2 else self.term(1 - b2, k, columns)).astype(BF16)
            send1.start()

    def relay_again(self):
        b0, b1, b2 = self.b
        for columns, one, s1, r1, s2, r2, send1, send2 in self.parts:
            send1.wait_recv()
            if one == 2:
                total = self.term(1 - b2, b1, columns) + wide(r1[1 - b2])
            else:
                total = self.term(b2, 1 - b1, columns) + wide(r1[1 - b1])
            s2[...] = total.astype(BF16)
            send2.start()

    def end(self, store):
        b0, b1, b2 = self.b
        for columns, one, s1, r1, s2, r2, send1, send2 in self.parts:
            send2.wait_recv()
            store(columns, self.term(b2, b1, columns) + wide(r1[b2 if one == 2 else b1]) + wide(r2[...]))
        for copy in [self.first] + [copy for part in self.parts for copy in part[6:]]:
            copy.wait_send()


def kernel_params(collective_id):
    return pltpu.CompilerParams(
        collective_id=collective_id, has_side_effects=True, vmem_limit_bytes=VMEM_LIMIT
    )


def unit_and_factor(x):
    factor = lax.rsqrt(jnp.mean(x * x, -1, keepdims=True) + EPSILON)
    return x * factor, factor


def lane_ids(rows):
    return lax.broadcasted_iota(jnp.int32, (rows, LANES), 1)


def inside_document(spans, rows, first_row):
    row = lax.broadcasted_iota(jnp.int32, (rows, LANES), 0) + first_row
    return (row >= spans[0:1, :]) & (row < spans[1:2, :])


def widen_keys(kv, spans, first_row, kx, vx):
    rows = kv.shape[0]
    lane = lane_ids(rows)
    inside = inside_document(spans, rows, first_row)
    both = wide(kv)
    kx[...] = jnp.where(lane < HEAD_SIZE, both, jnp.where(inside, 1.0, 0.0)).astype(BF16)
    vx[...] = jnp.where(lane < HEAD_SIZE, pltpu.roll(both, HEAD_SIZE, 1), 1.0).astype(BF16)


def dot_last(a, b):
    return lax.dot_general(a, b, (((1,), (1,)), ((), ())), preferred_element_type=F32)


def fill_tables(t, lengths, freq, cosine, sine, spans):
    rows = cosine.shape[0]
    ends, total = [], 0
    for d in range(NDOCS):
        total = total + lengths[d]
        ends.append(total)
    lane = lax.broadcasted_iota(jnp.int32, spans.shape, 1)
    row = lax.broadcasted_iota(jnp.int32, spans.shape, 0)
    first, past = jnp.zeros(spans.shape, jnp.int32), jnp.full(spans.shape, 2**30, jnp.int32)
    for d in range(NDOCS):
        first = jnp.where(lane == HEAD_SIZE + d, ends[d] - lengths[d], first)
        past = jnp.where(lane == HEAD_SIZE + d, ends[d], past)
    spans[...] = jnp.where(row == 0, first, past)
    half = HEAD_SIZE // 2
    parts = LANES // half
    few = rows // parts
    shape = (few, LANES)
    token = lax.broadcasted_iota(jnp.int32, shape, 0) + lax.div(lax.broadcasted_iota(jnp.int32, shape, 1), half) * few
    token = token + t * rows
    start = jnp.zeros(shape, jnp.int32)
    for d in range(NDOCS):
        start = jnp.where(token >= ends[d], ends[d], start)
    angles = (token - start).astype(F32) * freq[...]
    cos, sin = jnp.cos(angles), jnp.sin(angles)
    for i in range(parts):
        here, lanes = slice(i * few, (i + 1) * few), slice(i * half, (i + 1) * half)
        cosine[here, :] = jnp.concatenate([cos[:, lanes]] * parts, 1)
        sine[here, :] = jnp.concatenate([-sin[:, lanes], sin[:, lanes]] * (parts // 2), 1)


def front_kernel(dims, tokens, wq, wk, wv, wo, w_gate, w_up, gains, freq, lengths,
                 cosine, sine, spans, tok_full, wqkv, normed, heads, qx, kv_all, acc, mixed, wo_full, wide_full, all_gains,
                 tok, q_in, k_in, v_in, qkv_cut, qkv, gains_in, slab_g, slab_u, cut, norm, kv, kx, vx, packed,
                 send, recv, line_send, line_recv, local):
    team = Team(*dims)
    B, F, T = dims
    t, y, f, p = team.t, team.y, team.f, team.p
    sems = Sems(send, recv)
    own_rows, width = tokens.shape
    rows = own_rows * B * F
    depth = width // F
    part, block = rows // 2, rows // 4
    hidden = cut.shape[-1] // 2
    parity = lax.rem(t, 2)

    def home(src, dst, i):
        copy = pltpu.make_async_copy(src, dst, local.at[i])
        copy.start()
        return copy

    token_rows = lambda i: pl.ds(pl.multiple_of(i * own_rows, 16), own_rows)
    shard_rows = lambda i: pl.ds(pl.multiple_of(i * depth, 16), depth)
    token_load = home(tokens, tok.at[token_rows(p)], 0)
    small_loads = [home(wq, q_in, 1), home(wk, k_in, 2), home(wv, v_in, 3)]
    gain_load = home(gains, gains_in.at[f], 4)
    slab_loads = [home(w_gate, slab_g, 5), home(w_up, slab_u, 6)]
    homes = [home(wo, wo_full.at[f], 7)]
    greet(team_peers(team) + line_peers(team))

    half = own_rows // 2
    gather_tok = Gather(
        sems, p, B * F, team.member, tokens, lambda i: tok.at[token_rows(i)],
        lambda i, k: tok.at[pl.ds(pl.multiple_of(i * own_rows + k * half, 16), half)],
        "tall",
    )
    few = packed.shape[1] // 2

    def gather_half(which):
        return Gather(
            sems, p, B * F, team.member, packed.at[which], lambda i: mixed.at[which, i],
            lambda i, k: mixed.at[which, i, pl.ds(k * few, few)],
            "both" if which else "tall",
        )

    gather_mixed = [gather_half(0), gather_half(1)]
    partners = []
    for m in range(1, F):
        to = f
        for bit in (1, 2, 4):
            if m & bit:
                to = flip(to, bit)
        partners.append(to)
    gain_sends = [sems.copy(gains, gains_in.at[f], team.same_row(to)) for to in partners]
    half_depth = depth // 2
    some = pl.ds(pl.multiple_of(parity * half_depth, 16), half_depth)
    near = team.other_team(t + 1 - 2 * parity)
    some_of = lambda i: pl.ds(pl.multiple_of(i * depth + parity * half_depth, 16), half_depth)
    qkv_sends = [sems.copy(qkv_cut.at[partners[0]], qkv.at[shard_rows(f)], team.same_row(partners[0]))]
    qkv_shares = []
    for to in partners[1:]:
        qkv_sends.append(sems.copy(qkv_cut.at[to, some], qkv.at[some_of(f)], team.same_row(to)))
        qkv_shares.append(sems.copy(qkv.at[some_of(to)], qkv.at[some_of(to)], near))
    wide_near = sems.copy(cut.at[partners[0]], wide_full.at[f], team.same_row(partners[0]))
    wide_sends, wide_shares = [[], []], [[], []]
    quarter = half_depth // 2
    for i in range(2):
        some = pl.ds(pl.multiple_of(parity * half_depth + i * quarter, 16), quarter)
        for to in partners[1:]:
            wide_sends[i].append(sems.copy(cut.at[to, some], wide_full.at[f, some], team.same_row(to)))
            wide_shares[i].append(sems.copy(wide_full.at[to, some], wide_full.at[to, some], near))
    if B == 2 and F == 4:
        one, two = flip(f, 1), flip(f, 2)
        other = team.member(lax.rem(p + F, B * F))
        wo_half = lambda k: pl.ds(pl.multiple_of(k * half_depth, 16), half_depth)
        mine, theirs = wo_half(y), wo_half(1 - y)
        wo_first = [
            sems.copy(wo, wo_full.at[f], team.same_row(one)),
            sems.copy(wo.at[mine], wo_full.at[f, mine], team.same_row(two)),
        ]
        ref = wo_full.at[two, mine]
        wo_relay = [sems.copy(ref, ref, other), sems.copy(ref, ref, team.same_row(one))]
        ref = wo_full.at[two, theirs]
        wo_last = [sems.copy(ref, ref, team.same_row(one))]

    def line_copy(d, source, to, r):
        here = pl.ds(pl.multiple_of(r * block, block), block)
        return pltpu.make_async_remote_copy(
            src_ref=kv.at[here], dst_ref=kv_all.at[source, here], send_sem=line_send.at[d, r],
            recv_sem=line_recv.at[source, r], device_id=team.other_team(to), device_id_type=MESH,
        )

    gather_tok.begin()
    for copy in gain_sends:
        copy.start()
    fill_tables(t, lengths, freq, cosine, sine, spans)
    for load in small_loads:
        load.wait()
    for i in range(F):
        for row in range(B):
            h = i * B + row

            @pl.when(y == row)
            def _():
                qkv_cut[i, :, 0:QW] = q_in[:, h * QW : (h + 1) * QW]
                qkv_cut[i, :, QW : QW + HEAD_SIZE] = k_in[:, h * HEAD_SIZE : (h + 1) * HEAD_SIZE]
                qkv_cut[i, :, QW + HEAD_SIZE : QW + 2 * HEAD_SIZE] = v_in[:, h * HEAD_SIZE : (h + 1) * HEAD_SIZE]

    for copy in qkv_sends:
        copy.start()
    qkv[shard_rows(f), :] = qkv_cut[f]
    for load in slab_loads:
        load.wait()

    @pl.loop(0, depth // 32)
    def _(r):
        here = pl.ds(pl.multiple_of(r * 32, 32), 32)
        for j in range(F):
            for row in range(B):
                q = j * B + row

                @pl.when(y == row)
                def _():
                    cut[j, here, 0:hidden] = slab_g[here, q * hidden : (q + 1) * hidden]
                    cut[j, here, hidden : 2 * hidden] = slab_u[here, q * hidden : (q + 1) * hidden]

    gather_tok.relay()
    for arrived, onward in zip(qkv_sends[1:], qkv_shares):
        arrived.wait_recv()
        onward.start()
    for copy in wide_sends[0] + [wide_near]:
        copy.start()
    if B == 2 and F == 4:
        for copy in wo_first:
            copy.start()
    else:
        gather_wo = Gather(
            sems, f, F, team.same_row, wo, lambda i: wo_full.at[i],
            lambda i, k: wo_full.at[i, pl.ds(k * half_depth, half_depth)],
        )
        gather_wo.begin()
    for copy in wide_sends[1]:
        copy.start()
    homes.append(home(cut.at[f], wide_full.at[f], 9))
    gather_tok.end()
    token_load.wait()
    gain_load.wait()
    for copy in gain_sends:
        copy.wait_recv()
    homes.append(home(tok, tok_full, 11))

    all_gains[...] = jnp.zeros_like(all_gains)
    for i in range(F):
        for k, count in ((0, depth), (1, depth), (2, HEAD_SIZE // F), (3, HEAD_SIZE // F)):
            all_gains[k : k + 1, i * count : (i + 1) * count] = wide(gains_in[i])[k : k + 1, 0:count]
    gain_q, gain_k = all_gains[2:3, 0:HEAD_SIZE], all_gains[3:4, 0:HEAD_SIZE]

    @pl.loop(0, rows // block)
    def _(r):
        here = pl.ds(pl.multiple_of(r * block, block), block)
        unit, factor = unit_and_factor(wide(tok[here, :]))
        norm[here, :] = (unit * all_gains[0:1, :]).astype(BF16)

    for copy in qkv_sends[:1] + qkv_shares:
        copy.wait_recv()
    homes += [home(norm, normed, 12), home(qkv, wqkv, 13)]

    lane = lane_ids(block)
    same_head = lax.div(lax.broadcasted_iota(jnp.int32, (LANES, LANES), 0), HEAD_SIZE) == lax.div(
        lax.broadcasted_iota(jnp.int32, (LANES, LANES), 1), HEAD_SIZE
    )
    same_head = jnp.where(same_head, 1.0, 0.0).astype(BF16)
    gain_pairs = [jnp.concatenate([gain_q, gain_q], 1), jnp.concatenate([gain_q, gain_k], 1)]

    @pl.loop(0, rows // block)
    def _(r):
        here = pl.ds(pl.multiple_of(r * block, block), block)
        projected = jnp.dot(norm[here, :], qkv[...], preferred_element_type=F32)
        apart = jnp.where(inside_document(spans, block, t * rows + r * block), 0.0, -APART)
        cos, sin = cosine[here, :], sine[here, :]
        turned = []
        for i in range(2):
            x = projected[:, i * LANES : (i + 1) * LANES]
            heads[i, here, :] = x
            square = x * x
            high = square.astype(BF16)
            rest = (square - wide(high)).astype(BF16)
            total = jnp.dot(high, same_head, preferred_element_type=F32) + jnp.dot(
                rest, same_head, preferred_element_type=F32
            )
            u = x * lax.rsqrt(total * (1.0 / HEAD_SIZE) + EPSILON) * gain_pairs[i]
            first = lax.rem(lane, HEAD_SIZE) < HEAD_SIZE // 2
            swapped = jnp.where(first, pltpu.roll(u, LANES - HEAD_SIZE // 2, 1), pltpu.roll(u, HEAD_SIZE // 2, 1))
            turned.append(wide((u * cos + swapped * sin).astype(BF16)))
        for h in range(GROUP):
            q = turned[h // 2] * HEAD_SIZE ** (-0.5)
            q = pltpu.roll(q, HEAD_SIZE, 1) if h % 2 else q
            qx[h, here, :] = jnp.where(lane < HEAD_SIZE, q, apart).astype(BF16)
        values = projected[:, (GROUP + 1) * HEAD_SIZE : (GROUP + 2) * HEAD_SIZE]
        keys = pltpu.roll(turned[1], HEAD_SIZE, 1)
        kv[here, :] = jnp.where(lane < HEAD_SIZE, keys, jnp.concatenate([values, values], 1)).astype(BF16)
        for d in range(1, T):

            @pl.when(t + d < T)
            def _():
                line_copy(d, t, t + d, r).start()

    kv_all[t] = kv[...]
    widen_keys(kv[...], spans, t * rows, kx.at[t], vx.at[t])
    causal = lax.broadcasted_iota(jnp.int32, (part, part), 1) <= lax.broadcasted_iota(jnp.int32, (part, part), 0)

    def piece(q, source, k, masked):
        scores = dot_last(q, kx[source, k * part : (k + 1) * part, :])
        weights = jnp.exp(scores)
        if masked:
            weights = jnp.where(causal, weights, 0.0)
        return jnp.dot(weights.astype(BF16), vx[source, k * part : (k + 1) * part, :], preferred_element_type=F32)

    def pass_weights(i):
        for arrived, onward in zip(wide_sends[i], wide_shares[i]):
            arrived.wait_recv()
            onward.start()

    def pass_wo():
        if B == 2 and F == 4:
            wo_first[1].wait_recv()
            for copy in wo_relay:
                copy.start()
        else:
            gather_wo.relay()

    for which in range(2):
        mine = slice(which * part, (which + 1) * part)

        @pl.loop(0, GROUP)
        def _(h):
            q = qx[h, mine, :]
            total = piece(q, t, which, True)
            acc[h, mine, :] = total + piece(q, t, 0, False) if which else total

        pass_weights(which)
        if which:
            gather_mixed[0].relay()

        @pl.loop(1, t + 1)
        def _(j):
            source = t - j
            if which == 0:
                for r in range(4):
                    line_copy(0, source, t, r).wait_recv()
                widen_keys(kv_all[source], spans, source * rows, kx.at[source], vx.at[source])

            @pl.loop(0, GROUP)
            def _(h):
                q = qx[h, mine, :]
                acc[h, mine, :] = acc[h, mine, :] + piece(q, source, 0, False) + piece(q, source, 1, False)

        for h in range(GROUP):
            out = acc[h, mine, 0:HEAD_SIZE] / acc[h, mine, HEAD_SIZE : 2 * HEAD_SIZE]
            out = out.astype(BF16)
            if h < 2:
                packed[which, 0:part, h * HEAD_SIZE : (h + 1) * HEAD_SIZE] = out
            else:
                packed[which, part : part + part // 2, 0:HEAD_SIZE] = out[0 : part // 2]
                packed[which, part : part + part // 2, HEAD_SIZE : 2 * HEAD_SIZE] = out[part // 2 : part]
        homes.append(home(packed.at[which], mixed.at[which, p], 14 + which))
        gather_mixed[which].begin()
        if which == 0:
            pass_wo()

    gather_mixed[0].end()
    gather_mixed[1].relay()
    if B == 2 and F == 4:
        wo_relay[0].wait_recv()
        wo_last[0].start()
    gather_mixed[1].end()
    if B == 2 and F == 4:
        for copy in (wo_first[0], wo_relay[1], wo_last[0]):
            copy.wait_recv()
        for copy in wo_first + wo_relay + wo_last:
            copy.wait_send()
    else:
        gather_wo.end()
    for copy in [wide_near] + wide_shares[0] + wide_shares[1]:
        copy.wait_recv()
    for copy in [wide_near] + wide_sends[0] + wide_sends[1] + wide_shares[0] + wide_shares[1]:
        copy.wait_send()
    for copy in gain_sends + qkv_sends + qkv_shares:
        copy.wait_send()
    for copy in homes:
        copy.wait()
    for d in range(1, T):

        @pl.when(t + d < T)
        def _():
            for r in range(4):
                line_copy(d, t, t + d, r).wait_send()


def front(dims, tokens, wq, wk, wv, wo, w_gate, w_up, gains, freq, lengths):
    B, F, T = dims
    own_rows, width = tokens.shape
    n = B * F
    rows = own_rows * n
    depth, ff = w_gate.shape
    hidden = ff // n
    few = QW + 2 * HEAD_SIZE
    copies = 4 * Gather.COPIES + (F - 1) + 3 * (2 * F - 3)
    packed = (rows // 2 + rows // 4, LANES)
    shape = lambda *s: jax.ShapeDtypeStruct(s, BF16)
    wide_shape = lambda *s: jax.ShapeDtypeStruct(s, F32)
    vmem = lambda *s: pltpu.VMEM(s, BF16)
    return pl.pallas_call(
        functools.partial(front_kernel, dims),
        out_shape=(
            wide_shape(rows, LANES), wide_shape(rows, LANES), jax.ShapeDtypeStruct((8, LANES), jnp.int32),
            shape(rows, width), shape(width, few), shape(rows, width), wide_shape((GROUP + 1) // 2, rows, LANES),
            shape(GROUP, rows, LANES), shape(T, rows, LANES), wide_shape(GROUP, rows, LANES), shape(2, n, *packed),
            shape(F, depth, width), shape(F, depth, 2 * hidden),
            wide_shape(8, width),
        ),
        in_specs=[ANY] * 8 + [VMEM, pl.BlockSpec(memory_space=pltpu.SMEM)],
        out_specs=[VMEM] * 3 + [ANY] * 3 + [VMEM] * 4 + [ANY] * 3 + [VMEM],
        scratch_shapes=[
            vmem(rows, width), vmem(*wq.shape), vmem(*wk.shape), vmem(*wv.shape), vmem(F, depth, few), vmem(width, few),
            vmem(F, *gains.shape), vmem(depth, ff), vmem(depth, ff), vmem(F, depth, 2 * hidden),
            vmem(rows, width), vmem(rows, LANES), vmem(T, rows, LANES), vmem(T, rows, LANES), vmem(2, *packed),
            pltpu.SemaphoreType.DMA((copies,)),
            pltpu.SemaphoreType.DMA((copies,)),
            pltpu.SemaphoreType.DMA((T, 4)),
            pltpu.SemaphoreType.DMA((T, 4)),
            pltpu.SemaphoreType.DMA((16,)),
        ],
        compiler_params=kernel_params(1),
        name="front",
    )(tokens, wq, wk, wv, wo, w_gate, w_up, gains, freq, lengths)


def feed_kernel(dims, tok_in, mixed_in, wo_in, wide_in, down_in, dy_in, gain, grad_hidden, g_down,
                g_wide, g_last, own_resid, layer_out, tok, mixed, wo, w_wide, w_down, dy, rows_in, hid, both, act, dwide,
                resid, down, gd, gw, gl, *rest):
    scratch, (send, recv, local) = rest[:9], rest[9:]
    team = Team(*dims)
    B, F, y, p = team.B, team.F, team.y, team.p
    rows, width = tok.shape
    own_rows = own_resid.shape[0]
    hidden = w_down.shape[0]
    early = gw.shape[1]
    block = resid.shape[0]
    n = B * F
    dy_rows = lambda i: pl.ds(pl.multiple_of(i * own_rows, 16), own_rows)
    loads = [
        pltpu.make_async_copy(src, dst, local.at[i])
        for i, (src, dst) in enumerate(
            [(mixed_in, mixed), (wo_in, wo), (tok_in, tok), (wide_in, w_wide),
             (down_in.at[pl.ds(pl.multiple_of(y * hidden, 16), hidden)], w_down), (dy_in, dy.at[dy_rows(p)])]
        )
    ]
    for load in loads:
        load.start()
    greet([team.member(flip(p, bit)) for bit in (1, 2, 4)])
    sems = Sems(send, recv)
    scatter = Scatter(sems, team, down, scratch, "both")
    half = own_rows // 2
    gather = Gather(
        sems, p, n, team.member, dy_in, lambda i: dy.at[dy_rows(i)],
        lambda i, k: dy.at[pl.ds(pl.multiple_of(i * own_rows + k * half, 16), half)],
    )
    gather.begin()
    for load in loads[:3]:
        load.wait()

    @pl.loop(0, rows // block)
    def _(r):
        here = pl.ds(pl.multiple_of(r * block, block), block)
        which, later = lax.div(r, 2), lax.rem(r, 2)
        place = pl.ds(pl.multiple_of(later * block, block), block)
        for i in range(n):
            h = i % F * B + i // F
            first = h * QW
            rows_in[:, first : first + 2 * HEAD_SIZE] = mixed[which, i, place, :]
            last = mixed[which, i, 2 * block : 3 * block, :]
            last = jnp.where(later == 0, wide(last[:, :HEAD_SIZE]), wide(last[:, HEAD_SIZE:]))
            rows_in[:, first + 2 * HEAD_SIZE : first + QW] = last.astype(BF16)
        resid[...] = wide(tok[here, :]) + jnp.dot(rows_in[...], wo[...], preferred_element_type=F32)

        @pl.when(r == lax.div(p * own_rows, block))
        def _():
            own_resid[...] = resid[pl.ds(pl.multiple_of(lax.rem(p * own_rows, block), 8), own_rows), :]

        unit, factor = unit_and_factor(resid[...])
        hid[here, :] = (unit * gain[1:2, :]).astype(BF16)

    for load in loads[3:]:
        load.wait()
    gather.relay()

    @pl.loop(0, rows // block)
    def _(r):
        here = pl.ds(pl.multiple_of(r * block, block), block)
        product = jnp.dot(hid[here, :], w_wide[...], preferred_element_type=F32)
        gate, upper = product[:, :hidden], product[:, hidden:]
        both[0, here, :] = gate
        both[1, here, :] = upper
        sigma = 1.0 / (1.0 + jnp.exp(-gate))
        acts = (gate * sigma * upper).astype(BF16)
        act[here, :] = acts
        out = jnp.dot(acts, w_down[...], preferred_element_type=F32).astype(BF16)
        for i in range(block // own_rows):
            m = r * (block // own_rows) + i
            down[lax.div(m, 4), lax.rem(lax.div(m, 2), 2), lax.rem(m, 2)] = out[i * own_rows : (i + 1) * own_rows]

    scatter.begin()
    gather.end()

    @pl.loop(0, rows // block)
    def _(r):
        here = pl.ds(pl.multiple_of(r * block, block), block)
        pl.when(r == 1)(scatter.relay)
        gate, upper = both[0, here, :], both[1, here, :]
        sigma = 1.0 / (1.0 + jnp.exp(-gate))
        dact = dot_last(dy[here, :], w_down[...])
        dwide[here, 0:hidden] = (dact * upper * sigma * (1.0 + gate * (1.0 - sigma))).astype(BF16)
        dwide[here, hidden : 2 * hidden] = (dact * (gate * sigma)).astype(BF16)
        tok[here, :] = dot_last(dwide[here, :], w_wide[...]).astype(BF16)

    stores = []

    def store(src, dst):
        stores.append(pltpu.make_async_copy(src, dst, local.at[6 + len(stores)]))
        stores[-1].start()

    store(tok, grad_hidden)
    over_rows = lambda a, b: lax.dot_general(a, b, (((0,), (0,)), ((), ())), preferred_element_type=F32).astype(BF16)

    for first in range(0, hidden, 256):
        count = min(256, hidden - first)
        gd[first : first + count, :] = over_rows(act[:, first : first + count], dy[...])
    store(gd, g_down)
    scatter.relay_again()

    @pl.loop(0, width // 256)
    def _(r):
        here = pl.ds(pl.multiple_of(r * 256, 256), 256)
        product = over_rows(hid[:, here], dwide[...])
        gw[here, :] = product[:, :early]
        gl[here, 0 : 2 * hidden - early] = product[:, early:]
        pltpu.make_async_copy(gw.at[here], g_wide.at[here], local.at[10]).start()
        pltpu.make_async_copy(gl.at[here], g_last.at[here], local.at[11]).start()

    def put(columns, total):
        layer_out[:, columns] = own_resid[:, columns] + total

    scatter.end(put)
    for copy in stores:
        copy.wait()
    pltpu.make_async_copy(gw, g_wide, local.at[10]).wait()
    pltpu.make_async_copy(gl, g_last, local.at[11]).wait()


def feed(dims, tok, mixed, wo, w_wide, w_down, dy, gains):
    rows, width = tok.shape
    hidden = w_wide.shape[1] // 2
    own_rows = rows // KEY_VALUE_HEADS
    early = early_lanes(hidden)
    last = 2 * hidden - early + QW + 2 * HEAD_SIZE
    block = rows // 4
    shape = lambda s: jax.ShapeDtypeStruct(s, BF16)
    return pl.pallas_call(
        functools.partial(feed_kernel, dims),
        out_shape=(
            shape((rows, width)), shape((hidden, width)), shape((width, early)), shape((width, last)),
            jax.ShapeDtypeStruct((own_rows, width), F32), jax.ShapeDtypeStruct((own_rows, width), F32),
        ),
        in_specs=[ANY] * 6 + [VMEM],
        out_specs=[ANY] * 4 + [VMEM] * 2,
        scratch_shapes=[
            pltpu.VMEM((rows, width), BF16),
            pltpu.VMEM(mixed.shape, BF16),
            pltpu.VMEM(wo.shape, BF16),
            pltpu.VMEM(w_wide.shape, BF16),
            pltpu.VMEM((hidden, width), BF16),
            pltpu.VMEM((rows, width), BF16),
            pltpu.VMEM((block, width), BF16),
            pltpu.VMEM((rows, width), BF16),
            pltpu.VMEM((2, rows, hidden), F32),
            pltpu.VMEM((rows, hidden), BF16),
            pltpu.VMEM((rows, 2 * hidden), BF16),
            pltpu.VMEM((block, width), F32),
            pltpu.VMEM((2, 2, 2, own_rows, width), BF16),
            pltpu.VMEM((hidden, width), BF16),
            pltpu.VMEM((width, early), BF16),
            pltpu.VMEM((width, last), BF16),
        ]
        + scatter_shapes(own_rows, width, "both")
        + [
            pltpu.SemaphoreType.DMA((Scatter.COPIES + Gather.COPIES,)),
            pltpu.SemaphoreType.DMA((Scatter.COPIES + Gather.COPIES,)),
            pltpu.SemaphoreType.DMA((12,)),
        ],
        compiler_params=pltpu.CompilerParams(
            collective_id=2, has_side_effects=True, vmem_limit_bytes=60 * 1024 * 1024
        ),
        name="feed",
    )(tok, mixed, wo, w_wide, w_down, dy, gains)


HOP = 2
LAG = 3
UNITS = 4
ORDER = "both"


class GradSum:
    RED, LEFT, RIGHT, HAND, OVER, HOME, INTO = range(7)

    def __init__(self, team, kinds, red_recv, fin_recv, hand_recvs, bulk):
        self.team, self.kinds = team, kinds
        self.red_recv, self.fin_recv, self.hand_recvs, self.bulk = red_recv, fin_recv, hand_recvs, bulk
        self.opposite = team.member(lax.rem(team.p + team.F, team.B * team.F))
        self.low, self.high = team.T // 2 - 1, team.T // 2

    @staticmethod
    def steps(kinds, T):
        return max(first + rows // step for rows, step, first in kinds) + HOP * T + LAG

    def remote(self, src, dst, send_sem, recv_sem, device):
        return pltpu.make_async_remote_copy(
            src_ref=src, dst_ref=dst, send_sem=send_sem, recv_sem=recv_sem, device_id=device, device_id_type=MESH
        )

    def where(self, k, c):
        g, step, how = self.kinds[k][0], self.kinds[k][4], self.kinds[k][6]
        if how != "rows":
            return pl.ds(pl.multiple_of(c * step, 16), step), None, None
        F = self.team.F
        turn = lax.rem(c, F)
        to = lax.rem(turn, 2) * (F // 2) + lax.div(turn, 2)
        row = lax.div(c, F) * step
        return pl.ds(pl.multiple_of(to * (g.shape[0] // F) + row, 16), step), to, row

    def spare(self, k, c):
        step = self.kinds[k][4]
        return pl.ds(pl.multiple_of(lax.div(c, 2) * step, 16), step)

    def reduce(self, k, c, i, root):
        g, land, land2 = self.kinds[k][:3]
        team = self.team
        t, T = team.t, team.T
        at, _, _ = self.where(k, c)
        red = self.bulk.at[self.RED, k, 0]

        def inward(side, dst):
            to = team.other_team(t + 1 - 2 * side)
            self.remote(g.at[at], dst, red, self.red_recv.at[side, i], to).start()

        def add():
            g[at, :] = (wide(g[at, :]) + wide(land[at, :])).astype(BF16)

        @pl.when(t < root)
        def _():
            @pl.when(t > 0)
            def _():
                self.remote(g.at[at], land.at[at], red, self.red_recv.at[0, i], team.other_team(t)).wait_recv()
                add()

            inward(0, land.at[at])

        @pl.when(t > root)
        def _():
            @pl.when(t < T - 1)
            def _():
                self.remote(g.at[at], land.at[at], red, self.red_recv.at[1, i], team.other_team(t)).wait_recv()
                add()

            @pl.when(t - 1 == root)
            def _():
                inward(1, land2.at[self.spare(k, c)])

            @pl.when(t - 1 != root)
            def _():
                inward(1, land.at[at])

    def finish(self, k, c, i, root):
        g, land, land2, out, step, first, how = self.kinds[k]
        team, bulk = self.team, self.bulk
        B, F, T, t, y, f = team.B, team.F, team.T, team.t, team.y, team.f
        at, to, row = self.where(k, c)
        red = bulk.at[self.RED, k, 0]

        def outward(side):
            to_team = team.other_team(t - 1 + 2 * side)
            sem = bulk.at[self.RIGHT if side else self.LEFT, k, 0]
            return self.remote(land.at[at], land.at[at], sem, self.fin_recv.at[i], to_team)

        @pl.when(t == root)
        def _():
            total = wide(g[at, :])
            if self.low > 0:
                self.remote(g.at[at], land.at[at], red, self.red_recv.at[0, i], team.other_team(t)).wait_recv()
                total = total + wide(land[at, :])
                self.remote(g.at[at], land2.at[self.spare(k, c)], red, self.red_recv.at[1, i],
                            team.other_team(t)).wait_recv()
                total = total + wide(land2[self.spare(k, c), :])
            land[at, :] = total.astype(BF16)

        @pl.when(t != root)
        def _():
            outward(0).wait_recv()

        @pl.when((t <= root) & (t > 0))
        def _():
            outward(0).start()

        @pl.when((t >= root) & (t < T - 1))
        def _():
            outward(1).start()

        if how == "rows":
            dst = out.at[f * B + y, pl.ds(pl.multiple_of(row, 16), step)]

            @pl.when(to == f)
            def _():
                pltpu.make_async_copy(land.at[at], dst, bulk.at[self.HOME, k, 0]).start()
                if B == 2:
                    self.remote(land.at[at], dst, bulk.at[self.OVER, k, 0], bulk.at[self.INTO, k, 0],
                                self.opposite).start()

            @pl.when(to != f)
            def _():
                self.remote(land.at[at], dst, bulk.at[self.HAND, k, 0], self.hand_recvs[k].at[f, lax.div(row, step)],
                            team.same_row(to)).start()
        elif how == "stay":
            dst = out.at[y, at]
            pltpu.make_async_copy(land.at[at], dst, bulk.at[self.HOME, k, 0]).start()
            if B == 2:
                self.remote(land.at[at], dst, bulk.at[self.OVER, k, 0], bulk.at[self.INTO, k, 0],
                            self.opposite).start()
        else:
            for index in range(F):
                src = land.at[pl.ds(16 * index, 16)]
                for line in range(B):

                    @pl.when(team.p == line * F + index)
                    def _():
                        pltpu.make_async_copy(src, out.at[team.p], bulk.at[self.HOME, k, 0]).start()

                    @pl.when(team.p != line * F + index)
                    def _():
                        self.remote(src, out.at[team.p], bulk.at[self.HAND, k, 0], bulk.at[self.INTO, k, 0],
                                    (t * B + line, index)).start()

    def pass_over(self, k, c, i, root):
        g, land, land2, out, step, first, how = self.kinds[k]
        if how != "rows":
            return
        team = self.team
        at, to, row = self.where(k, c)

        @pl.when(to == team.f)
        def _():
            for d in range(1, team.F):
                source = lax.rem(team.f + d, team.F)
                ref = out.at[source * team.B + team.y, pl.ds(pl.multiple_of(row, 16), step)]
                self.remote(land.at[at], ref, self.bulk.at[self.HAND, k, 0],
                            self.hand_recvs[k].at[source, lax.div(row, step)], team.same_row(team.f)).wait_recv()
                if team.B == 2:
                    self.remote(ref, ref, self.bulk.at[self.OVER, k, 1], self.bulk.at[self.INTO, k, 0],
                                self.opposite).start()

    def each(self, i, body):
        root = self.low + lax.rem(lax.max(i, 0), 2)
        for k, (g, land, land2, out, step, first, how) in enumerate(self.kinds):
            count = g.shape[0] // step
            pl.when((i >= first) & (i < first + count))(functools.partial(body, k, i - first, i, root))

    def step(self, s):
        T, t = self.team.T, self.team.t
        self.each(s - HOP * lax.min(t, T - 1 - t), self.reduce)
        for parity in range(2):
            root = self.low + parity
            distance = jnp.where(t < root, root - t, t - root)
            i = s - HOP * (T // 2 + distance)
            for wait, body in ((0, self.finish), (LAG, self.pass_over)):
                j = i - wait
                pl.when((j >= 0) & (lax.rem(lax.max(j, 0), 2) == parity))(functools.partial(self.each, j, body))

    def drain(self, ref, sem):
        pltpu.make_async_copy(ref, ref, sem).wait()

    def end(self):
        bulk, B, F, T, t = self.bulk, self.team.B, self.team.F, self.team.T, self.team.t
        low, high = self.low, self.high
        for k, (g, land, land2, out, step, first, how) in enumerate(self.kinds):
            rows = g.shape[0]
            some = lambda n: g.at[pl.ds(0, n)]
            count = rows // step
            even = (count + 1 - first % 2) // 2 * step
            odd = rows - even

            def drain_some(condition, n, which):
                if n:

                    @pl.when(condition)
                    def _():
                        self.drain(some(n), bulk.at[which, k, 0])

            drain_some((t != low) & (t != high), rows, self.RED)
            drain_some(t == low, odd, self.RED)
            drain_some(t == high, even, self.RED)
            drain_some((t > 0) & (t <= low), rows, self.LEFT)
            drain_some(t == high, odd, self.LEFT)
            drain_some((t < T - 1) & (t >= high), rows, self.RIGHT)
            drain_some(t == low, even, self.RIGHT)
            if how == "rows":
                shard = rows // F
                self.drain(some(rows - shard), bulk.at[self.HAND, k, 0])
                self.drain(some(shard), bulk.at[self.HOME, k, 0])
                if B == 2:
                    self.drain(some(shard), bulk.at[self.OVER, k, 0])
                    self.drain(some(rows - shard), bulk.at[self.OVER, k, 1])
                    self.drain(g, bulk.at[self.INTO, k, 0])
            elif how == "stay":
                self.drain(g, bulk.at[self.HOME, k, 0])
                if B == 2:
                    self.drain(g, bulk.at[self.OVER, k, 0])
                    self.drain(g, bulk.at[self.INTO, k, 0])
            else:
                others = out.at[pl.ds(0, B * F - 1)]
                self.drain(out.at[0], bulk.at[self.HOME, k, 0])
                self.drain(others, bulk.at[self.HAND, k, 0])
                self.drain(others, bulk.at[self.INTO, k, 0])


def first_steps(dims):
    at = dict(scatter1=3, scatter2=12, resid=18, relay=24, heads=30, own_wo=30 + UNITS)
    at["attention"] = at["own_wo"] + 1
    at["keys"] = at["attention"] + 2 * GROUP * dims[2] + 1
    at["turn"] = at["keys"] + 1
    at["normed"] = at["turn"] + UNITS
    at["products"] = at["normed"] + 2
    at["again1"] = at["products"] + 3
    at["again2"] = at["again1"] + 6
    at["tokens"] = at["again2"] + 6
    return at


def early_lanes(hidden):
    return 2 * hidden // LANES * LANES


def grad_kinds(dims, depth, hidden):
    at = first_steps(dims)
    early = early_lanes(hidden)
    kinds, place = [], 0
    for rows, width, step, ready, how in (
        (hidden, depth, 32, 0, "stay"),
        (depth, early, 32, 0, "rows"),
        (QW, depth, 48, at["own_wo"] + 1, "stay"),
        (depth, 2 * hidden - early + QW + 2 * HEAD_SIZE, 192, at["products"] + 3, "rows"),
        (16 * dims[1], max(depth // dims[1], LANES), 16 * dims[1], at["tokens"] + 1, "gain"),
    ):
        place = max(place, ready)
        kinds.append((rows, width, step, place, how))
        place += rows // step
    return kinds


def back_kernel(dims, kinds, steps, grad_hidden, g_down, g_wide, g_last, resid, tokens, cotangent, gains, acc_in, qx_in,
                kv_all, spans, heads_in, cosine_in, sine_in, wo, wqkv, normed,
                out_down, out_wide, out_wo, out_last, out_gains, tokens_grad,
                xs, own_down, own_wide, own_gwo, own_last, own_gains,
                land_down, land_wide, land_wo, land_last, land_gains,
                also_down, also_wide, also_wo, also_last, also_gains,
                grad_resid, attn_own, big, dox, mixed, dq, dkv, kv_in, dkv_sum, turned, small, kx, vx, dk, dv, wq_in, own_wo,
                acc, qx, heads, cosine, sine, *rest):
    count = len(scatter_parts(resid.shape[-1], ORDER)) * 4 + 1
    scratch1, rest = rest[:count], rest[count:]
    send, recv, line_send, line_recv, red_recv, fin_recv, hand_wide, hand_last, bulk, local = rest
    team = Team(*dims)
    B, F, T = dims
    t, p = team.t, team.p
    at = first_steps(dims)
    own_rows, width = resid.shape
    rows = qx.shape[1]
    part = rows // 2
    small_block = rows // UNITS
    depth = width // F
    sems = Sems(send, recv)
    loads = [
        pltpu.make_async_copy(src, dst, local.at[i])
        for i, (src, dst) in enumerate(
            [(g_down, own_down), (grad_hidden, xs), (g_wide, own_wide), (g_last, own_last), (wqkv, wq_in),
             (wo.at[pl.ds(pl.multiple_of(team.y * QW, 16), QW)], own_wo), (acc_in, acc), (qx_in, qx),
             (heads_in, heads), (cosine_in, cosine), (sine_in, sine)]
        )
    ]
    for load in loads[:2]:
        load.start()
    own_gains[...] = jnp.zeros_like(own_gains)
    greet(team_peers(team) + line_peers(team))
    for load in loads[:2]:
        load.wait()
    for load in loads[2:]:
        load.start()
    scatter = Scatter(sems, team, xs, scratch1, ORDER)
    scatter.begin()
    again = Scatter(sems, team, xs, scratch1, ORDER)
    half = own_rows // 2
    gather = Gather(
        sems, p, B * F, team.member, attn_own,
        lambda i: big.at[pl.ds(pl.multiple_of(i * own_rows, 16), own_rows)],
        lambda i, k: big.at[pl.ds(pl.multiple_of(i * own_rows + k * half, 16), half)],
    )
    sums = GradSum(
        team,
        [
            (own, land, also, out) + kind[2:]
            for own, land, also, out, kind in zip(
                (own_down, own_wide, own_gwo, own_last, own_gains),
                (land_down, land_wide, land_wo, land_last, land_gains),
                (also_down, also_wide, also_wo, also_last, also_gains),
                (out_down, out_wide, out_wo, out_last, out_gains),
                kinds,
            )
        ],
        red_recv, fin_recv, [None, hand_wide, None, hand_last, None], bulk,
    )
    gain_attn, gain_ffn = gains[0:1, :], gains[1:2, :]
    gain_q, gain_k = gains[2:3, 0:HEAD_SIZE], gains[3:4, 0:HEAD_SIZE]
    home = pltpu.make_async_copy(attn_own, big.at[pl.ds(pl.multiple_of(p * own_rows, 16), own_rows)], local.at[11])
    fetch = pltpu.make_async_copy(normed, big, local.at[12])

    def resid_phase():
        def store(columns, total):
            grad_resid[:, columns] = total

        scatter.end(store)
        term = jnp.zeros((1, width), F32)
        for r in range(0, own_rows, 32):
            here = slice(r, r + 32)
            unit, factor = unit_and_factor(resid[here, :])
            upstream = grad_resid[here, :]
            term = term + jnp.sum(upstream * unit, 0, keepdims=True)
            total = wide(cotangent[here, :]) + norm_back(upstream, unit, factor, gain_ffn)
            grad_resid[here, :] = total
            attn_own[here, :] = total.astype(BF16)
        small[1:2, :] = term
        home.start()
        gather.begin()

    def heads_phase():
        gather.end()
        home.wait()

    def heads_unit(r):
        lane = lane_ids(small_block)
        here = pl.ds(pl.multiple_of(r * small_block, small_block), small_block)
        grad = dot_last(big[here, :], own_wo[...]).astype(BF16)
        for h in range(GROUP):
            sums_h = acc[h, here, :]
            total = pltpu.roll(sums_h, HEAD_SIZE, 1)
            out = sums_h / total
            mixed[here, h * HEAD_SIZE : (h + 1) * HEAD_SIZE] = out[:, :HEAD_SIZE].astype(BF16)
            do = wide(grad[:, h * HEAD_SIZE : (h + 1) * HEAD_SIZE])
            do = jnp.concatenate([do, jnp.zeros_like(do)], 1)
            delta = -jnp.sum(jnp.where(lane < HEAD_SIZE, do * out, 0.0), 1, keepdims=True)

            def put(x, first, value):
                for i in range(3):
                    x = jnp.where(lane == first + i, wide(value.astype(BF16)), x)
                    value = value - wide(value.astype(BF16))
                return x

            dox[h, here, :] = put(do, HEAD_SIZE, delta).astype(BF16)
            log_sum = -jnp.log(jnp.where(lane < HEAD_SIZE, total, sums_h))
            qx[h, here, :] = put(wide(qx[h, here, :]), HEAD_SIZE + NDOCS, log_sum).astype(BF16)

    def own_wo_phase():
        own_gwo[...] = lax.dot_general(
            mixed[...], big[...], (((0,), (0,)), ((), ())), preferred_element_type=F32
        ).astype(BF16)
        dq[...] = jnp.zeros_like(dq)

    causal = lax.broadcasted_iota(jnp.int32, (part, part), 0) <= lax.broadcasted_iota(jnp.int32, (part, part), 1)

    def piece(h, q_rows, k_rows, masked):
        q = qx[h, q_rows, :]
        do = dox[h, q_rows, :]
        keys = kx[k_rows, :]
        weights = jnp.exp(dot_last(keys, q))
        if masked:
            weights = jnp.where(causal, weights, 0.0)
        dscore = (weights * dot_last(vx[k_rows, :], do)).astype(BF16)
        dv[...] += jnp.dot(weights.astype(BF16), do, preferred_element_type=F32)
        dk[...] += jnp.dot(dscore, q, preferred_element_type=F32)
        dq[h, q_rows, :] += lax.dot_general(dscore, keys, (((0,), (0,)), ((), ())), preferred_element_type=F32)

    def line_copy(owner, source):
        return pltpu.make_async_remote_copy(
            src_ref=dkv.at[owner], dst_ref=dkv.at[source], send_sem=line_send.at[owner],
            recv_sem=line_recv.at[source], device_id=team.other_team(owner), device_id_type=MESH,
        )

    def fetch_keys(source):
        slot = lax.rem(source, 2)
        return pltpu.make_async_copy(kv_all.at[source], kv_in.at[slot], local.at[13 + slot])

    fetch_keys(t * 0).start()

    def attention_unit(source, k, h):
        @pl.when((k == 0) & (h == 0))
        def _():
            fetch_keys(source).wait()

            @pl.when(source < t)
            def _():
                fetch_keys(source + 1).start()

            widen_keys(kv_in[lax.rem(source, 2)], spans, source * rows, kx, vx)

        @pl.when(h == 0)
        def _():
            dk[...] = jnp.zeros_like(dk)
            dv[...] = jnp.zeros_like(dv)

        k_rows = pl.ds(pl.multiple_of(k * part, part), part)

        @pl.when(source < t)
        def _():
            for q in range(2):
                piece(h, slice(q * part, (q + 1) * part), k_rows, False)

        @pl.when(source == t)
        def _():
            for diagonal in range(2):

                @pl.when(k == diagonal)
                def _():
                    for q in range(diagonal, 2):
                        piece(h, slice(q * part, (q + 1) * part), slice(diagonal * part, (diagonal + 1) * part),
                              q == diagonal)

        @pl.when(h == GROUP - 1)
        def _():
            dkv[source, k_rows, :] = jnp.where(
                lane_ids(part) < HEAD_SIZE, dk[...], pltpu.roll(dv[...], HEAD_SIZE, 1)
            ).astype(BF16)

            @pl.when((k == 1) & (source < t))
            def _():
                line_copy(source, t).start()

    def keys_phase():
        fetch.start()
        dkv_sum[...] = wide(dkv[t])
        for d in range(1, T):

            @pl.when(t + d < T)
            def _():
                line_copy(t, t + d).wait_recv()
                dkv_sum[...] += wide(dkv[t + d])

        small[2:4, :] = jnp.zeros((2, width), F32)

    def turn_unit(r):
        here = pl.ds(pl.multiple_of(r * small_block, small_block), small_block)
        cos, sin = cosine[here, 0:HEAD_SIZE], sine[here, 0:HEAD_SIZE]
        q_term = jnp.zeros((1, HEAD_SIZE), F32)
        for h in range(GROUP + 1):
            if h < GROUP:
                u, gain = dq[h, here, 0:HEAD_SIZE] * HEAD_SIZE ** (-0.5), gain_q
            else:
                u, gain = dkv_sum[here, 0:HEAD_SIZE], gain_k
            u = u * cos - jnp.concatenate([u[:, HEAD_SIZE // 2 :], u[:, : HEAD_SIZE // 2]], 1) * sin
            unit, factor = unit_and_factor(heads[h // 2, here, h % 2 * HEAD_SIZE : (h % 2 + 1) * HEAD_SIZE])
            term = jnp.sum(u * unit, 0, keepdims=True)
            if h < GROUP:
                q_term = q_term + term
            else:
                small[3:4, 0:HEAD_SIZE] += term
            turned[here, h * HEAD_SIZE : (h + 1) * HEAD_SIZE] = norm_back(u, unit, factor, gain).astype(BF16)
        small[2:3, 0:HEAD_SIZE] += q_term
        h = GROUP + 1
        turned[here, h * HEAD_SIZE : (h + 1) * HEAD_SIZE] = dkv_sum[here, HEAD_SIZE : 2 * HEAD_SIZE].astype(BF16)

    def normed_unit(i):
        for m in range(4):
            here = pl.ds(pl.multiple_of((4 * i + m) * own_rows, own_rows), own_rows)
            xs[i, m // 2, m % 2] = dot_last(turned[here, :], wq_in[...]).astype(BF16)

    def products_phase():
        again.begin()
        fetch.wait()

    def products_unit(i):
        for j in range(2):
            r = pl.multiple_of((2 * i + j) * (width // 6), LANES)
            here = pl.ds(r, width // 6)
            own_last[here, own_last.shape[1] - turned.shape[1] :] = lax.dot_general(
                big[:, here], turned[...], (((0,), (0,)), ((), ())), preferred_element_type=F32
            ).astype(BF16)

    def tokens_phase():
        def store(columns, total):
            tokens_grad[:, columns] = total

        again.end(store)
        term = jnp.zeros((1, width), F32)
        for r in range(0, own_rows, 32):
            here = slice(r, r + 32)
            unit, factor = unit_and_factor(wide(tokens[here, :]))
            upstream = tokens_grad[here, :]
            term = term + jnp.sum(upstream * unit, 0, keepdims=True)
            tokens_grad[here, :] = grad_resid[here, :] + norm_back(upstream, unit, factor, gain_attn)
        small[0:1, :] = term
        lanes = own_gains.shape[1]
        row = lax.broadcasted_iota(jnp.int32, (16, lanes), 0)

        def cut(i, first, count):
            value = small[i : i + 1, first : first + count]
            if count < lanes:
                value = jnp.concatenate([value, jnp.zeros((1, lanes - count), F32)], 1)
            return jnp.where(row == i, jnp.broadcast_to(value, (16, lanes)), 0.0)

        for i in range(F):
            few = HEAD_SIZE // F
            own_gains[16 * i : 16 * i + 16, :] = (
                cut(0, i * depth, depth) + cut(1, i * depth, depth) + cut(2, i * few, few) + cut(3, i * few, few)
            ).astype(BF16)

    def late_loads():
        for load in loads[2:]:
            load.wait()

    @pl.loop(0, steps)
    def _(s):
        pl.when(s == at["scatter1"])(late_loads)
        sums.step(s)
        for name, body in (
            ("scatter1", scatter.relay), ("scatter2", scatter.relay_again), ("resid", resid_phase),
            ("relay", gather.relay), ("heads", heads_phase), ("own_wo", own_wo_phase), ("keys", keys_phase),
            ("products", products_phase), ("again1", again.relay), ("again2", again.relay_again),
            ("tokens", tokens_phase),
        ):
            pl.when(s == at[name])(body)
        for name, count, body in (
            ("heads", UNITS, heads_unit), ("turn", UNITS, turn_unit), ("normed", 2, normed_unit),
            ("products", 3, products_unit),
        ):
            i = s - at[name]
            pl.when((i >= 0) & (i < count))(functools.partial(body, i))
        unit = s - at["attention"]
        source = lax.div(unit, 2 * GROUP)

        @pl.when((unit >= 0) & (source <= t))
        def _():
            attention_unit(source, lax.rem(lax.div(unit, GROUP), 2), lax.rem(unit, GROUP))

    for d in range(1, T):

        @pl.when(t - d >= 0)
        def _():
            line_copy(t - d, t).wait_send()

    sums.end()


def backward(dims, grad_hidden, g_down, g_wide, g_last, resid, tokens, cotangent, gains, acc, qx, kv_all, spans,
             heads, cosine, sine, wo, wqkv, normed):
    B, F, T = dims
    own_rows, width = resid.shape
    rows = qx.shape[1]
    part = rows // 2
    hidden = g_down.shape[0]
    n = B * F
    kinds = grad_kinds(dims, width, hidden)
    steps = max(
        GradSum.steps([(rows_, step, first) for rows_, _, step, first, _ in kinds], T), first_steps(dims)["tokens"] + 1
    )
    positions = max(first + rows_ // step for rows_, _, step, first, _ in kinds)
    outs = []
    for rows_, wide_, step, first, how in kinds:
        if how == "rows":
            shape = (n, rows_ // F, wide_)
        elif how == "stay":
            shape = (B, rows_, wide_)
        else:
            shape = (n, 16, wide_)
        outs.append(jax.ShapeDtypeStruct(shape, BF16))
    outs.append(jax.ShapeDtypeStruct((own_rows, width), F32))
    eight = (2, 2, 2, own_rows, width)
    hands = [pltpu.SemaphoreType.DMA((F, kinds[k][0] // F // kinds[k][2])) for k in (1, 3)]
    copies = 2 * Scatter.COPIES + Gather.COPIES
    return pl.pallas_call(
        functools.partial(back_kernel, dims, kinds, steps),
        out_shape=outs,
        in_specs=[ANY] * 4 + [VMEM] * 4 + [ANY] * 3 + [VMEM] + [ANY] * 6,
        out_specs=[ANY] * 5 + [VMEM],
        scratch_shapes=[pltpu.VMEM(eight, BF16)]
        + [pltpu.VMEM((kind[0], kind[1]), BF16) for kind in kinds] * 2
        + [pltpu.VMEM(((kind[0] // kind[2] + 1) // 2 * kind[2], kind[1]), BF16) for kind in kinds]
        + [
            pltpu.VMEM((own_rows, width), F32),
            pltpu.VMEM((own_rows, width), BF16),
            pltpu.VMEM((rows, width), BF16),
            pltpu.VMEM(qx.shape, BF16),
            pltpu.VMEM((rows, QW), BF16),
            pltpu.VMEM(qx.shape, F32),
            pltpu.VMEM(kv_all.shape, BF16),
            pltpu.VMEM((2,) + kv_all.shape[1:], BF16),
            pltpu.VMEM((rows, LANES), F32),
            pltpu.VMEM((rows, QW + 2 * HEAD_SIZE), BF16),
            pltpu.VMEM((8, width), F32),
            pltpu.VMEM((rows, LANES), BF16),
            pltpu.VMEM((rows, LANES), BF16),
            pltpu.VMEM((part, LANES), F32),
            pltpu.VMEM((part, LANES), F32),
            pltpu.VMEM(wqkv.shape, BF16),
            pltpu.VMEM((QW, width), BF16),
            pltpu.VMEM(acc.shape, F32),
            pltpu.VMEM(qx.shape, BF16),
            pltpu.VMEM(heads.shape, F32),
            pltpu.VMEM(cosine.shape, F32),
            pltpu.VMEM(sine.shape, F32),
        ]
        + scatter_shapes(own_rows, width, ORDER)
        + [
            pltpu.SemaphoreType.DMA((copies,)),
            pltpu.SemaphoreType.DMA((copies,)),
            pltpu.SemaphoreType.DMA((T,)),
            pltpu.SemaphoreType.DMA((T,)),
            pltpu.SemaphoreType.DMA((2, positions)),
            pltpu.SemaphoreType.DMA((positions,)),
            *hands,
            pltpu.SemaphoreType.DMA((7, len(kinds), 2)),
            pltpu.SemaphoreType.DMA((15,)),
        ],
        compiler_params=pltpu.CompilerParams(
            collective_id=3, has_side_effects=True, vmem_limit_bytes=60 * 1024 * 1024
        ),
        name="backward",
    )(grad_hidden.reshape(eight), g_down, g_wide, g_last, resid, tokens, cotangent, gains, acc, qx,
      kv_all, spans, heads, cosine, sine, wo, wqkv, normed)


def place_kernel(n, hidden, both, last, down, wo, layer, tokens, gains, gate_out, up_out, wq_out, wk_out, wv_out, down_out,
                 wo_out, layer_out, tokens_out, *gain_outs):
    early = both.shape[-1]
    tail = 2 * hidden - early
    for q in range(n):
        block, rest = wide(both[q]), wide(last[q])
        gate_out[:, q * hidden : (q + 1) * hidden] = block[:, :hidden]
        up_out[:, q * hidden : (q + 1) * hidden] = jnp.concatenate([block[:, hidden:], rest[:, :tail]], 1)
        wq_out[:, q * QW : (q + 1) * QW] = rest[:, tail : tail + QW]
        wk_out[:, q * HEAD_SIZE : (q + 1) * HEAD_SIZE] = rest[:, tail + QW : tail + QW + HEAD_SIZE]
        wv_out[:, q * HEAD_SIZE : (q + 1) * HEAD_SIZE] = rest[:, tail + QW + HEAD_SIZE :]
    down_out[...] = wide(down[...])
    wo_out[...] = wide(wo[...])

    @pl.when(pl.program_id(0) == 0)
    def _():
        layer_out[...] = layer[...].astype(BF16)
        tokens_out[...] = tokens[...].astype(BF16)
        total = wide(gains[0])
        for i in range(1, n):
            total = total + wide(gains[i])
        for i, gain_out in enumerate(gain_outs):
            gain_out[...] = total[i, : gain_out.shape[0]]


def place(hidden, both, last, down, wo, layer, tokens, gains):
    n, depth, early = both.shape
    width = down.shape[-1]
    down, wo = down.reshape(-1, width), wo.reshape(-1, width)
    step = 64
    count = depth // step
    many = lambda a: pl.BlockSpec((n, step, a.shape[-1]), lambda i: (0, i, 0))
    cut = lambda a: pl.BlockSpec((a.shape[0] // count, width), lambda i: (i, 0))
    out = lambda w: pl.BlockSpec((step, w), lambda i: (i, 0))
    whole = lambda dims: pl.BlockSpec(dims, lambda i: (0,) * len(dims))
    shape = lambda r, w: jax.ShapeDtypeStruct((r, w), F32)
    wq, wk = QW * n, HEAD_SIZE * n
    sizes = [depth, depth, HEAD_SIZE * depth // width, HEAD_SIZE * depth // width]
    return pl.pallas_call(
        functools.partial(place_kernel, n, hidden),
        grid=(count,),
        out_shape=(
            shape(depth, n * hidden), shape(depth, n * hidden), shape(depth, wq), shape(depth, wk), shape(depth, wk),
            shape(down.shape[0], width), shape(wo.shape[0], width), jax.ShapeDtypeStruct(layer.shape, BF16),
            jax.ShapeDtypeStruct(tokens.shape, BF16), *[jax.ShapeDtypeStruct((size,), F32) for size in sizes],
        ),
        in_specs=[many(both), many(last), cut(down), cut(wo), whole(layer.shape), whole(tokens.shape),
                  whole(gains.shape)],
        out_specs=[out(n * hidden), out(n * hidden), out(wq), out(wk), out(wk), cut(down), cut(wo),
                   whole(layer.shape), whole(tokens.shape), *[whole((size,)) for size in sizes]],
        compiler_params=pltpu.CompilerParams(vmem_limit_bytes=VMEM_LIMIT),
        name="place",
    )(both, last, down, wo, layer, tokens, gains)


def norm_back(upstream, unit_rows, factor, gain_row):
    lifted = upstream * gain_row
    return factor * (lifted - unit_rows * jnp.mean(lifted * unit_rows, -1, keepdims=True))


def on_device(
    tokens, lengths, wq, wk, wv, wo, w_gate, w_up, w_down, attn_gain, ffn_gain, q_gain, key_norm_gain, cotangent
):
    F = lax.axis_size("fsdp")
    B = KEY_VALUE_HEADS // F
    T = lax.axis_size("ctx") // B
    dims = (B, F, T)
    own_rows, width = tokens.shape
    rows = own_rows * KEY_VALUE_HEADS
    depth = width // F
    t = lax.axis_index("ctx") // B
    hidden = w_down.shape[0] // B

    lanes = max(depth, LANES)
    line = lambda a: jnp.pad(a, (0, lanes - a.shape[0]))
    gains = jnp.concatenate([line(attn_gain), line(ffn_gain), line(q_gain), line(key_norm_gain)])
    gains = jnp.pad(gains.reshape(4, lanes), ((0, 12), (0, 0)))
    half = HEAD_SIZE // 2
    freq = np.power(np.float32(ROPE_BASE), -(np.arange(LANES, dtype=np.float32) % half * np.float32(2.0) / HEAD_SIZE))
    freq = jnp.asarray(np.broadcast_to(freq, (8, LANES))[:1], F32)
    (cosine, sine, spans, tok_full, wqkv, normed, heads, qx, kv_all, acc, mixed, wo_full, wide_w, all_gains) = front(
        dims, tokens, wq, wk, wv, wo, w_gate, w_up, gains, freq, lengths
    )
    grad_hidden, g_down, g_wide, g_last, own_resid, layer_out = feed(
        dims, tok_full, mixed, wo_full.reshape(-1, width), wide_w.reshape(width, 2 * hidden), w_down,
        cotangent, all_gains,
    )
    out_down, out_wide, out_wo, out_last, out_gains, tokens_grad = backward(
        dims, grad_hidden, g_down, g_wide, g_last, own_resid, tokens, cotangent, all_gains, acc, qx, kv_all,
        spans, heads, cosine, sine, wo, wqkv, normed,
    )
    (gate_grad, up_grad, wq_grad, wk_grad, wv_grad, down_grad, wo_grad, layer_out, tokens_grad, *gain_grads) = place(
        hidden, out_wide, out_last, out_down, out_wo, layer_out, tokens_grad, out_gains
    )
    return (
        layer_out, tokens_grad, wq_grad, wk_grad, wv_grad, wo_grad, gate_grad, up_grad,
        down_grad, *gain_grads,
    )


def solution(mesh):
    rows = P(("ctx", "fsdp"), None)
    shard = P("fsdp", None)
    gain = P("fsdp")
    return jax.shard_map(
        on_device,
        mesh=mesh,
        in_specs=(rows, P(), shard, shard, shard, shard, shard, shard, shard, gain, gain, gain, gain, rows),
        out_specs=(rows, rows, shard, shard, shard, shard, shard, shard, shard, gain, gain, gain, gain),
        check_vma=False,
    )
```
